32 devices in a mesh: ctx: 8 (over y, x, core), head: 4 (over z).
Axes of the slice: x: 2, y: 2, z: 4, core: 2. Of those that a mesh axis runs over, the one named last changes fastest.
Arguments:
- query_rows: bfloat16 [4096, 16, 128], P('ctx', 'head'), may hold values from -45 to 45
- key_rows: bfloat16 [4096, 16, 128], P('ctx', 'head'), may hold values from -7 to 7
- value_rows: bfloat16 [4096, 16, 128], P('ctx', 'head'), may hold values from -6 to 6
- out_grad: bfloat16 [4096, 16, 128], P('ctx', 'head'), may hold values from -6 to 6
- global_pos: int32 [256], replicated, may hold values from 0 to 4095, as said below
Outputs:
- attn_out: bfloat16 [4096, 16, 128], P('ctx', 'head')
- query_grad: float32 [4096, 16, 128], P('ctx', 'head')
- key_grad: float32 [4096, 16, 128], P('ctx', 'head')
- value_grad: float32 [4096, 16, 128], P('ctx', 'head')
The draws below stay inside these ranges and needn't reach their ends.
Inputs may be any that keep to these rules, and one draw needn't show every extreme that they name: `global_pos`: distinct positions; the aligned block of 512 positions that holds the most of them holds exactly 64, and the other blocks hold counts that differ by at most one.
All inputs are finite; a program needn't handle non-finite values.
Results may differ from the reference program's by a relative error of at most 0.03.
Values may be sent and summed in bfloat16 or wider, within the bound.
No kernel may reach another device: no remote copies, remote signals or barrier semaphores. Data moves between devices by JAX's collectives and lax.ppermute only.
A program may use at most 128 MiB of HBM per device.

```python
import jax
import jax.numpy as jnp
from jax import lax

TOK_DEV = 512
H = 16
DH = 128
HALF = 512
G = 256
SEQ = 4096
GMAX = 64


def place_globals(key):
    base_key = jax.random.fold_in(key, 11)
    blocks = SEQ // TOK_DEV
    busiest = jax.random.randint(jax.random.fold_in(base_key, 1), (), 0, blocks)
    block_order = jax.random.permutation(jax.random.fold_in(base_key, 2), blocks - 1)
    serial = jnp.arange(G)
    beyond = jnp.maximum(serial - GMAX, 0)
    others = (busiest + 1 + block_order[beyond % (blocks - 1)]) % blocks
    owner_block = jnp.where(serial < GMAX, busiest, others)
    within = jnp.where(serial < GMAX, serial, beyond // (blocks - 1))

    def shuffle(number):
        return jax.random.permutation(jax.random.fold_in(base_key, 100 + number), TOK_DEV)
    shuffled = jax.vmap(shuffle)(jnp.arange(blocks))
    positions = owner_block * TOK_DEV + shuffled[owner_block, within]
    mixing = jax.random.permutation(jax.random.fold_in(base_key, 3), G)
    return positions[mixing].astype(jnp.int32)


def query_key_pair(key):
    base_key = jax.random.fold_in(key, 23)
    shape_all = (SEQ, H, DH)
    key_part = 1.6 * jnp.clip(jax.random.normal(jax.random.fold_in(base_key, 1), shape_all), -4.0, 4.0)
    query_part = 1.6 * jnp.clip(jax.random.normal(jax.random.fold_in(base_key, 2), shape_all), -4.0, 4.0)
    return (query_part, key_part)


def draw_query_rows(key, part):
    return query_key_pair(key)[0].astype(jnp.bfloat16)


def draw_key_rows(key, part):
    return query_key_pair(key)[1].astype(jnp.bfloat16)


def draw_global_pos(key, part):
    return place_globals(key)


def shard_levels(key, dims, shards, least, high):
    def one(position, blocks):
        steps = jax.random.uniform(jax.random.fold_in(jax.random.fold_in(key, 6), position), (blocks,), jnp.float32, least / len(shards), high / len(shards))
        return jnp.repeat(jnp.exp(steps), dims[position] // blocks).reshape((-1,) + (1,) * (len(dims) - position - 1))

    gain = one(*shards[0])
    for cut in shards[1:]:
        gain = gain * one(*cut)
    return gain


def gaussian(stream_key, shape, width, limit, shards=(), held_as=jnp.bfloat16):
    values = width * jax.random.normal(stream_key, shape, jnp.float32)
    if shards:
        values = values * shard_levels(stream_key, shape, shards, -0.22, 0.18)
    return jnp.clip(values, -limit, limit).astype(held_as)


def setup_inputs(seed: int = 0) -> dict:
    keys = jax.random.split(jax.random.key(seed), 6)
    return {
        "query_rows": draw_query_rows(jax.random.fold_in(keys[5], 71), 0),
        "key_rows": draw_key_rows(jax.random.fold_in(keys[5], 71), 0),
        "value_rows": gaussian(keys[2], (SEQ, H, DH), 1.0, 6.0, ((0, 8), (1, 4))),
        "out_grad": gaussian(keys[3], (SEQ, H, DH), 1.0, 6.0, ((0, 8), (1, 4))),
        "global_pos": draw_global_pos(jax.random.fold_in(keys[5], 71), 0),
    }


big_negative = -1e30


def head_scores(row_block, col_block, score_scale):
    return jnp.einsum("qhd,khd->hqk", row_block.astype(jnp.float32), col_block.astype(jnp.float32)) * score_scale


def heads_first(array):
    return jnp.transpose(array, (1, 0, 2))


def reference(query_rows, key_rows, value_rows, out_grad, global_pos):
    seq_rows = query_rows.shape[0]
    score_scale = DH ** -0.5
    block_rows = min(512, TOK_DEV)
    span_count = 1 + 2 * HALF // block_rows
    block_count = seq_rows // block_rows
    is_global = jnp.zeros((seq_rows,), dtype=bool).at[global_pos].set(True)
    excluded = jnp.pad(is_global, (HALF, HALF), constant_values=True)
    local_grad = jnp.where(is_global[:, None, None], jnp.zeros_like(out_grad), out_grad)
    pad_rows = ((HALF, HALF), (0, 0), (0, 0))
    key_pad = jnp.pad(key_rows, pad_rows)
    value_pad = jnp.pad(value_rows, pad_rows)
    global_keys = key_rows[global_pos]
    global_values = value_rows[global_pos]
    offsets = jnp.arange(block_rows)

    def one_block(running, number):
        grad_pad, key_grad_g, value_grad_g = running
        start_row = number * block_rows
        row_block = lax.dynamic_slice_in_dim(query_rows, start_row, block_rows, 0)
        grad_block = lax.dynamic_slice_in_dim(local_grad, start_row, block_rows, 0)
        key_sets = [(global_keys, global_values, None, 0)]
        for stretch in range(span_count):
            key_start = start_row + stretch * block_rows
            in_reach = jnp.abs(offsets[None, :] + stretch * block_rows - offsets[:, None] - HALF) <= HALF
            allowed = in_reach & jnp.logical_not(lax.dynamic_slice_in_dim(excluded, key_start, block_rows, 0))[None, :]
            key_sets.append((lax.dynamic_slice_in_dim(key_pad, key_start, block_rows, 0),
                             lax.dynamic_slice_in_dim(value_pad, key_start, block_rows, 0), allowed, key_start))
        logit_sets = []
        for key_block, value_block, allowed, key_start in key_sets:
            logits = head_scores(row_block, key_block, score_scale)
            if allowed is not None:
                logits = jnp.where(allowed[None], logits, big_negative)
            logit_sets.append(logits)
        row_max = logit_sets[0].max(axis=-1)
        for logits in logit_sets[1:]:
            row_max = jnp.maximum(row_max, logits.max(axis=-1))
        row_sum = jnp.zeros_like(row_max)
        for logits in logit_sets:
            row_sum = row_sum + jnp.sum(jnp.exp(logits - row_max[..., None]), axis=-1)
        log_sum = row_max + jnp.log(row_sum)
        local_out = jnp.zeros((block_rows, H, DH), jnp.float32)
        for (key_block, value_block, allowed, key_start), logits in zip(key_sets, logit_sets):
            weights = jnp.exp(logits - log_sum[..., None])
            rounded = lax.optimization_barrier(weights.astype(jnp.bfloat16)).astype(jnp.float32)
            local_out = local_out + jnp.einsum("hqk,khd->qhd", rounded, value_block.astype(jnp.float32))
        row_dot = jnp.sum(grad_block.astype(jnp.float32) * local_out, axis=-1).T
        query_part = jnp.zeros((block_rows, H, DH), jnp.float32)
        for (key_block, value_block, allowed, key_start), logits in zip(key_sets, logit_sets):
            weights = jnp.exp(logits - log_sum[..., None])
            rounded = lax.optimization_barrier(weights.astype(jnp.bfloat16)).astype(jnp.float32)
            grad_weights = jnp.einsum("qhd,khd->hqk", grad_block.astype(jnp.float32), value_block.astype(jnp.float32))
            grad_scores = weights * (grad_weights - row_dot[..., None])
            grad_scores = lax.optimization_barrier(grad_scores.astype(jnp.bfloat16)).astype(jnp.float32)
            query_part = query_part + score_scale * jnp.einsum("hqk,khd->qhd", grad_scores, key_block.astype(jnp.float32))
            key_part = score_scale * jnp.einsum("hqk,qhd->khd", grad_scores, row_block.astype(jnp.float32))
            value_part = jnp.einsum("hqk,qhd->khd", rounded, grad_block.astype(jnp.float32))
            if allowed is None:
                key_grad_g = key_grad_g + key_part
                value_grad_g = value_grad_g + value_part
            else:
                current = lax.dynamic_slice_in_dim(grad_pad, key_start, block_rows, 0)
                grad_pad = lax.dynamic_update_slice_in_dim(
                    grad_pad, current + jnp.stack([key_part, value_part], axis=1), key_start, 0)
        return (grad_pad, key_grad_g, value_grad_g), (local_out, query_part)

    start_state = (jnp.zeros((seq_rows + 2 * HALF, 2, H, DH), jnp.float32),
                   jnp.zeros((G, H, DH), jnp.float32), jnp.zeros((G, H, DH), jnp.float32))
    (grad_pad, key_grad_g, value_grad_g), (local_out, query_local) = lax.scan(
        one_block, start_state, jnp.arange(block_count))
    local_out = local_out.reshape(seq_rows, H, DH)
    query_local = query_local.reshape(seq_rows, H, DH)

    def global_head(operands):
        query_h, grad_h, key_h, value_h = operands
        logits = jnp.dot(query_h, key_h.T, preferred_element_type=jnp.float32) * score_scale
        row_max = jnp.max(logits, axis=-1)
        log_sum = row_max + jnp.log(jnp.sum(jnp.exp(logits - row_max[:, None]), axis=-1))
        weights = jnp.exp(logits - log_sum[:, None])
        out_h = jnp.dot(weights, value_h.astype(jnp.float32), precision=lax.Precision.HIGHEST)
        row_dot = jnp.sum(grad_h.astype(jnp.float32) * out_h, axis=-1)
        rounded = weights.astype(jnp.bfloat16)
        value_grad_h = jnp.dot(rounded.T, grad_h, preferred_element_type=jnp.float32)
        grad_weights = jnp.dot(grad_h, value_h.T, preferred_element_type=jnp.float32)
        grad_scores = (weights * (grad_weights - row_dot[:, None])).astype(jnp.bfloat16)
        query_grad_h = score_scale * jnp.dot(grad_scores, key_h, preferred_element_type=jnp.float32)
        key_grad_h = score_scale * jnp.dot(grad_scores.T, query_h, preferred_element_type=jnp.float32)
        return out_h, query_grad_h, key_grad_h, value_grad_h

    global_out, global_qgrad, key_from_global, value_from_global = lax.map(
        global_head, (heads_first(query_rows[global_pos]), heads_first(out_grad[global_pos]),
                      heads_first(key_rows), heads_first(value_rows)))
    attn_out = local_out.at[global_pos].set(heads_first(global_out)).astype(jnp.bfloat16)
    query_grad = query_local.at[global_pos].add(heads_first(global_qgrad))
    window = grad_pad[HALF:HALF + seq_rows]
    key_grad = (window[:, 0] + heads_first(key_from_global)).at[global_pos].add(key_grad_g)
    value_grad = (window[:, 1] + heads_first(value_from_global)).at[global_pos].add(value_grad_g)
    return attn_out, query_grad, key_grad, value_grad
```

```python
import functools
import math

import jax
import jax.numpy as jnp
from jax import lax
from jax.experimental import pallas as pl
from jax.experimental.pallas import tpu as pltpu
from jax.sharding import PartitionSpec as P

HALF = 512
TILE = 256
NEG = -1e30
LOG2E = 1.0 / math.log(2.0)
VMEM_BYTES = 56 * 1024 * 1024
BF = jnp.bfloat16
F32 = jnp.float32


def nt(a, b):
    return lax.dot_general(a, b, (((1,), (1,)), ((), ())), preferred_element_type=F32)


def nn(a, b):
    return lax.dot_general(a, b, (((1,), (0,)), ((), ())), preferred_element_type=F32)


def wide(column, width):
    return jnp.concatenate([column] * (width // column.shape[1]), axis=1)


def iota(shape, dim):
    return lax.broadcasted_iota(jnp.int32, shape, dim)


def params():
    return pltpu.CompilerParams(vmem_limit_bytes=VMEM_BYTES)


def pack_kernel(heads, slots, q, k, v, g, pos_row, pos_col, qd, kv, slot_rows, wide_rows):
    toks = q.shape[0] // heads
    count = pos_col.shape[0]
    base = lax.axis_index("ctx") * toks
    column = pos_col[...]
    tok = iota((count, toks), 1) + base
    hit = jnp.sum((column == tok).astype(F32), axis=0, keepdims=True)
    rank = jnp.sum(((column >= base) & (column < tok)).astype(F32), axis=0, keepdims=True)
    slot = iota((slots, toks), 0).astype(F32)
    pick = jnp.where((hit > 0) & (rank == slot), 1.0, 0.0).astype(BF)
    tok = iota((toks, count), 0) + base
    hit_column = jnp.sum((pos_row[...] == tok).astype(F32), axis=1, keepdims=True)
    for number, source in enumerate((q, k, v, g)):
        wide_rows[number] = source[...].astype(F32)
        for head in range(heads):
            rows = wide_rows[number, pl.ds(head, toks, stride=heads), :]
            narrow = rows.astype(BF)
            slot_rows[number, head] = nn(pick, narrow).astype(BF)
            if number == 0:
                qd[0, head] = narrow
            elif number == 3:
                qd[1, head] = jnp.where(hit_column > 0, 0.0, rows).astype(BF)
            else:
                kv[number - 1, head] = narrow


def mask_kernel(order, slots, seq_rows, pos_row, pos_col, bias, compact, expand, place):
    toks = place.shape[0]
    count = pos_col.shape[0]
    me = lax.axis_index("ctx")
    base = me * toks
    row, column = pos_row[...], pos_col[...]
    for start in range(0, bias.shape[0], TILE):
        key = iota((TILE, count), 0) + (base - HALF + start)
        hits = jnp.sum((row == key).astype(F32), axis=1, keepdims=True)
        key = key[:, :1]
        out = (hits > 0) | (key < 0) | (key >= seq_rows)
        bias[start : start + TILE, :] = jnp.broadcast_to(jnp.where(out, NEG, 0.0), (TILE, 128))
    tok = iota((toks, count), 0) + base
    hit = jnp.sum((row == tok).astype(F32), axis=1, keepdims=True)
    rank = jnp.sum(((row >= base) & (row < tok)).astype(F32), axis=1, keepdims=True)
    slot = iota((toks, slots), 1).astype(F32)
    place[...] = jnp.where((hit > 0) & (rank == slot), 1.0, 0.0).astype(BF)
    for part, relative in enumerate(order):
        low = (me ^ relative) * toks
        inside = jnp.sum((column < low).astype(jnp.int32), axis=0, keepdims=True)
        held = jnp.sum((column < low + toks).astype(jnp.int32), axis=0, keepdims=True) - inside
        slot = iota((slots, count), 0)
        target = iota((slots, count), 1)
        hot = (target == inside + slot) & (slot < held)
        expand[part * slots : (part + 1) * slots, :] = jnp.where(hot, 1.0, 0.0).astype(BF)
    compact[...] = expand[...].astype(F32).T.astype(BF)


def stats_kernel(scale2, compact, *refs):
    parts, (kv, rows, stats) = refs[:-3], refs[-3:]
    hot = compact[...]
    table = []
    for number in range(4):
        pieces = [part[i, number, 0] for part in parts for i in range(part.shape[0])]
        packed = nn(hot, jnp.concatenate(pieces, axis=0)).astype(BF)
        rows[number, 0] = packed
        table.append(packed)
    queries, _, _, grads = table
    scores = nt(kv[0, 0], queries) * scale2
    top = jnp.max(scores, axis=0, keepdims=True)
    weights = jnp.exp2(scores - top)
    stats[0, 0, 0:1, :] = top
    stats[0, 0, 1:2, :] = jnp.sum(weights, axis=0, keepdims=True)
    stats[0, 0, 2:3, :] = jnp.sum(weights * nt(kv[1, 0], grads), axis=0, keepdims=True)


def window(q_tile, pieces):
    out = []
    for piece in range(2 * HALF // TILE + 1):
        start = q_tile * TILE + piece * TILE
        out.append((start // HALF, start % HALF, start, piece))
    return out


def band(scores, piece):
    if piece == 0:
        return jnp.where(iota(scores.shape, 0) >= iota(scores.shape, 1), scores, NEG)
    if piece == 2 * HALF // TILE:
        return jnp.where(iota(scores.shape, 0) <= iota(scores.shape, 1), scores, NEG)
    return scores


def forward_kernel(scale2, qd, left, own, right, rows, bias, out, log_dot, score_buf):
    blocks = (left, own, right)
    toks = own.shape[2]
    value_t = [block[1, 0].T for block in blocks]
    global_t = rows[2, 0].T
    grad_t = qd[1, 0].T
    global_keys = rows[1, 0]
    for q_tile in range(toks // TILE):
        lanes = slice(q_tile * TILE, (q_tile + 1) * TILE)
        query = qd[0, 0, lanes, :]
        plan = window(q_tile, toks)
        top = None
        for which, offset, start, piece in plan:
            scores = nt(blocks[which][0, 0, offset : offset + TILE, :], query) * scale2
            scores = band(scores + wide(bias[start : start + TILE, :], TILE), piece)
            score_buf[piece * TILE : (piece + 1) * TILE, :] = scores
            best = jnp.max(scores, axis=0, keepdims=True)
            top = best if top is None else jnp.maximum(top, best)
        scores_g = nt(global_keys, query) * scale2
        top = jnp.maximum(top, jnp.max(scores_g, axis=0, keepdims=True))
        weights = jnp.exp2(scores_g - top)
        total = jnp.sum(weights, axis=0, keepdims=True)
        acc = nn(global_t, weights.astype(BF))
        for which, offset, start, piece in plan:
            weights = jnp.exp2(score_buf[piece * TILE : (piece + 1) * TILE, :] - top)
            total = total + jnp.sum(weights, axis=0, keepdims=True)
            acc = acc + nn(value_t[which][:, offset : offset + TILE], weights.astype(BF))
        acc = acc / total
        log_dot[0, 0:1, lanes] = top + jnp.log2(total)
        log_dot[0, 1:2, lanes] = jnp.sum(grad_t[:, lanes].astype(F32) * acc, axis=0, keepdims=True)
        out[0, lanes, :] = acc.T.astype(BF)


def backward_kernel(
    scale, scale2, slots, qd, left, own, right, rows, bias, log_dot, stats, expand, dq, dkv, sums
):
    blocks = (left, own, right)
    toks = own.shape[2]
    key_t = [block[0, 0].T for block in blocks]
    g_query, g_key, g_value, g_grad = (rows[i, 0] for i in range(4))
    g_key_t = g_key.T
    tops = stats[:, 0, 0:1, :]
    top = jnp.max(tops, axis=0)
    factor = jnp.exp2(tops - top[None])
    total = jnp.sum(stats[:, 0, 1:2, :] * factor, axis=0)
    g_dot = jnp.sum(stats[:, 0, 2:3, :] * factor, axis=0) / total
    g_log = top + jnp.log2(total)
    weights = jnp.exp2(nt(own[0, 0], g_query) * scale2 - g_log)
    narrow = weights.astype(BF)
    slopes = (weights * (nt(own[1, 0], g_grad) - g_dot)).astype(BF)
    dkv[0, 0] = nn(slopes, g_query) * scale
    dkv[1, 0] = nn(narrow, g_grad)
    g_out_t = nn(own[1, 0].T, narrow)
    g_dq_t = nn(key_t[1], slopes) * scale
    g_dk = jnp.zeros(g_key.shape, F32)
    g_dv = jnp.zeros(g_key.shape, F32)
    for q_tile in range(toks // TILE):
        lanes = slice(q_tile * TILE, (q_tile + 1) * TILE)
        query = qd[0, 0, lanes, :]
        grad = qd[1, 0, lanes, :]
        log_sum = log_dot[0, 0:1, lanes]
        dot = log_dot[0, 1:2, lanes]
        weights = jnp.exp2(nt(g_key, query) * scale2 - log_sum)
        slopes = (weights * (nt(g_value, grad) - dot)).astype(BF)
        g_dv = g_dv + nn(weights.astype(BF), grad)
        g_dk = g_dk + nn(slopes, query)
        acc = nn(g_key_t, slopes)
        for which, offset, start, piece in window(q_tile, toks):
            span = slice(offset, offset + TILE)
            scores = nt(blocks[which][0, 0, span, :], query) * scale2
            scores = band(scores + wide(bias[start : start + TILE, :], TILE), piece)
            weights = jnp.exp2(scores - log_sum)
            slopes = (weights * (nt(blocks[which][1, 0, span, :], grad) - dot)).astype(BF)
            acc = acc + nn(key_t[which][:, span], slopes)
            if which == 1:
                dkv[0, 0, span, :] += nn(slopes, query) * scale
                dkv[1, 0, span, :] += nn(weights.astype(BF), grad)
        dq[0, lanes, :] = (acc * scale).T
    hot = expand[...]
    for number, table in enumerate((g_out_t, g_dq_t, g_dk * scale, g_dv)):
        spread = nt if number < 2 else nn
        slot_rows = spread(hot, table.astype(BF)).astype(BF)
        for part in range(sums.shape[0]):
            sums[part, number, 0] = slot_rows[part * slots : (part + 1) * slots, :]


def rim_kernel(scale, scale2, own, bias, qd_low, qd_high, log_low, log_high, partial, dkv):
    toks = own.shape[2]
    for k_tile in range(toks // TILE):
        span = slice(k_tile * TILE, (k_tile + 1) * TILE)
        key = own[0, 0, span, :]
        value = own[1, 0, span, :]
        key_bias = wide(bias[HALF + k_tile * TILE : HALF + (k_tile + 1) * TILE, :], TILE)
        dk = jnp.zeros(key.shape, F32)
        dv = jnp.zeros(key.shape, F32)
        for low in (True, False):
            qd, log_dot = (qd_low, log_low) if low else (qd_high, log_high)
            tiles = range(k_tile, toks // TILE) if low else range(k_tile + 1)
            for q_tile in tiles:
                lanes = slice(q_tile * TILE, (q_tile + 1) * TILE)
                query = qd[0, 0, lanes, :]
                grad = qd[1, 0, lanes, :]
                scores = nt(key, query) * scale2 + key_bias
                if q_tile == k_tile:
                    scores = band(scores, 2 * HALF // TILE if low else 0)
                weights = jnp.exp2(scores - log_dot[0, 0:1, lanes])
                slopes = weights * (nt(value, grad) - log_dot[0, 1:2, lanes])
                dk = dk + nn(slopes.astype(BF), query)
                dv = dv + nn(weights.astype(BF), grad)
        dkv[0, 0, span, :] = partial[0, 0, span, :] + dk * scale
        dkv[1, 0, span, :] = partial[1, 0, span, :] + dv


def final_kernel(place, out, dq, dkv, sums, attn, query_grad, key_grad, value_grad, wide_rows):
    heads, toks = out.shape[0], out.shape[1]
    hot = place[...]
    is_global = jnp.sum(hot.astype(F32), axis=1, keepdims=True) > 0
    for head in range(heads):
        rows = pl.ds(head, toks, stride=heads)
        wide_rows[rows, :] = jnp.where(is_global, nn(hot, sums[0, head]), out[head].astype(F32))
        query_grad[rows, :] = dq[head] + nn(hot, sums[1, head])
        key_grad[rows, :] = dkv[0, head] + nn(hot, sums[2, head])
        value_grad[rows, :] = dkv[1, head] + nn(hot, sums[3, head])
    attn[...] = wide_rows[...].astype(BF)


def cost(flops, moved, exps=0):
    return pl.CostEstimate(flops=int(flops), bytes_accessed=int(moved), transcendentals=int(exps))


def struct(shape, dtype):
    return jax.ShapeDtypeStruct(shape, dtype)


def whole(shape):
    return pl.BlockSpec(shape, lambda head: (0,) * len(shape))


def per_head(shape, dim):
    block = tuple(1 if i == dim else size for i, size in enumerate(shape))
    return pl.BlockSpec(block, lambda head: tuple(head if i == dim else 0 for i in range(len(shape))))


def shards(query_rows, key_rows, value_rows, out_grad, global_pos):
    toks, heads, width = query_rows.shape
    count = global_pos.shape[0]
    devices = lax.axis_size("ctx")
    slots = max(16, 2 * count // devices)
    scale = width ** (-0.5)
    scale2 = scale * LOG2E
    bits = devices.bit_length() - 1
    doubling = list(range(1, bits)) + [0]
    order = [0]
    for bit in doubling:
        order = order + [one | (1 << bit) for one in order]
    pos_row = global_pos.reshape(1, count)
    pos_col = global_pos.reshape(count, 1)
    flat = [x.reshape(toks * heads, width) for x in (query_rows, key_rows, value_rows, out_grad)]

    def swap(value, bit):
        pairs = [(i, i ^ (1 << bit)) for i in range(devices)]
        return lax.ppermute(value, "ctx", pairs)

    def from_low(value):
        return lax.ppermute(value, "ctx", [(i, i + 1) for i in range(devices - 1)])

    def from_high(value):
        return lax.ppermute(value, "ctx", [(i + 1, i) for i in range(devices - 1)])

    pair_shape = (2, heads, toks, width)
    slot_shape = (4, heads, slots, width)
    qd, kv, slot_rows = pl.pallas_call(
        functools.partial(pack_kernel, heads, slots),
        out_shape=(struct(pair_shape, BF), struct(pair_shape, BF), struct(slot_shape, BF)),
        scratch_shapes=[pltpu.VMEM((4, toks * heads, width), F32)],
        compiler_params=params(),
        name="pack",
    )(*flat, pos_row, pos_col)

    held = [slot_rows[None]]
    kv_low, kv_high = from_low(kv), from_high(kv)
    for bit in doubling:
        held.append(swap(jnp.concatenate(held, axis=0) if len(held) > 1 else held[0], bit))
    qd_low, qd_high = from_low(qd), from_high(qd)

    bias, compact, expand, place = pl.pallas_call(
        functools.partial(mask_kernel, order, slots, toks * devices),
        out_shape=(
            struct((toks + 2 * HALF, 128), F32),
            struct((count, devices * slots), BF),
            struct((devices * slots, count), BF),
            struct((toks, slots), BF),
        ),
        compiler_params=params(),
        name="masks",
    )(pos_row, pos_col)

    row_shape = (4, heads, count, width)
    rows, stats = pl.pallas_call(
        functools.partial(stats_kernel, scale2),
        grid=(heads,),
        in_specs=[whole(compact.shape)]
        + [per_head(part.shape, 2) for part in held]
        + [per_head(pair_shape, 1)],
        out_specs=(per_head(row_shape, 1), per_head((1, heads, 3, count), 1)),
        out_shape=(struct(row_shape, BF), struct((1, heads, 3, count), F32)),
        compiler_params=params(),
        cost_estimate=cost(2.7e9, 4e6),
        name="global_stats",
    )(compact, *held, kv)

    for bit in range(bits):
        stats = jnp.concatenate([stats, swap(stats, bit)], axis=0)

    head_specs = [
        per_head(pair_shape, 1),
        per_head(pair_shape, 1),
        per_head(pair_shape, 1),
        per_head(pair_shape, 1),
        per_head(row_shape, 1),
        whole(bias.shape),
    ]
    out, log_dot = pl.pallas_call(
        functools.partial(forward_kernel, scale2),
        grid=(heads,),
        in_specs=head_specs,
        out_specs=(per_head((heads, toks, width), 0), per_head((heads, 2, toks), 0)),
        out_shape=(struct((heads, toks, width), BF), struct((heads, 2, toks), F32)),
        scratch_shapes=[pltpu.VMEM((2 * HALF + TILE, TILE), F32)],
        compiler_params=params(),
        cost_estimate=cost(4e9, 5e6, 3e6),
        name="forward",
    )(qd, kv_low, kv, kv_high, rows, bias)
    log_low, log_high = from_low(log_dot), from_high(log_dot)

    sum_shape = (devices, 4, heads, slots, width)
    dq, partial, sums = pl.pallas_call(
        functools.partial(backward_kernel, scale, scale2, slots),
        grid=(heads,),
        in_specs=head_specs
        + [per_head(log_dot.shape, 0), per_head(stats.shape, 1), whole(expand.shape)],
        out_specs=(
            per_head((heads, toks, width), 0),
            per_head(pair_shape, 1),
            per_head(sum_shape, 2),
        ),
        out_shape=(
            struct((heads, toks, width), F32),
            struct(pair_shape, F32),
            struct(sum_shape, BF),
        ),
        compiler_params=params(),
        cost_estimate=cost(8e9, 9e6, 3e6),
        name="backward",
    )(qd, kv_low, kv, kv_high, rows, bias, log_dot, stats, expand)

    for bit in reversed(doubling):
        half = sums.shape[0] // 2
        sums = sums[:half] + swap(sums[half:], bit)

    dkv = pl.pallas_call(
        functools.partial(rim_kernel, scale, scale2),
        grid=(heads,),
        in_specs=[
            per_head(pair_shape, 1),
            whole(bias.shape),
            per_head(pair_shape, 1),
            per_head(pair_shape, 1),
            per_head(log_dot.shape, 0),
            per_head(log_dot.shape, 0),
            per_head(pair_shape, 1),
        ],
        out_specs=per_head(pair_shape, 1),
        out_shape=struct(pair_shape, F32),
        compiler_params=params(),
        cost_estimate=cost(4e9, 8e6, 2e6),
        name="rim",
    )(kv, bias, qd_low, qd_high, log_low, log_high, partial)

    flat_shape = (toks * heads, width)
    outs = pl.pallas_call(
        final_kernel,
        out_shape=(
            struct(flat_shape, BF),
            struct(flat_shape, F32),
            struct(flat_shape, F32),
            struct(flat_shape, F32),
        ),
        scratch_shapes=[pltpu.VMEM(flat_shape, F32)],
        compiler_params=params(),
        name="final",
    )(place, out, dq, dkv, sums[0])
    return tuple(x.reshape(toks, heads, width) for x in outs)


def solution(mesh):
    spec = P("ctx", "head", None)
    return jax.shard_map(
        shards,
        mesh=mesh,
        in_specs=(spec, spec, spec, spec, P()),
        out_specs=(spec, spec, spec, spec),
        check_vma=False,
    )
```

```python
import functools
import math

import jax
import jax.numpy as jnp
from jax import lax
from jax.experimental import pallas as pl
from jax.experimental.pallas import tpu as pltpu
from jax.sharding import PartitionSpec as P

HALF = 512
TILE = 256
NEG = -1e30
LOG2E = 1.0 / math.log(2.0)
VMEM_BYTES = 63 * 1024 * 1024
BF = jnp.bfloat16
F32 = jnp.float32


def nt(a, b):
    return lax.dot_general(a, b, (((1,), (1,)), ((), ())), preferred_element_type=F32)


def nn(a, b):
    return lax.dot_general(a, b, (((1,), (0,)), ((), ())), preferred_element_type=F32)


def wide(column, width):
    return jnp.concatenate([column] * (width // column.shape[1]), axis=1)


def iota(shape, dim):
    return lax.broadcasted_iota(jnp.int32, shape, dim)


def params():
    return pltpu.CompilerParams(vmem_limit_bytes=VMEM_BYTES)


def as_column(row):
    return jnp.broadcast_to(row, (128, row.shape[1])).T[:, :1]


def pack_keys_kernel(heads, k, v, kv, wide_rows):
    toks = k.shape[0] // heads
    for number, source in enumerate((k, v)):
        wide_rows[number] = source[...].astype(F32)
        for head in range(heads):
            kv[number, head] = wide_rows[number, pl.ds(head, toks, stride=heads), :].astype(BF)


def pack_queries_kernel(heads, slots, q, g, kv, pos_row, qd, slot_rows, wide_rows, acc):
    step = pl.program_id(0)
    toks = q.shape[0] // heads
    row = pos_row[...]
    count = row.shape[1]
    base = lax.axis_index("ctx") * (toks * pl.num_programs(0))
    column = as_column(row)
    tok = iota((count, toks), 1) + (base + step * toks)
    hit = jnp.sum((column == tok).astype(F32), axis=0, keepdims=True)
    rank = jnp.sum(((column >= base) & (column < tok)).astype(F32), axis=0, keepdims=True)
    slot = iota((slots, toks), 0).astype(F32)
    pick = jnp.where((hit > 0) & (rank == slot), 1.0, 0.0).astype(BF)
    tok = iota((toks, count), 0) + (base + step * toks)
    hit_column = jnp.sum((row == tok).astype(F32), axis=1, keepdims=True)
    tables = [[], [kv[0, h] for h in range(heads)], [kv[1, h] for h in range(heads)], []]
    for number, source in ((0, q), (3, g)):
        wide_rows[number // 3] = source[...].astype(F32)
        for head in range(heads):
            rows = wide_rows[number // 3, pl.ds(head, toks, stride=heads), :]
            tables[number].append(rows.astype(BF))
            if number == 0:
                qd[0, head] = rows.astype(BF)
            else:
                qd[1, head] = jnp.where(hit_column > 0, 0.0, rows).astype(BF)
    for number in range(4):
        found = nn(pick, jnp.concatenate(tables[number], axis=1))
        for head in range(heads):
            part = found[:, head * 128 : (head + 1) * 128]
            acc[number, head] = jnp.where(step == 0, part, acc[number, head] + part)

    @pl.when(step == pl.num_programs(0) - 1)
    def _():
        slot_rows[...] = acc[...].astype(BF)


def mask_kernel(orders, slots, seq_rows, pos_row, bias, compact, expand, place):
    toks = place.shape[0]
    me = lax.axis_index("ctx")
    base = me * toks
    row = pos_row[...]
    count = row.shape[1]
    column = as_column(row)
    for start in range(0, bias.shape[0], TILE):
        key = iota((TILE, count), 0) + (base - HALF + start)
        hits = jnp.sum((row == key).astype(F32), axis=1, keepdims=True)
        key = key[:, :1]
        out = (hits > 0) | (key < 0) | (key >= seq_rows)
        bias[start : start + TILE, :] = jnp.broadcast_to(jnp.where(out, NEG, 0.0), (TILE, 128))
    tok = iota((toks, count), 0) + base
    hit = jnp.sum((row == tok).astype(F32), axis=1, keepdims=True)
    rank = jnp.sum(((row >= base) & (row < tok)).astype(F32), axis=1, keepdims=True)
    slot = iota((toks, slots), 1).astype(F32)
    place[...] = jnp.where((hit > 0) & (rank == slot), 1.0, 0.0).astype(BF)
    for part, (first, second) in enumerate(zip(*orders)):
        low = (me ^ jnp.where(me % 2 == 0, first, second)) * toks
        inside = jnp.sum((column < low).astype(jnp.int32), axis=0, keepdims=True)
        held = jnp.sum((column < low + toks).astype(jnp.int32), axis=0, keepdims=True) - inside
        slot = iota((slots, count), 0)
        target = iota((slots, count), 1)
        hot = (target == inside + slot) & (slot < held)
        expand[part * slots : (part + 1) * slots, :] = jnp.where(hot, 1.0, 0.0).astype(BF)
    compact[...] = expand[...].astype(F32).T.astype(BF)


def stats_kernel(scale2, compact, *refs):
    parts, (kv, rows, stats) = refs[:-3], refs[-3:]
    pieces = []
    for part in parts:
        for i in range(part.shape[0]):
            pieces.append(jnp.concatenate([part[i, number, 0] for number in range(4)], axis=1))
    packed = nn(compact[...], jnp.concatenate(pieces, axis=0)).astype(BF)
    width = kv.shape[3]
    table = [packed[:, number * width : (number + 1) * width] for number in range(4)]
    for number in range(4):
        rows[number, 0] = table[number]
    queries, _, _, grads = table
    scores = nt(kv[0, 0], queries) * scale2
    top = jnp.max(scores, axis=0, keepdims=True)
    weights = jnp.exp2(scores - top)
    stats[0, 0, 0:1, :] = top
    stats[0, 0, 1:2, :] = jnp.sum(weights, axis=0, keepdims=True)
    stats[0, 0, 2:3, :] = jnp.sum(weights * nt(kv[1, 0], grads), axis=0, keepdims=True)


def window(q_tile):
    out = []
    for piece in range(2 * HALF // TILE + 1):
        start = q_tile * TILE + piece * TILE
        out.append((start // HALF, start % HALF, start, piece))
    return out


def band(scores, piece):
    if piece == 0:
        return jnp.where(iota(scores.shape, 0) >= iota(scores.shape, 1), scores, NEG)
    if piece == 2 * HALF // TILE:
        return jnp.where(iota(scores.shape, 0) <= iota(scores.shape, 1), scores, NEG)
    return scores


def forward_kernel(scale2, qd, left, own, right, rows, bias, out, log_dot, score_buf):
    blocks = (left, own, right)
    toks = own.shape[2]
    value_t = [block[1, 0].T for block in blocks]
    global_t = rows[2, 0].T
    grad_t = qd[1, 0].T
    global_keys = rows[1, 0]
    for q_tile in range(toks // TILE):
        lanes = slice(q_tile * TILE, (q_tile + 1) * TILE)
        query = qd[0, 0, lanes, :]
        plan = window(q_tile)
        top = None
        for which, offset, start, piece in plan:
            scores = nt(blocks[which][0, 0, offset : offset + TILE, :], query) * scale2
            scores = band(scores + wide(bias[start : start + TILE, :], TILE), piece)
            score_buf[piece * TILE : (piece + 1) * TILE, :] = scores
            best = jnp.max(scores, axis=0, keepdims=True)
            top = best if top is None else jnp.maximum(top, best)
        scores_g = nt(global_keys, query) * scale2
        top = jnp.maximum(top, jnp.max(scores_g, axis=0, keepdims=True))
        weights = jnp.exp2(scores_g - top)
        total = jnp.sum(weights, axis=0, keepdims=True)
        acc = nn(global_t, weights.astype(BF))
        for which, offset, start, piece in plan:
            weights = jnp.exp2(score_buf[piece * TILE : (piece + 1) * TILE, :] - top)
            total = total + jnp.sum(weights, axis=0, keepdims=True)
            acc = acc + nn(value_t[which][:, offset : offset + TILE], weights.astype(BF))
        acc = acc / total
        log_dot[0, 0:1, lanes] = top + jnp.log2(total)
        log_dot[0, 1:2, lanes] = jnp.sum(grad_t[:, lanes].astype(F32) * acc, axis=0, keepdims=True)
        out[0, lanes, :] = acc.T.astype(BF)


def global_kernel(scale, scale2, slots, qd, own, rows, log_dot, stats, expand, dkv, sums):
    toks = own.shape[2]
    g_query, g_key, g_value, g_grad = (rows[i, 0] for i in range(4))
    tops = stats[:, 0, 0:1, :]
    top = jnp.max(tops, axis=0)
    factor = jnp.exp2(tops - top[None])
    total = jnp.sum(stats[:, 0, 1:2, :] * factor, axis=0)
    g_dot = jnp.sum(stats[:, 0, 2:3, :] * factor, axis=0) / total
    g_log = top + jnp.log2(total)
    weights = jnp.exp2(nt(own[0, 0], g_query) * scale2 - g_log)
    narrow = weights.astype(BF)
    slopes = (weights * (nt(own[1, 0], g_grad) - g_dot)).astype(BF)
    dkv[0, 0] = nn(slopes, g_query) * scale
    dkv[1, 0] = nn(narrow, g_grad)
    g_out = nn(own[1, 0].T, narrow).T
    g_dq = (nn(own[0, 0].T, slopes) * scale).T
    g_dk = jnp.zeros(g_key.shape, F32)
    g_dv = jnp.zeros(g_key.shape, F32)
    for q_tile in range(toks // TILE):
        lanes = slice(q_tile * TILE, (q_tile + 1) * TILE)
        query = qd[0, 0, lanes, :]
        grad = qd[1, 0, lanes, :]
        weights = jnp.exp2(nt(g_key, query) * scale2 - log_dot[0, 0:1, lanes])
        slopes = (weights * (nt(g_value, grad) - log_dot[0, 1:2, lanes])).astype(BF)
        g_dv = g_dv + nn(weights.astype(BF), grad)
        g_dk = g_dk + nn(slopes, query)
    tables = [table.astype(BF) for table in (g_out, g_dq, g_dk * scale, g_dv)]
    spread = nn(expand[...], jnp.concatenate(tables, axis=1)).astype(BF)
    width = own.shape[3]
    for part in range(sums.shape[0]):
        for number in range(4):
            sums[part, number, 0] = spread[
                part * slots : (part + 1) * slots, number * width : (number + 1) * width
            ]


def backward_kernel(scale, scale2, qd, left, own, right, rows, bias, log_dot, before, dq, dkv):
    blocks = (left, own, right)
    toks = own.shape[2]
    key_t = [block[0, 0].T for block in blocks]
    g_key, g_value = rows[1, 0], rows[2, 0]
    g_key_t = g_key.T
    dkv[...] = before[...]
    for q_tile in range(toks // TILE):
        lanes = slice(q_tile * TILE, (q_tile + 1) * TILE)
        query = qd[0, 0, lanes, :]
        grad = qd[1, 0, lanes, :]
        log_sum = log_dot[0, 0:1, lanes]
        dot = log_dot[0, 1:2, lanes]
        weights = jnp.exp2(nt(g_key, query) * scale2 - log_sum)
        slopes = (weights * (nt(g_value, grad) - dot)).astype(BF)
        acc = nn(g_key_t, slopes)
        for which, offset, start, piece in window(q_tile):
            span = slice(offset, offset + TILE)
            scores = nt(blocks[which][0, 0, span, :], query) * scale2
            scores = band(scores + wide(bias[start : start + TILE, :], TILE), piece)
            weights = jnp.exp2(scores - log_sum)
            slopes = (weights * (nt(blocks[which][1, 0, span, :], grad) - dot)).astype(BF)
            acc = acc + nn(key_t[which][:, span], slopes)
            if which == 1:
                dkv[0, 0, span, :] += nn(slopes, query) * scale
                dkv[1, 0, span, :] += nn(weights.astype(BF), grad)
        dq[0, lanes, :] = (acc * scale).T


def rim_kernel(scale, scale2, own, bias, qd_low, qd_high, log_low, log_high, partial, dkv):
    toks = own.shape[2]
    for k_tile in range(toks // TILE):
        span = slice(k_tile * TILE, (k_tile + 1) * TILE)
        key = own[0, 0, span, :]
        value = own[1, 0, span, :]
        key_bias = wide(bias[HALF + k_tile * TILE : HALF + (k_tile + 1) * TILE, :], TILE)
        dk = jnp.zeros(key.shape, F32)
        dv = jnp.zeros(key.shape, F32)
        for low in (True, False):
            qd, log_dot = (qd_low, log_low) if low else (qd_high, log_high)
            tiles = range(k_tile, toks // TILE) if low else range(k_tile + 1)
            for q_tile in tiles:
                lanes = slice(q_tile * TILE, (q_tile + 1) * TILE)
                query = qd[0, 0, lanes, :]
                grad = qd[1, 0, lanes, :]
                scores = nt(key, query) * scale2 + key_bias
                if q_tile == k_tile:
                    scores = band(scores, 2 * HALF // TILE if low else 0)
                weights = jnp.exp2(scores - log_dot[0, 0:1, lanes])
                slopes = weights * (nt(value, grad) - log_dot[0, 1:2, lanes])
                dk = dk + nn(slopes.astype(BF), query)
                dv = dv + nn(weights.astype(BF), grad)
        dkv[0, 0, span, :] = partial[0, 0, span, :] + dk * scale
        dkv[1, 0, span, :] = partial[1, 0, span, :] + dv


def final_kernel(place, out, dq, dkv, sums, attn, query_grad, key_grad, value_grad, wide_rows):
    heads, toks = out.shape[0], out.shape[1]
    hot = place[...]
    is_global = jnp.sum(hot.astype(F32), axis=1, keepdims=True) > 0
    for head in range(heads):
        rows = pl.ds(head, toks, stride=heads)
        wide_rows[rows, :] = jnp.where(is_global, nn(hot, sums[0, head]), out[head].astype(F32))
        query_grad[rows, :] = dq[head] + nn(hot, sums[1, head])
        key_grad[rows, :] = dkv[0, head] + nn(hot, sums[2, head])
        value_grad[rows, :] = dkv[1, head] + nn(hot, sums[3, head])
    attn[...] = wide_rows[...].astype(BF)


def cost(flops, moved, exps=0):
    return pl.CostEstimate(flops=int(flops), bytes_accessed=int(moved), transcendentals=int(exps))


def struct(shape, dtype):
    return jax.ShapeDtypeStruct(shape, dtype)


def whole(shape):
    return pl.BlockSpec(shape, lambda head: (0,) * len(shape))


def per_head(shape, dim):
    block = tuple(1 if i == dim else size for i, size in enumerate(shape))
    return pl.BlockSpec(block, lambda head: tuple(head if i == dim else 0 for i in range(len(shape))))


def shards(query_rows, key_rows, value_rows, out_grad, global_pos):
    toks, heads, width = query_rows.shape
    count = global_pos.shape[0]
    devices = lax.axis_size("ctx")
    slots = max(16, 2 * count // devices)
    scale = width ** (-0.5)
    scale2 = scale * LOG2E
    bits = devices.bit_length() - 1
    ways = [list(range(1, bits)) + [0], list(range(bits - 1, 0, -1)) + [0]]
    orders = []
    for way in ways:
        order = [0]
        for bit in way[:-1]:
            order = order + [one | (1 << bit) for one in order]
        orders.append(order)
    orders = [mine + [one | 1 for one in other] for mine, other in (orders, orders[::-1])]
    pos_row = global_pos.reshape(1, count)
    q_flat, k_flat, v_flat, g_flat = (
        x.reshape(toks * heads, width) for x in (query_rows, key_rows, value_rows, out_grad)
    )

    def swap(value, stage):
        pairs = [(i, i ^ (1 << ways[i % 2][stage])) for i in range(devices)]
        return lax.ppermute(value, "ctx", pairs)

    def from_low(value):
        return lax.ppermute(value, "ctx", [(i, i + 1) for i in range(devices - 1)])

    def from_high(value):
        return lax.ppermute(value, "ctx", [(i + 1, i) for i in range(devices - 1)])

    def after(value, earlier):
        return lax.optimization_barrier((value, earlier))[0]

    pair_shape = (2, heads, toks, width)
    slot_shape = (4, heads, slots, width)
    steps = 4
    flat_spec = pl.BlockSpec((toks * heads // steps, width), lambda i: (i, 0))
    pair_spec = pl.BlockSpec((2, heads, toks // steps, width), lambda i: (0, 0, i, 0))
    wide_pair = pltpu.VMEM((2, toks * heads // steps, width), F32)
    kv = pl.pallas_call(
        functools.partial(pack_keys_kernel, heads),
        grid=(steps,),
        in_specs=[flat_spec, flat_spec],
        out_specs=pair_spec,
        out_shape=struct(pair_shape, BF),
        scratch_shapes=[wide_pair],
        compiler_params=params(),
        name="pack_keys",
    )(k_flat, v_flat)
    kv_low, kv_high = from_low(kv), from_high(kv)

    qd, slot_rows = pl.pallas_call(
        functools.partial(pack_queries_kernel, heads, slots),
        grid=(steps,),
        in_specs=[flat_spec, flat_spec, pair_spec, whole((1, count))],
        out_specs=(pair_spec, whole(slot_shape)),
        out_shape=(struct(pair_shape, BF), struct(slot_shape, BF)),
        scratch_shapes=[wide_pair, pltpu.VMEM(slot_shape, F32)],
        compiler_params=params(),
        name="pack_queries",
    )(q_flat, g_flat, kv, pos_row)

    held = [slot_rows[None]]
    for stage in range(bits):
        send = jnp.concatenate(held, axis=0) if len(held) > 1 else held[0]
        if stage == bits - 1:
            send = after(send, (kv_low, kv_high))
        held.append(swap(send, stage))
    qd_late = after(qd, (kv_low, kv_high))
    qd_low, qd_high = from_low(qd_late), from_high(qd_late)

    bias, compact, expand, place = pl.pallas_call(
        functools.partial(mask_kernel, orders, slots, toks * devices),
        out_shape=(
            struct((toks + 2 * HALF, 128), F32),
            struct((count, devices * slots), BF),
            struct((devices * slots, count), BF),
            struct((toks, slots), BF),
        ),
        compiler_params=params(),
        name="masks",
    )(pos_row)

    row_shape = (4, heads, count, width)
    rows, stats = pl.pallas_call(
        functools.partial(stats_kernel, scale2),
        grid=(heads,),
        in_specs=[whole(compact.shape)]
        + [per_head(part.shape, 2) for part in held]
        + [per_head(pair_shape, 1)],
        out_specs=(per_head(row_shape, 1), per_head((1, heads, 3, count), 1)),
        out_shape=(struct(row_shape, BF), struct((1, heads, 3, count), F32)),
        compiler_params=params(),
        cost_estimate=cost(2.7e9, 4e6),
        name="global_stats",
    )(compact, *held, kv)

    for stage in range(bits):
        stats = jnp.concatenate([stats, swap(stats, stage)], axis=0)

    head_specs = [
        per_head(pair_shape, 1),
        per_head(pair_shape, 1),
        per_head(pair_shape, 1),
        per_head(pair_shape, 1),
        per_head(row_shape, 1),
        whole(bias.shape),
    ]
    out, log_dot = pl.pallas_call(
        functools.partial(forward_kernel, scale2),
        grid=(heads,),
        in_specs=head_specs,
        out_specs=(per_head((heads, toks, width), 0), per_head((heads, 2, toks), 0)),
        out_shape=(struct((heads, toks, width), BF), struct((heads, 2, toks), F32)),
        scratch_shapes=[pltpu.VMEM((2 * HALF + TILE, TILE), F32)],
        compiler_params=params(),
        cost_estimate=cost(4e9, 5e6, 3e6),
        name="forward",
    )(qd, kv_low, kv, kv_high, rows, bias)
    log_low, log_high = from_low(log_dot), from_high(log_dot)

    sum_shape = (devices, 4, heads, slots, width)
    dkv, sums = pl.pallas_call(
        functools.partial(global_kernel, scale, scale2, slots),
        grid=(heads,),
        in_specs=[
            per_head(pair_shape, 1),
            per_head(pair_shape, 1),
            per_head(row_shape, 1),
            per_head(log_dot.shape, 0),
            per_head(stats.shape, 1),
            whole(expand.shape),
        ],
        out_specs=(per_head(pair_shape, 1), per_head(sum_shape, 2)),
        out_shape=(struct(pair_shape, F32), struct(sum_shape, BF)),
        compiler_params=params(),
        cost_estimate=cost(4e9, 9e6, 1e6),
        name="globals",
    )(qd, kv, rows, log_dot, stats, expand)

    for stage in reversed(range(bits)):
        half = sums.shape[0] // 2
        sums = sums[:half] + swap(sums[half:], stage)

    dq, dkv = pl.pallas_call(
        functools.partial(backward_kernel, scale, scale2),
        grid=(heads,),
        in_specs=head_specs + [per_head(log_dot.shape, 0), per_head(pair_shape, 1)],
        out_specs=(per_head((heads, toks, width), 0), per_head(pair_shape, 1)),
        out_shape=(struct((heads, toks, width), F32), struct(pair_shape, F32)),
        compiler_params=params(),
        cost_estimate=cost(8e9, 9e6, 3e6),
        name="backward",
    )(qd, kv_low, kv, kv_high, rows, bias, after(log_dot, (qd_low, qd_high)), dkv)

    dkv = pl.pallas_call(
        functools.partial(rim_kernel, scale, scale2),
        grid=(heads,),
        in_specs=[
            per_head(pair_shape, 1),
            whole(bias.shape),
            per_head(pair_shape, 1),
            per_head(pair_shape, 1),
            per_head(log_dot.shape, 0),
            per_head(log_dot.shape, 0),
            per_head(pair_shape, 1),
        ],
        out_specs=per_head(pair_shape, 1),
        out_shape=struct(pair_shape, F32),
        compiler_params=params(),
        cost_estimate=cost(4e9, 8e6, 2e6),
        name="rim",
    )(kv, bias, qd_low, qd_high, log_low, log_high, dkv)

    flat_shape = (toks * heads, width)
    outs = pl.pallas_call(
        final_kernel,
        out_shape=(
            struct(flat_shape, BF),
            struct(flat_shape, F32),
            struct(flat_shape, F32),
            struct(flat_shape, F32),
        ),
        scratch_shapes=[pltpu.VMEM(flat_shape, F32)],
        compiler_params=params(),
        name="final",
    )(place, out, dq, dkv, sums[0])
    return tuple(x.reshape(toks, heads, width) for x in outs)


def solution(mesh):
    spec = P("ctx", "head", None)
    return jax.shard_map(
        shards,
        mesh=mesh,
        in_specs=(spec, spec, spec, spec, P()),
        out_specs=(spec, spec, spec, spec),
        check_vma=False,
    )
```

```python
import functools
import math

import jax
import jax.numpy as jnp
from jax import lax
from jax.experimental import pallas as pl
from jax.experimental.pallas import tpu as pltpu
from jax.sharding import PartitionSpec as P

HALF = 512
TILE = 256
NEG = -1e30
LOG2E = 1.0 / math.log(2.0)
VMEM_BYTES = 63 * 1024 * 1024
BF = jnp.bfloat16
F32 = jnp.float32


def nt(a, b):
    return lax.dot_general(a, b, (((1,), (1,)), ((), ())), preferred_element_type=F32)


def nn(a, b):
    return lax.dot_general(a, b, (((1,), (0,)), ((), ())), preferred_element_type=F32)


def wide(column, width):
    return jnp.concatenate([column] * (width // column.shape[1]), axis=1)


def iota(shape, dim):
    return lax.broadcasted_iota(jnp.int32, shape, dim)


def params():
    return pltpu.CompilerParams(vmem_limit_bytes=VMEM_BYTES)


def as_column(row):
    return jnp.broadcast_to(row, (128, row.shape[1])).T[:, :1]


def pack_keys_kernel(heads, k, v, kv, wide_rows):
    toks = k.shape[0] // heads
    for number, source in enumerate((k, v)):
        wide_rows[number] = source[...].astype(F32)
        for head in range(heads):
            kv[number, head] = wide_rows[number, pl.ds(head, toks, stride=heads), :].astype(BF)


def pack_queries_kernel(heads, slots, q, g, kv, pos_row, qd, slot_rows, wide_rows, acc):
    step = pl.program_id(0)
    toks = q.shape[0] // heads
    row = pos_row[...]
    count = row.shape[1]
    base = lax.axis_index("ctx") * (toks * pl.num_programs(0))
    column = as_column(row)
    tok = iota((count, toks), 1) + (base + step * toks)
    hit = jnp.sum((column == tok).astype(F32), axis=0, keepdims=True)
    rank = jnp.sum(((column >= base) & (column < tok)).astype(F32), axis=0, keepdims=True)
    slot = iota((slots, toks), 0).astype(F32)
    pick = jnp.where((hit > 0) & (rank == slot), 1.0, 0.0).astype(BF)
    tok = iota((toks, count), 0) + (base + step * toks)
    hit_column = jnp.sum((row == tok).astype(F32), axis=1, keepdims=True)
    tables = [[], [kv[0, h] for h in range(heads)], [kv[1, h] for h in range(heads)], []]
    for number, source in ((0, q), (3, g)):
        wide_rows[number // 3] = source[...].astype(F32)
        for head in range(heads):
            rows = wide_rows[number // 3, pl.ds(head, toks, stride=heads), :]
            tables[number].append(rows.astype(BF))
            if number == 0:
                qd[0, head] = rows.astype(BF)
            else:
                qd[1, head] = jnp.where(hit_column > 0, 0.0, rows).astype(BF)
    for number in range(4):
        found = nn(pick, jnp.concatenate(tables[number], axis=1))
        for head in range(heads):
            part = found[:, head * 128 : (head + 1) * 128]
            acc[number, head] = jnp.where(step == 0, part, acc[number, head] + part)

    @pl.when(step == pl.num_programs(0) - 1)
    def _():
        slot_rows[...] = acc[...].astype(BF)


def mask_kernel(orders, slots, seq_rows, pos_row, bias, bias_row, compact, expand, place):
    toks = place.shape[0]
    me = lax.axis_index("ctx")
    base = me * toks
    row = pos_row[...]
    count = row.shape[1]
    column = as_column(row)
    for start in range(0, bias.shape[0], TILE):
        key = iota((TILE, count), 0) + (base - HALF + start)
        hits = jnp.sum((row == key).astype(F32), axis=1, keepdims=True)
        key = key[:, :1]
        out = (hits > 0) | (key < 0) | (key >= seq_rows)
        bias[start : start + TILE, :] = jnp.broadcast_to(jnp.where(out, NEG, 0.0), (TILE, 128))
        key = iota((count, TILE), 1) + (base - HALF + start)
        hits = jnp.sum((column == key).astype(F32), axis=0, keepdims=True)
        key = key[0:1, :]
        out = (hits > 0) | (key < 0) | (key >= seq_rows)
        shape = (8, TILE)
        bias_row[:, start : start + TILE] = jnp.broadcast_to(jnp.where(out, NEG, 0.0), shape)
    tok = iota((toks, count), 0) + base
    hit = jnp.sum((row == tok).astype(F32), axis=1, keepdims=True)
    rank = jnp.sum(((row >= base) & (row < tok)).astype(F32), axis=1, keepdims=True)
    slot = iota((toks, slots), 1).astype(F32)
    place[...] = jnp.where((hit > 0) & (rank == slot), 1.0, 0.0).astype(BF)
    for part, (first, second) in enumerate(zip(*orders)):
        low = (me ^ jnp.where(me % 2 == 0, first, second)) * toks
        inside = jnp.sum((column < low).astype(jnp.int32), axis=0, keepdims=True)
        held = jnp.sum((column < low + toks).astype(jnp.int32), axis=0, keepdims=True) - inside
        slot = iota((slots, count), 0)
        target = iota((slots, count), 1)
        hot = (target == inside + slot) & (slot < held)
        expand[part * slots : (part + 1) * slots, :] = jnp.where(hot, 1.0, 0.0).astype(BF)
    compact[...] = expand[...].astype(F32).T.astype(BF)


def stats_kernel(scale2, compact, *refs):
    parts, (kv, rows, stats) = refs[:-3], refs[-3:]
    pieces = []
    for part in parts:
        for i in range(part.shape[0]):
            pieces.append(jnp.concatenate([part[i, number, 0] for number in range(4)], axis=1))
    packed = nn(compact[...], jnp.concatenate(pieces, axis=0)).astype(BF)
    width = kv.shape[3]
    table = [packed[:, number * width : (number + 1) * width] for number in range(4)]
    for number in range(4):
        rows[number, 0] = table[number]
    queries, _, _, grads = table
    scores = nt(kv[0, 0], queries) * scale2
    top = jnp.max(scores, axis=0, keepdims=True)
    weights = jnp.exp2(scores - top)
    stats[0, 0, 0:1, :] = top
    stats[0, 0, 1:2, :] = jnp.sum(weights, axis=0, keepdims=True)
    stats[0, 0, 2:3, :] = jnp.sum(weights * nt(kv[1, 0], grads), axis=0, keepdims=True)


def band(scores, low):
    rows, columns = iota(scores.shape, 0), iota(scores.shape, 1)
    return jnp.where(rows <= columns if low else rows >= columns, scores, NEG)


def join(blocks, number, buf):
    toks = blocks[0].shape[2]
    for place, block in enumerate(blocks):
        buf[place * toks : (place + 1) * toks, :] = block[number, 0]


def forward_kernel(
    scale2, qd, left, own, right, rows, bias, out, log_dot, keys, values, score_buf, prob_buf
):
    toks = own.shape[2]
    reach = 2 * HALF + TILE
    join((left, own, right), 0, keys)
    join((left, own, right), 1, values)
    global_keys, global_values = rows[1, 0], rows[2, 0]
    count = global_keys.shape[0]
    for q_tile in range(toks // TILE):
        lanes = slice(q_tile * TILE, (q_tile + 1) * TILE)
        query = qd[0, 0, lanes, :]
        best = None
        for piece in range(reach // TILE + 1):
            spot = slice(piece * TILE, (piece + 1) * TILE)
            start = (q_tile + piece) * TILE
            if piece < reach // TILE:
                scores = nt(query, keys[start : start + TILE, :]) * scale2
                scores = scores + bias[0:1, start : start + TILE]
                if piece == 0:
                    scores = band(scores, True)
                elif piece == reach // TILE - 1:
                    scores = band(scores, False)
            else:
                scores = nt(query, global_keys) * scale2
                spot = slice(piece * TILE, piece * TILE + count)
            score_buf[:, spot] = scores
            for lane in range(0, scores.shape[1], 128):
                part = scores[:, lane : lane + 128]
                best = part if best is None else jnp.maximum(best, part)
        top = jnp.max(best, axis=1, keepdims=True)
        total = None
        for lane in range(0, reach + count, 128):
            weights = jnp.exp2(score_buf[:, lane : lane + 128] - top)
            prob_buf[:, lane : lane + 128] = weights.astype(BF)
            total = weights if total is None else total + weights
        total = jnp.sum(total, axis=1, keepdims=True)
        acc = nn(prob_buf[:, 0:reach], values[q_tile * TILE : q_tile * TILE + reach, :])
        acc = acc + nn(prob_buf[:, reach : reach + count], global_values)
        acc = acc / total
        out[0, lanes, :] = acc.astype(BF)
        dot = jnp.sum(qd[1, 0, lanes, :].astype(F32) * acc, axis=1, keepdims=True)
        lane = iota((TILE, 128), 1)
        pair = jnp.where(lane == 0, top + jnp.log2(total), jnp.where(lane == 1, dot, 0.0))
        log_dot[0, :, lanes] = pair.T[0:2, :]


def global_kernel(scale, scale2, slots, qd, own, rows, log_dot, stats, expand, dkv, sums):
    toks = own.shape[2]
    g_query, g_key, g_value, g_grad = (rows[i, 0] for i in range(4))
    tops = stats[:, 0, 0:1, :]
    top = jnp.max(tops, axis=0)
    factor = jnp.exp2(tops - top[None])
    total = jnp.sum(stats[:, 0, 1:2, :] * factor, axis=0)
    g_dot = jnp.sum(stats[:, 0, 2:3, :] * factor, axis=0) / total
    g_log = top + jnp.log2(total)
    weights = jnp.exp2(nt(own[0, 0], g_query) * scale2 - g_log)
    narrow = weights.astype(BF)
    slopes = (weights * (nt(own[1, 0], g_grad) - g_dot)).astype(BF)
    dkv[0, 0] = nn(slopes, g_query) * scale
    dkv[1, 0] = nn(narrow, g_grad)
    g_out = nn(own[1, 0].T, narrow).T
    g_dq = (nn(own[0, 0].T, slopes) * scale).T
    query, grad = qd[0, 0], qd[1, 0]
    weights = jnp.exp2(nt(g_key, query) * scale2 - log_dot[0, 0:1, :])
    slopes = (weights * (nt(g_value, grad) - log_dot[0, 1:2, :])).astype(BF)
    g_dv = nn(weights.astype(BF), grad)
    g_dk = nn(slopes, query)
    tables = [table.astype(BF) for table in (g_out, g_dq, g_dk * scale, g_dv)]
    spread = nn(expand[...], jnp.concatenate(tables, axis=1)).astype(BF)
    width = own.shape[3]
    for part in range(sums.shape[0]):
        for number in range(4):
            sums[part, number, 0] = spread[
                part * slots : (part + 1) * slots, number * width : (number + 1) * width
            ]


def backward_kernel(
    scale, scale2, qd, left, own, right, rows, bias, log_dot, before, dq, dkv, keys, values, probs, slopes
):
    toks = own.shape[2]
    reach = 2 * HALF + TILE
    join((left, own, right), 0, keys)
    join((left, own, right), 1, values)
    key_t = keys[...].T
    g_key, g_value = rows[1, 0], rows[2, 0]
    weights = jnp.exp2(nt(g_key, qd[0, 0]) * scale2 - log_dot[0, 0:1, :])
    slope = (weights * (nt(g_value, qd[1, 0]) - log_dot[0, 1:2, :])).astype(BF)
    dq_t = nn(g_key.T, slope)
    for q_tile in range(toks // TILE):
        lanes = slice(q_tile * TILE, (q_tile + 1) * TILE)
        query = qd[0, 0, lanes, :]
        grad = qd[1, 0, lanes, :]
        log_sum = log_dot[0, 0:1, lanes]
        dot = log_dot[0, 1:2, lanes]
        for piece in range(reach // TILE):
            start = (q_tile + piece) * TILE
            span = slice(start, start + TILE)
            scores = nt(keys[span, :], query) * scale2 + wide(bias[span, :], TILE)
            if piece == 0:
                scores = band(scores, False)
            elif piece == reach // TILE - 1:
                scores = band(scores, True)
            weights = jnp.exp2(scores - log_sum)
            slopes[span, lanes] = (weights * (nt(values[span, :], grad) - dot)).astype(BF)
            if HALF <= start < HALF + toks:
                probs[start - HALF : start - HALF + TILE, lanes] = weights.astype(BF)
        span = slice(q_tile * TILE, q_tile * TILE + reach)
        acc = dq_t[:, lanes] + nn(key_t[:, span], slopes[span, lanes])
        dq[0, lanes, :] = (acc * scale).T
    dkv[0, 0] = before[0, 0] + nn(slopes[HALF : HALF + toks, :], qd[0, 0]) * scale
    dkv[1, 0] = before[1, 0] + nn(probs[...], qd[1, 0])


def rim_kernel(
    scale, scale2, own, bias, qd_low, qd_high, log_low, log_high, partial, dkv, queries, grads, probs, slopes
):
    toks = own.shape[2]
    reach = toks + TILE
    join((qd_low, qd_high), 0, queries)
    join((qd_low, qd_high), 1, grads)
    for k_tile in range(toks // TILE):
        span = slice(k_tile * TILE, (k_tile + 1) * TILE)
        key = own[0, 0, span, :]
        value = own[1, 0, span, :]
        key_bias = wide(bias[HALF + k_tile * TILE : HALF + (k_tile + 1) * TILE, :], TILE)
        for piece in range(reach // TILE):
            start = (k_tile + piece) * TILE
            log_dot, offset = (log_low, start) if start < toks else (log_high, start - toks)
            lanes = slice(offset, offset + TILE)
            scores = nt(key, queries[start : start + TILE, :]) * scale2 + key_bias
            if piece == 0:
                scores = band(scores, True)
            elif piece == reach // TILE - 1:
                scores = band(scores, False)
            weights = jnp.exp2(scores - log_dot[0, 0:1, lanes])
            slope = weights * (nt(value, grads[start : start + TILE, :]) - log_dot[0, 1:2, lanes])
            spot = slice(piece * TILE, (piece + 1) * TILE)
            probs[span, spot] = weights.astype(BF)
            slopes[span, spot] = slope.astype(BF)
        window = slice(k_tile * TILE, k_tile * TILE + reach)
        dkv[0, 0, span, :] = partial[0, 0, span, :] + nn(slopes[span, :], queries[window, :]) * scale
        dkv[1, 0, span, :] = partial[1, 0, span, :] + nn(probs[span, :], grads[window, :])


def final_kernel(place, out, dq, dkv, sums, attn, query_grad, key_grad, value_grad, wide_rows):
    heads, toks = out.shape[0], out.shape[1]
    hot = place[...]
    is_global = jnp.sum(hot.astype(F32), axis=1, keepdims=True) > 0
    for head in range(heads):
        rows = pl.ds(head, toks, stride=heads)
        wide_rows[rows, :] = jnp.where(is_global, nn(hot, sums[0, head]), out[head].astype(F32))
        query_grad[rows, :] = dq[head] + nn(hot, sums[1, head])
        key_grad[rows, :] = dkv[0, head] + nn(hot, sums[2, head])
        value_grad[rows, :] = dkv[1, head] + nn(hot, sums[3, head])
    attn[...] = wide_rows[...].astype(BF)


def cost(flops, moved, exps=0):
    return pl.CostEstimate(flops=int(flops), bytes_accessed=int(moved), transcendentals=int(exps))


def struct(shape, dtype):
    return jax.ShapeDtypeStruct(shape, dtype)


def whole(shape):
    return pl.BlockSpec(shape, lambda head: (0,) * len(shape))


def per_head(shape, dim):
    block = tuple(1 if i == dim else size for i, size in enumerate(shape))
    return pl.BlockSpec(block, lambda head: tuple(head if i == dim else 0 for i in range(len(shape))))


def shards(query_rows, key_rows, value_rows, out_grad, global_pos):
    toks, heads, width = query_rows.shape
    count = global_pos.shape[0]
    devices = lax.axis_size("ctx")
    slots = max(16, 2 * count // devices)
    scale = width ** (-0.5)
    scale2 = scale * LOG2E
    bits = devices.bit_length() - 1
    ways = [list(range(1, bits)) + [0], list(range(bits - 1, 0, -1)) + [0]]
    orders = []
    for way in ways:
        order = [0]
        for bit in way[:-1]:
            order = order + [one | (1 << bit) for one in order]
        orders.append(order)
    orders = [mine + [one | 1 for one in other] for mine, other in (orders, orders[::-1])]
    pos_row = global_pos.reshape(1, count)
    q_flat, k_flat, v_flat, g_flat = (
        x.reshape(toks * heads, width) for x in (query_rows, key_rows, value_rows, out_grad)
    )

    def swap(value, stage):
        pairs = [(i, i ^ (1 << ways[i % 2][stage])) for i in range(devices)]
        return lax.ppermute(value, "ctx", pairs)

    def from_low(value):
        return lax.ppermute(value, "ctx", [(i, i + 1) for i in range(devices - 1)])

    def from_high(value):
        return lax.ppermute(value, "ctx", [(i + 1, i) for i in range(devices - 1)])

    def after(value, earlier):
        return lax.optimization_barrier((value, earlier))[0]

    pair_shape = (2, heads, toks, width)
    slot_shape = (4, heads, slots, width)
    steps = 1
    flat_spec = pl.BlockSpec((toks * heads // steps, width), lambda i: (i, 0))
    pair_spec = pl.BlockSpec((2, heads, toks // steps, width), lambda i: (0, 0, i, 0))
    wide_pair = pltpu.VMEM((2, toks * heads // steps, width), F32)
    kv = pl.pallas_call(
        functools.partial(pack_keys_kernel, heads),
        grid=(steps,),
        in_specs=[flat_spec, flat_spec],
        out_specs=pair_spec,
        out_shape=struct(pair_shape, BF),
        scratch_shapes=[wide_pair],
        compiler_params=params(),
        name="pack_keys",
    )(k_flat, v_flat)
    kv_low, kv_high = from_low(kv), from_high(kv)

    qd, slot_rows = pl.pallas_call(
        functools.partial(pack_queries_kernel, heads, slots),
        grid=(steps,),
        in_specs=[flat_spec, flat_spec, pair_spec, whole((1, count))],
        out_specs=(pair_spec, whole(slot_shape)),
        out_shape=(struct(pair_shape, BF), struct(slot_shape, BF)),
        scratch_shapes=[wide_pair, pltpu.VMEM(slot_shape, F32)],
        compiler_params=params(),
        name="pack_queries",
    )(q_flat, g_flat, kv, pos_row)

    held = [slot_rows[None]]
    for stage in range(bits):
        send = jnp.concatenate(held, axis=0) if len(held) > 1 else held[0]
        if stage == bits - 1:
            send = after(send, (kv_low, kv_high))
        held.append(swap(send, stage))
    qd_late = after(qd, (kv_low, kv_high))
    qd_low, qd_high = from_low(qd_late), from_high(qd_late)

    span = toks + 2 * HALF
    bias, bias_row, compact, expand, place = pl.pallas_call(
        functools.partial(mask_kernel, orders, slots, toks * devices),
        out_shape=(
            struct((span, 128), F32),
            struct((8, span), F32),
            struct((count, devices * slots), BF),
            struct((devices * slots, count), BF),
            struct((toks, slots), BF),
        ),
        compiler_params=params(),
        name="masks",
    )(pos_row)

    row_shape = (4, heads, count, width)
    rows, stats = pl.pallas_call(
        functools.partial(stats_kernel, scale2),
        grid=(heads,),
        in_specs=[whole(compact.shape)]
        + [per_head(part.shape, 2) for part in held]
        + [per_head(pair_shape, 1)],
        out_specs=(per_head(row_shape, 1), per_head((1, heads, 3, count), 1)),
        out_shape=(struct(row_shape, BF), struct((1, heads, 3, count), F32)),
        compiler_params=params(),
        cost_estimate=cost(2.7e9, 4e6),
        name="global_stats",
    )(compact, *held, kv)

    for stage in range(bits):
        stats = jnp.concatenate([stats, swap(stats, stage)], axis=0)

    head_specs = [
        per_head(pair_shape, 1),
        per_head(pair_shape, 1),
        per_head(pair_shape, 1),
        per_head(pair_shape, 1),
        per_head(row_shape, 1),
    ]
    out, log_dot = pl.pallas_call(
        functools.partial(forward_kernel, scale2),
        grid=(heads,),
        in_specs=head_specs + [whole(bias_row.shape)],
        out_specs=(per_head((heads, toks, width), 0), per_head((heads, 2, toks), 0)),
        out_shape=(struct((heads, toks, width), BF), struct((heads, 2, toks), F32)),
        scratch_shapes=[
            pltpu.VMEM((span, width), BF),
            pltpu.VMEM((span, width), BF),
            pltpu.VMEM((TILE, 2 * HALF + TILE + count), F32),
            pltpu.VMEM((TILE, 2 * HALF + TILE + count), BF),
        ],
        compiler_params=params(),
        cost_estimate=cost(4e9, 5e6, 3e6),
        name="forward",
    )(qd, kv_low, kv, kv_high, rows, bias_row)
    log_low, log_high = from_low(log_dot), from_high(log_dot)

    sum_shape = (devices, 4, heads, slots, width)
    dkv, sums = pl.pallas_call(
        functools.partial(global_kernel, scale, scale2, slots),
        grid=(heads,),
        in_specs=[
            per_head(pair_shape, 1),
            per_head(pair_shape, 1),
            per_head(row_shape, 1),
            per_head(log_dot.shape, 0),
            per_head(stats.shape, 1),
            whole(expand.shape),
        ],
        out_specs=(per_head(pair_shape, 1), per_head(sum_shape, 2)),
        out_shape=(struct(pair_shape, F32), struct(sum_shape, BF)),
        compiler_params=params(),
        cost_estimate=cost(4e9, 9e6, 1e6),
        name="globals",
    )(qd, kv, rows, log_dot, stats, expand)

    for stage in reversed(range(bits)):
        half = sums.shape[0] // 2
        sums = sums[:half] + swap(sums[half:], stage)

    dq, dkv = pl.pallas_call(
        functools.partial(backward_kernel, scale, scale2),
        grid=(heads,),
        in_specs=head_specs
        + [whole(bias.shape), per_head(log_dot.shape, 0), per_head(pair_shape, 1)],
        out_specs=(per_head((heads, toks, width), 0), per_head(pair_shape, 1)),
        out_shape=(struct((heads, toks, width), F32), struct(pair_shape, F32)),
        scratch_shapes=[
            pltpu.VMEM((span, width), BF),
            pltpu.VMEM((span, width), BF),
            pltpu.VMEM((toks, toks), BF),
            pltpu.VMEM((span, toks), BF),
        ],
        compiler_params=params(),
        cost_estimate=cost(8e9, 9e6, 3e6),
        name="backward",
    )(qd, kv_low, kv, kv_high, rows, bias, after(log_dot, (qd_low, qd_high)), dkv)

    dkv = pl.pallas_call(
        functools.partial(rim_kernel, scale, scale2),
        grid=(heads,),
        in_specs=[
            per_head(pair_shape, 1),
            whole(bias.shape),
            per_head(pair_shape, 1),
            per_head(pair_shape, 1),
            per_head(log_dot.shape, 0),
            per_head(log_dot.shape, 0),
            per_head(pair_shape, 1),
        ],
        out_specs=per_head(pair_shape, 1),
        out_shape=struct(pair_shape, F32),
        scratch_shapes=[
            pltpu.VMEM((2 * toks, width), BF),
            pltpu.VMEM((2 * toks, width), BF),
            pltpu.VMEM((toks, toks + TILE), BF),
            pltpu.VMEM((toks, toks + TILE), BF),
        ],
        compiler_params=params(),
        cost_estimate=cost(4e9, 8e6, 2e6),
        name="rim",
    )(kv, bias, qd_low, qd_high, log_low, log_high, dkv)

    flat_shape = (toks * heads, width)
    steps = 2
    outs = pl.pallas_call(
        final_kernel,
        grid=(steps,),
        in_specs=[
            pl.BlockSpec((toks // steps, slots), lambda i: (i, 0)),
            pl.BlockSpec((heads, toks // steps, width), lambda i: (0, i, 0)),
            pl.BlockSpec((heads, toks // steps, width), lambda i: (0, i, 0)),
            pl.BlockSpec((2, heads, toks // steps, width), lambda i: (0, 0, i, 0)),
            whole(slot_shape),
        ],
        out_specs=[pl.BlockSpec((toks * heads // steps, width), lambda i: (i, 0))] * 4,
        out_shape=[struct(flat_shape, kind) for kind in (BF, F32, F32, F32)],
        scratch_shapes=[pltpu.VMEM((toks * heads // steps, width), F32)],
        compiler_params=params(),
        name="final",
    )(place, out, dq, dkv, sums[0])
    return tuple(x.reshape(toks, heads, width) for x in outs)


def solution(mesh):
    spec = P("ctx", "head", None)
    return jax.shard_map(
        shards,
        mesh=mesh,
        in_specs=(spec, spec, spec, spec, P()),
        out_specs=(spec, spec, spec, spec),
        check_vma=False,
    )
```

```python
import functools
import math

import jax
import jax.numpy as jnp
from jax import lax
from jax.experimental import pallas as pl
from jax.experimental.pallas import tpu as pltpu
from jax.sharding import PartitionSpec as P

HALF = 512
TILE = 256
NEG = -1e30
LOG2E = 1.0 / math.log(2.0)
VMEM_BYTES = 63 * 1024 * 1024
BF = jnp.bfloat16
F32 = jnp.float32


def nt(a, b):
    return lax.dot_general(a, b, (((1,), (1,)), ((), ())), preferred_element_type=F32)


def nn(a, b):
    return lax.dot_general(a, b, (((1,), (0,)), ((), ())), preferred_element_type=F32)


def wide(column, width):
    return jnp.concatenate([column] * (width // column.shape[1]), axis=1)


def iota(shape, dim):
    return lax.broadcasted_iota(jnp.int32, shape, dim)


def params():
    return pltpu.CompilerParams(vmem_limit_bytes=VMEM_BYTES)


def as_column(row):
    return jnp.broadcast_to(row, (128, row.shape[1])).T[:, :1]


def pack_keys_kernel(heads, k, v, kv, wide_rows):
    toks = k.shape[0] // heads
    for number, source in enumerate((k, v)):
        wide_rows[number] = source[...].astype(F32)
        for head in range(heads):
            kv[number, head] = wide_rows[number, pl.ds(head, toks, stride=heads), :].astype(BF)


def pack_queries_kernel(heads, slots, q, g, kv, pos_row, qd, slot_rows, wide_rows, acc):
    step = pl.program_id(0)
    toks = q.shape[0] // heads
    row = pos_row[...]
    count = row.shape[1]
    base = lax.axis_index("ctx") * (toks * pl.num_programs(0))
    column = as_column(row)
    tok = iota((count, toks), 1) + (base + step * toks)
    hit = jnp.sum((column == tok).astype(F32), axis=0, keepdims=True)
    rank = jnp.sum(((column >= base) & (column < tok)).astype(F32), axis=0, keepdims=True)
    slot = iota((slots, toks), 0).astype(F32)
    pick = jnp.where((hit > 0) & (rank == slot), 1.0, 0.0).astype(BF)
    tok = iota((toks, count), 0) + (base + step * toks)
    hit_column = jnp.sum((row == tok).astype(F32), axis=1, keepdims=True)
    tables = [[], [kv[0, h] for h in range(heads)], [kv[1, h] for h in range(heads)], []]
    for number, source in ((0, q), (3, g)):
        wide_rows[number // 3] = source[...].astype(F32)
        for head in range(heads):
            rows = wide_rows[number // 3, pl.ds(head, toks, stride=heads), :]
            tables[number].append(rows.astype(BF))
            if number == 0:
                qd[0, head] = rows.astype(BF)
            else:
                qd[1, head] = jnp.where(hit_column > 0, 0.0, rows).astype(BF)
    for number in range(4):
        found = nn(pick, jnp.concatenate(tables[number], axis=1))
        for head in range(heads):
            part = found[:, head * 128 : (head + 1) * 128]
            acc[number, head] = jnp.where(step == 0, part, acc[number, head] + part)

    @pl.when(step == pl.num_programs(0) - 1)
    def _():
        slot_rows[...] = acc[...].astype(BF)


def mask_kernel(orders, slots, seq_rows, pos_row, bias, bias_row, compact, expand, place):
    toks = place.shape[0]
    me = lax.axis_index("ctx")
    base = me * toks
    row = pos_row[...]
    count = row.shape[1]
    column = as_column(row)
    for start in range(0, bias.shape[0], TILE):
        key = iota((TILE, count), 0) + (base - HALF + start)
        hits = jnp.sum((row == key).astype(F32), axis=1, keepdims=True)
        key = key[:, :1]
        out = (hits > 0) | (key < 0) | (key >= seq_rows)
        bias[start : start + TILE, :] = jnp.broadcast_to(jnp.where(out, NEG, 0.0), (TILE, 128))
        key = iota((count, TILE), 1) + (base - HALF + start)
        hits = jnp.sum((column == key).astype(F32), axis=0, keepdims=True)
        key = key[0:1, :]
        out = (hits > 0) | (key < 0) | (key >= seq_rows)
        shape = (8, TILE)
        bias_row[:, start : start + TILE] = jnp.broadcast_to(jnp.where(out, NEG, 0.0), shape)
    tok = iota((toks, count), 0) + base
    hit = jnp.sum((row == tok).astype(F32), axis=1, keepdims=True)
    rank = jnp.sum(((row >= base) & (row < tok)).astype(F32), axis=1, keepdims=True)
    slot = iota((toks, slots), 1).astype(F32)
    place[...] = jnp.where((hit > 0) & (rank == slot), 1.0, 0.0).astype(BF)
    for part, (first, second) in enumerate(zip(*orders)):
        low = (me ^ jnp.where(me % 2 == 0, first, second)) * toks
        inside = jnp.sum((column < low).astype(jnp.int32), axis=0, keepdims=True)
        held = jnp.sum((column < low + toks).astype(jnp.int32), axis=0, keepdims=True) - inside
        slot = iota((slots, count), 0)
        target = iota((slots, count), 1)
        hot = (target == inside + slot) & (slot < held)
        expand[part * slots : (part + 1) * slots, :] = jnp.where(hot, 1.0, 0.0).astype(BF)
    compact[...] = expand[...].astype(F32).T.astype(BF)


def stats_kernel(scale2, compact, *refs):
    parts, (kv, rows, stats) = refs[:-3], refs[-3:]
    pieces = []
    for part in parts:
        for i in range(part.shape[0]):
            pieces.append(jnp.concatenate([part[i, number, 0] for number in range(4)], axis=1))
    packed = nn(compact[...], jnp.concatenate(pieces, axis=0)).astype(BF)
    width = kv.shape[3]
    table = [packed[:, number * width : (number + 1) * width] for number in range(4)]
    for number in range(4):
        rows[number, 0] = table[number]
    queries, _, _, grads = table
    scores = nt(kv[0, 0], queries) * scale2
    top = jnp.max(scores, axis=0, keepdims=True)
    weights = jnp.exp2(scores - top)
    stats[0, 0, 0:1, :] = top
    stats[0, 0, 1:2, :] = jnp.sum(weights, axis=0, keepdims=True)
    stats[0, 0, 2:3, :] = jnp.sum(weights * nt(kv[1, 0], grads), axis=0, keepdims=True)


def band(scores, low):
    rows, columns = iota(scores.shape, 0), iota(scores.shape, 1)
    return jnp.where(rows <= columns if low else rows >= columns, scores, NEG)


def join(blocks, number, buf):
    toks = blocks[0].shape[2]
    for place, block in enumerate(blocks):
        buf[place * toks : (place + 1) * toks, :] = block[number, 0]


def forward_kernel(
    scale2, qd, left, own, right, rows, bias, out, log_dot, keys, values, score_buf, prob_buf
):
    toks = own.shape[2]
    reach = 2 * HALF + TILE
    join((left, own, right), 0, keys)
    join((left, own, right), 1, values)
    global_keys, global_values = rows[1, 0], rows[2, 0]
    count = global_keys.shape[0]
    for q_tile in range(toks // TILE):
        lanes = slice(q_tile * TILE, (q_tile + 1) * TILE)
        query = qd[0, 0, lanes, :]
        best = None
        for piece in range(reach // TILE + 1):
            spot = slice(piece * TILE, (piece + 1) * TILE)
            start = (q_tile + piece) * TILE
            if piece < reach // TILE:
                scores = nt(query, keys[start : start + TILE, :]) * scale2
                scores = scores + bias[0:1, start : start + TILE]
                if piece == 0:
                    scores = band(scores, True)
                elif piece == reach // TILE - 1:
                    scores = band(scores, False)
            else:
                scores = nt(query, global_keys) * scale2
                spot = slice(piece * TILE, piece * TILE + count)
            score_buf[:, spot] = scores
            for lane in range(0, scores.shape[1], 128):
                part = scores[:, lane : lane + 128]
                best = part if best is None else jnp.maximum(best, part)
        top = jnp.max(best, axis=1, keepdims=True)
        total = None
        for lane in range(0, reach + count, 128):
            weights = jnp.exp2(score_buf[:, lane : lane + 128] - top)
            prob_buf[:, lane : lane + 128] = weights.astype(BF)
            total = weights if total is None else total + weights
        total = jnp.sum(total, axis=1, keepdims=True)
        acc = nn(prob_buf[:, 0:reach], values[q_tile * TILE : q_tile * TILE + reach, :])
        acc = acc + nn(prob_buf[:, reach : reach + count], global_values)
        acc = acc / total
        out[0, lanes, :] = acc.astype(BF)
        dot = jnp.sum(qd[1, 0, lanes, :].astype(F32) * acc, axis=1, keepdims=True)
        lane = iota((TILE, 128), 1)
        pair = jnp.where(lane == 0, top + jnp.log2(total), jnp.where(lane == 1, dot, 0.0))
        log_dot[0, :, lanes] = pair.T[0:2, :]


def global_kernel(scale, scale2, slots, qd, own, rows, log_dot, stats, expand, dkv, kept, sent):
    toks = own.shape[2]
    g_query, g_key, g_value, g_grad = (rows[i, 0] for i in range(4))
    tops = stats[:, 0, 0:1, :]
    top = jnp.max(tops, axis=0)
    factor = jnp.exp2(tops - top[None])
    total = jnp.sum(stats[:, 0, 1:2, :] * factor, axis=0)
    g_dot = jnp.sum(stats[:, 0, 2:3, :] * factor, axis=0) / total
    g_log = top + jnp.log2(total)
    weights = jnp.exp2(nt(own[0, 0], g_query) * scale2 - g_log)
    narrow = weights.astype(BF)
    slopes = (weights * (nt(own[1, 0], g_grad) - g_dot)).astype(BF)
    dkv[0, 0] = nn(slopes, g_query) * scale
    dkv[1, 0] = nn(narrow, g_grad)
    g_out = nn(own[1, 0].T, narrow).T
    g_dq = (nn(own[0, 0].T, slopes) * scale).T
    query, grad = qd[0, 0], qd[1, 0]
    weights = jnp.exp2(nt(g_key, query) * scale2 - log_dot[0, 0:1, :])
    slopes = (weights * (nt(g_value, grad) - log_dot[0, 1:2, :])).astype(BF)
    g_dv = nn(weights.astype(BF), grad)
    g_dk = nn(slopes, query)
    tables = [table.astype(BF) for table in (g_out, g_dq, g_dk * scale, g_dv)]
    spread = nn(expand[...], jnp.concatenate(tables, axis=1)).astype(BF)
    width = own.shape[3]
    half = kept.shape[0]
    for part in range(2 * half):
        sums = kept if part < half else sent
        for number in range(4):
            sums[part % half, number, 0] = spread[
                part * slots : (part + 1) * slots, number * width : (number + 1) * width
            ]


def backward_kernel(
    scale, scale2, qd, left, own, right, rows, bias, log_dot, before, dq, dkv, keys, values, probs, slopes
):
    toks = own.shape[2]
    reach = 2 * HALF + TILE
    join((left, own, right), 0, keys)
    join((left, own, right), 1, values)
    key_t = keys[...].T
    g_key, g_value = rows[1, 0], rows[2, 0]
    weights = jnp.exp2(nt(g_key, qd[0, 0]) * scale2 - log_dot[0, 0:1, :])
    slope = (weights * (nt(g_value, qd[1, 0]) - log_dot[0, 1:2, :])).astype(BF)
    dq_t = nn(g_key.T, slope)
    for q_tile in range(toks // TILE):
        lanes = slice(q_tile * TILE, (q_tile + 1) * TILE)
        query = qd[0, 0, lanes, :]
        grad = qd[1, 0, lanes, :]
        log_sum = log_dot[0, 0:1, lanes]
        dot = log_dot[0, 1:2, lanes]
        for piece in range(reach // TILE):
            start = (q_tile + piece) * TILE
            span = slice(start, start + TILE)
            scores = nt(keys[span, :], query) * scale2 + wide(bias[span, :], TILE)
            if piece == 0:
                scores = band(scores, False)
            elif piece == reach // TILE - 1:
                scores = band(scores, True)
            weights = jnp.exp2(scores - log_sum)
            slopes[span, lanes] = (weights * (nt(values[span, :], grad) - dot)).astype(BF)
            if HALF <= start < HALF + toks:
                probs[start - HALF : start - HALF + TILE, lanes] = weights.astype(BF)
        span = slice(q_tile * TILE, q_tile * TILE + reach)
        acc = dq_t[:, lanes] + nn(key_t[:, span], slopes[span, lanes])
        dq[0, lanes, :] = (acc * scale).T
    dkv[0, 0] = before[0, 0] + nn(slopes[HALF : HALF + toks, :], qd[0, 0]) * scale
    dkv[1, 0] = before[1, 0] + nn(probs[...], qd[1, 0])


def rim_kernel(
    scale, scale2, own, bias, qd_low, qd_high, log_low, log_high, partial, dkv, queries, grads, probs, slopes
):
    toks = own.shape[2]
    reach = toks + TILE
    join((qd_low, qd_high), 0, queries)
    join((qd_low, qd_high), 1, grads)
    for k_tile in range(toks // TILE):
        span = slice(k_tile * TILE, (k_tile + 1) * TILE)
        key = own[0, 0, span, :]
        value = own[1, 0, span, :]
        key_bias = wide(bias[HALF + k_tile * TILE : HALF + (k_tile + 1) * TILE, :], TILE)
        for piece in range(reach // TILE):
            start = (k_tile + piece) * TILE
            log_dot, offset = (log_low, start) if start < toks else (log_high, start - toks)
            lanes = slice(offset, offset + TILE)
            scores = nt(key, queries[start : start + TILE, :]) * scale2 + key_bias
            if piece == 0:
                scores = band(scores, True)
            elif piece == reach // TILE - 1:
                scores = band(scores, False)
            weights = jnp.exp2(scores - log_dot[0, 0:1, lanes])
            slope = weights * (nt(value, grads[start : start + TILE, :]) - log_dot[0, 1:2, lanes])
            spot = slice(piece * TILE, (piece + 1) * TILE)
            probs[span, spot] = weights.astype(BF)
            slopes[span, spot] = slope.astype(BF)
        window = slice(k_tile * TILE, k_tile * TILE + reach)
        dkv[0, 0, span, :] = partial[0, 0, span, :] + nn(slopes[span, :], queries[window, :]) * scale
        dkv[1, 0, span, :] = partial[1, 0, span, :] + nn(probs[span, :], grads[window, :])


def final_kernel(halves, place, out, sums, *refs):
    dqs, pairs = refs[:halves], refs[halves : 2 * halves]
    attn, query_grad, key_grad, value_grad, wide_rows = refs[2 * halves :]
    heads, toks = out.shape[0], out.shape[1]
    group = heads // halves
    hot = place[...]
    is_global = jnp.sum(hot.astype(F32), axis=1, keepdims=True) > 0
    for head in range(heads):
        dq, pair, part = dqs[head // group], pairs[head // group], head % group
        rows = pl.ds(head, toks, stride=heads)
        wide_rows[rows, :] = jnp.where(is_global, nn(hot, sums[0, head]), out[head].astype(F32))
        query_grad[rows, :] = dq[part] + nn(hot, sums[1, head])
        key_grad[rows, :] = pair[0, part] + nn(hot, sums[2, head])
        value_grad[rows, :] = pair[1, part] + nn(hot, sums[3, head])
    attn[...] = wide_rows[...].astype(BF)


def cost(flops, moved, exps=0):
    return pl.CostEstimate(flops=int(flops), bytes_accessed=int(moved), transcendentals=int(exps))


def struct(shape, dtype):
    return jax.ShapeDtypeStruct(shape, dtype)


def whole(shape):
    return pl.BlockSpec(shape, lambda head: (0,) * len(shape))


def per_head(shape, dim, first=0):
    block = tuple(1 if i == dim else size for i, size in enumerate(shape))
    return pl.BlockSpec(
        block, lambda head: tuple(head + first if i == dim else 0 for i in range(len(shape)))
    )


def shards(query_rows, key_rows, value_rows, out_grad, global_pos):
    toks, heads, width = query_rows.shape
    count = global_pos.shape[0]
    devices = lax.axis_size("ctx")
    slots = max(16, 2 * count // devices)
    scale = width ** (-0.5)
    scale2 = scale * LOG2E
    bits = devices.bit_length() - 1
    ways = [list(range(1, bits)) + [0], list(range(bits - 1, 0, -1)) + [0]]
    orders = []
    for way in ways:
        order = [0]
        for bit in way[:-1]:
            order = order + [one | (1 << bit) for one in order]
        orders.append(order)
    orders = [mine + [one | 1 for one in other] for mine, other in (orders, orders[::-1])]
    pos_row = global_pos.reshape(1, count)
    q_flat, k_flat, v_flat, g_flat = (
        x.reshape(toks * heads, width) for x in (query_rows, key_rows, value_rows, out_grad)
    )

    def swap(value, stage):
        pairs = [(i, i ^ (1 << ways[i % 2][stage])) for i in range(devices)]
        return lax.ppermute(value, "ctx", pairs)

    def from_low(value):
        return lax.ppermute(value, "ctx", [(i, i + 1) for i in range(devices - 1)])

    def from_high(value):
        return lax.ppermute(value, "ctx", [(i + 1, i) for i in range(devices - 1)])

    def after(value, earlier):
        return lax.optimization_barrier((value, earlier))[0]

    pair_shape = (2, heads, toks, width)
    slot_shape = (4, heads, slots, width)
    steps = 1
    flat_spec = pl.BlockSpec((toks * heads // steps, width), lambda i: (i, 0))
    pair_spec = pl.BlockSpec((2, heads, toks // steps, width), lambda i: (0, 0, i, 0))
    wide_pair = pltpu.VMEM((2, toks * heads // steps, width), F32)
    kv = pl.pallas_call(
        functools.partial(pack_keys_kernel, heads),
        grid=(steps,),
        in_specs=[flat_spec, flat_spec],
        out_specs=pair_spec,
        out_shape=struct(pair_shape, BF),
        scratch_shapes=[wide_pair],
        compiler_params=params(),
        name="pack_keys",
    )(k_flat, v_flat)

    qd, slot_rows = pl.pallas_call(
        functools.partial(pack_queries_kernel, heads, slots),
        grid=(steps,),
        in_specs=[flat_spec, flat_spec, pair_spec, whole((1, count))],
        out_specs=(pair_spec, whole(slot_shape)),
        out_shape=(struct(pair_shape, BF), struct(slot_shape, BF)),
        scratch_shapes=[wide_pair, pltpu.VMEM(slot_shape, F32)],
        compiler_params=params(),
        name="pack_queries",
    )(q_flat, g_flat, kv, pos_row)

    held = [slot_rows[None]]
    for stage in range(bits):
        send = jnp.concatenate(held, axis=0) if len(held) > 1 else held[0]
        held.append(swap(send, stage))
    kv_late = after(kv, held[1])
    kv_low, kv_high = from_low(kv_late), from_high(kv_late)
    qd_late = after(qd, (kv_low, kv_high))
    qd_low, qd_high = from_low(qd_late), from_high(qd_late)

    span = toks + 2 * HALF
    bias, bias_row, compact, expand, place = pl.pallas_call(
        functools.partial(mask_kernel, orders, slots, toks * devices),
        out_shape=(
            struct((span, 128), F32),
            struct((8, span), F32),
            struct((count, devices * slots), BF),
            struct((devices * slots, count), BF),
            struct((toks, slots), BF),
        ),
        compiler_params=params(),
        name="masks",
    )(pos_row)

    row_shape = (4, heads, count, width)
    rows, stats = pl.pallas_call(
        functools.partial(stats_kernel, scale2),
        grid=(heads,),
        in_specs=[whole(compact.shape)]
        + [per_head(part.shape, 2) for part in held]
        + [per_head(pair_shape, 1)],
        out_specs=(per_head(row_shape, 1), per_head((1, heads, 3, count), 1)),
        out_shape=(struct(row_shape, BF), struct((1, heads, 3, count), F32)),
        compiler_params=params(),
        cost_estimate=cost(2.7e9, 4e6),
        name="global_stats",
    )(compact, *held, kv)

    for stage in range(bits):
        stats = jnp.concatenate([stats, swap(stats, stage)], axis=0)

    head_specs = [
        per_head(pair_shape, 1),
        per_head(pair_shape, 1),
        per_head(pair_shape, 1),
        per_head(pair_shape, 1),
        per_head(row_shape, 1),
    ]
    out, log_dot = pl.pallas_call(
        functools.partial(forward_kernel, scale2),
        grid=(heads,),
        in_specs=head_specs + [whole(bias_row.shape)],
        out_specs=(per_head((heads, toks, width), 0), per_head((heads, 2, toks), 0)),
        out_shape=(struct((heads, toks, width), BF), struct((heads, 2, toks), F32)),
        scratch_shapes=[
            pltpu.VMEM((span, width), BF),
            pltpu.VMEM((span, width), BF),
            pltpu.VMEM((TILE, 2 * HALF + TILE + count), F32),
            pltpu.VMEM((TILE, 2 * HALF + TILE + count), BF),
        ],
        compiler_params=params(),
        cost_estimate=cost(4e9, 5e6, 3e6),
        name="forward",
    )(qd, kv_low, kv, kv_high, rows, bias_row)
    log_low, log_high = from_low(log_dot), from_high(log_dot)

    sum_shape = (devices // 2, 4, heads, slots, width)
    dkv, sums, sent = pl.pallas_call(
        functools.partial(global_kernel, scale, scale2, slots),
        grid=(heads,),
        in_specs=[
            per_head(pair_shape, 1),
            per_head(pair_shape, 1),
            per_head(row_shape, 1),
            per_head(log_dot.shape, 0),
            per_head(stats.shape, 1),
            whole(expand.shape),
        ],
        out_specs=(per_head(pair_shape, 1), per_head(sum_shape, 2), per_head(sum_shape, 2)),
        out_shape=(struct(pair_shape, F32), struct(sum_shape, BF), struct(sum_shape, BF)),
        compiler_params=params(),
        cost_estimate=cost(4e9, 9e6, 1e6),
        name="globals",
    )(qd, kv, rows, log_dot, stats, expand)

    sums = sums + swap(sent, bits - 1)
    for stage in reversed(range(bits - 1)):
        half = sums.shape[0] // 2
        sums = sums[:half] + swap(sums[half:], stage)

    halves = 2 if heads % 2 == 0 else 1
    group = heads // halves
    queries_part, pairs_part = [], []
    log_late = after(log_dot, (qd_low, qd_high))
    for half in range(halves):
        first = half * group
        dq, pair = pl.pallas_call(
            functools.partial(backward_kernel, scale, scale2),
            grid=(group,),
            in_specs=[per_head(pair_shape, 1, first)] * 4
            + [per_head(row_shape, 1, first), whole(bias.shape)]
            + [per_head(log_dot.shape, 0, first), per_head(pair_shape, 1, first)],
            out_specs=(
                per_head((group, toks, width), 0),
                per_head((2, group, toks, width), 1),
            ),
            out_shape=(
                struct((group, toks, width), F32),
                struct((2, group, toks, width), F32),
            ),
            scratch_shapes=[
                pltpu.VMEM((span, width), BF),
                pltpu.VMEM((span, width), BF),
                pltpu.VMEM((toks, toks), BF),
                pltpu.VMEM((span, toks), BF),
            ],
            compiler_params=params(),
            cost_estimate=cost(4e9, 5e6, 2e6),
            name="backward",
        )(qd, kv_low, kv, kv_high, rows, bias, log_late, dkv)
        queries_part.append(dq)
        pairs_part.append(pair)

    rim_part = []
    for half in range(halves):
        first = half * group
        rim_part.append(
            pl.pallas_call(
                functools.partial(rim_kernel, scale, scale2),
                grid=(group,),
                in_specs=[per_head(pair_shape, 1, first), whole(bias.shape)]
                + [per_head(pair_shape, 1, first)] * 2
                + [per_head(log_dot.shape, 0, first)] * 2
                + [per_head((2, group, toks, width), 1)],
                out_specs=per_head((2, group, toks, width), 1),
                out_shape=struct((2, group, toks, width), F32),
                scratch_shapes=[
                    pltpu.VMEM((2 * toks, width), BF),
                    pltpu.VMEM((2 * toks, width), BF),
                    pltpu.VMEM((toks, toks + TILE), BF),
                    pltpu.VMEM((toks, toks + TILE), BF),
                ],
                compiler_params=params(),
                cost_estimate=cost(2e9, 4e6, 1e6),
                name="rim",
            )(kv, bias, qd_low, qd_high, log_low, log_high, pairs_part[half])
        )

    flat_shape = (toks * heads, width)
    steps = 2
    outs = pl.pallas_call(
        functools.partial(final_kernel, halves),
        grid=(steps,),
        in_specs=[
            pl.BlockSpec((toks // steps, slots), lambda i: (i, 0)),
            pl.BlockSpec((heads, toks // steps, width), lambda i: (0, i, 0)),
            whole(slot_shape),
        ]
        + [pl.BlockSpec((group, toks // steps, width), lambda i: (0, i, 0))] * halves
        + [pl.BlockSpec((2, group, toks // steps, width), lambda i: (0, 0, i, 0))] * halves,
        out_specs=[pl.BlockSpec((toks * heads // steps, width), lambda i: (i, 0))] * 4,
        out_shape=[struct(flat_shape, kind) for kind in (BF, F32, F32, F32)],
        scratch_shapes=[pltpu.VMEM((toks * heads // steps, width), F32)],
        compiler_params=params(),
        name="final",
    )(place, out, sums[0], *queries_part, *rim_part)
    return tuple(x.reshape(toks, heads, width) for x in outs)


def solution(mesh):
    spec = P("ctx", "head", None)
    return jax.shard_map(
        shards,
        mesh=mesh,
        in_specs=(spec, spec, spec, spec, P()),
        out_specs=(spec, spec, spec, spec),
        check_vma=False,
    )
```

```python
import functools
import math

import jax
import jax.numpy as jnp
from jax import lax
from jax.experimental import pallas as pl
from jax.experimental.pallas import tpu as pltpu
from jax.sharding import PartitionSpec as P

HALF = 512
TILE = 256
NEG = -1e30
LOG2E = 1.0 / math.log(2.0)
VMEM_BYTES = 63 * 1024 * 1024
BF = jnp.bfloat16
F32 = jnp.float32


def nt(a, b):
    return lax.dot_general(a, b, (((1,), (1,)), ((), ())), preferred_element_type=F32)


def nn(a, b):
    return lax.dot_general(a, b, (((1,), (0,)), ((), ())), preferred_element_type=F32)


def wide(column, width):
    return jnp.concatenate([column] * (width // column.shape[1]), axis=1)


def iota(shape, dim):
    return lax.broadcasted_iota(jnp.int32, shape, dim)


def params():
    return pltpu.CompilerParams(vmem_limit_bytes=VMEM_BYTES)


def as_column(row):
    return jnp.broadcast_to(row, (128, row.shape[1])).T[:, :1]


def pack_keys_kernel(heads, k, v, k_out, v_out, wide_rows):
    toks = k.shape[0] // heads
    for number, (source, target) in enumerate(((k, k_out), (v, v_out))):
        wide_rows[number] = source[...].astype(F32)
        for head in range(heads):
            target[0, head] = wide_rows[number, pl.ds(head, toks, stride=heads), :].astype(BF)


def pack_queries_kernel(heads, slots, q, g, k, v, pos_row, qd, slot_rows, wide_rows, acc):
    step = pl.program_id(0)
    toks = q.shape[0] // heads
    row = pos_row[...]
    count = row.shape[1]
    base = lax.axis_index("ctx") * (toks * pl.num_programs(0))
    column = as_column(row)
    tok = iota((count, toks), 1) + (base + step * toks)
    hit = jnp.sum((column == tok).astype(F32), axis=0, keepdims=True)
    rank = jnp.sum(((column >= base) & (column < tok)).astype(F32), axis=0, keepdims=True)
    slot = iota((slots, toks), 0).astype(F32)
    pick = jnp.where((hit > 0) & (rank == slot), 1.0, 0.0).astype(BF)
    tok = iota((toks, count), 0) + (base + step * toks)
    hit_column = jnp.sum((row == tok).astype(F32), axis=1, keepdims=True)
    tables = [[], [k[0, h] for h in range(heads)], [v[0, h] for h in range(heads)], []]
    for number, source in ((0, q), (3, g)):
        wide_rows[number // 3] = source[...].astype(F32)
        for head in range(heads):
            rows = wide_rows[number // 3, pl.ds(head, toks, stride=heads), :]
            tables[number].append(rows.astype(BF))
            if number == 0:
                qd[0, head] = rows.astype(BF)
            else:
                qd[1, head] = jnp.where(hit_column > 0, 0.0, rows).astype(BF)
    for number in range(4):
        found = nn(pick, jnp.concatenate(tables[number], axis=1))
        for head in range(heads):
            part = found[:, head * 128 : (head + 1) * 128]
            acc[number, head] = jnp.where(step == 0, part, acc[number, head] + part)

    @pl.when(step == pl.num_programs(0) - 1)
    def _():
        slot_rows[...] = acc[...].astype(BF)


def mask_kernel(orders, slots, seq_rows, pos_row, bias, compact, expand, place):
    toks = place.shape[0]
    me = lax.axis_index("ctx")
    base = me * toks
    row = pos_row[...]
    count = row.shape[1]
    column = as_column(row)
    for start in range(0, bias.shape[0], TILE):
        key = iota((TILE, count), 0) + (base - HALF + start)
        hits = jnp.sum((row == key).astype(F32), axis=1, keepdims=True)
        key = key[:, :1]
        out = (hits > 0) | (key < 0) | (key >= seq_rows)
        bias[start : start + TILE, :] = jnp.broadcast_to(jnp.where(out, NEG, 0.0), (TILE, 128))
    tok = iota((toks, count), 0) + base
    hit = jnp.sum((row == tok).astype(F32), axis=1, keepdims=True)
    rank = jnp.sum(((row >= base) & (row < tok)).astype(F32), axis=1, keepdims=True)
    slot = iota((toks, slots), 1).astype(F32)
    place[...] = jnp.where((hit > 0) & (rank == slot), 1.0, 0.0).astype(BF)
    for part, (first, second) in enumerate(zip(*orders)):
        low = (me ^ jnp.where(me % 2 == 0, first, second)) * toks
        inside = jnp.sum((column < low).astype(jnp.int32), axis=0, keepdims=True)
        held = jnp.sum((column < low + toks).astype(jnp.int32), axis=0, keepdims=True) - inside
        slot = iota((slots, count), 0)
        target = iota((slots, count), 1)
        hot = (target == inside + slot) & (slot < held)
        expand[part * slots : (part + 1) * slots, :] = jnp.where(hot, 1.0, 0.0).astype(BF)
    compact[...] = expand[...].astype(F32).T.astype(BF)


def stats_kernel(scale2, compact, *refs):
    parts, (k, v, rows, stats) = refs[:-4], refs[-4:]
    pieces = []
    for part in parts:
        for i in range(part.shape[0]):
            pieces.append(jnp.concatenate([part[i, number, 0] for number in range(4)], axis=1))
    packed = nn(compact[...], jnp.concatenate(pieces, axis=0)).astype(BF)
    width = k.shape[3]
    table = [packed[:, number * width : (number + 1) * width] for number in range(4)]
    for number in range(4):
        rows[number, 0] = table[number]
    queries, _, _, grads = table
    scores = nt(k[0, 0], queries) * scale2
    top = jnp.max(scores, axis=0, keepdims=True)
    weights = jnp.exp2(scores - top)
    stats[0, 0, 0:1, :] = top
    stats[0, 0, 1:2, :] = jnp.sum(weights, axis=0, keepdims=True)
    stats[0, 0, 2:3, :] = jnp.sum(weights * nt(v[0, 0], grads), axis=0, keepdims=True)


def band(scores, low):
    rows, columns = iota(scores.shape, 0), iota(scores.shape, 1)
    return jnp.where(rows <= columns if low else rows >= columns, scores, NEG)


def join(blocks, number, buf):
    toks = blocks[0].shape[2]
    for place, block in enumerate(blocks):
        buf[place * toks : (place + 1) * toks, :] = block[number, 0]


def global_kernel(scale, scale2, k, v, rows, stats, dkv, ends):
    g_query, g_grad = rows[0, 0], rows[3, 0]
    tops = stats[:, 0, 0:1, :]
    top = jnp.max(tops, axis=0)
    factor = jnp.exp2(tops - top[None])
    total = jnp.sum(stats[:, 0, 1:2, :] * factor, axis=0)
    g_dot = jnp.sum(stats[:, 0, 2:3, :] * factor, axis=0) / total
    g_log = top + jnp.log2(total)
    weights = jnp.exp2(nt(k[0, 0], g_query) * scale2 - g_log)
    narrow = weights.astype(BF)
    slopes = (weights * (nt(v[0, 0], g_grad) - g_dot)).astype(BF)
    dkv[0, 0] = nn(slopes, g_query) * scale
    dkv[1, 0] = nn(narrow, g_grad)
    ends[0, 0] = nn(v[0, 0].T, narrow).T.astype(BF)
    ends[1, 0] = (nn(k[0, 0].T, slopes) * scale).T.astype(BF)


def local_kernel(
    scale, scale2, slots, qd, k_low, k_own, k_high, v_low, v_own, v_high, rows, bias, before, ends, expand,
    out, log_dot, dq, dkv, kept, sent, keys, values, score_buf, probs, slopes,
):
    toks = k_own.shape[2]
    reach = 2 * HALF + TILE
    span = keys.shape[0] - rows.shape[2]
    width = keys.shape[1]
    join((k_low, k_own, k_high), 0, keys)
    join((v_low, v_own, v_high), 0, values)
    keys[span:, :] = rows[1, 0]
    values[span:, :] = rows[2, 0]
    key_t = keys[...].T
    value_t = values[...].T
    grad_t = qd[1, 0].T
    for q_tile in range(toks // TILE):
        lanes = slice(q_tile * TILE, (q_tile + 1) * TILE)
        query = qd[0, 0, lanes, :]
        grad = qd[1, 0, lanes, :]
        starts = [q_tile * TILE + piece for piece in range(0, reach, TILE)]
        starts += list(range(span, keys.shape[0], TILE))
        best = None
        for piece, start in enumerate(starts):
            scores = nt(keys[start : start + TILE, :], query) * scale2
            if start < span:
                scores = scores + wide(bias[start : start + TILE, :], TILE)
            if piece == 0:
                scores = band(scores, False)
            elif piece == reach // TILE - 1:
                scores = band(scores, True)
            score_buf[piece * TILE : (piece + 1) * TILE, :] = scores
            part = jnp.max(scores.reshape(TILE // 8, 8, TILE), axis=0)
            best = part if best is None else jnp.maximum(best, part)
        top = jnp.max(best, axis=0, keepdims=True)
        total = None
        for piece, start in enumerate(starts):
            rows_ = slice(piece * TILE, (piece + 1) * TILE)
            weights = jnp.exp2(score_buf[rows_, :] - top)
            score_buf[rows_, :] = weights
            probs[start : start + TILE, lanes] = weights.astype(BF)
            part = jnp.sum(weights.reshape(TILE // 8, 8, TILE), axis=0)
            total = part if total is None else total + part
        total = jnp.sum(total, axis=0, keepdims=True)
        window = slice(q_tile * TILE, q_tile * TILE + reach)
        acc = nn(value_t[:, window], probs[window, lanes]) + nn(value_t[:, span:], probs[span:, lanes])
        inverse = 1.0 / total
        acc = acc * inverse
        dot = jnp.sum(grad_t[:, lanes].astype(F32) * acc, axis=0, keepdims=True)
        log_dot[0, 0:1, lanes] = top + jnp.log2(total)
        log_dot[0, 1:2, lanes] = dot
        out[0, lanes, :] = acc.T.astype(BF)
        for piece, start in enumerate(starts):
            weights = score_buf[piece * TILE : (piece + 1) * TILE, :] * inverse
            rise = nt(values[start : start + TILE, :], grad) - dot
            slopes[start : start + TILE, lanes] = (weights * rise).astype(BF)
            if HALF <= start < HALF + toks or start >= span:
                probs[start : start + TILE, lanes] = weights.astype(BF)
        acc = nn(key_t[:, window], slopes[window, lanes]) + nn(key_t[:, span:], slopes[span:, lanes])
        dq[0, lanes, :] = (acc * scale).T
    own = slice(HALF, HALF + toks)
    dkv[0, 0] = before[0, 0] + nn(slopes[own, :], qd[0, 0]) * scale
    dkv[1, 0] = before[1, 0] + nn(probs[own, :], qd[1, 0])
    g_dk = (nn(slopes[span:, :], qd[0, 0]) * scale).astype(BF)
    g_dv = nn(probs[span:, :], qd[1, 0]).astype(BF)
    spread = nn(expand[...], jnp.concatenate([ends[0, 0], ends[1, 0], g_dk, g_dv], axis=1)).astype(BF)
    half = kept.shape[0]
    for part in range(2 * half):
        sums = kept if part < half else sent
        for number in range(4):
            sums[part % half, number, 0] = spread[
                part * slots : (part + 1) * slots, number * width : (number + 1) * width
            ]


def rim_kernel(
    scale, scale2, k_own, v_own, bias, qd_low, qd_high, log_low, log_high, partial, dkv, queries, grads, probs, slopes
):
    toks = k_own.shape[2]
    reach = toks + TILE
    join((qd_low, qd_high), 0, queries)
    join((qd_low, qd_high), 1, grads)
    for k_tile in range(toks // TILE):
        span = slice(k_tile * TILE, (k_tile + 1) * TILE)
        key = k_own[0, 0, span, :]
        value = v_own[0, 0, span, :]
        key_bias = wide(bias[HALF + k_tile * TILE : HALF + (k_tile + 1) * TILE, :], TILE)
        for piece in range(reach // TILE):
            start = (k_tile + piece) * TILE
            log_dot, offset = (log_low, start) if start < toks else (log_high, start - toks)
            lanes = slice(offset, offset + TILE)
            scores = nt(key, queries[start : start + TILE, :]) * scale2 + key_bias
            if piece == 0:
                scores = band(scores, True)
            elif piece == reach // TILE - 1:
                scores = band(scores, False)
            weights = jnp.exp2(scores - log_dot[0, 0:1, lanes])
            slope = weights * (nt(value, grads[start : start + TILE, :]) - log_dot[0, 1:2, lanes])
            spot = slice(piece * TILE, (piece + 1) * TILE)
            probs[span, spot] = weights.astype(BF)
            slopes[span, spot] = slope.astype(BF)
        window = slice(k_tile * TILE, k_tile * TILE + reach)
        dkv[0, 0, span, :] = partial[0, 0, span, :] + nn(slopes[span, :], queries[window, :]) * scale
        dkv[1, 0, span, :] = partial[1, 0, span, :] + nn(probs[span, :], grads[window, :])


def final_kernel(
    place, out, sums, dq, dkv, attn, query_grad, key_grad, value_grad, wide_rows
):
    heads, toks = out.shape[0], out.shape[1]
    hot = place[...]
    is_global = jnp.sum(hot.astype(F32), axis=1, keepdims=True) > 0
    for head in range(heads):
        rows = pl.ds(head, toks, stride=heads)
        wide_rows[rows, :] = jnp.where(is_global, nn(hot, sums[0, head]), out[head].astype(F32))
        query_grad[rows, :] = dq[head] + nn(hot, sums[1, head])
        key_grad[rows, :] = dkv[0, head] + nn(hot, sums[2, head])
        value_grad[rows, :] = dkv[1, head] + nn(hot, sums[3, head])
    attn[...] = wide_rows[...].astype(BF)


def cost(flops, moved, exps=0):
    return pl.CostEstimate(flops=int(flops), bytes_accessed=int(moved), transcendentals=int(exps))


def struct(shape, dtype):
    return jax.ShapeDtypeStruct(shape, dtype)


def whole(shape):
    return pl.BlockSpec(shape, lambda head: (0,) * len(shape))


def per_head(shape, dim, first=0):
    block = tuple(1 if i == dim else size for i, size in enumerate(shape))
    return pl.BlockSpec(
        block, lambda head: tuple(head + first if i == dim else 0 for i in range(len(shape)))
    )


def shards(query_rows, key_rows, value_rows, out_grad, global_pos):
    toks, heads, width = query_rows.shape
    count = global_pos.shape[0]
    devices = lax.axis_size("ctx")
    slots = max(16, 2 * count // devices)
    scale = width ** (-0.5)
    scale2 = scale * LOG2E
    bits = devices.bit_length() - 1
    ways = [list(range(1, bits)) + [0], list(range(1, bits)) + [0]]
    orders = []
    for way in ways:
        order = [0]
        for bit in way[:-1]:
            order = order + [one | (1 << bit) for one in order]
        orders.append(order)
    orders = [mine + [one | 1 for one in other] for mine, other in (orders, orders[::-1])]
    pos_row = global_pos.reshape(1, count)
    q_flat, k_flat, v_flat, g_flat = (
        x.reshape(toks * heads, width) for x in (query_rows, key_rows, value_rows, out_grad)
    )

    def swap(value, stage):
        pairs = [(i, i ^ (1 << ways[i % 2][stage])) for i in range(devices)]
        return lax.ppermute(value, "ctx", pairs)

    def from_low(value):
        return lax.ppermute(value, "ctx", [(i, i + 1) for i in range(devices - 1)])

    def from_high(value):
        return lax.ppermute(value, "ctx", [(i + 1, i) for i in range(devices - 1)])

    def after(value, earlier):
        return lax.optimization_barrier((value, earlier))[0]

    pair_shape = (2, heads, toks, width)
    slot_shape = (4, heads, slots, width)
    steps = 1
    flat_spec = pl.BlockSpec((toks * heads // steps, width), lambda i: (i, 0))
    pair_spec = pl.BlockSpec((2, heads, toks // steps, width), lambda i: (0, 0, i, 0))
    wide_pair = pltpu.VMEM((2, toks * heads // steps, width), F32)
    lone_shape = (1, heads, toks, width)
    lone_spec = pl.BlockSpec((1, heads, toks // steps, width), lambda i: (0, 0, i, 0))
    k, v = pl.pallas_call(
        functools.partial(pack_keys_kernel, heads),
        grid=(steps,),
        in_specs=[flat_spec, flat_spec],
        out_specs=(lone_spec, lone_spec),
        out_shape=(struct(lone_shape, BF), struct(lone_shape, BF)),
        scratch_shapes=[wide_pair],
        compiler_params=params(),
        name="pack_keys",
    )(k_flat, v_flat)

    qd, slot_rows = pl.pallas_call(
        functools.partial(pack_queries_kernel, heads, slots),
        grid=(steps,),
        in_specs=[flat_spec, flat_spec, lone_spec, lone_spec, whole((1, count))],
        out_specs=(pair_spec, whole(slot_shape)),
        out_shape=(struct(pair_shape, BF), struct(slot_shape, BF)),
        scratch_shapes=[wide_pair, pltpu.VMEM(slot_shape, F32)],
        compiler_params=params(),
        name="pack_queries",
    )(q_flat, g_flat, k, v, pos_row)

    held = [slot_rows[None]]
    k_low, k_high = from_low(k), from_high(k)
    v_late = after(v, (k_low, k_high))
    v_low, v_high = from_low(v_late), from_high(v_late)
    for stage in range(bits):
        send = jnp.concatenate(held, axis=0) if len(held) > 1 else held[0]
        if stage == 1:
            send = after(send, (k_low, k_high))
        elif stage == bits - 1:
            send = after(send, (v_low, v_high))
        held.append(swap(send, stage))
    qd_late = after(qd, (v_low, v_high))
    qd_low, qd_high = from_low(qd_late), from_high(qd_late)

    span = toks + 2 * HALF
    bias, compact, expand, place = pl.pallas_call(
        functools.partial(mask_kernel, orders, slots, toks * devices),
        out_shape=(
            struct((span, 128), F32),
            struct((count, devices * slots), BF),
            struct((devices * slots, count), BF),
            struct((toks, slots), BF),
        ),
        compiler_params=params(),
        name="masks",
    )(pos_row)

    row_shape = (4, heads, count, width)
    rows, stats = pl.pallas_call(
        functools.partial(stats_kernel, scale2),
        grid=(heads,),
        in_specs=[whole(compact.shape)]
        + [per_head(part.shape, 2) for part in held]
        + [per_head(lone_shape, 1)] * 2,
        out_specs=(per_head(row_shape, 1), per_head((1, heads, 3, count), 1)),
        out_shape=(struct(row_shape, BF), struct((1, heads, 3, count), F32)),
        compiler_params=params(),
        cost_estimate=cost(2.7e9, 4e6),
        name="global_stats",
    )(compact, *held, k, v)

    for stage in range(bits):
        stats = jnp.concatenate([stats, swap(stats, stage)], axis=0)

    ends_shape = (2, heads, count, width)
    dkv, ends = pl.pallas_call(
        functools.partial(global_kernel, scale, scale2),
        grid=(heads,),
        in_specs=[per_head(lone_shape, 1)] * 2 + [per_head(row_shape, 1), per_head(stats.shape, 1)],
        out_specs=(per_head(pair_shape, 1), per_head(ends_shape, 1)),
        out_shape=(struct(pair_shape, F32), struct(ends_shape, BF)),
        compiler_params=params(),
        cost_estimate=cost(2e9, 5e6, 1e6),
        name="global_queries",
    )(k, v, rows, stats)

    sum_shape = (devices // 2, 4, heads, slots, width)
    out, log_dot, dq, dkv, sums, sent = pl.pallas_call(
        functools.partial(local_kernel, scale, scale2, slots),
        grid=(heads,),
        in_specs=[per_head(pair_shape, 1)]
        + [per_head(lone_shape, 1)] * 6
        + [per_head(row_shape, 1), whole(bias.shape), per_head(pair_shape, 1)]
        + [per_head(ends_shape, 1), whole(expand.shape)],
        out_specs=(
            per_head((heads, toks, width), 0),
            per_head((heads, 2, toks), 0),
            per_head((heads, toks, width), 0),
            per_head(pair_shape, 1),
            per_head(sum_shape, 2),
            per_head(sum_shape, 2),
        ),
        out_shape=(
            struct((heads, toks, width), BF),
            struct((heads, 2, toks), F32),
            struct((heads, toks, width), F32),
            struct(pair_shape, F32),
            struct(sum_shape, BF),
            struct(sum_shape, BF),
        ),
        scratch_shapes=[
            pltpu.VMEM((span + count, width), BF),
            pltpu.VMEM((span + count, width), BF),
            pltpu.VMEM((2 * HALF + TILE + count, TILE), F32),
            pltpu.VMEM((span + count, toks), BF),
            pltpu.VMEM((span + count, toks), BF),
        ],
        compiler_params=params(),
        cost_estimate=cost(2e9, 5e6, 3e6),
        name="local",
    )(qd, k_low, k, k_high, v_low, v, v_high, rows, bias, dkv, ends, expand)
    log_low, log_high = from_low(log_dot), from_high(log_dot)

    sums = after(sums, (qd_low, qd_high)) + swap(sent, bits - 1)
    for stage in reversed(range(bits - 1)):
        half = sums.shape[0] // 2
        sums = sums[:half] + swap(sums[half:], stage)

    dkv = pl.pallas_call(
        functools.partial(rim_kernel, scale, scale2),
        grid=(heads,),
        in_specs=[per_head(lone_shape, 1)] * 2
        + [whole(bias.shape)]
        + [per_head(pair_shape, 1)] * 2
        + [per_head(log_dot.shape, 0)] * 2
        + [per_head(pair_shape, 1)],
        out_specs=per_head(pair_shape, 1),
        out_shape=struct(pair_shape, F32),
        scratch_shapes=[
            pltpu.VMEM((2 * toks, width), BF),
            pltpu.VMEM((2 * toks, width), BF),
            pltpu.VMEM((toks, toks + TILE), BF),
            pltpu.VMEM((toks, toks + TILE), BF),
        ],
        compiler_params=params(),
        cost_estimate=cost(4e9, 8e6, 2e6),
        name="rim",
    )(k, v, bias, qd_low, qd_high, log_low, log_high, dkv)

    flat_shape = (toks * heads, width)
    steps = 2
    outs = pl.pallas_call(
        final_kernel,
        grid=(steps,),
        in_specs=[
            pl.BlockSpec((toks // steps, slots), lambda i: (i, 0)),
            pl.BlockSpec((heads, toks // steps, width), lambda i: (0, i, 0)),
            whole(slot_shape),
            pl.BlockSpec((heads, toks // steps, width), lambda i: (0, i, 0)),
            pl.BlockSpec((2, heads, toks // steps, width), lambda i: (0, 0, i, 0)),
        ],
        out_specs=[pl.BlockSpec((toks * heads // steps, width), lambda i: (i, 0))] * 4,
        out_shape=[struct(flat_shape, kind) for kind in (BF, F32, F32, F32)],
        scratch_shapes=[pltpu.VMEM((toks * heads // steps, width), F32)],
        compiler_params=params(),
        name="final",
    )(place, out, sums[0], dq, dkv)
    return tuple(x.reshape(toks, heads, width) for x in outs)


def solution(mesh):
    spec = P("ctx", "head", None)
    return jax.shard_map(
        shards,
        mesh=mesh,
        in_specs=(spec, spec, spec, spec, P()),
        out_specs=(spec, spec, spec, spec),
        check_vma=False,
    )
```

```python
import functools
import math

import jax
import jax.numpy as jnp
from jax import lax
from jax.experimental import pallas as pl
from jax.experimental.pallas import tpu as pltpu
from jax.sharding import PartitionSpec as P

HALF = 512
TILE = 256
NEG = -1e30
LOG2E = 1.0 / math.log(2.0)
VMEM_BYTES = 63 * 1024 * 1024
BF = jnp.bfloat16
F32 = jnp.float32


def nt(a, b):
    return lax.dot_general(a, b, (((1,), (1,)), ((), ())), preferred_element_type=F32)


def nn(a, b):
    return lax.dot_general(a, b, (((1,), (0,)), ((), ())), preferred_element_type=F32)


def wide(column, width):
    return jnp.concatenate([column] * (width // column.shape[1]), axis=1)


def iota(shape, dim):
    return lax.broadcasted_iota(jnp.int32, shape, dim)


def params():
    return pltpu.CompilerParams(vmem_limit_bytes=VMEM_BYTES)


def as_column(row):
    return jnp.broadcast_to(row, (128, row.shape[1])).T[:, :1]


def pack_keys_kernel(heads, k, v, k_out, v_out, wide_rows):
    toks = k.shape[0] // heads
    for number, (source, target) in enumerate(((k, k_out), (v, v_out))):
        wide_rows[number] = source[...].astype(F32)
        for head in range(heads):
            target[0, head] = wide_rows[number, pl.ds(head, toks, stride=heads), :].astype(BF)


def pack_queries_kernel(heads, q, g, pos_row, qd, wide_rows):
    toks = q.shape[0] // heads
    tok = iota((toks, pos_row.shape[1]), 0) + lax.axis_index("ctx") * toks
    hit = jnp.sum((pos_row[...] == tok).astype(F32), axis=1, keepdims=True)
    for number, source in enumerate((q, g)):
        wide_rows[number] = source[...].astype(F32)
        for head in range(heads):
            rows = wide_rows[number, pl.ds(head, toks, stride=heads), :]
            qd[number, head] = (rows if number == 0 else jnp.where(hit > 0, 0.0, rows)).astype(BF)


def slots_kernel(heads, slots, q, k, v, g, pos_row, slot_rows):
    row = pos_row[...]
    count = row.shape[1]
    toks = q.shape[0] // heads
    base = lax.axis_index("ctx") * toks
    column = as_column(row)
    place = iota((count, toks * heads), 1)
    tok = place // heads + base
    hit = jnp.sum((column == tok).astype(F32), axis=0, keepdims=True)
    rank = jnp.sum(((column >= base) & (column < tok)).astype(F32), axis=0, keepdims=True)
    wanted = jnp.where(hit > 0, rank, -1.0)
    slot = iota((slots, toks * heads), 0).astype(F32)
    member = iota((slots, toks * heads), 1) % heads
    table = jnp.concatenate([source[...] for source in (q, k, v, g)], axis=1)
    width = q.shape[1]
    for head in range(heads):
        pick = jnp.where((wanted == slot) & (member == head), 1.0, 0.0).astype(BF)
        found = nn(pick, table).astype(BF)
        for number in range(4):
            slot_rows[number, head] = found[:, number * width : (number + 1) * width]


def mask_kernel(slots, seq_rows, pos_row, bias, compact, place):
    toks = place.shape[0]
    me = lax.axis_index("ctx")
    base = me * toks
    row = pos_row[...]
    count = row.shape[1]
    column = as_column(row)
    for start in range(0, bias.shape[0], TILE):
        key = iota((TILE, count), 0) + (base - HALF + start)
        hits = jnp.sum((row == key).astype(F32), axis=1, keepdims=True)
        key = key[:, :1]
        out = (hits > 0) | (key < 0) | (key >= seq_rows)
        bias[start : start + TILE, :] = jnp.broadcast_to(jnp.where(out, NEG, 0.0), (TILE, 128))
    tok = iota((toks, count), 0) + base
    hit = jnp.sum((row == tok).astype(F32), axis=1, keepdims=True)
    order = jnp.sum((row < tok).astype(F32), axis=1, keepdims=True)
    target = iota((toks, count), 1).astype(F32)
    place[...] = jnp.where((hit > 0) & (order == target), 1.0, 0.0).astype(BF)
    owner = iota((count, compact.shape[1]), 1) // slots
    inside = jnp.sum((column < owner * toks).astype(jnp.int32), axis=0, keepdims=True)
    held = jnp.sum((column < (owner + 1) * toks).astype(jnp.int32), axis=0, keepdims=True) - inside
    slot = iota(compact.shape, 1) % slots
    hot = (iota(compact.shape, 0) == inside + slot) & (slot < held)
    compact[...] = jnp.where(hot, 1.0, 0.0).astype(BF)


def stats_kernel(scale2, compact, gathered, k, v, rows, stats):
    pieces = []
    for owner in range(gathered.shape[0]):
        pieces.append(jnp.concatenate([gathered[owner, number, 0] for number in range(4)], axis=1))
    packed = nn(compact[...], jnp.concatenate(pieces, axis=0)).astype(BF)
    width = k.shape[3]
    table = [packed[:, number * width : (number + 1) * width] for number in range(4)]
    for number in range(4):
        rows[number, 0] = table[number]
    queries, _, _, grads = table
    scores = nt(k[0, 0], queries) * scale2
    top = jnp.max(scores, axis=0, keepdims=True)
    weights = jnp.exp2(scores - top)
    stats[0, 0, 0:1, :] = top
    stats[0, 0, 1:2, :] = jnp.sum(weights, axis=0, keepdims=True)
    stats[0, 0, 2:3, :] = jnp.sum(weights * nt(v[0, 0], grads), axis=0, keepdims=True)


def band(scores, low):
    rows, columns = iota(scores.shape, 0), iota(scores.shape, 1)
    return jnp.where(rows <= columns if low else rows >= columns, scores, NEG)


def join(blocks, number, buf):
    toks = blocks[0].shape[2]
    for place, block in enumerate(blocks):
        buf[place * toks : (place + 1) * toks, :] = block[number, 0]


def global_kernel(scale, scale2, k, v, rows, stats, dkv, ends):
    g_query, g_grad = rows[0, 0], rows[3, 0]
    tops = stats[:, 0, 0:1, :]
    top = jnp.max(tops, axis=0)
    factor = jnp.exp2(tops - top[None])
    total = jnp.sum(stats[:, 0, 1:2, :] * factor, axis=0)
    g_dot = jnp.sum(stats[:, 0, 2:3, :] * factor, axis=0) / total
    g_log = top + jnp.log2(total)
    weights = jnp.exp2(nt(k[0, 0], g_query) * scale2 - g_log)
    narrow = weights.astype(BF)
    slopes = (weights * (nt(v[0, 0], g_grad) - g_dot)).astype(BF)
    dkv[0, 0] = nn(slopes, g_query) * scale
    dkv[1, 0] = nn(narrow, g_grad)
    ends[0, 0] = nn(v[0, 0].T, narrow).T.astype(BF)
    ends[1, 0] = (nn(k[0, 0].T, slopes) * scale).T.astype(BF)


def local_kernel(
    scale, scale2, qd, k_low, k_own, k_high, v_low, v_own, v_high, rows, bias,
    out, log_dot, dq, dkv, sums, keys, values, score_buf, probs, slopes,
):
    toks = k_own.shape[2]
    reach = 2 * HALF + TILE
    span = keys.shape[0] - rows.shape[2]
    width = keys.shape[1]
    join((k_low, k_own, k_high), 0, keys)
    join((v_low, v_own, v_high), 0, values)
    keys[span:, :] = rows[1, 0]
    values[span:, :] = rows[2, 0]
    key_t = keys[...].T
    value_t = values[...].T
    grad_t = qd[1, 0].T
    for q_tile in range(toks // TILE):
        lanes = slice(q_tile * TILE, (q_tile + 1) * TILE)
        query = qd[0, 0, lanes, :]
        grad = qd[1, 0, lanes, :]
        starts = [q_tile * TILE + piece for piece in range(0, reach, TILE)]
        starts += list(range(span, keys.shape[0], TILE))
        best = None
        for piece, start in enumerate(starts):
            scores = nt(keys[start : start + TILE, :], query) * scale2
            if start < span:
                scores = scores + wide(bias[start : start + TILE, :], TILE)
            if piece == 0:
                scores = band(scores, False)
            elif piece == reach // TILE - 1:
                scores = band(scores, True)
            score_buf[piece * TILE : (piece + 1) * TILE, :] = scores
            part = jnp.max(scores.reshape(TILE // 8, 8, TILE), axis=0)
            best = part if best is None else jnp.maximum(best, part)
        top = jnp.max(best, axis=0, keepdims=True)
        total = None
        for piece, start in enumerate(starts):
            rows_ = slice(piece * TILE, (piece + 1) * TILE)
            weights = jnp.exp2(score_buf[rows_, :] - top)
            score_buf[rows_, :] = weights
            probs[start : start + TILE, lanes] = weights.astype(BF)
            part = jnp.sum(weights.reshape(TILE // 8, 8, TILE), axis=0)
            total = part if total is None else total + part
        total = jnp.sum(total, axis=0, keepdims=True)
        window = slice(q_tile * TILE, q_tile * TILE + reach)
        acc = nn(value_t[:, window], probs[window, lanes]) + nn(value_t[:, span:], probs[span:, lanes])
        inverse = 1.0 / total
        acc = acc * inverse
        dot = jnp.sum(grad_t[:, lanes].astype(F32) * acc, axis=0, keepdims=True)
        log_dot[0, 0:1, lanes] = top + jnp.log2(total)
        log_dot[0, 1:2, lanes] = dot
        out[0, lanes, :] = acc.T.astype(BF)
        for piece, start in enumerate(starts):
            weights = score_buf[piece * TILE : (piece + 1) * TILE, :] * inverse
            rise = nt(values[start : start + TILE, :], grad) - dot
            slopes[start : start + TILE, lanes] = (weights * rise).astype(BF)
            if HALF <= start < HALF + toks or start >= span:
                probs[start : start + TILE, lanes] = weights.astype(BF)
        acc = nn(key_t[:, window], slopes[window, lanes]) + nn(key_t[:, span:], slopes[span:, lanes])
        dq[0, lanes, :] = (acc * scale).T
    own = slice(HALF, HALF + toks)
    dkv[0, 0] = nn(slopes[own, :], qd[0, 0]) * scale
    dkv[1, 0] = nn(probs[own, :], qd[1, 0])
    sums[0, 0] = (nn(slopes[span:, :], qd[0, 0]) * scale).astype(BF)
    sums[1, 0] = nn(probs[span:, :], qd[1, 0]).astype(BF)


def rim_kernel(
    scale, scale2, k_own, v_own, bias, qd_low, qd_high, log_low, log_high, partial, dkv, queries, grads, probs, slopes
):
    toks = k_own.shape[2]
    reach = toks + TILE
    join((qd_low, qd_high), 0, queries)
    join((qd_low, qd_high), 1, grads)
    for k_tile in range(toks // TILE):
        span = slice(k_tile * TILE, (k_tile + 1) * TILE)
        key = k_own[0, 0, span, :]
        value = v_own[0, 0, span, :]
        key_bias = wide(bias[HALF + k_tile * TILE : HALF + (k_tile + 1) * TILE, :], TILE)
        for piece in range(reach // TILE):
            start = (k_tile + piece) * TILE
            log_dot, offset = (log_low, start) if start < toks else (log_high, start - toks)
            lanes = slice(offset, offset + TILE)
            scores = nt(key, queries[start : start + TILE, :]) * scale2 + key_bias
            if piece == 0:
                scores = band(scores, True)
            elif piece == reach // TILE - 1:
                scores = band(scores, False)
            weights = jnp.exp2(scores - log_dot[0, 0:1, lanes])
            slope = weights * (nt(value, grads[start : start + TILE, :]) - log_dot[0, 1:2, lanes])
            spot = slice(piece * TILE, (piece + 1) * TILE)
            probs[span, spot] = weights.astype(BF)
            slopes[span, spot] = slope.astype(BF)
        window = slice(k_tile * TILE, k_tile * TILE + reach)
        dkv[0, 0, span, :] = partial[0, 0, span, :] + nn(slopes[span, :], queries[window, :]) * scale
        dkv[1, 0, span, :] = partial[1, 0, span, :] + nn(probs[span, :], grads[window, :])


def final_kernel(
    place, out, ends, sums, dq, dkv, extra, attn, query_grad, key_grad, value_grad, wide_rows
):
    heads, toks = out.shape[0], out.shape[1]
    hot = place[...]
    is_global = jnp.sum(hot.astype(F32), axis=1, keepdims=True) > 0
    for head in range(heads):
        rows = pl.ds(head, toks, stride=heads)
        wide_rows[rows, :] = jnp.where(is_global, nn(hot, ends[0, head]), out[head].astype(F32))
        query_grad[rows, :] = dq[head] + nn(hot, ends[1, head])
        key_grad[rows, :] = dkv[0, head] + extra[0, head] + nn(hot, sums[0, head])
        value_grad[rows, :] = dkv[1, head] + extra[1, head] + nn(hot, sums[1, head])
    attn[...] = wide_rows[...].astype(BF)


def cost(flops, moved, exps=0):
    return pl.CostEstimate(flops=int(flops), bytes_accessed=int(moved), transcendentals=int(exps))


def struct(shape, dtype):
    return jax.ShapeDtypeStruct(shape, dtype)


def whole(shape):
    return pl.BlockSpec(shape, lambda head: (0,) * len(shape))


def per_head(shape, dim, first=0):
    block = tuple(1 if i == dim else size for i, size in enumerate(shape))
    return pl.BlockSpec(
        block, lambda head: tuple(head + first if i == dim else 0 for i in range(len(shape)))
    )


def shards(query_rows, key_rows, value_rows, out_grad, global_pos):
    toks, heads, width = query_rows.shape
    count = global_pos.shape[0]
    devices = lax.axis_size("ctx")
    slots = max(16, 2 * count // devices)
    scale = width ** (-0.5)
    scale2 = scale * LOG2E
    pos_row = global_pos.reshape(1, count)
    q_flat, k_flat, v_flat, g_flat = (
        x.reshape(toks * heads, width) for x in (query_rows, key_rows, value_rows, out_grad)
    )

    def from_low(value):
        return lax.ppermute(value, "ctx", [(i, i + 1) for i in range(devices - 1)])

    def from_high(value):
        return lax.ppermute(value, "ctx", [(i + 1, i) for i in range(devices - 1)])

    def after(value, earlier):
        return lax.optimization_barrier((value, earlier))[0]

    pair_shape = (2, heads, toks, width)
    slot_shape = (4, heads, slots, width)
    steps = 1
    flat_spec = pl.BlockSpec((toks * heads // steps, width), lambda i: (i, 0))
    pair_spec = pl.BlockSpec((2, heads, toks // steps, width), lambda i: (0, 0, i, 0))
    wide_pair = pltpu.VMEM((2, toks * heads // steps, width), F32)
    lone_shape = (1, heads, toks, width)
    lone_spec = pl.BlockSpec((1, heads, toks // steps, width), lambda i: (0, 0, i, 0))
    k, v = pl.pallas_call(
        functools.partial(pack_keys_kernel, heads),
        grid=(steps,),
        in_specs=[flat_spec, flat_spec],
        out_specs=(lone_spec, lone_spec),
        out_shape=(struct(lone_shape, BF), struct(lone_shape, BF)),
        scratch_shapes=[wide_pair],
        compiler_params=params(),
        name="pack_keys",
    )(k_flat, v_flat)

    qd = pl.pallas_call(
        functools.partial(pack_queries_kernel, heads),
        grid=(steps,),
        in_specs=[flat_spec, flat_spec, whole((1, count))],
        out_specs=pair_spec,
        out_shape=struct(pair_shape, BF),
        scratch_shapes=[wide_pair],
        compiler_params=params(),
        name="pack_queries",
    )(q_flat, g_flat, pos_row)
    slot_rows = pl.pallas_call(
        functools.partial(slots_kernel, heads, slots),
        out_shape=struct(slot_shape, BF),
        compiler_params=params(),
        name="slots",
    )(q_flat, k_flat, v_flat, g_flat, pos_row)
    gathered = lax.all_gather(slot_rows, "ctx")

    k_low, k_high = from_low(k), from_high(k)
    v_low, v_high = from_low(v), from_high(v)
    gathered = after(gathered, (k_low, k_high, v_low, v_high))

    span = toks + 2 * HALF
    bias, compact, place = pl.pallas_call(
        functools.partial(mask_kernel, slots, toks * devices),
        out_shape=(
            struct((span, 128), F32),
            struct((count, devices * slots), BF),
            struct((toks, count), BF),
        ),
        compiler_params=params(),
        name="masks",
    )(pos_row)

    row_shape = (4, heads, count, width)
    rows, stats = pl.pallas_call(
        functools.partial(stats_kernel, scale2),
        grid=(heads,),
        in_specs=[whole(compact.shape), per_head(gathered.shape, 2)]
        + [per_head(lone_shape, 1)] * 2,
        out_specs=(per_head(row_shape, 1), per_head((1, heads, 3, count), 1)),
        out_shape=(struct(row_shape, BF), struct((1, heads, 3, count), F32)),
        compiler_params=params(),
        cost_estimate=cost(2.7e9, 4e6),
        name="global_stats",
    )(compact, gathered, k, v)

    stats = lax.all_gather(stats, "ctx", axis=0, tiled=True)
    qd_late = after(qd, rows)
    qd_low, qd_high = from_low(qd_late), from_high(qd_late)

    ends_shape = (2, heads, count, width)
    extra, ends = pl.pallas_call(
        functools.partial(global_kernel, scale, scale2),
        grid=(heads,),
        in_specs=[per_head(lone_shape, 1)] * 2 + [per_head(row_shape, 1), per_head(stats.shape, 1)],
        out_specs=(per_head(pair_shape, 1), per_head(ends_shape, 1)),
        out_shape=(struct(pair_shape, F32), struct(ends_shape, BF)),
        compiler_params=params(),
        cost_estimate=cost(2e9, 5e6, 1e6),
        name="global_queries",
    )(k, v, rows, stats)

    ends = lax.psum(ends, "ctx")

    out, log_dot, dq, dkv, sums = pl.pallas_call(
        functools.partial(local_kernel, scale, scale2),
        grid=(heads,),
        in_specs=[per_head(pair_shape, 1)]
        + [per_head(lone_shape, 1)] * 6
        + [per_head(row_shape, 1), whole(bias.shape)],
        out_specs=(
            per_head((heads, toks, width), 0),
            per_head((heads, 2, toks), 0),
            per_head((heads, toks, width), 0),
            per_head(pair_shape, 1),
            per_head(ends_shape, 1),
        ),
        out_shape=(
            struct((heads, toks, width), BF),
            struct((heads, 2, toks), F32),
            struct((heads, toks, width), F32),
            struct(pair_shape, F32),
            struct(ends_shape, BF),
        ),
        scratch_shapes=[
            pltpu.VMEM((span + count, width), BF),
            pltpu.VMEM((span + count, width), BF),
            pltpu.VMEM((2 * HALF + TILE + count, TILE), F32),
            pltpu.VMEM((span + count, toks), BF),
            pltpu.VMEM((span + count, toks), BF),
        ],
        compiler_params=params(),
        cost_estimate=cost(2e9, 5e6, 3e6),
        name="local",
    )(qd, k_low, k, k_high, v_low, v, v_high, rows, bias)
    log_low, log_high = from_low(log_dot), from_high(log_dot)

    sums = lax.psum(sums, "ctx")

    dkv = pl.pallas_call(
        functools.partial(rim_kernel, scale, scale2),
        grid=(heads,),
        in_specs=[per_head(lone_shape, 1)] * 2
        + [whole(bias.shape)]
        + [per_head(pair_shape, 1)] * 2
        + [per_head(log_dot.shape, 0)] * 2
        + [per_head(pair_shape, 1)],
        out_specs=per_head(pair_shape, 1),
        out_shape=struct(pair_shape, F32),
        scratch_shapes=[
            pltpu.VMEM((2 * toks, width), BF),
            pltpu.VMEM((2 * toks, width), BF),
            pltpu.VMEM((toks, toks + TILE), BF),
            pltpu.VMEM((toks, toks + TILE), BF),
        ],
        compiler_params=params(),
        cost_estimate=cost(4e9, 8e6, 2e6),
        name="rim",
    )(k, v, bias, qd_low, qd_high, log_low, log_high, dkv)

    flat_shape = (toks * heads, width)
    steps = 2
    outs = pl.pallas_call(
        final_kernel,
        grid=(steps,),
        in_specs=[
            pl.BlockSpec((toks // steps, count), lambda i: (i, 0)),
            pl.BlockSpec((heads, toks // steps, width), lambda i: (0, i, 0)),
            whole(ends_shape),
            whole(ends_shape),
            pl.BlockSpec((heads, toks // steps, width), lambda i: (0, i, 0)),
            pl.BlockSpec((2, heads, toks // steps, width), lambda i: (0, 0, i, 0)),
            pl.BlockSpec((2, heads, toks // steps, width), lambda i: (0, 0, i, 0)),
        ],
        out_specs=[pl.BlockSpec((toks * heads // steps, width), lambda i: (i, 0))] * 4,
        out_shape=[struct(flat_shape, kind) for kind in (BF, F32, F32, F32)],
        scratch_shapes=[pltpu.VMEM((toks * heads // steps, width), F32)],
        compiler_params=params(),
        name="final",
    )(place, out, ends, sums, dq, dkv, extra)
    return tuple(x.reshape(toks, heads, width) for x in outs)


def solution(mesh):
    spec = P("ctx", "head", None)
    return jax.shard_map(
        shards,
        mesh=mesh,
        in_specs=(spec, spec, spec, spec, P()),
        out_specs=(spec, spec, spec, spec),
        check_vma=False,
    )
```

```python
import functools
import math

import jax
import jax.numpy as jnp
from jax import lax
from jax.experimental import pallas as pl
from jax.experimental.pallas import tpu as pltpu
from jax.sharding import PartitionSpec as P

HALF = 512
TILE = 256
NEG = -1e30
LOG2E = 1.0 / math.log(2.0)
VMEM_BYTES = 63 * 1024 * 1024
BF = jnp.bfloat16
F32 = jnp.float32


def nt(a, b):
    return lax.dot_general(a, b, (((1,), (1,)), ((), ())), preferred_element_type=F32)


def nn(a, b):
    return lax.dot_general(a, b, (((1,), (0,)), ((), ())), preferred_element_type=F32)


def wide(column, width):
    return jnp.concatenate([column] * (width // column.shape[1]), axis=1)


def iota(shape, dim):
    return lax.broadcasted_iota(jnp.int32, shape, dim)


def params():
    return pltpu.CompilerParams(vmem_limit_bytes=VMEM_BYTES)


def as_column(row):
    return jnp.broadcast_to(row, (128, row.shape[1])).T[:, :1]


def pack_keys_kernel(heads, k, v, k_out, v_out, wide_rows):
    toks = k.shape[0] // heads
    for number, (source, target) in enumerate(((k, k_out), (v, v_out))):
        wide_rows[number] = source[...].astype(F32)
        for head in range(heads):
            target[0, head] = wide_rows[number, pl.ds(head, toks, stride=heads), :].astype(BF)


def pack_queries_kernel(heads, slots, q, g, k, v, pos_row, qd, slot_rows, wide_rows, acc):
    step = pl.program_id(0)
    toks = q.shape[0] // heads
    row = pos_row[...]
    count = row.shape[1]
    base = lax.axis_index("ctx") * (toks * pl.num_programs(0))
    column = as_column(row)
    tok = iota((count, toks), 1) + (base + step * toks)
    hit = jnp.sum((column == tok).astype(F32), axis=0, keepdims=True)
    rank = jnp.sum(((column >= base) & (column < tok)).astype(F32), axis=0, keepdims=True)
    slot = iota((slots, toks), 0).astype(F32)
    pick = jnp.where((hit > 0) & (rank == slot), 1.0, 0.0).astype(BF)
    tok = iota((toks, count), 0) + (base + step * toks)
    hit_column = jnp.sum((row == tok).astype(F32), axis=1, keepdims=True)
    tables = [[], [k[0, h] for h in range(heads)], [v[0, h] for h in range(heads)], []]
    for number, source in ((0, q), (3, g)):
        wide_rows[number // 3] = source[...].astype(F32)
        for head in range(heads):
            rows = wide_rows[number // 3, pl.ds(head, toks, stride=heads), :]
            tables[number].append(rows.astype(BF))
            if number == 0:
                qd[0, head] = rows.astype(BF)
            else:
                qd[1, head] = jnp.where(hit_column > 0, 0.0, rows).astype(BF)
    for number in range(4):
        found = nn(pick, jnp.concatenate(tables[number], axis=1))
        for head in range(heads):
            part = found[:, head * 128 : (head + 1) * 128]
            acc[number, head] = jnp.where(step == 0, part, acc[number, head] + part)

    @pl.when(step == pl.num_programs(0) - 1)
    def _():
        slot_rows[...] = acc[...].astype(BF)


def owner_map(column, owner, toks, slots, shape):
    inside = jnp.sum((column < owner * toks).astype(jnp.int32), axis=0, keepdims=True)
    held = jnp.sum((column < (owner + 1) * toks).astype(jnp.int32), axis=0, keepdims=True) - inside
    slot = iota(shape, 1) % slots
    hot = (iota(shape, 0) == inside + slot) & (slot < held)
    return jnp.where(hot, 1.0, 0.0).astype(BF)


def mask_kernel(orders, slots, seq_rows, pos_row, bias, compact, expand, place):
    toks = place.shape[0]
    me = lax.axis_index("ctx")
    base = me * toks
    row = pos_row[...]
    count = row.shape[1]
    column = as_column(row)
    for start in range(0, bias.shape[0], TILE):
        key = iota((TILE, count), 0) + (base - HALF + start)
        hits = jnp.sum((row == key).astype(F32), axis=1, keepdims=True)
        key = key[:, :1]
        out = (hits > 0) | (key < 0) | (key >= seq_rows)
        bias[start : start + TILE, :] = jnp.broadcast_to(jnp.where(out, NEG, 0.0), (TILE, 128))
    tok = iota((toks, count), 0) + base
    hit = jnp.sum((row == tok).astype(F32), axis=1, keepdims=True)
    rank = jnp.sum(((row >= base) & (row < tok)).astype(F32), axis=1, keepdims=True)
    slot = iota((toks, slots), 1).astype(F32)
    place[...] = jnp.where((hit > 0) & (rank == slot), 1.0, 0.0).astype(BF)
    part = iota((1, compact.shape[1]), 1) // slots
    owner = jnp.zeros_like(part)
    for number, (first, second) in enumerate(zip(*orders)):
        owner = jnp.where(part == number, me ^ jnp.where(me % 2 == 0, first, second), owner)
    compact[...] = owner_map(column, owner, toks, slots, compact.shape)
    owner = iota((1, compact.shape[1]), 1) // slots
    hot = owner_map(column, owner, toks, slots, compact.shape)
    expand[...] = hot.astype(F32).T.astype(BF)


def stats_kernel(scale2, compact, *refs):
    parts, (k, v, rows, stats) = refs[:-4], refs[-4:]
    pieces = []
    for part in parts:
        for i in range(part.shape[0]):
            pieces.append(jnp.concatenate([part[i, number, 0] for number in range(4)], axis=1))
    packed = nn(compact[...], jnp.concatenate(pieces, axis=0)).astype(BF)
    width = k.shape[3]
    table = [packed[:, number * width : (number + 1) * width] for number in range(4)]
    for number in range(4):
        rows[number, 0] = table[number]
    queries, _, _, grads = table
    scores = nt(k[0, 0], queries) * scale2
    top = jnp.max(scores, axis=0, keepdims=True)
    weights = jnp.exp2(scores - top)
    stats[0, 0, 0:1, :] = top
    stats[0, 0, 1:2, :] = jnp.sum(weights, axis=0, keepdims=True)
    stats[0, 0, 2:3, :] = jnp.sum(weights * nt(v[0, 0], grads), axis=0, keepdims=True)


def band(scores, low):
    rows, columns = iota(scores.shape, 0), iota(scores.shape, 1)
    return jnp.where(rows <= columns if low else rows >= columns, scores, NEG)


def join(blocks, number, buf):
    toks = blocks[0].shape[2]
    for place, block in enumerate(blocks):
        buf[place * toks : (place + 1) * toks, :] = block[number, 0]


def put_in_slots(expand, tables, sums):
    owners, kinds, _, slots, width = sums.shape
    spread = nn(expand, jnp.concatenate(tables, axis=1)).astype(BF)
    for owner in range(owners):
        for kind in range(kinds):
            sums[owner, kind, 0] = spread[
                owner * slots : (owner + 1) * slots, kind * width : (kind + 1) * width
            ]


def global_kernel(scale, scale2, k, v, rows, stats, expand, dkv, ends):
    g_query, g_grad = rows[0, 0], rows[3, 0]
    tops = stats[:, 0, 0:1, :]
    top = jnp.max(tops, axis=0)
    factor = jnp.exp2(tops - top[None])
    total = jnp.sum(stats[:, 0, 1:2, :] * factor, axis=0)
    g_dot = jnp.sum(stats[:, 0, 2:3, :] * factor, axis=0) / total
    g_log = top + jnp.log2(total)
    weights = jnp.exp2(nt(k[0, 0], g_query) * scale2 - g_log)
    narrow = weights.astype(BF)
    slopes = (weights * (nt(v[0, 0], g_grad) - g_dot)).astype(BF)
    dkv[0, 0] = nn(slopes, g_query) * scale
    dkv[1, 0] = nn(narrow, g_grad)
    out = nn(v[0, 0].T, narrow).T.astype(BF)
    dq = (nn(k[0, 0].T, slopes) * scale).T.astype(BF)
    put_in_slots(expand[...], (out, dq), ends)


def local_kernel(
    scale, scale2, qd, k_low, k_own, k_high, v_low, v_own, v_high, rows, bias, expand,
    out, log_dot, dq, dkv, sums, keys, values, score_buf, probs, slopes,
):
    toks = k_own.shape[2]
    reach = 2 * HALF + TILE
    span = keys.shape[0] - rows.shape[2]
    width = keys.shape[1]
    join((k_low, k_own, k_high), 0, keys)
    join((v_low, v_own, v_high), 0, values)
    keys[span:, :] = rows[1, 0]
    values[span:, :] = rows[2, 0]
    key_t = keys[...].T
    value_t = values[...].T
    grad_t = qd[1, 0].T
    for q_tile in range(toks // TILE):
        lanes = slice(q_tile * TILE, (q_tile + 1) * TILE)
        query = qd[0, 0, lanes, :]
        grad = qd[1, 0, lanes, :]
        starts = [q_tile * TILE + piece for piece in range(0, reach, TILE)]
        starts += list(range(span, keys.shape[0], TILE))
        best = None
        for piece, start in enumerate(starts):
            scores = nt(keys[start : start + TILE, :], query) * scale2
            if start < span:
                scores = scores + wide(bias[start : start + TILE, :], TILE)
            if piece == 0:
                scores = band(scores, False)
            elif piece == reach // TILE - 1:
                scores = band(scores, True)
            score_buf[piece * TILE : (piece + 1) * TILE, :] = scores
            part = jnp.max(scores.reshape(TILE // 8, 8, TILE), axis=0)
            best = part if best is None else jnp.maximum(best, part)
        top = jnp.max(best, axis=0, keepdims=True)
        total = None
        for piece, start in enumerate(starts):
            rows_ = slice(piece * TILE, (piece + 1) * TILE)
            weights = jnp.exp2(score_buf[rows_, :] - top)
            score_buf[rows_, :] = weights
            probs[start : start + TILE, lanes] = weights.astype(BF)
            part = jnp.sum(weights.reshape(TILE // 8, 8, TILE), axis=0)
            total = part if total is None else total + part
        total = jnp.sum(total, axis=0, keepdims=True)
        window = slice(q_tile * TILE, q_tile * TILE + reach)
        acc = nn(value_t[:, window], probs[window, lanes]) + nn(value_t[:, span:], probs[span:, lanes])
        inverse = 1.0 / total
        acc = acc * inverse
        dot = jnp.sum(grad_t[:, lanes].astype(F32) * acc, axis=0, keepdims=True)
        log_dot[0, 0:1, lanes] = top + jnp.log2(total)
        log_dot[0, 1:2, lanes] = dot
        out[0, lanes, :] = acc.T.astype(BF)
        for piece, start in enumerate(starts):
            weights = score_buf[piece * TILE : (piece + 1) * TILE, :] * inverse
            rise = nt(values[start : start + TILE, :], grad) - dot
            slopes[start : start + TILE, lanes] = (weights * rise).astype(BF)
            if HALF <= start < HALF + toks or start >= span:
                probs[start : start + TILE, lanes] = weights.astype(BF)
        acc = nn(key_t[:, window], slopes[window, lanes]) + nn(key_t[:, span:], slopes[span:, lanes])
        dq[0, lanes, :] = (acc * scale).T
    own = slice(HALF, HALF + toks)
    dkv[0, 0] = nn(slopes[own, :], qd[0, 0]) * scale
    dkv[1, 0] = nn(probs[own, :], qd[1, 0])
    g_dk = (nn(slopes[span:, :], qd[0, 0]) * scale).astype(BF)
    g_dv = nn(probs[span:, :], qd[1, 0]).astype(BF)
    put_in_slots(expand[...], (g_dk, g_dv), sums)


def rim_kernel(
    scale, scale2, k_own, v_own, bias, qd_low, qd_high, log_low, log_high, partial, dkv, queries, grads, probs, slopes
):
    toks = k_own.shape[2]
    reach = toks + TILE
    join((qd_low, qd_high), 0, queries)
    join((qd_low, qd_high), 1, grads)
    for k_tile in range(toks // TILE):
        span = slice(k_tile * TILE, (k_tile + 1) * TILE)
        key = k_own[0, 0, span, :]
        value = v_own[0, 0, span, :]
        key_bias = wide(bias[HALF + k_tile * TILE : HALF + (k_tile + 1) * TILE, :], TILE)
        for piece in range(reach // TILE):
            start = (k_tile + piece) * TILE
            log_dot, offset = (log_low, start) if start < toks else (log_high, start - toks)
            lanes = slice(offset, offset + TILE)
            scores = nt(key, queries[start : start + TILE, :]) * scale2 + key_bias
            if piece == 0:
                scores = band(scores, True)
            elif piece == reach // TILE - 1:
                scores = band(scores, False)
            weights = jnp.exp2(scores - log_dot[0, 0:1, lanes])
            slope = weights * (nt(value, grads[start : start + TILE, :]) - log_dot[0, 1:2, lanes])
            spot = slice(piece * TILE, (piece + 1) * TILE)
            probs[span, spot] = weights.astype(BF)
            slopes[span, spot] = slope.astype(BF)
        window = slice(k_tile * TILE, k_tile * TILE + reach)
        dkv[0, 0, span, :] = partial[0, 0, span, :] + nn(slopes[span, :], queries[window, :]) * scale
        dkv[1, 0, span, :] = partial[1, 0, span, :] + nn(probs[span, :], grads[window, :])


def final_kernel(
    place, out, ends, sums, dq, dkv, extra, attn, query_grad, key_grad, value_grad, wide_rows
):
    heads, toks = out.shape[0], out.shape[1]
    hot = place[...]
    is_global = jnp.sum(hot.astype(F32), axis=1, keepdims=True) > 0
    for head in range(heads):
        rows = pl.ds(head, toks, stride=heads)
        tables = []
        for source, kind in ((ends, 0), (ends, 1), (sums, 0), (sums, 1)):
            table = source[0, kind, head].astype(F32)
            for device in range(1, source.shape[0]):
                table = table + source[device, kind, head].astype(F32)
            tables.append(table.astype(BF))
        width = out.shape[2]
        added = nn(hot, jnp.concatenate(tables, axis=1))
        added = [added[:, i * width : (i + 1) * width] for i in range(4)]
        wide_rows[rows, :] = jnp.where(is_global, added[0], out[head].astype(F32))
        query_grad[rows, :] = dq[head] + added[1]
        key_grad[rows, :] = dkv[0, head] + extra[0, head] + added[2]
        value_grad[rows, :] = dkv[1, head] + extra[1, head] + added[3]
    attn[...] = wide_rows[...].astype(BF)


def cost(flops, moved, exps=0):
    return pl.CostEstimate(flops=int(flops), bytes_accessed=int(moved), transcendentals=int(exps))


def struct(shape, dtype):
    return jax.ShapeDtypeStruct(shape, dtype)


def whole(shape):
    return pl.BlockSpec(shape, lambda head: (0,) * len(shape))


def per_head(shape, dim, first=0):
    block = tuple(1 if i == dim else size for i, size in enumerate(shape))
    return pl.BlockSpec(
        block, lambda head: tuple(head + first if i == dim else 0 for i in range(len(shape)))
    )


def shards(query_rows, key_rows, value_rows, out_grad, global_pos):
    toks, heads, width = query_rows.shape
    count = global_pos.shape[0]
    devices = lax.axis_size("ctx")
    slots = max(16, 2 * count // devices)
    scale = width ** (-0.5)
    scale2 = scale * LOG2E
    bits = devices.bit_length() - 1
    ways = [list(range(1, bits)) + [0], list(range(bits - 1, 0, -1)) + [0]]
    orders = []
    for way in ways:
        order = [0]
        for bit in way[:-1]:
            order = order + [one | (1 << bit) for one in order]
        orders.append(order)
    orders = [mine + [one | 1 for one in other] for mine, other in (orders, orders[::-1])]
    pos_row = global_pos.reshape(1, count)
    q_flat, k_flat, v_flat, g_flat = (
        x.reshape(toks * heads, width) for x in (query_rows, key_rows, value_rows, out_grad)
    )

    def swap(value, stage):
        pairs = [(i, i ^ (1 << ways[i % 2][stage])) for i in range(devices)]
        return lax.ppermute(value, "ctx", pairs)

    def from_low(value):
        return lax.ppermute(value, "ctx", [(i, i + 1) for i in range(devices - 1)])

    def from_high(value):
        return lax.ppermute(value, "ctx", [(i + 1, i) for i in range(devices - 1)])

    def after(value, earlier):
        return lax.optimization_barrier((value, earlier))[0]

    pair_shape = (2, heads, toks, width)
    slot_shape = (4, heads, slots, width)
    steps = 1
    flat_spec = pl.BlockSpec((toks * heads // steps, width), lambda i: (i, 0))
    pair_spec = pl.BlockSpec((2, heads, toks // steps, width), lambda i: (0, 0, i, 0))
    wide_pair = pltpu.VMEM((2, toks * heads // steps, width), F32)
    lone_shape = (1, heads, toks, width)
    lone_spec = pl.BlockSpec((1, heads, toks // steps, width), lambda i: (0, 0, i, 0))
    k, v = pl.pallas_call(
        functools.partial(pack_keys_kernel, heads),
        grid=(steps,),
        in_specs=[flat_spec, flat_spec],
        out_specs=(lone_spec, lone_spec),
        out_shape=(struct(lone_shape, BF), struct(lone_shape, BF)),
        scratch_shapes=[wide_pair],
        compiler_params=params(),
        name="pack_keys",
    )(k_flat, v_flat)

    qd, slot_rows = pl.pallas_call(
        functools.partial(pack_queries_kernel, heads, slots),
        grid=(steps,),
        in_specs=[flat_spec, flat_spec, lone_spec, lone_spec, whole((1, count))],
        out_specs=(pair_spec, whole(slot_shape)),
        out_shape=(struct(pair_shape, BF), struct(slot_shape, BF)),
        scratch_shapes=[wide_pair, pltpu.VMEM(slot_shape, F32)],
        compiler_params=params(),
        name="pack_queries",
    )(q_flat, g_flat, k, v, pos_row)

    held = [slot_rows[None]]
    for stage in range(bits):
        held.append(swap(jnp.concatenate(held, axis=0) if stage else held[0], stage))
    k_late = after(k, held[1])
    k_low, k_high = from_low(k_late), from_high(k_late)
    v_late = after(v, (k_low, k_high))
    v_low, v_high = from_low(v_late), from_high(v_late)

    span = toks + 2 * HALF
    bias, compact, expand, place = pl.pallas_call(
        functools.partial(mask_kernel, orders, slots, toks * devices),
        out_shape=(
            struct((span, 128), F32),
            struct((count, devices * slots), BF),
            struct((devices * slots, count), BF),
            struct((toks, slots), BF),
        ),
        compiler_params=params(),
        name="masks",
    )(pos_row)

    row_shape = (4, heads, count, width)
    rows, stats = pl.pallas_call(
        functools.partial(stats_kernel, scale2),
        grid=(heads,),
        in_specs=[whole(compact.shape)]
        + [per_head(part.shape, 2) for part in held]
        + [per_head(lone_shape, 1)] * 2,
        out_specs=(per_head(row_shape, 1), per_head((1, heads, 3, count), 1)),
        out_shape=(struct(row_shape, BF), struct((1, heads, 3, count), F32)),
        compiler_params=params(),
        cost_estimate=cost(2.7e9, 4e6),
        name="global_stats",
    )(compact, *held, k, v)

    stats = jnp.broadcast_to(stats, (devices,) + stats.shape[1:])
    stats = lax.all_to_all(stats, "ctx", 0, 0, tiled=True)
    qd_late = after(qd, (v_low, v_high))
    qd_low, qd_high = from_low(qd_late), from_high(qd_late)

    ends_shape = (devices, 2, heads, slots, width)
    extra, ends = pl.pallas_call(
        functools.partial(global_kernel, scale, scale2),
        grid=(heads,),
        in_specs=[per_head(lone_shape, 1)] * 2
        + [per_head(row_shape, 1), per_head(stats.shape, 1), whole(expand.shape)],
        out_specs=(per_head(pair_shape, 1), per_head(ends_shape, 2)),
        out_shape=(struct(pair_shape, F32), struct(ends_shape, BF)),
        compiler_params=params(),
        cost_estimate=cost(2e9, 5e6, 1e6),
        name="global_queries",
    )(k, v, rows, stats, expand)

    ends = lax.all_to_all(ends, "ctx", 0, 0, tiled=True)

    out, log_dot, dq, dkv, sums = pl.pallas_call(
        functools.partial(local_kernel, scale, scale2),
        grid=(heads,),
        in_specs=[per_head(pair_shape, 1)]
        + [per_head(lone_shape, 1)] * 6
        + [per_head(row_shape, 1), whole(bias.shape), whole(expand.shape)],
        out_specs=(
            per_head((heads, toks, width), 0),
            per_head((heads, 2, toks), 0),
            per_head((heads, toks, width), 0),
            per_head(pair_shape, 1),
            per_head(ends_shape, 2),
        ),
        out_shape=(
            struct((heads, toks, width), BF),
            struct((heads, 2, toks), F32),
            struct((heads, toks, width), F32),
            struct(pair_shape, F32),
            struct(ends_shape, BF),
        ),
        scratch_shapes=[
            pltpu.VMEM((span + count, width), BF),
            pltpu.VMEM((span + count, width), BF),
            pltpu.VMEM((2 * HALF + TILE + count, TILE), F32),
            pltpu.VMEM((span + count, toks), BF),
            pltpu.VMEM((span + count, toks), BF),
        ],
        compiler_params=params(),
        cost_estimate=cost(2e9, 5e6, 3e6),
        name="local",
    )(qd, k_low, k, k_high, v_low, v, v_high, rows, bias, expand)
    log_low, log_high = from_low(log_dot), from_high(log_dot)

    sums = lax.all_to_all(sums, "ctx", 0, 0, tiled=True)

    dkv = pl.pallas_call(
        functools.partial(rim_kernel, scale, scale2),
        grid=(heads,),
        in_specs=[per_head(lone_shape, 1)] * 2
        + [whole(bias.shape)]
        + [per_head(pair_shape, 1)] * 2
        + [per_head(log_dot.shape, 0)] * 2
        + [per_head(pair_shape, 1)],
        out_specs=per_head(pair_shape, 1),
        out_shape=struct(pair_shape, F32),
        scratch_shapes=[
            pltpu.VMEM((2 * toks, width), BF),
            pltpu.VMEM((2 * toks, width), BF),
            pltpu.VMEM((toks, toks + TILE), BF),
            pltpu.VMEM((toks, toks + TILE), BF),
        ],
        compiler_params=params(),
        cost_estimate=cost(4e9, 8e6, 2e6),
        name="rim",
    )(k, v, bias, qd_low, qd_high, log_low, log_high, dkv)

    flat_shape = (toks * heads, width)
    steps = 2
    outs = pl.pallas_call(
        final_kernel,
        grid=(steps,),
        in_specs=[
            pl.BlockSpec((toks // steps, slots), lambda i: (i, 0)),
            pl.BlockSpec((heads, toks // steps, width), lambda i: (0, i, 0)),
            whole(ends_shape),
            whole(ends_shape),
            pl.BlockSpec((heads, toks // steps, width), lambda i: (0, i, 0)),
            pl.BlockSpec((2, heads, toks // steps, width), lambda i: (0, 0, i, 0)),
            pl.BlockSpec((2, heads, toks // steps, width), lambda i: (0, 0, i, 0)),
        ],
        out_specs=[pl.BlockSpec((toks * heads // steps, width), lambda i: (i, 0))] * 4,
        out_shape=[struct(flat_shape, kind) for kind in (BF, F32, F32, F32)],
        scratch_shapes=[pltpu.VMEM((toks * heads // steps, width), F32)],
        compiler_params=params(),
        name="final",
    )(place, out, ends, sums, dq, dkv, extra)
    return tuple(x.reshape(toks, heads, width) for x in outs)


def solution(mesh):
    spec = P("ctx", "head", None)
    return jax.shard_map(
        shards,
        mesh=mesh,
        in_specs=(spec, spec, spec, spec, P()),
        out_specs=(spec, spec, spec, spec),
        check_vma=False,
    )
```

```python
import functools
import math

import jax
import jax.numpy as jnp
from jax import lax
from jax.experimental import pallas as pl
from jax.experimental.pallas import tpu as pltpu
from jax.sharding import PartitionSpec as P

HALF = 512
TILE = 256
NEG = -1e30
LOG2E = 1.0 / math.log(2.0)
VMEM_BYTES = 63 * 1024 * 1024
BF = jnp.bfloat16
F32 = jnp.float32


def nt(a, b):
    return lax.dot_general(a, b, (((1,), (1,)), ((), ())), preferred_element_type=F32)


def nn(a, b):
    return lax.dot_general(a, b, (((1,), (0,)), ((), ())), preferred_element_type=F32)


def wide(column, width):
    return jnp.concatenate([column] * (width // column.shape[1]), axis=1)


def iota(shape, dim):
    return lax.broadcasted_iota(jnp.int32, shape, dim)


def params():
    return pltpu.CompilerParams(vmem_limit_bytes=VMEM_BYTES)


def as_column(row):
    return jnp.broadcast_to(row, (128, row.shape[1])).T[:, :1]


def pack_keys_kernel(heads, k, v, kv, wide_rows):
    toks = k.shape[0] // heads
    for number, source in enumerate((k, v)):
        wide_rows[number] = source[...].astype(F32)
        for head in range(heads):
            kv[number, head] = wide_rows[number, pl.ds(head, toks, stride=heads), :].astype(BF)


def pack_queries_kernel(heads, slots, q, g, kv, pos_row, qd, slot_rows, wide_rows, acc):
    step = pl.program_id(0)
    toks = q.shape[0] // heads
    row = pos_row[...]
    count = row.shape[1]
    base = lax.axis_index("ctx") * (toks * pl.num_programs(0))
    column = as_column(row)
    tok = iota((count, toks), 1) + (base + step * toks)
    hit = jnp.sum((column == tok).astype(F32), axis=0, keepdims=True)
    rank = jnp.sum(((column >= base) & (column < tok)).astype(F32), axis=0, keepdims=True)
    slot = iota((slots, toks), 0).astype(F32)
    pick = jnp.where((hit > 0) & (rank == slot), 1.0, 0.0).astype(BF)
    tok = iota((toks, count), 0) + (base + step * toks)
    hit_column = jnp.sum((row == tok).astype(F32), axis=1, keepdims=True)
    tables = [[], [kv[0, h] for h in range(heads)], [kv[1, h] for h in range(heads)], []]
    for number, source in ((0, q), (3, g)):
        wide_rows[number // 3] = source[...].astype(F32)
        for head in range(heads):
            rows = wide_rows[number // 3, pl.ds(head, toks, stride=heads), :]
            tables[number].append(rows.astype(BF))
            if number == 0:
                qd[0, head] = rows.astype(BF)
            else:
                qd[1, head] = jnp.where(hit_column > 0, 0.0, rows).astype(BF)
    for number in range(4):
        found = nn(pick, jnp.concatenate(tables[number], axis=1))
        for head in range(heads):
            part = found[:, head * 128 : (head + 1) * 128]
            acc[number, head] = jnp.where(step == 0, part, acc[number, head] + part)

    @pl.when(step == pl.num_programs(0) - 1)
    def _():
        slot_rows[...] = acc[...].astype(BF)


def owner_map(column, owner, toks, slots, shape):
    inside = jnp.sum((column < owner * toks).astype(jnp.int32), axis=0, keepdims=True)
    held = jnp.sum((column < (owner + 1) * toks).astype(jnp.int32), axis=0, keepdims=True) - inside
    slot = iota(shape, 1) % slots
    hot = (iota(shape, 0) == inside + slot) & (slot < held)
    return jnp.where(hot, 1.0, 0.0).astype(BF)


def mask_kernel(orders, slots, seq_rows, pos_row, bias, compact, expand, place):
    toks = place.shape[0]
    me = lax.axis_index("ctx")
    base = me * toks
    row = pos_row[...]
    count = row.shape[1]
    column = as_column(row)
    for start in range(0, bias.shape[0], TILE):
        key = iota((TILE, count), 0) + (base - HALF + start)
        hits = jnp.sum((row == key).astype(F32), axis=1, keepdims=True)
        key = key[:, :1]
        out = (hits > 0) | (key < 0) | (key >= seq_rows)
        bias[start : start + TILE, :] = jnp.broadcast_to(jnp.where(out, NEG, 0.0), (TILE, 128))
    tok = iota((toks, count), 0) + base
    hit = jnp.sum((row == tok).astype(F32), axis=1, keepdims=True)
    rank = jnp.sum(((row >= base) & (row < tok)).astype(F32), axis=1, keepdims=True)
    slot = iota((toks, slots), 1).astype(F32)
    place[...] = jnp.where((hit > 0) & (rank == slot), 1.0, 0.0).astype(BF)
    part = iota((1, compact.shape[1]), 1) // slots
    owner = jnp.zeros_like(part)
    for number, (first, second) in enumerate(zip(*orders)):
        owner = jnp.where(part == number, me ^ jnp.where(me % 2 == 0, first, second), owner)
    compact[...] = owner_map(column, owner, toks, slots, compact.shape)
    owner = iota((1, compact.shape[1]), 1) // slots
    hot = owner_map(column, owner, toks, slots, compact.shape)
    expand[...] = hot.astype(F32).T.astype(BF)


def stats_kernel(scale2, compact, *refs):
    parts, (kv, rows, stats) = refs[:-3], refs[-3:]
    pieces = []
    for part in parts:
        for i in range(part.shape[0]):
            pieces.append(jnp.concatenate([part[i, number, 0] for number in range(4)], axis=1))
    packed = nn(compact[...], jnp.concatenate(pieces, axis=0)).astype(BF)
    width = kv.shape[3]
    table = [packed[:, number * width : (number + 1) * width] for number in range(4)]
    for number in range(4):
        rows[number, 0] = table[number]
    queries, _, _, grads = table
    scores = nt(kv[0, 0], queries) * scale2
    top = jnp.max(scores, axis=0, keepdims=True)
    weights = jnp.exp2(scores - top)
    stats[0, 0, 0:1, :] = top
    stats[0, 0, 1:2, :] = jnp.sum(weights, axis=0, keepdims=True)
    stats[0, 0, 2:3, :] = jnp.sum(weights * nt(kv[1, 0], grads), axis=0, keepdims=True)


def band(scores, low):
    rows, columns = iota(scores.shape, 0), iota(scores.shape, 1)
    return jnp.where(rows <= columns if low else rows >= columns, scores, NEG)


def join(blocks, number, buf):
    toks = blocks[0].shape[2]
    for place, block in enumerate(blocks):
        buf[place * toks : (place + 1) * toks, :] = block[number, 0]


def put_in_slots(expand, tables, sums):
    owners, kinds, _, slots, width = sums.shape
    spread = nn(expand, jnp.concatenate(tables, axis=1)).astype(BF)
    for owner in range(owners):
        for kind in range(kinds):
            sums[owner, kind, 0] = spread[
                owner * slots : (owner + 1) * slots, kind * width : (kind + 1) * width
            ]


def global_kernel(scale, scale2, kv, rows, stats, expand, dkv, ends):
    g_query, g_grad = rows[0, 0], rows[3, 0]
    tops = stats[:, 0, 0:1, :]
    top = jnp.max(tops, axis=0)
    factor = jnp.exp2(tops - top[None])
    total = jnp.sum(stats[:, 0, 1:2, :] * factor, axis=0)
    g_dot = jnp.sum(stats[:, 0, 2:3, :] * factor, axis=0) / total
    g_log = top + jnp.log2(total)
    weights = jnp.exp2(nt(kv[0, 0], g_query) * scale2 - g_log)
    narrow = weights.astype(BF)
    slopes = (weights * (nt(kv[1, 0], g_grad) - g_dot)).astype(BF)
    dkv[0, 0] = nn(slopes, g_query) * scale
    dkv[1, 0] = nn(narrow, g_grad)
    out = nn(kv[1, 0].T, narrow).T.astype(BF)
    dq = (nn(kv[0, 0].T, slopes) * scale).T.astype(BF)
    put_in_slots(expand[...], (out, dq), ends)


def local_kernel(
    scale, scale2, qd, low, kv, high, rows, bias, expand,
    out, log_dot, dq, dkv, sums, keys, values, score_buf, probs, slopes,
):
    toks = kv.shape[2]
    reach = 2 * HALF + TILE
    span = keys.shape[0] - rows.shape[2]
    width = keys.shape[1]
    join((low, kv, high), 0, keys)
    join((low, kv, high), 1, values)
    keys[span:, :] = rows[1, 0]
    values[span:, :] = rows[2, 0]
    key_t = keys[...].T
    value_t = values[...].T
    grad_t = qd[1, 0].T
    for q_tile in range(toks // TILE):
        lanes = slice(q_tile * TILE, (q_tile + 1) * TILE)
        query = qd[0, 0, lanes, :]
        grad = qd[1, 0, lanes, :]
        starts = [q_tile * TILE + piece for piece in range(0, reach, TILE)]
        starts += list(range(span, keys.shape[0], TILE))
        best = None
        for piece, start in enumerate(starts):
            scores = nt(keys[start : start + TILE, :], query) * scale2
            if start < span:
                scores = scores + wide(bias[start : start + TILE, :], TILE)
            if piece == 0:
                scores = band(scores, False)
            elif piece == reach // TILE - 1:
                scores = band(scores, True)
            score_buf[q_tile, piece * TILE : (piece + 1) * TILE, :] = scores
            part = jnp.max(scores.reshape(TILE // 8, 8, TILE), axis=0)
            best = part if best is None else jnp.maximum(best, part)
        top = jnp.max(best, axis=0, keepdims=True)
        total = None
        for piece, start in enumerate(starts):
            rows_ = slice(piece * TILE, (piece + 1) * TILE)
            weights = jnp.exp2(score_buf[q_tile, rows_, :] - top)
            score_buf[q_tile, rows_, :] = weights
            probs[start : start + TILE, lanes] = weights.astype(BF)
            part = jnp.sum(weights.reshape(TILE // 8, 8, TILE), axis=0)
            total = part if total is None else total + part
        total = jnp.sum(total, axis=0, keepdims=True)
        window = slice(q_tile * TILE, q_tile * TILE + reach)
        acc = nn(value_t[:, window], probs[window, lanes]) + nn(value_t[:, span:], probs[span:, lanes])
        inverse = 1.0 / total
        acc = acc * inverse
        dot = jnp.sum(grad_t[:, lanes].astype(F32) * acc, axis=0, keepdims=True)
        log_dot[0, 0:1, lanes] = top + jnp.log2(total)
        log_dot[0, 1:2, lanes] = dot
        out[0, lanes, :] = acc.T.astype(BF)
        for piece, start in enumerate(starts):
            weights = score_buf[q_tile, piece * TILE : (piece + 1) * TILE, :] * inverse
            rise = nt(values[start : start + TILE, :], grad) - dot
            slopes[start : start + TILE, lanes] = (weights * rise).astype(BF)
            if HALF <= start < HALF + toks or start >= span:
                probs[start : start + TILE, lanes] = weights.astype(BF)
        acc = nn(key_t[:, window], slopes[window, lanes]) + nn(key_t[:, span:], slopes[span:, lanes])
        dq[0, lanes, :] = (acc * scale).T
    own = slice(HALF, HALF + toks)
    dkv[0, 0] = nn(slopes[own, :], qd[0, 0]) * scale
    dkv[1, 0] = nn(probs[own, :], qd[1, 0])
    g_dk = (nn(slopes[span:, :], qd[0, 0]) * scale).astype(BF)
    g_dv = nn(probs[span:, :], qd[1, 0]).astype(BF)
    put_in_slots(expand[...], (g_dk, g_dv), sums)


def rim_kernel(
    scale, scale2, kv, bias, qd_low, qd_high, log_low, log_high, partial, dkv, queries, grads, probs, slopes
):
    toks = kv.shape[2]
    reach = toks + TILE
    join((qd_low, qd_high), 0, queries)
    join((qd_low, qd_high), 1, grads)
    for k_tile in range(toks // TILE):
        span = slice(k_tile * TILE, (k_tile + 1) * TILE)
        key = kv[0, 0, span, :]
        value = kv[1, 0, span, :]
        key_bias = wide(bias[HALF + k_tile * TILE : HALF + (k_tile + 1) * TILE, :], TILE)
        for piece in range(reach // TILE):
            start = (k_tile + piece) * TILE
            log_dot, offset = (log_low, start) if start < toks else (log_high, start - toks)
            lanes = slice(offset, offset + TILE)
            scores = nt(key, queries[start : start + TILE, :]) * scale2 + key_bias
            if piece == 0:
                scores = band(scores, True)
            elif piece == reach // TILE - 1:
                scores = band(scores, False)
            weights = jnp.exp2(scores - log_dot[0, 0:1, lanes])
            slope = weights * (nt(value, grads[start : start + TILE, :]) - log_dot[0, 1:2, lanes])
            spot = slice(piece * TILE, (piece + 1) * TILE)
            probs[span, spot] = weights.astype(BF)
            slopes[span, spot] = slope.astype(BF)
        window = slice(k_tile * TILE, k_tile * TILE + reach)
        dkv[0, 0, span, :] = partial[0, 0, span, :] + nn(slopes[span, :], queries[window, :]) * scale
        dkv[1, 0, span, :] = partial[1, 0, span, :] + nn(probs[span, :], grads[window, :])


def final_kernel(
    place, out, ends, sums, dq, dkv, extra, attn, query_grad, key_grad, value_grad, wide_rows
):
    heads, toks = out.shape[0], out.shape[1]
    hot = place[...]
    is_global = jnp.sum(hot.astype(F32), axis=1, keepdims=True) > 0
    for head in range(heads):
        rows = pl.ds(head, toks, stride=heads)
        tables = []
        for source, kind in ((ends, 0), (ends, 1), (sums, 0), (sums, 1)):
            table = source[0, kind, head].astype(F32)
            for device in range(1, source.shape[0]):
                table = table + source[device, kind, head].astype(F32)
            tables.append(table.astype(BF))
        width = out.shape[2]
        added = nn(hot, jnp.concatenate(tables, axis=1))
        added = [added[:, i * width : (i + 1) * width] for i in range(4)]
        wide_rows[rows, :] = jnp.where(is_global, added[0], out[head].astype(F32))
        query_grad[rows, :] = dq[head] + added[1]
        key_grad[rows, :] = dkv[0, head] + extra[0, head] + added[2]
        value_grad[rows, :] = dkv[1, head] + extra[1, head] + added[3]
    attn[...] = wide_rows[...].astype(BF)


def cost(flops, moved, exps=0):
    return pl.CostEstimate(flops=int(flops), bytes_accessed=int(moved), transcendentals=int(exps))


def struct(shape, dtype):
    return jax.ShapeDtypeStruct(shape, dtype)


def whole(shape):
    return pl.BlockSpec(shape, lambda head: (0,) * len(shape))


def per_head(shape, dim, first=0):
    block = tuple(1 if i == dim else size for i, size in enumerate(shape))
    return pl.BlockSpec(
        block, lambda head: tuple(head + first if i == dim else 0 for i in range(len(shape)))
    )


def shards(query_rows, key_rows, value_rows, out_grad, global_pos):
    toks, heads, width = query_rows.shape
    count = global_pos.shape[0]
    devices = lax.axis_size("ctx")
    slots = max(16, 2 * count // devices)
    scale = width ** (-0.5)
    scale2 = scale * LOG2E
    bits = devices.bit_length() - 1
    ways = [list(range(1, bits)) + [0], list(range(bits - 1, 0, -1)) + [0]]
    orders = []
    for way in ways:
        order = [0]
        for bit in way[:-1]:
            order = order + [one | (1 << bit) for one in order]
        orders.append(order)
    orders = [mine + [one | 1 for one in other] for mine, other in (orders, orders[::-1])]
    pos_row = global_pos.reshape(1, count)
    q_flat, k_flat, v_flat, g_flat = (
        x.reshape(toks * heads, width) for x in (query_rows, key_rows, value_rows, out_grad)
    )

    def swap(value, stage):
        pairs = [(i, i ^ (1 << ways[i % 2][stage])) for i in range(devices)]
        return lax.ppermute(value, "ctx", pairs)

    def from_low(value):
        return lax.ppermute(value, "ctx", [(i, i + 1) for i in range(devices - 1)])

    def from_high(value):
        return lax.ppermute(value, "ctx", [(i + 1, i) for i in range(devices - 1)])

    def after(value, earlier):
        return lax.optimization_barrier((value, earlier))[0]

    pair_shape = (2, heads, toks, width)
    slot_shape = (4, heads, slots, width)
    steps = 1
    flat_spec = pl.BlockSpec((toks * heads // steps, width), lambda i: (i, 0))
    pair_spec = pl.BlockSpec((2, heads, toks // steps, width), lambda i: (0, 0, i, 0))
    wide_pair = pltpu.VMEM((2, toks * heads // steps, width), F32)
    kv = pl.pallas_call(
        functools.partial(pack_keys_kernel, heads),
        grid=(steps,),
        in_specs=[flat_spec, flat_spec],
        out_specs=pair_spec,
        out_shape=struct(pair_shape, BF),
        scratch_shapes=[wide_pair],
        compiler_params=params(),
        name="pack_keys",
    )(k_flat, v_flat)

    qd, slot_rows = pl.pallas_call(
        functools.partial(pack_queries_kernel, heads, slots),
        grid=(steps,),
        in_specs=[flat_spec, flat_spec, pair_spec, whole((1, count))],
        out_specs=(pair_spec, whole(slot_shape)),
        out_shape=(struct(pair_shape, BF), struct(slot_shape, BF)),
        scratch_shapes=[wide_pair, pltpu.VMEM(slot_shape, F32)],
        compiler_params=params(),
        name="pack_queries",
    )(q_flat, g_flat, kv, pos_row)

    span = toks + 2 * HALF
    bias, compact, expand, place = pl.pallas_call(
        functools.partial(mask_kernel, orders, slots, toks * devices),
        out_shape=(
            struct((span, 128), F32),
            struct((count, devices * slots), BF),
            struct((devices * slots, count), BF),
            struct((toks, slots), BF),
        ),
        compiler_params=params(),
        name="masks",
    )(pos_row)

    held = [slot_rows[None]]
    for stage in range(bits):
        send = jnp.concatenate(held, axis=0) if stage else held[0]
        held.append(swap(after(send, place) if stage == 1 else send, stage))
    kv_late = after(kv, held[1])
    kv_low, kv_high = from_low(kv_late), from_high(kv_late)

    row_shape = (4, heads, count, width)
    rows, stats = pl.pallas_call(
        functools.partial(stats_kernel, scale2),
        grid=(heads,),
        in_specs=[whole(compact.shape)]
        + [per_head(part.shape, 2) for part in held]
        + [per_head(pair_shape, 1)],
        out_specs=(per_head(row_shape, 1), per_head((1, heads, 3, count), 1)),
        out_shape=(struct(row_shape, BF), struct((1, heads, 3, count), F32)),
        compiler_params=params(),
        cost_estimate=cost(1e6, 1e6),
        name="global_stats",
    )(compact, *held, kv)

    stats = after(stats, (kv_low, kv_high))
    stats = jnp.broadcast_to(stats, (devices,) + stats.shape[1:])
    stats = lax.all_to_all(stats, "ctx", 0, 0, tiled=True)
    qd_late = after(qd, (kv_low, kv_high, rows))
    qd_low, qd_high = from_low(qd_late), from_high(qd_late)

    ends_shape = (devices, 2, heads, slots, width)
    extra, ends = pl.pallas_call(
        functools.partial(global_kernel, scale, scale2),
        grid=(heads,),
        in_specs=[per_head(pair_shape, 1), per_head(row_shape, 1)]
        + [per_head(stats.shape, 1), whole(expand.shape)],
        out_specs=(per_head(pair_shape, 1), per_head(ends_shape, 2)),
        out_shape=(struct(pair_shape, F32), struct(ends_shape, BF)),
        compiler_params=params(),
        cost_estimate=cost(2e9, 5e6, 1e6),
        name="global_queries",
    )(kv, rows, stats, expand)

    ends = lax.all_to_all(ends, "ctx", 0, 0, tiled=True)

    out, log_dot, dq, dkv, sums = pl.pallas_call(
        functools.partial(local_kernel, scale, scale2),
        grid=(heads,),
        in_specs=[per_head(pair_shape, 1)]
        + [per_head(pair_shape, 1)] * 3
        + [per_head(row_shape, 1), whole(bias.shape), whole(expand.shape)],
        out_specs=(
            per_head((heads, toks, width), 0),
            per_head((heads, 2, toks), 0),
            per_head((heads, toks, width), 0),
            per_head(pair_shape, 1),
            per_head(ends_shape, 2),
        ),
        out_shape=(
            struct((heads, toks, width), BF),
            struct((heads, 2, toks), F32),
            struct((heads, toks, width), F32),
            struct(pair_shape, F32),
            struct(ends_shape, BF),
        ),
        scratch_shapes=[
            pltpu.VMEM((span + count, width), BF),
            pltpu.VMEM((span + count, width), BF),
            pltpu.VMEM((toks // TILE, 2 * HALF + TILE + count, TILE), F32),
            pltpu.VMEM((span + count, toks), BF),
            pltpu.VMEM((span + count, toks), BF),
        ],
        compiler_params=params(),
        cost_estimate=cost(2e9, 5e6, 3e6),
        name="local",
    )(qd, kv_low, kv, kv_high, rows, bias, after(expand, extra))
    log_late = after(log_dot, (qd_low, qd_high))
    log_low, log_high = from_low(log_late), from_high(log_late)

    sums = lax.all_to_all(sums, "ctx", 0, 0, tiled=True)

    dkv = pl.pallas_call(
        functools.partial(rim_kernel, scale, scale2),
        grid=(heads,),
        in_specs=[per_head(pair_shape, 1), whole(bias.shape)]
        + [per_head(pair_shape, 1)] * 2
        + [per_head(log_dot.shape, 0)] * 2
        + [per_head(pair_shape, 1)],
        out_specs=per_head(pair_shape, 1),
        out_shape=struct(pair_shape, F32),
        scratch_shapes=[
            pltpu.VMEM((2 * toks, width), BF),
            pltpu.VMEM((2 * toks, width), BF),
            pltpu.VMEM((toks, toks + TILE), BF),
            pltpu.VMEM((toks, toks + TILE), BF),
        ],
        compiler_params=params(),
        cost_estimate=cost(4e9, 8e6, 2e6),
        name="rim",
    )(kv, after(bias, ends), qd_low, qd_high, log_low, log_high, dkv)

    flat_shape = (toks * heads, width)
    steps = 2
    outs = pl.pallas_call(
        final_kernel,
        grid=(steps,),
        in_specs=[
            pl.BlockSpec((toks // steps, slots), lambda i: (i, 0)),
            pl.BlockSpec((heads, toks // steps, width), lambda i: (0, i, 0)),
            whole(ends_shape),
            whole(ends_shape),
            pl.BlockSpec((heads, toks // steps, width), lambda i: (0, i, 0)),
            pl.BlockSpec((2, heads, toks // steps, width), lambda i: (0, 0, i, 0)),
            pl.BlockSpec((2, heads, toks // steps, width), lambda i: (0, 0, i, 0)),
        ],
        out_specs=[pl.BlockSpec((toks * heads // steps, width), lambda i: (i, 0))] * 4,
        out_shape=[struct(flat_shape, kind) for kind in (BF, F32, F32, F32)],
        scratch_shapes=[pltpu.VMEM((toks * heads // steps, width), F32)],
        compiler_params=params(),
        name="final",
    )(place, out, ends, sums, dq, dkv, extra)
    return tuple(x.reshape(toks, heads, width) for x in outs)


def solution(mesh):
    spec = P("ctx", "head", None)
    return jax.shard_map(
        shards,
        mesh=mesh,
        in_specs=(spec, spec, spec, spec, P()),
        out_specs=(spec, spec, spec, spec),
        check_vma=False,
    )
```

```python
import functools
import math

import jax
import jax.numpy as jnp
from jax import lax
from jax.experimental import pallas as pl
from jax.experimental.pallas import tpu as pltpu
from jax.sharding import PartitionSpec as P

HALF = 512
TILE = 256
NEG = -1e30
LOG2E = 1.0 / math.log(2.0)
VMEM_BYTES = 63 * 1024 * 1024
BF = jnp.bfloat16
F32 = jnp.float32


def nt(a, b):
    return lax.dot_general(a, b, (((1,), (1,)), ((), ())), preferred_element_type=F32)


def nn(a, b):
    return lax.dot_general(a, b, (((1,), (0,)), ((), ())), preferred_element_type=F32)


def wide(column, width):
    return jnp.concatenate([column] * (width // column.shape[1]), axis=1)


def iota(shape, dim):
    return lax.broadcasted_iota(jnp.int32, shape, dim)


def params():
    return pltpu.CompilerParams(vmem_limit_bytes=VMEM_BYTES)


def as_column(row):
    return jnp.broadcast_to(row, (128, row.shape[1])).T[:, :1]


def pack_keys_kernel(heads, k, v, kv, *refs):
    parts, wide_rows = refs[:-1], refs[-1]
    group = heads // len(parts)
    toks = k.shape[0] // heads
    for number, source in enumerate((k, v)):
        wide_rows[number] = source[...].astype(F32)
        for head in range(heads):
            rows = wide_rows[number, pl.ds(head, toks, stride=heads), :].astype(BF)
            kv[number, head] = rows
            parts[head // group][number, head % group] = rows


def pack_queries_kernel(heads, slots, q, g, kv, pos_row, qd, slot_rows, wide_rows, acc):
    step = pl.program_id(0)
    toks = q.shape[0] // heads
    row = pos_row[...]
    count = row.shape[1]
    base = lax.axis_index("ctx") * (toks * pl.num_programs(0))
    column = as_column(row)
    tok = iota((count, toks), 1) + (base + step * toks)
    hit = jnp.sum((column == tok).astype(F32), axis=0, keepdims=True)
    rank = jnp.sum(((column >= base) & (column < tok)).astype(F32), axis=0, keepdims=True)
    slot = iota((slots, toks), 0).astype(F32)
    pick = jnp.where((hit > 0) & (rank == slot), 1.0, 0.0).astype(BF)
    tok = iota((toks, count), 0) + (base + step * toks)
    hit_column = jnp.sum((row == tok).astype(F32), axis=1, keepdims=True)
    tables = [[], [kv[0, h] for h in range(heads)], [kv[1, h] for h in range(heads)], []]
    for number, source in ((0, q), (3, g)):
        wide_rows[number // 3] = source[...].astype(F32)
        for head in range(heads):
            rows = wide_rows[number // 3, pl.ds(head, toks, stride=heads), :]
            tables[number].append(rows.astype(BF))
            if number == 0:
                qd[0, head] = rows.astype(BF)
            else:
                qd[1, head] = jnp.where(hit_column > 0, 0.0, rows).astype(BF)
    for number in range(4):
        found = nn(pick, jnp.concatenate(tables[number], axis=1))
        for head in range(heads):
            part = found[:, head * 128 : (head + 1) * 128]
            acc[number, head] = jnp.where(step == 0, part, acc[number, head] + part)

    @pl.when(step == pl.num_programs(0) - 1)
    def _():
        slot_rows[...] = acc[...].astype(BF)


def owner_map(column, owner, toks, slots, shape):
    inside = jnp.sum((column < owner * toks).astype(jnp.int32), axis=0, keepdims=True)
    held = jnp.sum((column < (owner + 1) * toks).astype(jnp.int32), axis=0, keepdims=True) - inside
    slot = iota(shape, 1) % slots
    hot = (iota(shape, 0) == inside + slot) & (slot < held)
    return jnp.where(hot, 1.0, 0.0).astype(BF)


def mask_kernel(order, slots, seq_rows, pos_row, bias, compact, expand, place):
    toks = place.shape[0]
    me = lax.axis_index("ctx")
    base = me * toks
    row = pos_row[...]
    count = row.shape[1]
    column = as_column(row)
    for start in range(0, bias.shape[0], TILE):
        key = iota((TILE, count), 0) + (base - HALF + start)
        hits = jnp.sum((row == key).astype(F32), axis=1, keepdims=True)
        key = key[:, :1]
        out = (hits > 0) | (key < 0) | (key >= seq_rows)
        bias[start : start + TILE, :] = jnp.broadcast_to(jnp.where(out, NEG, 0.0), (TILE, 128))
    tok = iota((toks, count), 0) + base
    hit = jnp.sum((row == tok).astype(F32), axis=1, keepdims=True)
    rank = jnp.sum(((row >= base) & (row < tok)).astype(F32), axis=1, keepdims=True)
    slot = iota((toks, slots), 1).astype(F32)
    place[...] = jnp.where((hit > 0) & (rank == slot), 1.0, 0.0).astype(BF)
    part = iota((1, compact.shape[1]), 1) // slots
    owner = jnp.zeros_like(part)
    for number, relative in enumerate(order):
        owner = jnp.where(part == number, me ^ relative, owner)
    compact[...] = owner_map(column, owner, toks, slots, compact.shape)
    owner = iota((1, compact.shape[1]), 1) // slots
    hot = owner_map(column, owner, toks, slots, compact.shape)
    expand[...] = hot.astype(F32).T.astype(BF)


def stats_kernel(scale2, compact, *refs):
    parts, (kv, rows, stats) = refs[:-3], refs[-3:]
    pieces = []
    for part in parts:
        for i in range(part.shape[0]):
            pieces.append(jnp.concatenate([part[i, number, 0] for number in range(4)], axis=1))
    packed = nn(compact[...], jnp.concatenate(pieces, axis=0)).astype(BF)
    width = kv.shape[3]
    table = [packed[:, number * width : (number + 1) * width] for number in range(4)]
    for number in range(4):
        rows[number, 0] = table[number]
    queries, _, _, grads = table
    scores = nt(kv[0, 0], queries) * scale2
    top = jnp.max(scores, axis=0, keepdims=True)
    weights = jnp.exp2(scores - top)
    stats[0, 0, 0:1, :] = top
    stats[0, 0, 1:2, :] = jnp.sum(weights, axis=0, keepdims=True)
    stats[0, 0, 2:3, :] = jnp.sum(weights * nt(kv[1, 0], grads), axis=0, keepdims=True)


def band(scores, low):
    rows, columns = iota(scores.shape, 0), iota(scores.shape, 1)
    return jnp.where(rows <= columns if low else rows >= columns, scores, NEG)


def join(blocks, number, buf):
    toks = blocks[0].shape[2]
    for place, block in enumerate(blocks):
        buf[place * toks : (place + 1) * toks, :] = block[number, 0]


def put_in_slots(expand, tables, sums):
    owners, kinds, _, slots, width = sums.shape
    spread = nn(expand, jnp.concatenate(tables, axis=1)).astype(BF)
    for owner in range(owners):
        for kind in range(kinds):
            sums[owner, kind, 0] = spread[
                owner * slots : (owner + 1) * slots, kind * width : (kind + 1) * width
            ]


def global_kernel(scale, scale2, kv, rows, stats, expand, dkv, ends):
    g_query, g_grad = rows[0, 0], rows[3, 0]
    tops = stats[:, 0, 0:1, :]
    top = jnp.max(tops, axis=0)
    factor = jnp.exp2(tops - top[None])
    total = jnp.sum(stats[:, 0, 1:2, :] * factor, axis=0)
    g_dot = jnp.sum(stats[:, 0, 2:3, :] * factor, axis=0) / total
    g_log = top + jnp.log2(total)
    weights = jnp.exp2(nt(kv[0, 0], g_query) * scale2 - g_log)
    narrow = weights.astype(BF)
    slopes = (weights * (nt(kv[1, 0], g_grad) - g_dot)).astype(BF)
    dkv[0, 0] = nn(slopes, g_query) * scale
    dkv[1, 0] = nn(narrow, g_grad)
    out = nn(kv[1, 0].T, narrow).T.astype(BF)
    dq = (nn(kv[0, 0].T, slopes) * scale).T.astype(BF)
    put_in_slots(expand[...], (out, dq), ends)


def local_kernel(scale, scale2, made, qd, low, kv, high, rows, bias, expand, *refs):
    out, log_dot, dq, dkv, sums, keys, values, score_buf, probs, slopes = refs[made:]
    toks = kv.shape[2]
    reach = 2 * HALF + TILE
    span = keys.shape[0] - rows.shape[2]
    width = keys.shape[1]
    join((low, kv, high), 0, keys)
    join((low, kv, high), 1, values)
    keys[span:, :] = rows[1, 0]
    values[span:, :] = rows[2, 0]
    key_t = keys[...].T
    value_t = values[...].T
    grad_t = qd[1, 0].T
    for q_tile in range(toks // TILE):
        lanes = slice(q_tile * TILE, (q_tile + 1) * TILE)
        query = qd[0, 0, lanes, :]
        grad = qd[1, 0, lanes, :]
        starts = [q_tile * TILE + piece for piece in range(0, reach, TILE)]
        starts += list(range(span, keys.shape[0], TILE))
        best = None
        for piece, start in enumerate(starts):
            scores = nt(keys[start : start + TILE, :], query) * scale2
            if start < span:
                scores = scores + wide(bias[start : start + TILE, :], TILE)
            if piece == 0:
                scores = band(scores, False)
            elif piece == reach // TILE - 1:
                scores = band(scores, True)
            score_buf[q_tile, piece * TILE : (piece + 1) * TILE, :] = scores
            part = jnp.max(scores.reshape(TILE // 8, 8, TILE), axis=0)
            best = part if best is None else jnp.maximum(best, part)
        top = jnp.max(best, axis=0, keepdims=True)
        total = None
        for piece, start in enumerate(starts):
            rows_ = slice(piece * TILE, (piece + 1) * TILE)
            weights = jnp.exp2(score_buf[q_tile, rows_, :] - top)
            score_buf[q_tile, rows_, :] = weights
            probs[start : start + TILE, lanes] = weights.astype(BF)
            part = jnp.sum(weights.reshape(TILE // 8, 8, TILE), axis=0)
            total = part if total is None else total + part
        total = jnp.sum(total, axis=0, keepdims=True)
        window = slice(q_tile * TILE, q_tile * TILE + reach)
        acc = nn(value_t[:, window], probs[window, lanes]) + nn(value_t[:, span:], probs[span:, lanes])
        inverse = 1.0 / total
        acc = acc * inverse
        dot = jnp.sum(grad_t[:, lanes].astype(F32) * acc, axis=0, keepdims=True)
        log_dot[0, 0:1, lanes] = top + jnp.log2(total)
        log_dot[0, 1:2, lanes] = dot
        out[0, lanes, :] = acc.T.astype(BF)
        for piece, start in enumerate(starts):
            weights = score_buf[q_tile, piece * TILE : (piece + 1) * TILE, :] * inverse
            rise = nt(values[start : start + TILE, :], grad) - dot
            slopes[start : start + TILE, lanes] = (weights * rise).astype(BF)
            if HALF <= start < HALF + toks or start >= span:
                probs[start : start + TILE, lanes] = weights.astype(BF)
        acc = nn(key_t[:, window], slopes[window, lanes]) + nn(key_t[:, span:], slopes[span:, lanes])
        dq[0, lanes, :] = (acc * scale).T
    own = slice(HALF, HALF + toks)
    dkv[0, 0] = nn(slopes[own, :], qd[0, 0]) * scale
    dkv[1, 0] = nn(probs[own, :], qd[1, 0])
    g_dk = (nn(slopes[span:, :], qd[0, 0]) * scale).astype(BF)
    g_dv = nn(probs[span:, :], qd[1, 0]).astype(BF)
    put_in_slots(expand[...], (g_dk, g_dv), sums)


def rim_kernel(
    scale, scale2, kv, bias, qd_low, qd_high, log_low, log_high, partial, dkv, queries, grads, probs, slopes
):
    toks = kv.shape[2]
    reach = toks + TILE
    join((qd_low, qd_high), 0, queries)
    join((qd_low, qd_high), 1, grads)
    for k_tile in range(toks // TILE):
        span = slice(k_tile * TILE, (k_tile + 1) * TILE)
        key = kv[0, 0, span, :]
        value = kv[1, 0, span, :]
        key_bias = wide(bias[HALF + k_tile * TILE : HALF + (k_tile + 1) * TILE, :], TILE)
        for piece in range(reach // TILE):
            start = (k_tile + piece) * TILE
            log_dot, offset = (log_low, start) if start < toks else (log_high, start - toks)
            lanes = slice(offset, offset + TILE)
            scores = nt(key, queries[start : start + TILE, :]) * scale2 + key_bias
            if piece == 0:
                scores = band(scores, True)
            elif piece == reach // TILE - 1:
                scores = band(scores, False)
            weights = jnp.exp2(scores - log_dot[0, 0:1, lanes])
            slope = weights * (nt(value, grads[start : start + TILE, :]) - log_dot[0, 1:2, lanes])
            spot = slice(piece * TILE, (piece + 1) * TILE)
            probs[span, spot] = weights.astype(BF)
            slopes[span, spot] = slope.astype(BF)
        window = slice(k_tile * TILE, k_tile * TILE + reach)
        dkv[0, 0, span, :] = partial[0, 0, span, :] + nn(slopes[span, :], queries[window, :]) * scale
        dkv[1, 0, span, :] = partial[1, 0, span, :] + nn(probs[span, :], grads[window, :])


def final_kernel(
    place, out, ends, sums, dq, dkv, extra, attn, query_grad, key_grad, value_grad, wide_rows
):
    heads, toks = out.shape[0], out.shape[1]
    hot = place[...]
    is_global = jnp.sum(hot.astype(F32), axis=1, keepdims=True) > 0
    for head in range(heads):
        rows = pl.ds(head, toks, stride=heads)
        tables = []
        for source, kind in ((ends, 0), (ends, 1), (sums, 0), (sums, 1)):
            table = source[0, kind, head].astype(F32)
            for device in range(1, source.shape[0]):
                table = table + source[device, kind, head].astype(F32)
            tables.append(table.astype(BF))
        width = out.shape[2]
        added = nn(hot, jnp.concatenate(tables, axis=1))
        added = [added[:, i * width : (i + 1) * width] for i in range(4)]
        wide_rows[rows, :] = jnp.where(is_global, added[0], out[head].astype(F32))
        query_grad[rows, :] = dq[head] + added[1]
        key_grad[rows, :] = dkv[0, head] + extra[0, head] + added[2]
        value_grad[rows, :] = dkv[1, head] + extra[1, head] + added[3]
    attn[...] = wide_rows[...].astype(BF)


def cost(flops, moved, exps=0):
    return pl.CostEstimate(flops=int(flops), bytes_accessed=int(moved), transcendentals=int(exps))


def struct(shape, dtype):
    return jax.ShapeDtypeStruct(shape, dtype)


def whole(shape):
    return pl.BlockSpec(shape, lambda head: (0,) * len(shape))


def per_head(shape, dim, first=0):
    block = tuple(1 if i == dim else size for i, size in enumerate(shape))
    return pl.BlockSpec(
        block, lambda head: tuple(head + first if i == dim else 0 for i in range(len(shape)))
    )


def shards(query_rows, key_rows, value_rows, out_grad, global_pos):
    toks, heads, width = query_rows.shape
    count = global_pos.shape[0]
    devices = lax.axis_size("ctx")
    slots = max(16, 2 * count // devices)
    scale = width ** (-0.5)
    scale2 = scale * LOG2E
    bits = devices.bit_length() - 1
    stages = [
        [mask << low for mask in range(1, 1 << min(2, bits - low))] for low in range(1, bits, 2)
    ] + [[1]]
    order = [0]
    for stage in stages:
        order = order + [one ^ mask for mask in stage for one in order]
    pos_row = global_pos.reshape(1, count)
    q_flat, k_flat, v_flat, g_flat = (
        x.reshape(toks * heads, width) for x in (query_rows, key_rows, value_rows, out_grad)
    )

    def swap(value, mask):
        return lax.ppermute(value, "ctx", [(i, i ^ mask) for i in range(devices)])

    def from_low(value):
        return lax.ppermute(value, "ctx", [(i, i + 1) for i in range(devices - 1)])

    def from_high(value):
        return lax.ppermute(value, "ctx", [(i + 1, i) for i in range(devices - 1)])

    def after(value, earlier):
        return lax.optimization_barrier((value, earlier))[0]

    pair_shape = (2, heads, toks, width)
    slot_shape = (4, heads, slots, width)
    steps = 1
    flat_spec = pl.BlockSpec((toks * heads // steps, width), lambda i: (i, 0))
    pair_spec = pl.BlockSpec((2, heads, toks // steps, width), lambda i: (0, 0, i, 0))
    wide_pair = pltpu.VMEM((2, toks * heads // steps, width), F32)
    halves = 2 if heads % 2 == 0 else 1
    group = heads // halves
    part_shape = (2, group, toks, width)
    kv, *kv_parts = pl.pallas_call(
        functools.partial(pack_keys_kernel, heads),
        out_shape=[struct(pair_shape, BF)] + [struct(part_shape, BF)] * halves,
        scratch_shapes=[wide_pair],
        compiler_params=params(),
        name="pack_keys",
    )(k_flat, v_flat)

    qd, slot_rows = pl.pallas_call(
        functools.partial(pack_queries_kernel, heads, slots),
        grid=(steps,),
        in_specs=[flat_spec, flat_spec, pair_spec, whole((1, count))],
        out_specs=(pair_spec, whole(slot_shape)),
        out_shape=(struct(pair_shape, BF), struct(slot_shape, BF)),
        scratch_shapes=[wide_pair, pltpu.VMEM(slot_shape, F32)],
        compiler_params=params(),
        name="pack_queries",
    )(q_flat, g_flat, kv, pos_row)

    span = toks + 2 * HALF
    bias, compact, expand, place = pl.pallas_call(
        functools.partial(mask_kernel, order, slots, toks * devices),
        out_shape=(
            struct((span, 128), F32),
            struct((count, devices * slots), BF),
            struct((devices * slots, count), BF),
            struct((toks, slots), BF),
        ),
        compiler_params=params(),
        name="masks",
    )(pos_row)

    lows, highs = [], []
    for part in kv_parts:
        if lows:
            part = after(part, (lows[-1], highs[-1]))
        lows.append(from_low(part))
        highs.append(from_high(part))
    held = [slot_rows[None]]
    for stage in stages:
        send = jnp.concatenate(held, axis=0) if len(held) > 1 else held[0]
        if stage == [1]:
            send = after(send, (lows[0], highs[0], place))
        held += [swap(send, mask) for mask in stage]

    row_shape = (4, heads, count, width)
    rows, stats = pl.pallas_call(
        functools.partial(stats_kernel, scale2),
        grid=(heads,),
        in_specs=[whole(compact.shape)]
        + [per_head(part.shape, 2) for part in held]
        + [per_head(pair_shape, 1)],
        out_specs=(per_head(row_shape, 1), per_head((1, heads, 3, count), 1)),
        out_shape=(struct(row_shape, BF), struct((1, heads, 3, count), F32)),
        compiler_params=params(),
        cost_estimate=cost(1e6, 1e6),
        name="global_stats",
    )(compact, *held, kv)

    stats = jnp.broadcast_to(stats, (devices,) + stats.shape[1:])
    stats = lax.all_to_all(stats, "ctx", 0, 0, tiled=True)

    ends_shape = (devices, 2, heads, slots, width)
    made = ()
    for part in range(halves):
        if part == halves - 1:
            early = made[1] if made else rows
            qd_late = after(qd, (lows[-1], highs[-1], early))
            qd_low, qd_high = from_low(qd_late), from_high(qd_late)
            stats = after(stats, early)
            extra, ends = pl.pallas_call(
                functools.partial(global_kernel, scale, scale2),
                grid=(heads,),
                in_specs=[per_head(pair_shape, 1), per_head(row_shape, 1)]
                + [per_head(stats.shape, 1), whole(expand.shape)],
                out_specs=(per_head(pair_shape, 1), per_head(ends_shape, 2)),
                out_shape=(struct(pair_shape, F32), struct(ends_shape, BF)),
                compiler_params=params(),
                cost_estimate=cost(2e9, 5e6, 1e6),
                name="global_queries",
            )(kv, rows, stats, expand)

            ends = lax.all_to_all(ends, "ctx", 0, 0, tiled=True)
            expand_late = after(expand, extra)
        first = part * group
        whole_in = [
            per_head(pair_shape, 1, first),
            per_head(part_shape, 1),
            per_head(pair_shape, 1, first),
            per_head(part_shape, 1),
            per_head(row_shape, 1, first),
            whole(bias.shape),
            whole(expand.shape),
        ]
        made = pl.pallas_call(
            functools.partial(local_kernel, scale, scale2, len(made)),
            grid=(group,),
            in_specs=whole_in + [pl.BlockSpec(memory_space=pl.ANY)] * len(made),
            out_specs=(
                per_head((heads, toks, width), 0, first),
                per_head((heads, 2, toks), 0, first),
                per_head((heads, toks, width), 0, first),
                per_head(pair_shape, 1, first),
                per_head(ends_shape, 2, first),
            ),
            out_shape=(
                struct((heads, toks, width), BF),
                struct((heads, 2, toks), F32),
                struct((heads, toks, width), F32),
                struct(pair_shape, F32),
                struct(ends_shape, BF),
            ),
            scratch_shapes=[
                pltpu.VMEM((span + count, width), BF),
                pltpu.VMEM((span + count, width), BF),
                pltpu.VMEM((toks // TILE, 2 * HALF + TILE + count, TILE), F32),
                pltpu.VMEM((span + count, toks), BF),
                pltpu.VMEM((span + count, toks), BF),
            ],
            input_output_aliases={len(whole_in) + i: i for i in range(len(made))},
            compiler_params=params(),
            cost_estimate=cost(1e6, 1e6),
            name="local",
        )(
            qd,
            lows[part],
            kv,
            highs[part],
            rows,
            bias,
            expand_late if part == halves - 1 else expand,
            *made,
        )
    out, log_dot, dq, dkv, sums = made
    log_late = after(log_dot, (qd_low, qd_high))
    log_low, log_high = from_low(log_late), from_high(log_late)

    sums = lax.all_to_all(sums, "ctx", 0, 0, tiled=True)

    dkv = pl.pallas_call(
        functools.partial(rim_kernel, scale, scale2),
        grid=(heads,),
        in_specs=[per_head(pair_shape, 1), whole(bias.shape)]
        + [per_head(pair_shape, 1)] * 2
        + [per_head(log_dot.shape, 0)] * 2
        + [per_head(pair_shape, 1)],
        out_specs=per_head(pair_shape, 1),
        out_shape=struct(pair_shape, F32),
        scratch_shapes=[
            pltpu.VMEM((2 * toks, width), BF),
            pltpu.VMEM((2 * toks, width), BF),
            pltpu.VMEM((toks, toks + TILE), BF),
            pltpu.VMEM((toks, toks + TILE), BF),
        ],
        compiler_params=params(),
        cost_estimate=cost(4e9, 8e6, 2e6),
        name="rim",
    )(kv, after(bias, ends), qd_low, qd_high, log_low, log_high, dkv)

    flat_shape = (toks * heads, width)
    steps = 2
    outs = pl.pallas_call(
        final_kernel,
        grid=(steps,),
        in_specs=[
            pl.BlockSpec((toks // steps, slots), lambda i: (i, 0)),
            pl.BlockSpec((heads, toks // steps, width), lambda i: (0, i, 0)),
            whole(ends_shape),
            whole(ends_shape),
            pl.BlockSpec((heads, toks // steps, width), lambda i: (0, i, 0)),
            pl.BlockSpec((2, heads, toks // steps, width), lambda i: (0, 0, i, 0)),
            pl.BlockSpec((2, heads, toks // steps, width), lambda i: (0, 0, i, 0)),
        ],
        out_specs=[pl.BlockSpec((toks * heads // steps, width), lambda i: (i, 0))] * 4,
        out_shape=[struct(flat_shape, kind) for kind in (BF, F32, F32, F32)],
        scratch_shapes=[pltpu.VMEM((toks * heads // steps, width), F32)],
        compiler_params=params(),
        name="final",
    )(place, out, ends, sums, dq, dkv, extra)
    return tuple(x.reshape(toks, heads, width) for x in outs)


def solution(mesh):
    spec = P("ctx", "head", None)
    return jax.shard_map(
        shards,
        mesh=mesh,
        in_specs=(spec, spec, spec, spec, P()),
        out_specs=(spec, spec, spec, spec),
        check_vma=False,
    )
```

```python
import functools
import math

import jax
import jax.numpy as jnp
from jax import lax
from jax.experimental import pallas as pl
from jax.experimental.pallas import tpu as pltpu
from jax.sharding import PartitionSpec as P

HALF = 512
TILE = 256
NEG = -1e30
LOG2E = 1.0 / math.log(2.0)
VMEM_BYTES = 63 * 1024 * 1024
BF = jnp.bfloat16
F32 = jnp.float32


def nt(a, b):
    return lax.dot_general(a, b, (((1,), (1,)), ((), ())), preferred_element_type=F32)


def nn(a, b):
    return lax.dot_general(a, b, (((1,), (0,)), ((), ())), preferred_element_type=F32)


def wide(column, width):
    return jnp.concatenate([column] * (width // column.shape[1]), axis=1)


def iota(shape, dim):
    return lax.broadcasted_iota(jnp.int32, shape, dim)


def params():
    return pltpu.CompilerParams(vmem_limit_bytes=VMEM_BYTES)


def as_column(row):
    return jnp.broadcast_to(row, (128, row.shape[1])).T[:, :1]


def pack_keys_kernel(heads, k, v, kv, *refs):
    parts, wide_rows = refs[:-1], refs[-1]
    group = heads // len(parts)
    toks = k.shape[0] // heads
    for number, source in enumerate((k, v)):
        wide_rows[number] = source[...].astype(F32)
        for head in range(heads):
            rows = wide_rows[number, pl.ds(head, toks, stride=heads), :].astype(BF)
            kv[number, head] = rows
            parts[head // group][number, head % group] = rows


def pack_queries_kernel(heads, slots, q, g, kv, pos_row, qd, slot_rows, wide_rows, acc):
    step = pl.program_id(0)
    toks = q.shape[0] // heads
    row = pos_row[...]
    count = row.shape[1]
    base = lax.axis_index("ctx") * (toks * pl.num_programs(0))
    column = as_column(row)
    tok = iota((count, toks), 1) + (base + step * toks)
    hit = jnp.sum((column == tok).astype(F32), axis=0, keepdims=True)
    rank = jnp.sum(((column >= base) & (column < tok)).astype(F32), axis=0, keepdims=True)
    slot = iota((slots, toks), 0).astype(F32)
    pick = jnp.where((hit > 0) & (rank == slot), 1.0, 0.0).astype(BF)
    tok = iota((toks, count), 0) + (base + step * toks)
    hit_column = jnp.sum((row == tok).astype(F32), axis=1, keepdims=True)
    tables = [[], [kv[0, h] for h in range(heads)], [kv[1, h] for h in range(heads)], []]
    for number, source in ((0, q), (3, g)):
        wide_rows[number // 3] = source[...].astype(F32)
        for head in range(heads):
            rows = wide_rows[number // 3, pl.ds(head, toks, stride=heads), :]
            tables[number].append(rows.astype(BF))
            if number == 0:
                qd[0, head] = rows.astype(BF)
            else:
                qd[1, head] = jnp.where(hit_column > 0, 0.0, rows).astype(BF)
    for number in range(4):
        found = nn(pick, jnp.concatenate(tables[number], axis=1))
        for head in range(heads):
            part = found[:, head * 128 : (head + 1) * 128]
            acc[number, head] = jnp.where(step == 0, part, acc[number, head] + part)

    @pl.when(step == pl.num_programs(0) - 1)
    def _():
        slot_rows[...] = acc[...].astype(BF)


def owner_map(column, owner, toks, slots, shape):
    inside = jnp.sum((column < owner * toks).astype(jnp.int32), axis=0, keepdims=True)
    held = jnp.sum((column < (owner + 1) * toks).astype(jnp.int32), axis=0, keepdims=True) - inside
    slot = iota(shape, 1) % slots
    hot = (iota(shape, 0) == inside + slot) & (slot < held)
    return jnp.where(hot, 1.0, 0.0).astype(BF)


def mask_kernel(order, slots, seq_rows, pos_row, bias, compact, expand, place):
    toks = place.shape[0]
    me = lax.axis_index("ctx")
    base = me * toks
    row = pos_row[...]
    count = row.shape[1]
    column = as_column(row)
    for start in range(0, bias.shape[0], TILE):
        key = iota((TILE, count), 0) + (base - HALF + start)
        hits = jnp.sum((row == key).astype(F32), axis=1, keepdims=True)
        key = key[:, :1]
        out = (hits > 0) | (key < 0) | (key >= seq_rows)
        bias[start : start + TILE, :] = jnp.broadcast_to(jnp.where(out, NEG, 0.0), (TILE, 128))
    tok = iota((toks, count), 0) + base
    hit = jnp.sum((row == tok).astype(F32), axis=1, keepdims=True)
    rank = jnp.sum(((row >= base) & (row < tok)).astype(F32), axis=1, keepdims=True)
    slot = iota((toks, slots), 1).astype(F32)
    place[...] = jnp.where((hit > 0) & (rank == slot), 1.0, 0.0).astype(BF)
    part = iota((1, compact.shape[1]), 1) // slots
    owner = jnp.zeros_like(part)
    for number, relative in enumerate(order):
        owner = jnp.where(part == number, me ^ relative, owner)
    compact[...] = owner_map(column, owner, toks, slots, compact.shape)
    owner = iota((1, compact.shape[1]), 1) // slots
    hot = owner_map(column, owner, toks, slots, compact.shape)
    expand[...] = hot.astype(F32).T.astype(BF)


def stats_kernel(scale2, compact, *refs):
    parts, (kv, rows, stats) = refs[:-3], refs[-3:]
    pieces = []
    for part in parts:
        for i in range(part.shape[0]):
            pieces.append(jnp.concatenate([part[i, number, 0] for number in range(4)], axis=1))
    packed = nn(compact[...], jnp.concatenate(pieces, axis=0)).astype(BF)
    width = kv.shape[3]
    table = [packed[:, number * width : (number + 1) * width] for number in range(4)]
    for number in range(4):
        rows[number, 0] = table[number]
    queries, _, _, grads = table
    scores = nt(kv[0, 0], queries) * scale2
    top = jnp.max(scores, axis=0, keepdims=True)
    weights = jnp.exp2(scores - top)
    stats[0, 0, 0:1, :] = top
    stats[0, 0, 1:2, :] = jnp.sum(weights, axis=0, keepdims=True)
    stats[0, 0, 2:3, :] = jnp.sum(weights * nt(kv[1, 0], grads), axis=0, keepdims=True)


def band(scores, low):
    rows, columns = iota(scores.shape, 0), iota(scores.shape, 1)
    return jnp.where(rows <= columns if low else rows >= columns, scores, NEG)


def join(blocks, number, buf):
    toks = blocks[0].shape[2]
    for place, block in enumerate(blocks):
        buf[place * toks : (place + 1) * toks, :] = block[number, 0]


def put_in_slots(expand, tables, sums):
    owners, kinds, _, slots, width = sums.shape
    spread = nn(expand, jnp.concatenate(tables, axis=1)).astype(BF)
    for owner in range(owners):
        for kind in range(kinds):
            sums[owner, kind, 0] = spread[
                owner * slots : (owner + 1) * slots, kind * width : (kind + 1) * width
            ]


def global_kernel(scale, scale2, kv, rows, stats, expand, dkv, ends):
    g_query, g_grad = rows[0, 0], rows[3, 0]
    tops = stats[:, 0, 0:1, :]
    top = jnp.max(tops, axis=0)
    factor = jnp.exp2(tops - top[None])
    total = jnp.sum(stats[:, 0, 1:2, :] * factor, axis=0)
    g_dot = jnp.sum(stats[:, 0, 2:3, :] * factor, axis=0) / total
    g_log = top + jnp.log2(total)
    weights = jnp.exp2(nt(kv[0, 0], g_query) * scale2 - g_log)
    narrow = weights.astype(BF)
    slopes = (weights * (nt(kv[1, 0], g_grad) - g_dot)).astype(BF)
    dkv[0, 0] = (nt(g_query.T, slopes) * scale).T
    dkv[1, 0] = nt(g_grad.T, narrow).T
    out = nn(kv[1, 0].T, narrow).T.astype(BF)
    dq = (nn(kv[0, 0].T, slopes) * scale).T.astype(BF)
    put_in_slots(expand[...], (out, dq), ends)


def local_kernel(scale, scale2, halves, group, qd, kv, *refs):
    lows, highs, refs = refs[:halves], refs[halves : 2 * halves], refs[2 * halves :]
    rows, bias, expand, out, log_dot, dq, dkv, sums, keys, values, score_buf, probs, slopes = refs
    toks = kv.shape[2]
    reach = 2 * HALF + TILE
    span = keys.shape[0] - rows.shape[2]
    for part in range(halves):

        @pl.when(pl.program_id(0) // group == part)
        def _():
            join((lows[part], kv, highs[part]), 0, keys)
            join((lows[part], kv, highs[part]), 1, values)

    keys[span:, :] = rows[1, 0]
    values[span:, :] = rows[2, 0]
    key_t, value_t = keys[...].T, values[...].T
    query_t, grad_t = qd[0, 0].T, qd[1, 0].T
    tiles = range(toks // TILE)
    lanes = [slice(tile * TILE, (tile + 1) * TILE) for tile in tiles]
    windows = [slice(tile * TILE, tile * TILE + reach) for tile in tiles]
    starts = [
        list(range(tile * TILE, tile * TILE + reach, TILE)) + list(range(span, keys.shape[0], TILE))
        for tile in tiles
    ]
    best, top, total, scaled, dots = ([None] * len(tiles) for _ in range(5))

    def score(tile, piece):
        start = starts[tile][piece]
        scores = nn(keys[start : start + TILE, :], query_t[:, lanes[tile]]) * scale2
        if start < span:
            scores = scores + wide(bias[start : start + TILE, :], TILE)
        if piece == 0:
            scores = band(scores, False)
        elif piece == reach // TILE - 1:
            scores = band(scores, True)
        score_buf[tile, piece * TILE : (piece + 1) * TILE, :] = scores
        part = jnp.max(scores.reshape(TILE // 8, 8, TILE), axis=0)
        best[tile] = part if best[tile] is None else jnp.maximum(best[tile], part)

    def weigh(tile, piece):
        if top[tile] is None:
            top[tile] = jnp.max(best[tile], axis=0, keepdims=True)
        start = starts[tile][piece]
        weights = jnp.exp2(score_buf[tile, piece * TILE : (piece + 1) * TILE, :] - top[tile])
        probs[start : start + TILE, lanes[tile]] = weights.astype(BF)
        part = jnp.sum(weights.reshape(TILE // 8, 8, TILE), axis=0)
        total[tile] = part if total[tile] is None else total[tile] + part

    def attend(tile):
        whole_sum = jnp.sum(total[tile], axis=0, keepdims=True)
        inverse = 1.0 / whole_sum
        grads = grad_t[:, lanes[tile]].astype(F32)
        acc = nn(value_t[:, windows[tile]], probs[windows[tile], lanes[tile]])
        acc = (acc + nn(value_t[:, span:], probs[span:, lanes[tile]])) * inverse
        dot = jnp.sum(grads * acc, axis=0, keepdims=True)
        log_dot[0, 0:1, lanes[tile]] = top[tile] + jnp.log2(whole_sum)
        log_dot[0, 1:2, lanes[tile]] = dot
        out[0, lanes[tile], :] = acc.T.astype(BF)
        scaled[tile] = (grads * inverse).astype(BF)
        dots[tile] = dot * inverse

    def slope(tile, piece):
        start = starts[tile][piece]
        rise = nn(values[start : start + TILE, :], scaled[tile]) - dots[tile]
        weights = probs[start : start + TILE, lanes[tile]].astype(F32)
        slopes[start : start + TILE, lanes[tile]] = (weights * rise).astype(BF)

    def query_gradient(tile):
        acc = nn(key_t[:, windows[tile]], slopes[windows[tile], lanes[tile]])
        acc = acc + nn(key_t[:, span:], slopes[span:, lanes[tile]])
        dq[0, lanes[tile], :] = (acc * scale).T

    for step in range(len(tiles) + 2):
        for piece in range(len(starts[0])):
            if 0 <= step - 2:
                slope(step - 2, piece)
            if 0 <= step - 1 < len(tiles):
                weigh(step - 1, piece)
            if step < len(tiles):
                score(step, piece)
        if 0 <= step - 2:
            query_gradient(step - 2)
        if 0 <= step - 1 < len(tiles):
            attend(step - 1)
    own = slice(HALF, HALF + toks)
    grads = jnp.concatenate(scaled, axis=1)
    dkv[0, 0] = (nt(query_t, slopes[own, :]) * scale).T
    dkv[1, 0] = nt(grads, probs[own, :]).T
    g_dk = (nt(query_t, slopes[span:, :]) * scale).T.astype(BF)
    g_dv = nt(grads, probs[span:, :]).T.astype(BF)
    put_in_slots(expand[...], (g_dk, g_dv), sums)


def rim_kernel(
    scale, scale2, kv, bias, qd_low, qd_high, log_low, log_high, partial, dkv, probs, slopes
):
    toks = kv.shape[2]
    reach = toks + TILE
    query_t = jnp.concatenate([qd_low[0, 0].T, qd_high[0, 0].T], axis=1)
    grad_t = jnp.concatenate([qd_low[1, 0].T, qd_high[1, 0].T], axis=1)
    for k_tile in range(toks // TILE):
        span = slice(k_tile * TILE, (k_tile + 1) * TILE)
        key = kv[0, 0, span, :]
        value = kv[1, 0, span, :]
        key_bias = wide(bias[HALF + k_tile * TILE : HALF + (k_tile + 1) * TILE, :], TILE)
        for piece in range(reach // TILE):
            start = (k_tile + piece) * TILE
            log_dot, offset = (log_low, start) if start < toks else (log_high, start - toks)
            lanes = slice(offset, offset + TILE)
            scores = nn(key, query_t[:, start : start + TILE]) * scale2 + key_bias
            if piece == 0:
                scores = band(scores, True)
            elif piece == reach // TILE - 1:
                scores = band(scores, False)
            weights = jnp.exp2(scores - log_dot[0, 0:1, lanes])
            rise = nn(value, grad_t[:, start : start + TILE]) - log_dot[0, 1:2, lanes]
            spot = slice(piece * TILE, (piece + 1) * TILE)
            probs[span, spot] = weights.astype(BF)
            slopes[span, spot] = (weights * rise).astype(BF)
    for k_tile in range(toks // TILE):
        span = slice(k_tile * TILE, (k_tile + 1) * TILE)
        window = slice(k_tile * TILE, k_tile * TILE + reach)
        dk = (nt(query_t[:, window], slopes[span, :]) * scale).T
        dkv[0, 0, span, :] = partial[0, 0, span, :] + dk
        dkv[1, 0, span, :] = partial[1, 0, span, :] + nt(grad_t[:, window], probs[span, :]).T


def final_kernel(
    place, out, ends, sums, dq, dkv, extra, attn, query_grad, key_grad, value_grad, wide_rows
):
    heads, toks = out.shape[0], out.shape[1]
    hot = place[...]
    is_global = jnp.sum(hot.astype(F32), axis=1, keepdims=True) > 0
    for head in range(heads):
        rows = pl.ds(head, toks, stride=heads)
        tables = []
        for source, kind in ((ends, 0), (ends, 1), (sums, 0), (sums, 1)):
            table = source[0, kind, head].astype(F32)
            for device in range(1, source.shape[0]):
                table = table + source[device, kind, head].astype(F32)
            tables.append(table.astype(BF))
        width = out.shape[2]
        added = nn(hot, jnp.concatenate(tables, axis=1))
        added = [added[:, i * width : (i + 1) * width] for i in range(4)]
        wide_rows[rows, :] = jnp.where(is_global, added[0], out[head].astype(F32))
        query_grad[rows, :] = dq[head] + added[1]
        key_grad[rows, :] = dkv[0, head] + extra[0, head] + added[2]
        value_grad[rows, :] = dkv[1, head] + extra[1, head] + added[3]
    attn[...] = wide_rows[...].astype(BF)


def cost(flops, moved, exps=0):
    return pl.CostEstimate(flops=int(flops), bytes_accessed=int(moved), transcendentals=int(exps))


def struct(shape, dtype):
    return jax.ShapeDtypeStruct(shape, dtype)


def whole(shape):
    return pl.BlockSpec(shape, lambda head: (0,) * len(shape))


def per_head(shape, dim, first=0):
    block = tuple(1 if i == dim else size for i, size in enumerate(shape))
    return pl.BlockSpec(
        block, lambda head: tuple(head + first if i == dim else 0 for i in range(len(shape)))
    )


def shards(query_rows, key_rows, value_rows, out_grad, global_pos):
    toks, heads, width = query_rows.shape
    count = global_pos.shape[0]
    devices = lax.axis_size("ctx")
    slots = max(16, 2 * count // devices)
    scale = width ** (-0.5)
    scale2 = scale * LOG2E
    bits = devices.bit_length() - 1
    stages = [
        [mask << low for mask in range(1, 1 << min(2, bits - low))] for low in range(1, bits, 2)
    ] + [[1]]
    order = [0]
    for stage in stages:
        order = order + [one ^ mask for mask in stage for one in order]
    pos_row = global_pos.reshape(1, count)
    q_flat, k_flat, v_flat, g_flat = (
        x.reshape(toks * heads, width) for x in (query_rows, key_rows, value_rows, out_grad)
    )

    def swap(value, mask):
        return lax.ppermute(value, "ctx", [(i, i ^ mask) for i in range(devices)])

    def from_low(value):
        return lax.ppermute(value, "ctx", [(i, i + 1) for i in range(devices - 1)])

    def from_high(value):
        return lax.ppermute(value, "ctx", [(i + 1, i) for i in range(devices - 1)])

    def after(value, earlier):
        return lax.optimization_barrier((value, earlier))[0]

    pair_shape = (2, heads, toks, width)
    slot_shape = (4, heads, slots, width)
    steps = 1
    flat_spec = pl.BlockSpec((toks * heads // steps, width), lambda i: (i, 0))
    pair_spec = pl.BlockSpec((2, heads, toks // steps, width), lambda i: (0, 0, i, 0))
    wide_pair = pltpu.VMEM((2, toks * heads // steps, width), F32)
    halves = 2 if heads % 2 == 0 else 1
    group = heads // halves
    part_shape = (2, group, toks, width)
    kv, *kv_parts = pl.pallas_call(
        functools.partial(pack_keys_kernel, heads),
        out_shape=[struct(pair_shape, BF)] + [struct(part_shape, BF)] * halves,
        scratch_shapes=[wide_pair],
        compiler_params=params(),
        name="pack_keys",
    )(k_flat, v_flat)

    qd, slot_rows = pl.pallas_call(
        functools.partial(pack_queries_kernel, heads, slots),
        grid=(steps,),
        in_specs=[flat_spec, flat_spec, pair_spec, whole((1, count))],
        out_specs=(pair_spec, whole(slot_shape)),
        out_shape=(struct(pair_shape, BF), struct(slot_shape, BF)),
        scratch_shapes=[wide_pair, pltpu.VMEM(slot_shape, F32)],
        compiler_params=params(),
        name="pack_queries",
    )(q_flat, g_flat, kv, pos_row)

    span = toks + 2 * HALF
    bias, compact, expand, place = pl.pallas_call(
        functools.partial(mask_kernel, order, slots, toks * devices),
        out_shape=(
            struct((span, 128), F32),
            struct((count, devices * slots), BF),
            struct((devices * slots, count), BF),
            struct((toks, slots), BF),
        ),
        compiler_params=params(),
        name="masks",
    )(pos_row)

    lows, highs = [], []
    for part in kv_parts:
        if lows:
            part = after(part, (lows[-1], highs[-1]))
        lows.append(from_low(part))
        highs.append(from_high(part))
    held = [slot_rows[None]]
    for stage in stages:
        send = jnp.concatenate(held, axis=0) if len(held) > 1 else held[0]
        if stage == [1]:
            send = after(send, (lows[0], highs[0], place))
        held += [swap(send, mask) for mask in stage]

    row_shape = (4, heads, count, width)
    rows, stats = pl.pallas_call(
        functools.partial(stats_kernel, scale2),
        grid=(heads,),
        in_specs=[whole(compact.shape)]
        + [per_head(part.shape, 2) for part in held]
        + [per_head(pair_shape, 1)],
        out_specs=(per_head(row_shape, 1), per_head((1, heads, 3, count), 1)),
        out_shape=(struct(row_shape, BF), struct((1, heads, 3, count), F32)),
        compiler_params=params(),
        cost_estimate=cost(1e6, 1e6),
        name="global_stats",
    )(compact, *held, kv)

    kv_done = (lows, highs)
    stats = after(stats, kv_done)
    stats = jnp.broadcast_to(stats, (devices,) + stats.shape[1:])
    stats = lax.all_to_all(stats, "ctx", 0, 0, tiled=True)
    qd_late = after(qd, (kv_done, rows))
    qd_low, qd_high = from_low(qd_late), from_high(qd_late)

    def half_head(part):
        return pl.BlockSpec(
            (2, 1, toks, width), lambda head: (0, jnp.clip(head - part * group, 0, group - 1), 0, 0)
        )

    ends_shape = (devices, 2, heads, slots, width)
    out, log_dot, dq, dkv, sums = pl.pallas_call(
        functools.partial(local_kernel, scale, scale2, halves, group),
        grid=(heads,),
        in_specs=[per_head(pair_shape, 1)] * 2
        + [half_head(part) for part in range(halves)] * 2
        + [per_head(row_shape, 1), whole(bias.shape), whole(expand.shape)],
        out_specs=(
            per_head((heads, toks, width), 0),
            per_head((heads, 2, toks), 0),
            per_head((heads, toks, width), 0),
            per_head(pair_shape, 1),
            per_head(ends_shape, 2),
        ),
        out_shape=(
            struct((heads, toks, width), BF),
            struct((heads, 2, toks), F32),
            struct((heads, toks, width), F32),
            struct(pair_shape, F32),
            struct(ends_shape, BF),
        ),
        scratch_shapes=[
            pltpu.VMEM((span + count, width), BF),
            pltpu.VMEM((span + count, width), BF),
            pltpu.VMEM((toks // TILE, 2 * HALF + TILE + count, TILE), F32),
            pltpu.VMEM((span + count, toks), BF),
            pltpu.VMEM((span + count, toks), BF),
        ],
        compiler_params=params(),
        cost_estimate=cost(1e6, 1e6),
        name="local",
    )(qd, kv, *lows, *highs, rows, bias, expand)
    log_late = after(log_dot, (qd_low, qd_high))
    log_low, log_high = from_low(log_late), from_high(log_late)

    extra, ends = pl.pallas_call(
        functools.partial(global_kernel, scale, scale2),
        grid=(heads,),
        in_specs=[per_head(pair_shape, 1), per_head(row_shape, 1)]
        + [per_head(stats.shape, 1), whole(expand.shape)],
        out_specs=(per_head(pair_shape, 1), per_head(ends_shape, 2)),
        out_shape=(struct(pair_shape, F32), struct(ends_shape, BF)),
        compiler_params=params(),
        cost_estimate=cost(2e9, 5e6, 1e6),
        name="global_queries",
    )(kv, rows, after(stats, log_dot), expand)
    ends = lax.all_to_all(ends, "ctx", 0, 0, tiled=True)
    sums = lax.all_to_all(sums, "ctx", 0, 0, tiled=True)

    dkv = pl.pallas_call(
        functools.partial(rim_kernel, scale, scale2),
        grid=(heads,),
        in_specs=[per_head(pair_shape, 1), whole(bias.shape)]
        + [per_head(pair_shape, 1)] * 2
        + [per_head(log_dot.shape, 0)] * 2
        + [per_head(pair_shape, 1)],
        out_specs=per_head(pair_shape, 1),
        out_shape=struct(pair_shape, F32),
        scratch_shapes=[
            pltpu.VMEM((toks, toks + TILE), BF),
            pltpu.VMEM((toks, toks + TILE), BF),
        ],
        compiler_params=params(),
        cost_estimate=cost(4e9, 8e6, 2e6),
        name="rim",
    )(kv, bias, qd_low, qd_high, log_low, log_high, dkv)

    flat_shape = (toks * heads, width)
    steps = 2
    outs = pl.pallas_call(
        final_kernel,
        grid=(steps,),
        in_specs=[
            pl.BlockSpec((toks // steps, slots), lambda i: (i, 0)),
            pl.BlockSpec((heads, toks // steps, width), lambda i: (0, i, 0)),
            whole(ends_shape),
            whole(ends_shape),
            pl.BlockSpec((heads, toks // steps, width), lambda i: (0, i, 0)),
            pl.BlockSpec((2, heads, toks // steps, width), lambda i: (0, 0, i, 0)),
            pl.BlockSpec((2, heads, toks // steps, width), lambda i: (0, 0, i, 0)),
        ],
        out_specs=[pl.BlockSpec((toks * heads // steps, width), lambda i: (i, 0))] * 4,
        out_shape=[struct(flat_shape, kind) for kind in (BF, F32, F32, F32)],
        scratch_shapes=[pltpu.VMEM((toks * heads // steps, width), F32)],
        compiler_params=params(),
        name="final",
    )(place, out, ends, sums, dq, dkv, extra)
    return tuple(x.reshape(toks, heads, width) for x in outs)


def solution(mesh):
    spec = P("ctx", "head", None)
    return jax.shard_map(
        shards,
        mesh=mesh,
        in_specs=(spec, spec, spec, spec, P()),
        out_specs=(spec, spec, spec, spec),
        check_vma=False,
    )
```

```python
import functools
import math

import jax
import jax.numpy as jnp
from jax import lax
from jax.experimental import pallas as pl
from jax.experimental.pallas import tpu as pltpu
from jax.sharding import PartitionSpec as P

HALF = 512
TILE = 256
NEG = -1e30
LOG2E = 1.0 / math.log(2.0)
VMEM_BYTES = 63 * 1024 * 1024
BF = jnp.bfloat16
F32 = jnp.float32


def nt(a, b):
    return lax.dot_general(a, b, (((1,), (1,)), ((), ())), preferred_element_type=F32)


def nn(a, b):
    return lax.dot_general(a, b, (((1,), (0,)), ((), ())), preferred_element_type=F32)


def wide(column, width):
    return jnp.concatenate([column] * (width // column.shape[1]), axis=1)


def iota(shape, dim):
    return lax.broadcasted_iota(jnp.int32, shape, dim)


def params():
    return pltpu.CompilerParams(vmem_limit_bytes=VMEM_BYTES)


def as_column(row):
    return jnp.broadcast_to(row, (128, row.shape[1])).T[:, :1]


def pack_keys_kernel(heads, k, v, kv, *refs):
    parts, wide_rows = refs[:-1], refs[-1]
    group = heads // len(parts)
    toks = k.shape[0] // heads
    for number, source in enumerate((k, v)):
        wide_rows[number] = source[...].astype(F32)
        for head in range(heads):
            rows = wide_rows[number, pl.ds(head, toks, stride=heads), :].astype(BF)
            kv[number, head] = rows
            parts[head // group][number, head % group] = rows


def pack_queries_kernel(heads, slots, q, g, kv, pos_row, qd, slot_rows, wide_rows, acc):
    step = pl.program_id(0)
    toks = q.shape[0] // heads
    row = pos_row[...]
    count = row.shape[1]
    base = lax.axis_index("ctx") * (toks * pl.num_programs(0))
    column = as_column(row)
    tok = iota((count, toks), 1) + (base + step * toks)
    hit = jnp.sum((column == tok).astype(F32), axis=0, keepdims=True)
    rank = jnp.sum(((column >= base) & (column < tok)).astype(F32), axis=0, keepdims=True)
    slot = iota((slots, toks), 0).astype(F32)
    pick = jnp.where((hit > 0) & (rank == slot), 1.0, 0.0).astype(BF)
    tok = iota((toks, count), 0) + (base + step * toks)
    hit_column = jnp.sum((row == tok).astype(F32), axis=1, keepdims=True)
    tables = [[], [kv[0, h] for h in range(heads)], [kv[1, h] for h in range(heads)], []]
    for number, source in ((0, q), (3, g)):
        wide_rows[number // 3] = source[...].astype(F32)
        for head in range(heads):
            rows = wide_rows[number // 3, pl.ds(head, toks, stride=heads), :]
            tables[number].append(rows.astype(BF))
            if number == 0:
                qd[0, head] = rows.astype(BF)
            else:
                qd[1, head] = jnp.where(hit_column > 0, 0.0, rows).astype(BF)
    for number in range(4):
        found = nn(pick, jnp.concatenate(tables[number], axis=1))
        for head in range(heads):
            part = found[:, head * 128 : (head + 1) * 128]
            acc[number, head] = jnp.where(step == 0, part, acc[number, head] + part)

    @pl.when(step == pl.num_programs(0) - 1)
    def _():
        slot_rows[...] = acc[...].astype(BF)


def owner_map(column, owner, toks, slots, shape):
    inside = jnp.sum((column < owner * toks).astype(jnp.int32), axis=0, keepdims=True)
    held = jnp.sum((column < (owner + 1) * toks).astype(jnp.int32), axis=0, keepdims=True) - inside
    slot = iota(shape, 1) % slots
    hot = (iota(shape, 0) == inside + slot) & (slot < held)
    return jnp.where(hot, 1.0, 0.0).astype(BF)


def mask_kernel(order, slots, seq_rows, pos_row, bias, compact, expand, place):
    toks = place.shape[0]
    me = lax.axis_index("ctx")
    base = me * toks
    row = pos_row[...]
    count = row.shape[1]
    column = as_column(row)
    for start in range(0, bias.shape[0], TILE):
        key = iota((TILE, count), 0) + (base - HALF + start)
        hits = jnp.sum((row == key).astype(F32), axis=1, keepdims=True)
        key = key[:, :1]
        out = (hits > 0) | (key < 0) | (key >= seq_rows)
        bias[start : start + TILE, :] = jnp.broadcast_to(jnp.where(out, NEG, 0.0), (TILE, 128))
    tok = iota((toks, count), 0) + base
    hit = jnp.sum((row == tok).astype(F32), axis=1, keepdims=True)
    rank = jnp.sum(((row >= base) & (row < tok)).astype(F32), axis=1, keepdims=True)
    slot = iota((toks, slots), 1).astype(F32)
    place[...] = jnp.where((hit > 0) & (rank == slot), 1.0, 0.0).astype(BF)
    part = iota((1, compact.shape[1]), 1) // slots
    owner = jnp.zeros_like(part)
    for number, relative in enumerate(order):
        owner = jnp.where(part == number, me ^ relative, owner)
    compact[...] = owner_map(column, owner, toks, slots, compact.shape)
    owner = iota((1, compact.shape[1]), 1) // slots
    hot = owner_map(column, owner, toks, slots, compact.shape)
    expand[...] = hot.astype(F32).T.astype(BF)


def stats_kernel(scale2, compact, *refs):
    parts, (kv, rows, stats) = refs[:-3], refs[-3:]
    pieces = []
    for part in parts:
        for i in range(part.shape[0]):
            pieces.append(jnp.concatenate([part[i, number, 0] for number in range(4)], axis=1))
    packed = nn(compact[...], jnp.concatenate(pieces, axis=0)).astype(BF)
    width = kv.shape[3]
    table = [packed[:, number * width : (number + 1) * width] for number in range(4)]
    for number in range(4):
        rows[number, 0] = table[number]
    queries, _, _, grads = table
    scores = nt(kv[0, 0], queries) * scale2
    top = jnp.max(scores, axis=0, keepdims=True)
    weights = jnp.exp2(scores - top)
    total = jnp.sum(weights, axis=0, keepdims=True)
    dot = jnp.sum(weights * nt(kv[1, 0], grads), axis=0, keepdims=True)
    line = iota(stats.shape[2:], 0)
    found = jnp.where(line == 0, top, jnp.where(line == 1, total, dot))
    for device in range(stats.shape[0]):
        stats[device, 0] = found


def band(scores, low):
    rows, columns = iota(scores.shape, 0), iota(scores.shape, 1)
    return jnp.where(rows <= columns if low else rows >= columns, scores, NEG)


def put_in_slots(expand, tables, sums):
    owners, kinds, _, slots, width = sums.shape
    spread = nn(expand, jnp.concatenate(tables, axis=1)).astype(BF)
    for owner in range(owners):
        for kind in range(kinds):
            sums[owner, kind, 0] = spread[
                owner * slots : (owner + 1) * slots, kind * width : (kind + 1) * width
            ]


def global_kernel(scale, scale2, kv, rows, stats, expand, before, dkv, ends):
    g_query, g_grad = rows[0, 0], rows[3, 0]
    tops = stats[:, 0, 0:1, :]
    top = jnp.max(tops, axis=0)
    factor = jnp.exp2(tops - top[None])
    total = jnp.sum(stats[:, 0, 1:2, :] * factor, axis=0)
    g_dot = jnp.sum(stats[:, 0, 2:3, :] * factor, axis=0) / total
    g_log = top + jnp.log2(total)
    weights = jnp.exp2(nt(kv[0, 0], g_query) * scale2 - g_log)
    narrow = weights.astype(BF)
    slopes = (weights * (nt(kv[1, 0], g_grad) - g_dot)).astype(BF)
    dkv[0, 0] = before[0, 0] + nn(slopes, g_query) * scale
    dkv[1, 0] = before[1, 0] + nn(narrow, g_grad)
    out = nn(kv[1, 0].T, narrow).T.astype(BF)
    dq = (nn(kv[0, 0].T, slopes) * scale).T.astype(BF)
    put_in_slots(expand[...], (out, dq), ends)


def local_kernel(scale, scale2, halves, group, qd, kv, *refs):
    nears, fars, refs = refs[:halves], refs[halves : 2 * halves], refs[2 * halves :]
    rows, bias, expand, out, log_dot, dq, dkv, sums, keys, values, score_buf, probs, slopes = refs
    toks = kv.shape[2]
    reach = 2 * HALF + TILE
    span = keys.shape[0] - rows.shape[2]
    near = 2 * (1 - lax.axis_index("ctx") % 2)
    for part in range(halves):

        @pl.when(pl.program_id(0) // group == part)
        def _():
            for block, place in ((nears[part], near), (kv, 1), (fars[part], 2 - near)):
                spot = pl.ds(pl.multiple_of(place * toks, toks), toks)
                keys[spot, :] = block[0, 0]
                values[spot, :] = block[1, 0]

    keys[span:, :] = rows[1, 0]
    values[span:, :] = rows[2, 0]
    key_t, value_t = keys[...].T, values[...].T
    query_t, grad_t = qd[0, 0].T, qd[1, 0].T
    tiles = range(toks // TILE)
    lanes = [slice(tile * TILE, (tile + 1) * TILE) for tile in tiles]
    windows = [slice(tile * TILE, tile * TILE + reach) for tile in tiles]
    starts = [
        list(range(tile * TILE, tile * TILE + reach, TILE)) + list(range(span, keys.shape[0], TILE))
        for tile in tiles
    ]
    best, top, total, scaled, dots = ([None] * len(tiles) for _ in range(5))

    def score(tile, piece):
        start = starts[tile][piece]
        scores = nn(keys[start : start + TILE, :], query_t[:, lanes[tile]]) * scale2
        if start < span:
            scores = scores + wide(bias[start : start + TILE, :], TILE)
        if piece == 0:
            scores = band(scores, False)
        elif piece == reach // TILE - 1:
            scores = band(scores, True)
        score_buf[tile, piece * TILE : (piece + 1) * TILE, :] = scores
        part = jnp.max(scores.reshape(TILE // 8, 8, TILE), axis=0)
        best[tile] = part if best[tile] is None else jnp.maximum(best[tile], part)

    def weigh(tile, piece):
        if top[tile] is None:
            top[tile] = jnp.max(best[tile], axis=0, keepdims=True)
        start = starts[tile][piece]
        weights = jnp.exp2(score_buf[tile, piece * TILE : (piece + 1) * TILE, :] - top[tile])
        probs[start : start + TILE, lanes[tile]] = weights.astype(BF)
        part = jnp.sum(weights.reshape(TILE // 8, 8, TILE), axis=0)
        total[tile] = part if total[tile] is None else total[tile] + part

    def attend(tile):
        whole_sum = jnp.sum(total[tile], axis=0, keepdims=True)
        inverse = 1.0 / whole_sum
        grads = grad_t[:, lanes[tile]].astype(F32)
        acc = nn(value_t[:, windows[tile]], probs[windows[tile], lanes[tile]])
        acc = (acc + nn(value_t[:, span:], probs[span:, lanes[tile]])) * inverse
        dot = jnp.sum(grads * acc, axis=0, keepdims=True)
        log_dot[0, 0:1, lanes[tile]] = top[tile] + jnp.log2(whole_sum)
        log_dot[0, 1:2, lanes[tile]] = dot
        out[0, lanes[tile], :] = acc.T.astype(BF)
        scaled[tile] = (grads * inverse).astype(BF)
        dots[tile] = dot * inverse

    def slope(tile, piece):
        start = starts[tile][piece]
        rise = nn(values[start : start + TILE, :], scaled[tile]) - dots[tile]
        weights = probs[start : start + TILE, lanes[tile]].astype(F32)
        slopes[start : start + TILE, lanes[tile]] = (weights * rise).astype(BF)

    def query_gradient(tile):
        acc = nn(key_t[:, windows[tile]], slopes[windows[tile], lanes[tile]])
        acc = acc + nn(key_t[:, span:], slopes[span:, lanes[tile]])
        dq[0, lanes[tile], :] = (acc * scale).T

    for step in range(len(tiles) + 2):
        for piece in range(len(starts[0])):
            if 0 <= step - 2:
                slope(step - 2, piece)
            if 0 <= step - 1 < len(tiles):
                weigh(step - 1, piece)
            if step < len(tiles):
                score(step, piece)
        if 0 <= step - 2:
            query_gradient(step - 2)
        if 0 <= step - 1 < len(tiles):
            attend(step - 1)
    own = slice(HALF, HALF + toks)
    grads = jnp.concatenate(scaled, axis=1)
    dkv[0, 0] = (nt(query_t, slopes[own, :]) * scale).T
    dkv[1, 0] = nt(grads, probs[own, :]).T
    g_dk = (nt(query_t, slopes[span:, :]) * scale).T.astype(BF)
    g_dv = nt(grads, probs[span:, :]).T.astype(BF)
    put_in_slots(expand[...], (g_dk, g_dv), sums)


def rim_kernel(
    scale, scale2, kv, bias, qd_near, qd_far, log_near, log_far, partial, dkv,
    queries, grads, logs, probs, slopes,
):
    toks = kv.shape[2]
    reach = toks + TILE
    near = 1 - lax.axis_index("ctx") % 2
    for qd, log_dot, place in ((qd_near, log_near, near), (qd_far, log_far, 1 - near)):
        spot = pl.ds(pl.multiple_of(place * toks, toks), toks)
        queries[spot, :] = qd[0, 0]
        grads[spot, :] = qd[1, 0]
        logs[place] = log_dot[0]
    for k_tile in range(toks // TILE):
        span = slice(k_tile * TILE, (k_tile + 1) * TILE)
        key = kv[0, 0, span, :]
        value = kv[1, 0, span, :]
        key_bias = wide(bias[HALF + k_tile * TILE : HALF + (k_tile + 1) * TILE, :], TILE)
        for piece in range(reach // TILE):
            start = (k_tile + piece) * TILE
            side, lanes = start // toks, slice(start % toks, start % toks + TILE)
            scores = nt(key, queries[start : start + TILE, :]) * scale2 + key_bias
            if piece == 0:
                scores = band(scores, True)
            elif piece == reach // TILE - 1:
                scores = band(scores, False)
            weights = jnp.exp2(scores - logs[side, 0:1, lanes])
            slope = weights * (nt(value, grads[start : start + TILE, :]) - logs[side, 1:2, lanes])
            spot = slice(piece * TILE, (piece + 1) * TILE)
            probs[span, spot] = weights.astype(BF)
            slopes[span, spot] = slope.astype(BF)
        window = slice(k_tile * TILE, k_tile * TILE + reach)
        dkv[0, 0, span, :] = partial[0, 0, span, :] + nn(slopes[span, :], queries[window, :]) * scale
        dkv[1, 0, span, :] = partial[1, 0, span, :] + nn(probs[span, :], grads[window, :])


def final_kernel(
    place, out, ends, sums, dq, dkv, attn, query_grad, key_grad, value_grad, wide_rows
):
    heads, toks = out.shape[0], out.shape[1]
    hot = place[...]
    is_global = jnp.sum(hot.astype(F32), axis=1, keepdims=True) > 0
    for head in range(heads):
        rows = pl.ds(head, toks, stride=heads)
        tables = []
        for source, kind in ((ends, 0), (ends, 1), (sums, 0), (sums, 1)):
            table = source[0, kind, head].astype(F32)
            for device in range(1, source.shape[0]):
                table = table + source[device, kind, head].astype(F32)
            tables.append(table.astype(BF))
        width = out.shape[2]
        added = nn(hot, jnp.concatenate(tables, axis=1))
        added = [added[:, i * width : (i + 1) * width] for i in range(4)]
        wide_rows[rows, :] = jnp.where(is_global, added[0], out[head].astype(F32))
        query_grad[rows, :] = dq[head] + added[1]
        key_grad[rows, :] = dkv[0, head] + added[2]
        value_grad[rows, :] = dkv[1, head] + added[3]
    attn[...] = wide_rows[...].astype(BF)


def cost(flops, moved, exps=0):
    return pl.CostEstimate(flops=int(flops), bytes_accessed=int(moved), transcendentals=int(exps))


def struct(shape, dtype):
    return jax.ShapeDtypeStruct(shape, dtype)


def whole(shape):
    return pl.BlockSpec(shape, lambda head: (0,) * len(shape))


def per_head(shape, dim, first=0):
    block = tuple(1 if i == dim else size for i, size in enumerate(shape))
    return pl.BlockSpec(
        block, lambda head: tuple(head + first if i == dim else 0 for i in range(len(shape)))
    )


def shards(query_rows, key_rows, value_rows, out_grad, global_pos):
    toks, heads, width = query_rows.shape
    count = global_pos.shape[0]
    devices = lax.axis_size("ctx")
    slots = max(16, 2 * count // devices)
    scale = width ** (-0.5)
    scale2 = scale * LOG2E
    bits = devices.bit_length() - 1
    stages = [
        [mask << low for mask in range(1, 1 << min(2, bits - low))] for low in range(1, bits, 2)
    ] + [[1]]
    order = [0]
    for stage in stages:
        order = order + [one ^ mask for mask in stage for one in order]
    pos_row = global_pos.reshape(1, count)
    q_flat, k_flat, v_flat, g_flat = (
        x.reshape(toks * heads, width) for x in (query_rows, key_rows, value_rows, out_grad)
    )

    def swap(value, mask):
        return lax.ppermute(value, "ctx", [(i, i ^ mask) for i in range(devices)])

    def from_near(value):
        return swap(value, 1)

    def from_far(value):
        pairs = [(i, i + 1) for i in range(1, devices - 1, 2)]
        return lax.ppermute(value, "ctx", pairs + [(j, i) for i, j in pairs])

    def after(value, earlier):
        return lax.optimization_barrier((value, earlier))[0]

    pair_shape = (2, heads, toks, width)
    slot_shape = (4, heads, slots, width)
    steps = 1
    flat_spec = pl.BlockSpec((toks * heads // steps, width), lambda i: (i, 0))
    pair_spec = pl.BlockSpec((2, heads, toks // steps, width), lambda i: (0, 0, i, 0))
    wide_pair = pltpu.VMEM((2, toks * heads // steps, width), F32)
    halves = 2 if heads % 2 == 0 else 1
    group = heads // halves
    part_shape = (2, group, toks, width)
    kv, *kv_parts = pl.pallas_call(
        functools.partial(pack_keys_kernel, heads),
        out_shape=[struct(pair_shape, BF)] + [struct(part_shape, BF)] * halves,
        scratch_shapes=[wide_pair],
        compiler_params=params(),
        name="pack_keys",
    )(k_flat, v_flat)

    qd, slot_rows = pl.pallas_call(
        functools.partial(pack_queries_kernel, heads, slots),
        grid=(steps,),
        in_specs=[flat_spec, flat_spec, pair_spec, whole((1, count))],
        out_specs=(pair_spec, whole(slot_shape)),
        out_shape=(struct(pair_shape, BF), struct(slot_shape, BF)),
        scratch_shapes=[wide_pair, pltpu.VMEM(slot_shape, F32)],
        compiler_params=params(),
        name="pack_queries",
    )(q_flat, g_flat, kv, pos_row)

    span = toks + 2 * HALF
    bias, compact, expand, place = pl.pallas_call(
        functools.partial(mask_kernel, order, slots, toks * devices),
        out_shape=(
            struct((span, 128), F32),
            struct((count, devices * slots), BF),
            struct((devices * slots, count), BF),
            struct((toks, slots), BF),
        ),
        compiler_params=params(),
        name="masks",
    )(pos_row)

    nears, fars = [], []
    for part in kv_parts:
        if fars:
            part = after(part, (nears[-1], fars[-1]))
        fars.append(from_far(part))
        nears.append(from_near(part))
    held = [slot_rows[None]]
    for stage in stages:
        send = jnp.concatenate(held, axis=0) if len(held) > 1 else held[0]
        if stage == [1]:
            send = after(send, (nears[0], fars[0], place))
        held += [swap(send, mask) for mask in stage]

    row_shape = (4, heads, count, width)
    rows, stats = pl.pallas_call(
        functools.partial(stats_kernel, scale2),
        grid=(heads,),
        in_specs=[whole(compact.shape)]
        + [per_head(part.shape, 2) for part in held]
        + [per_head(pair_shape, 1)],
        out_specs=(per_head(row_shape, 1), per_head((devices, heads, 8, count), 1)),
        out_shape=(struct(row_shape, BF), struct((devices, heads, 8, count), F32)),
        compiler_params=params(),
        cost_estimate=cost(1e6, 1e6),
        name="global_stats",
    )(compact, *held, kv)

    kv_done = (nears, fars)
    stats = after(stats, kv_done)
    stats = lax.all_to_all(stats, "ctx", 0, 0, tiled=True)
    qd_late = after(qd, (kv_done, rows))
    qd_far, qd_near = from_far(qd_late), from_near(qd_late)

    def half_head(part):
        return pl.BlockSpec(
            (2, 1, toks, width), lambda head: (0, jnp.clip(head - part * group, 0, group - 1), 0, 0)
        )

    ends_shape = (devices, 2, heads, slots, width)
    out, log_dot, dq, dkv, sums = pl.pallas_call(
        functools.partial(local_kernel, scale, scale2, halves, group),
        grid=(heads,),
        in_specs=[per_head(pair_shape, 1)] * 2
        + [half_head(part) for part in range(halves)] * 2
        + [per_head(row_shape, 1), whole(bias.shape), whole(expand.shape)],
        out_specs=(
            per_head((heads, toks, width), 0),
            per_head((heads, 2, toks), 0),
            per_head((heads, toks, width), 0),
            per_head(pair_shape, 1),
            per_head(ends_shape, 2),
        ),
        out_shape=(
            struct((heads, toks, width), BF),
            struct((heads, 2, toks), F32),
            struct((heads, toks, width), F32),
            struct(pair_shape, F32),
            struct(ends_shape, BF),
        ),
        scratch_shapes=[
            pltpu.VMEM((span + count, width), BF),
            pltpu.VMEM((span + count, width), BF),
            pltpu.VMEM((toks // TILE, 2 * HALF + TILE + count, TILE), F32),
            pltpu.VMEM((span + count, toks), BF),
            pltpu.VMEM((span + count, toks), BF),
        ],
        compiler_params=params(),
        cost_estimate=cost(1e6, 1e6),
        name="local",
    )(qd, kv, *nears, *fars, rows, bias, expand)
    log_far, log_near = from_far(log_dot), from_near(log_dot)

    dkv, ends = pl.pallas_call(
        functools.partial(global_kernel, scale, scale2),
        grid=(heads,),
        in_specs=[per_head(pair_shape, 1), per_head(row_shape, 1)]
        + [per_head(stats.shape, 1), whole(expand.shape), per_head(pair_shape, 1)],
        out_specs=(per_head(pair_shape, 1), per_head(ends_shape, 2)),
        out_shape=(struct(pair_shape, F32), struct(ends_shape, BF)),
        input_output_aliases={4: 0},
        compiler_params=params(),
        cost_estimate=cost(1e6, 1e6),
        name="global_queries",
    )(kv, rows, after(stats, (qd_near, qd_far)), expand, dkv)
    ends = lax.all_to_all(ends, "ctx", 0, 0, tiled=True)
    sums = lax.all_to_all(sums, "ctx", 0, 0, tiled=True)

    dkv = pl.pallas_call(
        functools.partial(rim_kernel, scale, scale2),
        grid=(heads,),
        in_specs=[per_head(pair_shape, 1), whole(bias.shape)]
        + [per_head(pair_shape, 1)] * 2
        + [per_head(log_dot.shape, 0)] * 2
        + [per_head(pair_shape, 1)],
        out_specs=per_head(pair_shape, 1),
        out_shape=struct(pair_shape, F32),
        scratch_shapes=[
            pltpu.VMEM((2 * toks, width), BF),
            pltpu.VMEM((2 * toks, width), BF),
            pltpu.VMEM((2, 2, toks), F32),
            pltpu.VMEM((toks, toks + TILE), BF),
            pltpu.VMEM((toks, toks + TILE), BF),
        ],
        compiler_params=params(),
        cost_estimate=cost(1e6, 1e6),
        name="rim",
    )(kv, bias, qd_near, qd_far, log_near, log_far, dkv)

    flat_shape = (toks * heads, width)
    steps = 2
    outs = pl.pallas_call(
        final_kernel,
        grid=(steps,),
        in_specs=[
            pl.BlockSpec((toks // steps, slots), lambda i: (i, 0)),
            pl.BlockSpec((heads, toks // steps, width), lambda i: (0, i, 0)),
            whole(ends_shape),
            whole(ends_shape),
            pl.BlockSpec((heads, toks // steps, width), lambda i: (0, i, 0)),
            pl.BlockSpec((2, heads, toks // steps, width), lambda i: (0, 0, i, 0)),
        ],
        out_specs=[pl.BlockSpec((toks * heads // steps, width), lambda i: (i, 0))] * 4,
        out_shape=[struct(flat_shape, kind) for kind in (BF, F32, F32, F32)],
        scratch_shapes=[pltpu.VMEM((toks * heads // steps, width), F32)],
        compiler_params=params(),
        name="final",
    )(place, out, ends, sums, dq, dkv)
    return tuple(x.reshape(toks, heads, width) for x in outs)


def solution(mesh):
    spec = P("ctx", "head", None)
    return jax.shard_map(
        shards,
        mesh=mesh,
        in_specs=(spec, spec, spec, spec, P()),
        out_specs=(spec, spec, spec, spec),
        check_vma=False,
    )
```

```python
import functools
import math

import jax
import jax.numpy as jnp
from jax import lax
from jax.experimental import pallas as pl
from jax.experimental.pallas import tpu as pltpu
from jax.sharding import PartitionSpec as P

HALF = 512
TILE = 256
NEG = -1e30
LOG2E = 1.0 / math.log(2.0)
VMEM_BYTES = 63 * 1024 * 1024
BF = jnp.bfloat16
F32 = jnp.float32


def nt(a, b):
    return lax.dot_general(a, b, (((1,), (1,)), ((), ())), preferred_element_type=F32)


def nn(a, b):
    return lax.dot_general(a, b, (((1,), (0,)), ((), ())), preferred_element_type=F32)


def wide(column, width):
    return jnp.concatenate([column] * (width // column.shape[1]), axis=1)


def iota(shape, dim):
    return lax.broadcasted_iota(jnp.int32, shape, dim)


def params():
    return pltpu.CompilerParams(vmem_limit_bytes=VMEM_BYTES)


def as_column(row):
    return jnp.broadcast_to(row, (128, row.shape[1])).T[:, :1]


def pack_keys_kernel(heads, k, v, kv, *refs):
    parts, wide_rows = refs[:-1], refs[-1]
    group = heads // len(parts)
    toks = k.shape[0] // heads
    for number, source in enumerate((k, v)):
        wide_rows[number] = source[...].astype(F32)
        for head in range(heads):
            rows = wide_rows[number, pl.ds(head, toks, stride=heads), :].astype(BF)
            kv[number, head] = rows
            parts[head // group][number, head % group] = rows


def pack_queries_kernel(heads, slots, q, g, kv, pos_row, qd, slot_rows, wide_rows, acc):
    step = pl.program_id(0)
    toks = q.shape[0] // heads
    row = pos_row[...]
    count = row.shape[1]
    base = lax.axis_index("ctx") * (toks * pl.num_programs(0))
    column = as_column(row)
    tok = iota((count, toks), 1) + (base + step * toks)
    hit = jnp.sum((column == tok).astype(F32), axis=0, keepdims=True)
    rank = jnp.sum(((column >= base) & (column < tok)).astype(F32), axis=0, keepdims=True)
    slot = iota((slots, toks), 0).astype(F32)
    pick = jnp.where((hit > 0) & (rank == slot), 1.0, 0.0).astype(BF)
    tok = iota((toks, count), 0) + (base + step * toks)
    hit_column = jnp.sum((row == tok).astype(F32), axis=1, keepdims=True)
    tables = [[], [kv[0, h] for h in range(heads)], [kv[1, h] for h in range(heads)], []]
    for number, source in ((0, q), (3, g)):
        wide_rows[number // 3] = source[...].astype(F32)
        for head in range(heads):
            rows = wide_rows[number // 3, pl.ds(head, toks, stride=heads), :]
            tables[number].append(rows.astype(BF))
            if number == 0:
                qd[0, head] = rows.astype(BF)
            else:
                qd[1, head] = jnp.where(hit_column > 0, 0.0, rows).astype(BF)
    for number in range(4):
        found = nn(pick, jnp.concatenate(tables[number], axis=1))
        for head in range(heads):
            part = found[:, head * 128 : (head + 1) * 128]
            acc[number, head] = jnp.where(step == 0, part, acc[number, head] + part)

    @pl.when(step == pl.num_programs(0) - 1)
    def _():
        slot_rows[...] = acc[...].astype(BF)


def owner_map(column, owner, toks, slots, shape):
    inside = jnp.sum((column < owner * toks).astype(jnp.int32), axis=0, keepdims=True)
    held = jnp.sum((column < (owner + 1) * toks).astype(jnp.int32), axis=0, keepdims=True) - inside
    slot = iota(shape, 1) % slots
    hot = (iota(shape, 0) == inside + slot) & (slot < held)
    return jnp.where(hot, 1.0, 0.0).astype(BF)


def mask_kernel(order, slots, seq_rows, pos_row, bias, compact, expand, place):
    toks = place.shape[0]
    me = lax.axis_index("ctx")
    base = me * toks
    row = pos_row[...]
    count = row.shape[1]
    column = as_column(row)
    for start in range(0, bias.shape[0], TILE):
        key = iota((TILE, count), 0) + (base - HALF + start)
        hits = jnp.sum((row == key).astype(F32), axis=1, keepdims=True)
        key = key[:, :1]
        out = (hits > 0) | (key < 0) | (key >= seq_rows)
        bias[start : start + TILE, :] = jnp.broadcast_to(jnp.where(out, NEG, 0.0), (TILE, 128))
    tok = iota((toks, count), 0) + base
    hit = jnp.sum((row == tok).astype(F32), axis=1, keepdims=True)
    rank = jnp.sum(((row >= base) & (row < tok)).astype(F32), axis=1, keepdims=True)
    slot = iota((toks, slots), 1).astype(F32)
    place[...] = jnp.where((hit > 0) & (rank == slot), 1.0, 0.0).astype(BF)
    part = iota((1, compact.shape[1]), 1) // slots
    owner = jnp.zeros_like(part)
    for number, relative in enumerate(order):
        owner = jnp.where(part == number, me ^ relative, owner)
    compact[...] = owner_map(column, owner, toks, slots, compact.shape)
    expand[...] = compact[...].astype(F32).T.astype(BF)


def stats_kernel(scale2, compact, *refs):
    parts, (kv, rows, stats) = refs[:-3], refs[-3:]
    pieces = []
    for part in parts:
        for i in range(part.shape[0]):
            pieces.append(jnp.concatenate([part[i, number, 0] for number in range(4)], axis=1))
    packed = nn(compact[...], jnp.concatenate(pieces, axis=0)).astype(BF)
    width = kv.shape[3]
    table = [packed[:, number * width : (number + 1) * width] for number in range(4)]
    for number in range(4):
        rows[number, 0] = table[number]
    queries, _, _, grads = table
    scores = nt(kv[0, 0], queries) * scale2
    top = jnp.max(scores, axis=0, keepdims=True)
    weights = jnp.exp2(scores - top)
    total = jnp.sum(weights, axis=0, keepdims=True)
    dot = jnp.sum(weights * nt(kv[1, 0], grads), axis=0, keepdims=True)
    line = iota(stats.shape[2:], 0)
    found = jnp.where(line == 0, top, jnp.where(line == 1, total, dot))
    for device in range(stats.shape[0]):
        stats[device, 0] = found


def band(scores, low):
    rows, columns = iota(scores.shape, 0), iota(scores.shape, 1)
    return jnp.where(rows <= columns if low else rows >= columns, scores, NEG)


def put_in_slots(expand, tables, kept, sent):
    owners, kinds, _, slots, width = kept.shape
    spread = nn(expand, jnp.concatenate(tables, axis=1)).astype(BF)
    for owner in range(2 * owners):
        for kind in range(kinds):
            (kept if owner < owners else sent)[owner % owners, kind, 0] = spread[
                owner * slots : (owner + 1) * slots, kind * width : (kind + 1) * width
            ]


def fold_kernel(kept_ends, got_ends, kept_sums, got_sums, *outs):
    for part, out in enumerate(outs):
        out[0:2] = (kept_ends[part].astype(F32) + got_ends[part].astype(F32)).astype(BF)
        out[2:4] = (kept_sums[part].astype(F32) + got_sums[part].astype(F32)).astype(BF)


def global_kernel(scale, scale2, kv, rows, stats, expand, dkv, kept, sent):
    g_query, g_grad = rows[0, 0], rows[3, 0]
    tops = stats[:, 0, 0:1, :]
    top = jnp.max(tops, axis=0)
    factor = jnp.exp2(tops - top[None])
    total = jnp.sum(stats[:, 0, 1:2, :] * factor, axis=0)
    g_dot = jnp.sum(stats[:, 0, 2:3, :] * factor, axis=0) / total
    g_log = top + jnp.log2(total)
    weights = jnp.exp2(nt(kv[0, 0], g_query) * scale2 - g_log)
    narrow = weights.astype(BF)
    slopes = (weights * (nt(kv[1, 0], g_grad) - g_dot)).astype(BF)
    dkv[0, 0] = nn(slopes, g_query) * scale
    dkv[1, 0] = nn(narrow, g_grad)
    out = nn(kv[1, 0].T, narrow).T.astype(BF)
    dq = (nn(kv[0, 0].T, slopes) * scale).T.astype(BF)
    put_in_slots(expand[...], (out, dq), kept, sent)


def local_kernel(scale, scale2, halves, group, qd, kv, *refs):
    nears, fars, refs = refs[:halves], refs[halves : 2 * halves], refs[2 * halves :]
    rows, bias, expand, before, out, log_dot, dq, dkv, kept, sent = refs[:-5]
    keys, values, score_buf, probs, slopes = refs[-5:]
    toks = kv.shape[2]
    reach = 2 * HALF + TILE
    span = keys.shape[0] - rows.shape[2]
    near = 2 * (1 - lax.axis_index("ctx") % 2)
    for part in range(halves):

        @pl.when(pl.program_id(0) // group == part)
        def _():
            for block, place in ((nears[part], near), (kv, 1), (fars[part], 2 - near)):
                spot = pl.ds(pl.multiple_of(place * toks, toks), toks)
                keys[spot, :] = block[0, 0]
                values[spot, :] = block[1, 0]

    keys[span:, :] = rows[1, 0]
    values[span:, :] = rows[2, 0]
    key_t, value_t = keys[...].T, values[...].T
    query_t, grad_t = qd[0, 0].T, qd[1, 0].T
    tiles = range(toks // TILE)
    lanes = [slice(tile * TILE, (tile + 1) * TILE) for tile in tiles]
    windows = [slice(tile * TILE, tile * TILE + reach) for tile in tiles]
    starts = [
        list(range(tile * TILE, tile * TILE + reach, TILE)) + list(range(span, keys.shape[0], TILE))
        for tile in tiles
    ]
    best, top, total, scaled, dots = ([None] * len(tiles) for _ in range(5))

    def score(tile, piece):
        start = starts[tile][piece]
        scores = nn(keys[start : start + TILE, :], query_t[:, lanes[tile]]) * scale2
        if start < span:
            scores = scores + wide(bias[start : start + TILE, :], TILE)
        if piece == 0:
            scores = band(scores, False)
        elif piece == reach // TILE - 1:
            scores = band(scores, True)
        score_buf[tile, piece * TILE : (piece + 1) * TILE, :] = scores
        part = jnp.max(scores.reshape(TILE // 8, 8, TILE), axis=0)
        best[tile] = part if best[tile] is None else jnp.maximum(best[tile], part)

    def weigh(tile, piece):
        if top[tile] is None:
            top[tile] = jnp.max(best[tile], axis=0, keepdims=True)
        start = starts[tile][piece]
        weights = jnp.exp2(score_buf[tile, piece * TILE : (piece + 1) * TILE, :] - top[tile])
        probs[start : start + TILE, lanes[tile]] = weights.astype(BF)
        part = jnp.sum(weights.reshape(TILE // 8, 8, TILE), axis=0)
        total[tile] = part if total[tile] is None else total[tile] + part

    def attend(tile):
        whole_sum = jnp.sum(total[tile], axis=0, keepdims=True)
        inverse = 1.0 / whole_sum
        grads = grad_t[:, lanes[tile]].astype(F32)
        acc = nn(value_t[:, windows[tile]], probs[windows[tile], lanes[tile]])
        acc = (acc + nn(value_t[:, span:], probs[span:, lanes[tile]])) * inverse
        dot = jnp.sum(grads * acc, axis=0, keepdims=True)
        log_dot[0, 0:1, lanes[tile]] = top[tile] + jnp.log2(whole_sum)
        log_dot[0, 1:2, lanes[tile]] = dot
        out[0, lanes[tile], :] = acc.T.astype(BF)
        scaled[tile] = (grads * inverse).astype(BF)
        dots[tile] = dot * inverse

    def slope(tile, piece):
        start = starts[tile][piece]
        rise = nn(values[start : start + TILE, :], scaled[tile]) - dots[tile]
        weights = probs[start : start + TILE, lanes[tile]].astype(F32)
        slopes[start : start + TILE, lanes[tile]] = (weights * rise).astype(BF)

    def query_gradient(tile):
        acc = nn(key_t[:, windows[tile]], slopes[windows[tile], lanes[tile]])
        acc = acc + nn(key_t[:, span:], slopes[span:, lanes[tile]])
        dq[0, lanes[tile], :] = (acc * scale).T

    for step in range(len(tiles) + 2):
        for piece in range(len(starts[0])):
            if 0 <= step - 2:
                slope(step - 2, piece)
            if 0 <= step - 1 < len(tiles):
                weigh(step - 1, piece)
            if step < len(tiles):
                score(step, piece)
        if 0 <= step - 2:
            query_gradient(step - 2)
        if 0 <= step - 1 < len(tiles):
            attend(step - 1)
    own = slice(HALF, HALF + toks)
    grads = jnp.concatenate(scaled, axis=1)
    dkv[0, 0] = before[0, 0] + (nt(query_t, slopes[own, :]) * scale).T
    dkv[1, 0] = before[1, 0] + nt(grads, probs[own, :]).T
    g_dk = (nt(query_t, slopes[span:, :]) * scale).T.astype(BF)
    g_dv = nt(grads, probs[span:, :]).T.astype(BF)
    put_in_slots(expand[...], (g_dk, g_dv), kept, sent)


def rim_kernel(
    scale, scale2, kv, bias, qd_near, qd_far, log_near, log_far, partial, dkv,
    queries, grads, logs, probs, slopes,
):
    toks = kv.shape[2]
    reach = toks + TILE
    near = 1 - lax.axis_index("ctx") % 2
    for qd, log_dot, place in ((qd_near, log_near, near), (qd_far, log_far, 1 - near)):
        spot = pl.ds(pl.multiple_of(place * toks, toks), toks)
        queries[spot, :] = qd[0, 0]
        grads[spot, :] = qd[1, 0]
        logs[place] = log_dot[0]
    for k_tile in range(toks // TILE):
        span = slice(k_tile * TILE, (k_tile + 1) * TILE)
        key = kv[0, 0, span, :]
        value = kv[1, 0, span, :]
        key_bias = wide(bias[HALF + k_tile * TILE : HALF + (k_tile + 1) * TILE, :], TILE)
        for piece in range(reach // TILE):
            start = (k_tile + piece) * TILE
            side, lanes = start // toks, slice(start % toks, start % toks + TILE)
            scores = nt(key, queries[start : start + TILE, :]) * scale2 + key_bias
            if piece == 0:
                scores = band(scores, True)
            elif piece == reach // TILE - 1:
                scores = band(scores, False)
            weights = jnp.exp2(scores - logs[side, 0:1, lanes])
            slope = weights * (nt(value, grads[start : start + TILE, :]) - logs[side, 1:2, lanes])
            spot = slice(piece * TILE, (piece + 1) * TILE)
            probs[span, spot] = weights.astype(BF)
            slopes[span, spot] = slope.astype(BF)
        window = slice(k_tile * TILE, k_tile * TILE + reach)
        dkv[0, 0, span, :] = partial[0, 0, span, :] + nn(slopes[span, :], queries[window, :]) * scale
        dkv[1, 0, span, :] = partial[1, 0, span, :] + nn(probs[span, :], grads[window, :])


def final_kernel(
    sources, place, out, dq, dkv, *refs
):
    parts, refs = refs[:sources], refs[sources:]
    attn, query_grad, key_grad, value_grad, wide_rows = refs
    heads, toks = out.shape[0], out.shape[1]
    hot = place[...]
    is_global = jnp.sum(hot.astype(F32), axis=1, keepdims=True) > 0
    for head in range(heads):
        rows = pl.ds(head, toks, stride=heads)
        tables = []
        for kind in range(4):
            table = parts[0][kind, head].astype(F32)
            for part in parts[1:]:
                table = table + part[kind, head].astype(F32)
            tables.append(table.astype(BF))
        width = out.shape[2]
        added = nn(hot, jnp.concatenate(tables, axis=1))
        added = [added[:, i * width : (i + 1) * width] for i in range(4)]
        wide_rows[rows, :] = jnp.where(is_global, added[0], out[head].astype(F32))
        query_grad[rows, :] = dq[head] + added[1]
        key_grad[rows, :] = dkv[0, head] + added[2]
        value_grad[rows, :] = dkv[1, head] + added[3]
    attn[...] = wide_rows[...].astype(BF)


def cost(flops, moved, exps=0):
    return pl.CostEstimate(flops=int(flops), bytes_accessed=int(moved), transcendentals=int(exps))


def struct(shape, dtype):
    return jax.ShapeDtypeStruct(shape, dtype)


def whole(shape):
    return pl.BlockSpec(shape, lambda head: (0,) * len(shape))


def per_head(shape, dim, first=0):
    block = tuple(1 if i == dim else size for i, size in enumerate(shape))
    return pl.BlockSpec(
        block, lambda head: tuple(head + first if i == dim else 0 for i in range(len(shape)))
    )


def shards(query_rows, key_rows, value_rows, out_grad, global_pos):
    toks, heads, width = query_rows.shape
    count = global_pos.shape[0]
    devices = lax.axis_size("ctx")
    slots = max(16, 2 * count // devices)
    scale = width ** (-0.5)
    scale2 = scale * LOG2E
    bits = devices.bit_length() - 1
    stages = [
        [mask << low for mask in range(1, 1 << min(2, bits - low))] for low in range(1, bits, 2)
    ] + [[1]]
    order = [0]
    for stage in stages:
        order = order + [one ^ mask for mask in stage for one in order]
    pos_row = global_pos.reshape(1, count)
    q_flat, k_flat, v_flat, g_flat = (
        x.reshape(toks * heads, width) for x in (query_rows, key_rows, value_rows, out_grad)
    )

    def swap(value, mask):
        return lax.ppermute(value, "ctx", [(i, i ^ mask) for i in range(devices)])

    def from_near(value):
        return swap(value, 1)

    def from_far(value):
        pairs = [(i, i + 1) for i in range(1, devices - 1, 2)]
        return lax.ppermute(value, "ctx", pairs + [(j, i) for i, j in pairs])

    def after(value, earlier):
        return lax.optimization_barrier((value, earlier))[0]

    pair_shape = (2, heads, toks, width)
    slot_shape = (4, heads, slots, width)
    steps = 1
    flat_spec = pl.BlockSpec((toks * heads // steps, width), lambda i: (i, 0))
    pair_spec = pl.BlockSpec((2, heads, toks // steps, width), lambda i: (0, 0, i, 0))
    wide_pair = pltpu.VMEM((2, toks * heads // steps, width), F32)
    halves = 2 if heads % 2 == 0 else 1
    group = heads // halves
    part_shape = (2, group, toks, width)
    kv, *kv_parts = pl.pallas_call(
        functools.partial(pack_keys_kernel, heads),
        out_shape=[struct(pair_shape, BF)] + [struct(part_shape, BF)] * halves,
        scratch_shapes=[wide_pair],
        compiler_params=params(),
        name="pack_keys",
    )(k_flat, v_flat)

    qd, slot_rows = pl.pallas_call(
        functools.partial(pack_queries_kernel, heads, slots),
        grid=(steps,),
        in_specs=[flat_spec, flat_spec, pair_spec, whole((1, count))],
        out_specs=(pair_spec, whole(slot_shape)),
        out_shape=(struct(pair_shape, BF), struct(slot_shape, BF)),
        scratch_shapes=[wide_pair, pltpu.VMEM(slot_shape, F32)],
        compiler_params=params(),
        name="pack_queries",
    )(q_flat, g_flat, kv, pos_row)

    span = toks + 2 * HALF
    bias, compact, expand, place = pl.pallas_call(
        functools.partial(mask_kernel, order, slots, toks * devices),
        out_shape=(
            struct((span, 128), F32),
            struct((count, devices * slots), BF),
            struct((devices * slots, count), BF),
            struct((toks, slots), BF),
        ),
        compiler_params=params(),
        name="masks",
    )(pos_row)

    nears, fars = [], []
    for part in kv_parts:
        if fars:
            part = after(part, (nears[-1], fars[-1]))
        fars.append(from_far(part))
        nears.append(from_near(part))
    held = [slot_rows[None]]
    for stage in stages:
        send = jnp.concatenate(held, axis=0) if len(held) > 1 else held[0]
        if stage == [1]:
            send = after(send, (nears[0], fars[0], place))
        held += [swap(send, mask) for mask in stage]

    row_shape = (4, heads, count, width)
    rows, stats = pl.pallas_call(
        functools.partial(stats_kernel, scale2),
        grid=(heads,),
        in_specs=[whole(compact.shape)]
        + [per_head(part.shape, 2) for part in held]
        + [per_head(pair_shape, 1)],
        out_specs=(per_head(row_shape, 1), per_head((devices, heads, 8, count), 1)),
        out_shape=(struct(row_shape, BF), struct((devices, heads, 8, count), F32)),
        compiler_params=params(),
        cost_estimate=cost(1e6, 1e6),
        name="global_stats",
    )(compact, *held, kv)

    kv_done = (nears, fars)
    stats = lax.all_to_all(stats, "ctx", 0, 0, tiled=True)
    qd_late = after(qd, (kv_done, stats))
    qd_far, qd_near = from_far(qd_late), from_near(qd_late)

    sum_shape = (devices // 2, 2, heads, slots, width)
    sum_struct = struct(sum_shape, BF)
    extra, kept_ends, sent_ends = pl.pallas_call(
        functools.partial(global_kernel, scale, scale2),
        grid=(heads,),
        in_specs=[per_head(pair_shape, 1), per_head(row_shape, 1)]
        + [per_head(stats.shape, 1), whole(expand.shape)],
        out_specs=(per_head(pair_shape, 1), per_head(sum_shape, 2), per_head(sum_shape, 2)),
        out_shape=(struct(pair_shape, F32), sum_struct, sum_struct),
        compiler_params=params(),
        cost_estimate=cost(1e6, 1e6),
        name="global_queries",
    )(kv, rows, stats, expand)
    got_ends = from_near(sent_ends)

    def half_head(part):
        return pl.BlockSpec(
            (2, 1, toks, width), lambda head: (0, jnp.clip(head - part * group, 0, group - 1), 0, 0)
        )

    out, log_dot, dq, dkv, kept_sums, sent_sums = pl.pallas_call(
        functools.partial(local_kernel, scale, scale2, halves, group),
        grid=(heads,),
        in_specs=[per_head(pair_shape, 1)] * 2
        + [half_head(part) for part in range(halves)] * 2
        + [per_head(row_shape, 1), whole(bias.shape), whole(expand.shape)]
        + [per_head(pair_shape, 1)],
        out_specs=(
            per_head((heads, toks, width), 0),
            per_head((heads, 2, toks), 0),
            per_head((heads, toks, width), 0),
            per_head(pair_shape, 1),
            per_head(sum_shape, 2),
            per_head(sum_shape, 2),
        ),
        out_shape=(
            struct((heads, toks, width), BF),
            struct((heads, 2, toks), F32),
            struct((heads, toks, width), F32),
            struct(pair_shape, F32),
            sum_struct,
            sum_struct,
        ),
        scratch_shapes=[
            pltpu.VMEM((span + count, width), BF),
            pltpu.VMEM((span + count, width), BF),
            pltpu.VMEM((toks // TILE, 2 * HALF + TILE + count, TILE), F32),
            pltpu.VMEM((span + count, toks), BF),
            pltpu.VMEM((span + count, toks), BF),
        ],
        compiler_params=params(),
        cost_estimate=cost(1e6, 1e6),
        name="local",
    )(qd, kv, *nears, *fars, rows, bias, expand, extra)
    log_far, log_near = from_far(log_dot), from_near(log_dot)

    got_sums = from_near(sent_sums)
    first = stages[0]
    halos = (qd_near, qd_far, log_near, log_far)
    parts = pl.pallas_call(
        fold_kernel,
        out_shape=[struct((4, heads, slots, width), BF)] * (devices // 2),
        compiler_params=params(),
        name="fold",
    )(kept_ends, got_ends, kept_sums, after(got_sums, halos))
    for stage in reversed(stages[1:-1]):
        size = len(parts) // (len(stage) + 1)
        kept = parts[:size]
        for number, mask in enumerate(stage):
            sent = parts[(number + 1) * size : (number + 2) * size]
            kept = [one + swap(other, mask) for one, other in zip(kept, sent)]
        parts = kept
    parts = [parts[0]] + [swap(part, mask) for part, mask in zip(parts[1:], first)]

    dkv = pl.pallas_call(
        functools.partial(rim_kernel, scale, scale2),
        grid=(heads,),
        in_specs=[per_head(pair_shape, 1), whole(bias.shape)]
        + [per_head(pair_shape, 1)] * 2
        + [per_head(log_dot.shape, 0)] * 2
        + [per_head(pair_shape, 1)],
        out_specs=per_head(pair_shape, 1),
        out_shape=struct(pair_shape, F32),
        scratch_shapes=[
            pltpu.VMEM((2 * toks, width), BF),
            pltpu.VMEM((2 * toks, width), BF),
            pltpu.VMEM((2, 2, toks), F32),
            pltpu.VMEM((toks, toks + TILE), BF),
            pltpu.VMEM((toks, toks + TILE), BF),
        ],
        compiler_params=params(),
        cost_estimate=cost(1e6, 1e6),
        name="rim",
    )(kv, bias, qd_near, qd_far, log_near, log_far, dkv)

    flat_shape = (toks * heads, width)
    steps = 2
    outs = pl.pallas_call(
        functools.partial(final_kernel, len(parts)),
        grid=(steps,),
        in_specs=[
            pl.BlockSpec((toks // steps, slots), lambda i: (i, 0)),
            pl.BlockSpec((heads, toks // steps, width), lambda i: (0, i, 0)),
            pl.BlockSpec((heads, toks // steps, width), lambda i: (0, i, 0)),
            pl.BlockSpec((2, heads, toks // steps, width), lambda i: (0, 0, i, 0)),
        ]
        + [whole((4, heads, slots, width))] * len(parts),
        out_specs=[pl.BlockSpec((toks * heads // steps, width), lambda i: (i, 0))] * 4,
        out_shape=[struct(flat_shape, kind) for kind in (BF, F32, F32, F32)],
        scratch_shapes=[pltpu.VMEM((toks * heads // steps, width), F32)],
        compiler_params=params(),
        name="final",
    )(place, out, dq, dkv, *parts)
    return tuple(x.reshape(toks, heads, width) for x in outs)


def solution(mesh):
    spec = P("ctx", "head", None)
    return jax.shard_map(
        shards,
        mesh=mesh,
        in_specs=(spec, spec, spec, spec, P()),
        out_specs=(spec, spec, spec, spec),
        check_vma=False,
    )
```

```python
import functools
import math

import jax
import jax.numpy as jnp
from jax import lax
from jax.experimental import pallas as pl
from jax.experimental.pallas import tpu as pltpu
from jax.sharding import PartitionSpec as P

HALF = 512
TILE = 256
NEG = -1e30
LOG2E = 1.0 / math.log(2.0)
VMEM_BYTES = 63 * 1024 * 1024
BF = jnp.bfloat16
F32 = jnp.float32


def nt(a, b):
    return lax.dot_general(a, b, (((1,), (1,)), ((), ())), preferred_element_type=F32)


def nn(a, b):
    return lax.dot_general(a, b, (((1,), (0,)), ((), ())), preferred_element_type=F32)


def wide(column, width):
    return jnp.concatenate([column] * (width // column.shape[1]), axis=1)


def iota(shape, dim):
    return lax.broadcasted_iota(jnp.int32, shape, dim)


def params():
    return pltpu.CompilerParams(vmem_limit_bytes=VMEM_BYTES)


def as_column(row):
    return jnp.broadcast_to(row, (128, row.shape[1])).T[:, :1]


def pack_keys_kernel(heads, k, v, kv, wide_rows):
    toks = k.shape[0] // heads
    for number, source in enumerate((k, v)):
        wide_rows[number] = source[...].astype(F32)
        for head in range(heads):
            kv[number, head] = wide_rows[number, pl.ds(head, toks, stride=heads), :].astype(BF)


def pack_queries_kernel(heads, slots, q, g, kv, pos_row, qd, slot_rows, wide_rows, acc):
    step = pl.program_id(0)
    toks = q.shape[0] // heads
    row = pos_row[...]
    count = row.shape[1]
    base = lax.axis_index("ctx") * (toks * pl.num_programs(0))
    column = as_column(row)
    tok = iota((count, toks), 1) + (base + step * toks)
    hit = jnp.sum((column == tok).astype(F32), axis=0, keepdims=True)
    rank = jnp.sum(((column >= base) & (column < tok)).astype(F32), axis=0, keepdims=True)
    slot = iota((slots, toks), 0).astype(F32)
    pick = jnp.where((hit > 0) & (rank == slot), 1.0, 0.0).astype(BF)
    tok = iota((toks, count), 0) + (base + step * toks)
    hit_column = jnp.sum((row == tok).astype(F32), axis=1, keepdims=True)
    tables = [[], [kv[0, h] for h in range(heads)], [kv[1, h] for h in range(heads)], []]
    for number, source in ((0, q), (3, g)):
        wide_rows[number // 3] = source[...].astype(F32)
        for head in range(heads):
            rows = wide_rows[number // 3, pl.ds(head, toks, stride=heads), :]
            tables[number].append(rows.astype(BF))
            if number == 0:
                qd[0, head] = rows.astype(BF)
            else:
                qd[1, head] = jnp.where(hit_column > 0, 0.0, rows).astype(BF)
    for number in range(4):
        found = nn(pick, jnp.concatenate(tables[number], axis=1))
        for head in range(heads):
            part = found[:, head * 128 : (head + 1) * 128]
            acc[number, head] = jnp.where(step == 0, part, acc[number, head] + part)

    @pl.when(step == pl.num_programs(0) - 1)
    def _():
        slot_rows[...] = acc[...].astype(BF)


def owner_map(column, owner, toks, slots, shape):
    inside = jnp.sum((column < owner * toks).astype(jnp.int32), axis=0, keepdims=True)
    held = jnp.sum((column < (owner + 1) * toks).astype(jnp.int32), axis=0, keepdims=True) - inside
    slot = iota(shape, 1) % slots
    hot = (iota(shape, 0) == inside + slot) & (slot < held)
    return jnp.where(hot, 1.0, 0.0).astype(BF)


def mask_kernel(order, slots, seq_rows, pos_row, bias, compact, expand, place):
    toks = place.shape[0]
    me = lax.axis_index("ctx")
    base = me * toks
    row = pos_row[...]
    count = row.shape[1]
    column = as_column(row)
    for start in range(0, bias.shape[0], TILE):
        key = iota((TILE, count), 0) + (base - HALF + start)
        hits = jnp.sum((row == key).astype(F32), axis=1, keepdims=True)
        key = key[:, :1]
        out = (hits > 0) | (key < 0) | (key >= seq_rows)
        bias[start : start + TILE, :] = jnp.broadcast_to(jnp.where(out, NEG, 0.0), (TILE, 128))
    tok = iota((toks, count), 0) + base
    hit = jnp.sum((row == tok).astype(F32), axis=1, keepdims=True)
    rank = jnp.sum(((row >= base) & (row < tok)).astype(F32), axis=1, keepdims=True)
    slot = iota((toks, slots), 1).astype(F32)
    place[...] = jnp.where((hit > 0) & (rank == slot), 1.0, 0.0).astype(BF)
    part = iota((1, compact.shape[1]), 1) // slots
    owner = jnp.zeros_like(part)
    for number, relative in enumerate(order):
        owner = jnp.where(part == number, me ^ relative, owner)
    compact[...] = owner_map(column, owner, toks, slots, compact.shape)
    expand[...] = compact[...].astype(F32).T.astype(BF)


def stats_kernel(scale2, compact, *refs):
    parts, (kv, rows, stats) = refs[:-3], refs[-3:]
    pieces = []
    for part in parts:
        for i in range(part.shape[0]):
            pieces.append(jnp.concatenate([part[i, number, 0] for number in range(4)], axis=1))
    packed = nn(compact[...], jnp.concatenate(pieces, axis=0)).astype(BF)
    width = kv.shape[3]
    table = [packed[:, number * width : (number + 1) * width] for number in range(4)]
    for number in range(4):
        rows[number, 0] = table[number]
    queries, _, _, grads = table
    scores = nt(kv[0, 0], queries) * scale2
    top = jnp.max(scores, axis=0, keepdims=True)
    weights = jnp.exp2(scores - top)
    total = jnp.sum(weights, axis=0, keepdims=True)
    dot = jnp.sum(weights * nt(kv[1, 0], grads), axis=0, keepdims=True)
    line = iota(stats.shape[2:], 0)
    found = jnp.where(line == 0, top, jnp.where(line == 1, total, dot))
    for device in range(stats.shape[0]):
        stats[device, 0] = found


def band(scores, low):
    rows, columns = iota(scores.shape, 0), iota(scores.shape, 1)
    return jnp.where(rows <= columns if low else rows >= columns, scores, NEG)


def put_in_slots(expand, tables, kept, sent):
    owners, kinds, _, slots, width = kept.shape
    spread = nn(expand, jnp.concatenate(tables, axis=1)).astype(BF)
    for owner in range(2 * owners):
        for kind in range(kinds):
            (kept if owner < owners else sent)[owner % owners, kind, 0] = spread[
                owner * slots : (owner + 1) * slots, kind * width : (kind + 1) * width
            ]


def fold_kernel(kept_ends, got_ends, kept_sums, got_sums, *outs):
    for part, out in enumerate(outs):
        out[0:2] = (kept_ends[part].astype(F32) + got_ends[part].astype(F32)).astype(BF)
        out[2:4] = (kept_sums[part].astype(F32) + got_sums[part].astype(F32)).astype(BF)


def global_kernel(scale, scale2, kv, rows, stats, expand, before, dkv, kept, sent):
    g_query, g_grad = rows[0, 0], rows[3, 0]
    tops = stats[:, 0, 0:1, :]
    top = jnp.max(tops, axis=0)
    factor = jnp.exp2(tops - top[None])
    total = jnp.sum(stats[:, 0, 1:2, :] * factor, axis=0)
    g_dot = jnp.sum(stats[:, 0, 2:3, :] * factor, axis=0) / total
    g_log = top + jnp.log2(total)
    weights = jnp.exp2(nt(kv[0, 0], g_query) * scale2 - g_log)
    narrow = weights.astype(BF)
    slopes = (weights * (nt(kv[1, 0], g_grad) - g_dot)).astype(BF)
    dkv[0, 0] = before[0, 0] + nn(slopes, g_query) * scale
    dkv[1, 0] = before[1, 0] + nn(narrow, g_grad)
    out = nn(kv[1, 0].T, narrow).T.astype(BF)
    dq = (nn(kv[0, 0].T, slopes) * scale).T.astype(BF)
    put_in_slots(expand[...], (out, dq), kept, sent)


def local_kernel(
    scale, scale2, qd, kv, kv_near, kv_far, rows, bias, expand,
    out, log_dot, dq, dkv, kept, sent, keys, values, score_buf, probs, slopes,
):
    toks = kv.shape[2]
    reach = 2 * HALF + TILE
    span = keys.shape[0] - rows.shape[2]
    near = 2 * (1 - lax.axis_index("ctx") % 2)
    for block, place in ((kv_near, near), (kv, 1), (kv_far, 2 - near)):
        spot = pl.ds(pl.multiple_of(place * toks, toks), toks)
        keys[spot, :] = block[0, 0]
        values[spot, :] = block[1, 0]
    keys[span:, :] = rows[1, 0]
    values[span:, :] = rows[2, 0]
    key_t, value_t = keys[...].T, values[...].T
    query_t, grad_t = qd[0, 0].T, qd[1, 0].T
    tiles = range(toks // TILE)
    lanes = [slice(tile * TILE, (tile + 1) * TILE) for tile in tiles]
    windows = [slice(tile * TILE, tile * TILE + reach) for tile in tiles]
    starts = [
        list(range(tile * TILE, tile * TILE + reach, TILE)) + list(range(span, keys.shape[0], TILE))
        for tile in tiles
    ]
    best, top, total, scaled, dots = ([None] * len(tiles) for _ in range(5))

    def score(tile, piece):
        start = starts[tile][piece]
        scores = nn(keys[start : start + TILE, :], query_t[:, lanes[tile]]) * scale2
        if start < span:
            scores = scores + wide(bias[start : start + TILE, :], TILE)
        if piece == 0:
            scores = band(scores, False)
        elif piece == reach // TILE - 1:
            scores = band(scores, True)
        score_buf[tile, piece * TILE : (piece + 1) * TILE, :] = scores
        part = jnp.max(scores.reshape(TILE // 8, 8, TILE), axis=0)
        best[tile] = part if best[tile] is None else jnp.maximum(best[tile], part)

    def weigh(tile, piece):
        if top[tile] is None:
            top[tile] = jnp.max(best[tile], axis=0, keepdims=True)
        start = starts[tile][piece]
        weights = jnp.exp2(score_buf[tile, piece * TILE : (piece + 1) * TILE, :] - top[tile])
        probs[start : start + TILE, lanes[tile]] = weights.astype(BF)
        part = jnp.sum(weights.reshape(TILE // 8, 8, TILE), axis=0)
        total[tile] = part if total[tile] is None else total[tile] + part

    def attend(tile):
        whole_sum = jnp.sum(total[tile], axis=0, keepdims=True)
        inverse = 1.0 / whole_sum
        grads = grad_t[:, lanes[tile]].astype(F32)
        acc = nn(value_t[:, windows[tile]], probs[windows[tile], lanes[tile]])
        acc = (acc + nn(value_t[:, span:], probs[span:, lanes[tile]])) * inverse
        dot = jnp.sum(grads * acc, axis=0, keepdims=True)
        log_dot[0, 0:1, lanes[tile]] = top[tile] + jnp.log2(whole_sum)
        log_dot[0, 1:2, lanes[tile]] = dot
        out[0, lanes[tile], :] = acc.T.astype(BF)
        scaled[tile] = (grads * inverse).astype(BF)
        dots[tile] = dot * inverse

    def slope(tile, piece):
        start = starts[tile][piece]
        rise = nn(values[start : start + TILE, :], scaled[tile]) - dots[tile]
        weights = probs[start : start + TILE, lanes[tile]].astype(F32)
        slopes[start : start + TILE, lanes[tile]] = (weights * rise).astype(BF)

    def query_gradient(tile):
        acc = nn(key_t[:, windows[tile]], slopes[windows[tile], lanes[tile]])
        acc = acc + nn(key_t[:, span:], slopes[span:, lanes[tile]])
        dq[0, lanes[tile], :] = (acc * scale).T

    for step in range(len(tiles) + 2):
        for piece in range(len(starts[0])):
            if 0 <= step - 2:
                slope(step - 2, piece)
            if 0 <= step - 1 < len(tiles):
                weigh(step - 1, piece)
            if step < len(tiles):
                score(step, piece)
        if 0 <= step - 2:
            query_gradient(step - 2)
        if 0 <= step - 1 < len(tiles):
            attend(step - 1)
    own = slice(HALF, HALF + toks)
    grads = jnp.concatenate(scaled, axis=1)
    dkv[0, 0] = (nt(query_t, slopes[own, :]) * scale).T
    dkv[1, 0] = nt(grads, probs[own, :]).T
    g_dk = (nt(query_t, slopes[span:, :]) * scale).T.astype(BF)
    g_dv = nt(grads, probs[span:, :]).T.astype(BF)
    put_in_slots(expand[...], (g_dk, g_dv), kept, sent)


def rim_kernel(
    scale, scale2, kv, bias, qd_near, qd_far, log_near, log_far, partial, dkv,
    queries, grads, logs, probs, slopes,
):
    toks = kv.shape[2]
    reach = toks + TILE
    near = 1 - lax.axis_index("ctx") % 2
    for qd, log_dot, place in ((qd_near, log_near, near), (qd_far, log_far, 1 - near)):
        spot = pl.ds(pl.multiple_of(place * toks, toks), toks)
        queries[spot, :] = qd[0, 0]
        grads[spot, :] = qd[1, 0]
        logs[place] = log_dot[0]
    for k_tile in range(toks // TILE):
        span = slice(k_tile * TILE, (k_tile + 1) * TILE)
        key = kv[0, 0, span, :]
        value = kv[1, 0, span, :]
        key_bias = wide(bias[HALF + k_tile * TILE : HALF + (k_tile + 1) * TILE, :], TILE)
        for piece in range(reach // TILE):
            start = (k_tile + piece) * TILE
            side, lanes = start // toks, slice(start % toks, start % toks + TILE)
            scores = nt(key, queries[start : start + TILE, :]) * scale2 + key_bias
            if piece == 0:
                scores = band(scores, True)
            elif piece == reach // TILE - 1:
                scores = band(scores, False)
            weights = jnp.exp2(scores - logs[side, 0:1, lanes])
            slope = weights * (nt(value, grads[start : start + TILE, :]) - logs[side, 1:2, lanes])
            spot = slice(piece * TILE, (piece + 1) * TILE)
            probs[span, spot] = weights.astype(BF)
            slopes[span, spot] = slope.astype(BF)
        window = slice(k_tile * TILE, k_tile * TILE + reach)
        dkv[0, 0, span, :] = partial[0, 0, span, :] + nn(slopes[span, :], queries[window, :]) * scale
        dkv[1, 0, span, :] = partial[1, 0, span, :] + nn(probs[span, :], grads[window, :])


def final_kernel(
    sources, place, out, dq, dkv, *refs
):
    parts, refs = refs[:sources], refs[sources:]
    attn, query_grad, key_grad, value_grad, wide_rows = refs
    heads, toks = out.shape[0], out.shape[1]
    hot = place[...]
    is_global = jnp.sum(hot.astype(F32), axis=1, keepdims=True) > 0
    for head in range(heads):
        rows = pl.ds(head, toks, stride=heads)
        tables = []
        for kind in range(4):
            table = parts[0][kind, head].astype(F32)
            for part in parts[1:]:
                table = table + part[kind, head].astype(F32)
            tables.append(table.astype(BF))
        width = out.shape[2]
        added = nn(hot, jnp.concatenate(tables, axis=1))
        added = [added[:, i * width : (i + 1) * width] for i in range(4)]
        wide_rows[rows, :] = jnp.where(is_global, added[0], out[head].astype(F32))
        query_grad[rows, :] = dq[head] + added[1]
        key_grad[rows, :] = dkv[0, head] + added[2]
        value_grad[rows, :] = dkv[1, head] + added[3]
    attn[...] = wide_rows[...].astype(BF)


def cost(flops, moved, exps=0):
    return pl.CostEstimate(flops=int(flops), bytes_accessed=int(moved), transcendentals=int(exps))


def struct(shape, dtype):
    return jax.ShapeDtypeStruct(shape, dtype)


def whole(shape):
    return pl.BlockSpec(shape, lambda head: (0,) * len(shape))


def per_head(shape, dim, first=0):
    block = tuple(1 if i == dim else size for i, size in enumerate(shape))
    return pl.BlockSpec(
        block, lambda head: tuple(head + first if i == dim else 0 for i in range(len(shape)))
    )


def shards(query_rows, key_rows, value_rows, out_grad, global_pos):
    toks, heads, width = query_rows.shape
    count = global_pos.shape[0]
    devices = lax.axis_size("ctx")
    slots = max(16, 2 * count // devices)
    scale = width ** (-0.5)
    scale2 = scale * LOG2E
    bits = devices.bit_length() - 1
    stages = [
        [mask << low for mask in range(1, 1 << min(2, bits - low))] for low in range(1, bits, 2)
    ] + [[1]]
    order = [0]
    for stage in stages:
        order = order + [one ^ mask for mask in stage for one in order]
    pos_row = global_pos.reshape(1, count)
    q_flat, k_flat, v_flat, g_flat = (
        x.reshape(toks * heads, width) for x in (query_rows, key_rows, value_rows, out_grad)
    )

    def swap(value, mask):
        return lax.ppermute(value, "ctx", [(i, i ^ mask) for i in range(devices)])

    def from_near(value):
        return swap(value, 1)

    def from_far(value):
        pairs = [(i, i + 1) for i in range(1, devices - 1, 2)]
        return lax.ppermute(value, "ctx", pairs + [(j, i) for i, j in pairs])

    def after(value, earlier):
        return lax.optimization_barrier((value, earlier))[0]

    pair_shape = (2, heads, toks, width)
    slot_shape = (4, heads, slots, width)
    steps = 1
    flat_spec = pl.BlockSpec((toks * heads // steps, width), lambda i: (i, 0))
    pair_spec = pl.BlockSpec((2, heads, toks // steps, width), lambda i: (0, 0, i, 0))
    wide_pair = pltpu.VMEM((2, toks * heads // steps, width), F32)
    kv = pl.pallas_call(
        functools.partial(pack_keys_kernel, heads),
        out_shape=struct(pair_shape, BF),
        scratch_shapes=[wide_pair],
        compiler_params=params(),
        name="pack_keys",
    )(k_flat, v_flat)

    qd, slot_rows = pl.pallas_call(
        functools.partial(pack_queries_kernel, heads, slots),
        grid=(steps,),
        in_specs=[flat_spec, flat_spec, pair_spec, whole((1, count))],
        out_specs=(pair_spec, whole(slot_shape)),
        out_shape=(struct(pair_shape, BF), struct(slot_shape, BF)),
        scratch_shapes=[wide_pair, pltpu.VMEM(slot_shape, F32)],
        compiler_params=params(),
        name="pack_queries",
    )(q_flat, g_flat, kv, pos_row)

    span = toks + 2 * HALF
    bias, compact, expand, place = pl.pallas_call(
        functools.partial(mask_kernel, order, slots, toks * devices),
        out_shape=(
            struct((span, 128), F32),
            struct((count, devices * slots), BF),
            struct((devices * slots, count), BF),
            struct((toks, slots), BF),
        ),
        compiler_params=params(),
        name="masks",
    )(pos_row)

    kv_far, kv_near = from_far(kv), from_near(kv)
    held = [slot_rows[None]]
    for stage in stages:
        send = jnp.concatenate(held, axis=0) if len(held) > 1 else held[0]
        if stage == [1]:
            send = after(send, (kv_near, kv_far, place))
        held += [swap(send, mask) for mask in stage]

    row_shape = (4, heads, count, width)
    rows, stats = pl.pallas_call(
        functools.partial(stats_kernel, scale2),
        grid=(heads,),
        in_specs=[whole(compact.shape)]
        + [per_head(part.shape, 2) for part in held]
        + [per_head(pair_shape, 1)],
        out_specs=(per_head(row_shape, 1), per_head((devices, heads, 8, count), 1)),
        out_shape=(struct(row_shape, BF), struct((devices, heads, 8, count), F32)),
        compiler_params=params(),
        cost_estimate=cost(1e6, 1e6),
        name="global_stats",
    )(compact, *held, kv)

    stats = lax.all_to_all(stats, "ctx", 0, 0, tiled=True)
    qd_late = after(qd, (kv_near, kv_far))
    qd_far, qd_near = from_far(qd_late), from_near(qd_late)

    sum_shape = (devices // 2, 2, heads, slots, width)
    sum_struct = struct(sum_shape, BF)
    out, log_dot, dq, dkv, kept_sums, sent_sums = pl.pallas_call(
        functools.partial(local_kernel, scale, scale2),
        grid=(heads,),
        in_specs=[per_head(pair_shape, 1)] * 4
        + [per_head(row_shape, 1), whole(bias.shape), whole(expand.shape)],
        out_specs=(
            per_head((heads, toks, width), 0),
            per_head((heads, 2, toks), 0),
            per_head((heads, toks, width), 0),
            per_head(pair_shape, 1),
            per_head(sum_shape, 2),
            per_head(sum_shape, 2),
        ),
        out_shape=(
            struct((heads, toks, width), BF),
            struct((heads, 2, toks), F32),
            struct((heads, toks, width), F32),
            struct(pair_shape, F32),
            sum_struct,
            sum_struct,
        ),
        scratch_shapes=[
            pltpu.VMEM((span + count, width), BF),
            pltpu.VMEM((span + count, width), BF),
            pltpu.VMEM((toks // TILE, 2 * HALF + TILE + count, TILE), F32),
            pltpu.VMEM((span + count, toks), BF),
            pltpu.VMEM((span + count, toks), BF),
        ],
        compiler_params=params(),
        cost_estimate=cost(1e6, 1e6),
        name="local",
    )(qd, kv, kv_near, kv_far, rows, bias, expand)
    log_far, log_near = from_far(log_dot), from_near(log_dot)

    dkv, kept_ends, sent_ends = pl.pallas_call(
        functools.partial(global_kernel, scale, scale2),
        grid=(heads,),
        in_specs=[per_head(pair_shape, 1), per_head(row_shape, 1)]
        + [per_head(stats.shape, 1), whole(expand.shape), per_head(pair_shape, 1)],
        out_specs=(per_head(pair_shape, 1), per_head(sum_shape, 2), per_head(sum_shape, 2)),
        out_shape=(struct(pair_shape, F32), sum_struct, sum_struct),
        input_output_aliases={4: 0},
        compiler_params=params(),
        cost_estimate=cost(1e6, 1e6),
        name="global_queries",
    )(kv, rows, after(stats, (log_dot, qd_near, qd_far)), expand, dkv)
    got_sums = from_near(sent_sums)
    got_ends = from_near(after(sent_ends, (log_near, log_far)))

    sum_shape = (devices // 2, 2, heads, slots, width)
    sum_struct = struct(sum_shape, BF)
    out, log_dot, dq, dkv, kept_sums, sent_sums = pl.pallas_call(
        functools.partial(local_kernel, scale, scale2),
        grid=(heads,),
        in_specs=[per_head(pair_shape, 1)] * 4
        + [per_head(row_shape, 1), whole(bias.shape), whole(expand.shape)],
        out_specs=(
            per_head((heads, toks, width), 0),
            per_head((heads, 2, toks), 0),
            per_head((heads, toks, width), 0),
            per_head(pair_shape, 1),
            per_head(sum_shape, 2),
            per_head(sum_shape, 2),
        ),
        out_shape=(
            struct((heads, toks, width), BF),
            struct((heads, 2, toks), F32),
            struct((heads, toks, width), F32),
            struct(pair_shape, F32),
            sum_struct,
            sum_struct,
        ),
        scratch_shapes=[
            pltpu.VMEM((span + count, width), BF),
            pltpu.VMEM((span + count, width), BF),
            pltpu.VMEM((toks // TILE, 2 * HALF + TILE + count, TILE), F32),
            pltpu.VMEM((span + count, toks), BF),
            pltpu.VMEM((span + count, toks), BF),
        ],
        compiler_params=params(),
        cost_estimate=cost(1e6, 1e6),
        name="local",
    )(qd, kv, kv_near, kv_far, rows, bias, expand)
    log_far, log_near = from_far(log_dot), from_near(log_dot)

    dkv, kept_ends, sent_ends = pl.pallas_call(
        functools.partial(global_kernel, scale, scale2),
        grid=(heads,),
        in_specs=[per_head(pair_shape, 1), per_head(row_shape, 1)]
        + [per_head(stats.shape, 1), whole(expand.shape), per_head(pair_shape, 1)],
        out_specs=(per_head(pair_shape, 1), per_head(sum_shape, 2), per_head(sum_shape, 2)),
        out_shape=(struct(pair_shape, F32), sum_struct, sum_struct),
        input_output_aliases={4: 0},
        compiler_params=params(),
        cost_estimate=cost(1e6, 1e6),
        name="global_queries",
    )(kv, rows, after(stats, (log_dot, qd_near, qd_far)), expand, dkv)
    got_sums = from_near(sent_sums)
    got_ends = from_near(after(sent_ends, (log_near, log_far)))

    def half_head(part):
        return pl.BlockSpec(
            (2, 1, toks, width), lambda head: (0, jnp.clip(head - part * group, 0, group - 1), 0, 0)
        )

    first = stages[0]
    parts = pl.pallas_call(
        fold_kernel,
        out_shape=[struct((4, heads, slots, width), BF)] * (devices // 2),
        compiler_params=params(),
        name="fold",
    )(kept_ends, got_ends, kept_sums, got_sums)
    for stage in reversed(stages[1:-1]):
        size = len(parts) // (len(stage) + 1)
        kept = parts[:size]
        for number, mask in enumerate(stage):
            sent = parts[(number + 1) * size : (number + 2) * size]
            kept = [one + swap(other, mask) for one, other in zip(kept, sent)]
        parts = kept
    parts = [parts[0]] + [swap(part, mask) for part, mask in zip(parts[1:], first)]

    dkv = pl.pallas_call(
        functools.partial(rim_kernel, scale, scale2),
        grid=(heads,),
        in_specs=[per_head(pair_shape, 1), whole(bias.shape)]
        + [per_head(pair_shape, 1)] * 2
        + [per_head(log_dot.shape, 0)] * 2
        + [per_head(pair_shape, 1)],
        out_specs=per_head(pair_shape, 1),
        out_shape=struct(pair_shape, F32),
        scratch_shapes=[
            pltpu.VMEM((2 * toks, width), BF),
            pltpu.VMEM((2 * toks, width), BF),
            pltpu.VMEM((2, 2, toks), F32),
            pltpu.VMEM((toks, toks + TILE), BF),
            pltpu.VMEM((toks, toks + TILE), BF),
        ],
        compiler_params=params(),
        cost_estimate=cost(1e6, 1e6),
        name="rim",
    )(kv, bias, qd_near, qd_far, log_near, log_far, dkv)

    flat_shape = (toks * heads, width)
    steps = 2
    outs = pl.pallas_call(
        functools.partial(final_kernel, len(parts)),
        grid=(steps,),
        in_specs=[
            pl.BlockSpec((toks // steps, slots), lambda i: (i, 0)),
            pl.BlockSpec((heads, toks // steps, width), lambda i: (0, i, 0)),
            pl.BlockSpec((heads, toks // steps, width), lambda i: (0, i, 0)),
            pl.BlockSpec((2, heads, toks // steps, width), lambda i: (0, 0, i, 0)),
        ]
        + [whole((4, heads, slots, width))] * len(parts),
        out_specs=[pl.BlockSpec((toks * heads // steps, width), lambda i: (i, 0))] * 4,
        out_shape=[struct(flat_shape, kind) for kind in (BF, F32, F32, F32)],
        scratch_shapes=[pltpu.VMEM((toks * heads // steps, width), F32)],
        compiler_params=params(),
        name="final",
    )(place, out, dq, dkv, *parts)
    return tuple(x.reshape(toks, heads, width) for x in outs)


def solution(mesh):
    spec = P("ctx", "head", None)
    return jax.shard_map(
        shards,
        mesh=mesh,
        in_specs=(spec, spec, spec, spec, P()),
        out_specs=(spec, spec, spec, spec),
        check_vma=False,
    )
```

```python
import functools
import math

import jax
import jax.numpy as jnp
from jax import lax
from jax.experimental import pallas as pl
from jax.experimental.pallas import tpu as pltpu
from jax.sharding import PartitionSpec as P

HALF = 512
TILE = 256
NEG = -1e30
LOG2E = 1.0 / math.log(2.0)
VMEM_BYTES = 63 * 1024 * 1024
BF = jnp.bfloat16
F32 = jnp.float32


def nt(a, b):
    return lax.dot_general(a, b, (((1,), (1,)), ((), ())), preferred_element_type=F32)


def nn(a, b):
    return lax.dot_general(a, b, (((1,), (0,)), ((), ())), preferred_element_type=F32)


def wide(column, width):
    return jnp.concatenate([column] * (width // column.shape[1]), axis=1)


def iota(shape, dim):
    return lax.broadcasted_iota(jnp.int32, shape, dim)


def params():
    return pltpu.CompilerParams(vmem_limit_bytes=VMEM_BYTES)


def as_column(row):
    return jnp.broadcast_to(row, (128, row.shape[1])).T[:, :1]


def pack_keys_kernel(heads, k, v, kv, wide_rows):
    toks = k.shape[0] // heads
    for number, source in enumerate((k, v)):
        wide_rows[number] = source[...].astype(F32)
        for head in range(heads):
            kv[number, head] = wide_rows[number, pl.ds(head, toks, stride=heads), :].astype(BF)


def pack_queries_kernel(heads, slots, q, g, kv, pos_row, qd, slot_rows, wide_rows, acc):
    step = pl.program_id(0)
    toks = q.shape[0] // heads
    row = pos_row[...]
    count = row.shape[1]
    base = lax.axis_index("ctx") * (toks * pl.num_programs(0))
    column = as_column(row)
    tok = iota((count, toks), 1) + (base + step * toks)
    hit = jnp.sum((column == tok).astype(F32), axis=0, keepdims=True)
    rank = jnp.sum(((column >= base) & (column < tok)).astype(F32), axis=0, keepdims=True)
    slot = iota((slots, toks), 0).astype(F32)
    pick = jnp.where((hit > 0) & (rank == slot), 1.0, 0.0).astype(BF)
    tok = iota((toks, count), 0) + (base + step * toks)
    hit_column = jnp.sum((row == tok).astype(F32), axis=1, keepdims=True)
    tables = [[], [kv[0, h] for h in range(heads)], [kv[1, h] for h in range(heads)], []]
    for number, source in ((0, q), (3, g)):
        wide_rows[number // 3] = source[...].astype(F32)
        for head in range(heads):
            rows = wide_rows[number // 3, pl.ds(head, toks, stride=heads), :]
            tables[number].append(rows.astype(BF))
            if number == 0:
                qd[0, head] = rows.astype(BF)
            else:
                qd[1, head] = jnp.where(hit_column > 0, 0.0, rows).astype(BF)
    for number in range(4):
        found = nn(pick, jnp.concatenate(tables[number], axis=1))
        for head in range(heads):
            part = found[:, head * 128 : (head + 1) * 128]
            acc[number, head] = jnp.where(step == 0, part, acc[number, head] + part)

    @pl.when(step == pl.num_programs(0) - 1)
    def _():
        slot_rows[...] = acc[...].astype(BF)


def owner_map(column, owner, toks, slots, shape):
    inside = jnp.sum((column < owner * toks).astype(jnp.int32), axis=0, keepdims=True)
    held = jnp.sum((column < (owner + 1) * toks).astype(jnp.int32), axis=0, keepdims=True) - inside
    slot = iota(shape, 1) % slots
    hot = (iota(shape, 0) == inside + slot) & (slot < held)
    return jnp.where(hot, 1.0, 0.0).astype(BF)


def mask_kernel(order, slots, seq_rows, pos_row, bias, compact, expand, place):
    toks = place.shape[0]
    me = lax.axis_index("ctx")
    base = me * toks
    row = pos_row[...]
    count = row.shape[1]
    column = as_column(row)
    for start in range(0, bias.shape[0], TILE):
        key = iota((TILE, count), 0) + (base - HALF + start)
        hits = jnp.sum((row == key).astype(F32), axis=1, keepdims=True)
        key = key[:, :1]
        out = (hits > 0) | (key < 0) | (key >= seq_rows)
        bias[start : start + TILE, :] = jnp.broadcast_to(jnp.where(out, NEG, 0.0), (TILE, 128))
    tok = iota((toks, count), 0) + base
    hit = jnp.sum((row == tok).astype(F32), axis=1, keepdims=True)
    rank = jnp.sum(((row >= base) & (row < tok)).astype(F32), axis=1, keepdims=True)
    slot = iota((toks, slots), 1).astype(F32)
    place[...] = jnp.where((hit > 0) & (rank == slot), 1.0, 0.0).astype(BF)
    part = iota((1, compact.shape[1]), 1) // slots
    owner = jnp.zeros_like(part)
    for number, relative in enumerate(order):
        owner = jnp.where(part == number, me ^ relative, owner)
    compact[...] = owner_map(column, owner, toks, slots, compact.shape)
    expand[...] = compact[...].astype(F32).T.astype(BF)


def stats_kernel(scale2, compact, *refs):
    parts, (kv, rows, stats) = refs[:-3], refs[-3:]
    pieces = []
    for part in parts:
        for i in range(part.shape[0]):
            pieces.append(jnp.concatenate([part[i, number, 0] for number in range(4)], axis=1))
    packed = nn(compact[...], jnp.concatenate(pieces, axis=0)).astype(BF)
    width = kv.shape[3]
    table = [packed[:, number * width : (number + 1) * width] for number in range(4)]
    for number in range(4):
        rows[number, 0] = table[number]
    queries, _, _, grads = table
    scores = nt(kv[0, 0], queries) * scale2
    top = jnp.max(scores, axis=0, keepdims=True)
    weights = jnp.exp2(scores - top)
    total = jnp.sum(weights, axis=0, keepdims=True)
    dot = jnp.sum(weights * nt(kv[1, 0], grads), axis=0, keepdims=True)
    line = iota(stats.shape[2:], 0)
    found = jnp.where(line == 0, top, jnp.where(line == 1, total, dot))
    for device in range(stats.shape[0]):
        stats[device, 0] = found


def band(scores, low):
    rows, columns = iota(scores.shape, 0), iota(scores.shape, 1)
    return jnp.where(rows <= columns if low else rows >= columns, scores, NEG)


def put_in_slots(expand, tables, kept, sent):
    owners, kinds, _, slots, width = kept.shape
    spread = nn(expand, jnp.concatenate(tables, axis=1)).astype(BF)
    for owner in range(2 * owners):
        for kind in range(kinds):
            (kept if owner < owners else sent)[owner % owners, kind, 0] = spread[
                owner * slots : (owner + 1) * slots, kind * width : (kind + 1) * width
            ]


def fold_kernel(kept_ends, got_ends, kept_sums, got_sums, *outs):
    for part, out in enumerate(outs):
        out[0:2] = (kept_ends[part].astype(F32) + got_ends[part].astype(F32)).astype(BF)
        out[2:4] = (kept_sums[part].astype(F32) + got_sums[part].astype(F32)).astype(BF)


def global_kernel(scale, scale2, kv, rows, stats, expand, dkv, kept, sent):
    g_query, g_grad = rows[0, 0], rows[3, 0]
    tops = stats[:, 0, 0:1, :]
    top = jnp.max(tops, axis=0)
    factor = jnp.exp2(tops - top[None])
    total = jnp.sum(stats[:, 0, 1:2, :] * factor, axis=0)
    g_dot = jnp.sum(stats[:, 0, 2:3, :] * factor, axis=0) / total
    g_log = top + jnp.log2(total)
    weights = jnp.exp2(nt(kv[0, 0], g_query) * scale2 - g_log)
    narrow = weights.astype(BF)
    slopes = (weights * (nt(kv[1, 0], g_grad) - g_dot)).astype(BF)
    dkv[0, 0] = nn(slopes, g_query) * scale
    dkv[1, 0] = nn(narrow, g_grad)
    out = nn(kv[1, 0].T, narrow).T.astype(BF)
    dq = (nn(kv[0, 0].T, slopes) * scale).T.astype(BF)
    put_in_slots(expand[...], (out, dq), kept, sent)


def local_kernel(
    scale, scale2, qd, kv, kv_near, kv_far, rows, bias, expand, before,
    out, log_dot, dq, dkv, kept, sent, keys, values, score_buf, probs, slopes,
):
    toks = kv.shape[2]
    reach = 2 * HALF + TILE
    span = keys.shape[0] - rows.shape[2]
    near = 2 * (1 - lax.axis_index("ctx") % 2)
    for block, place in ((kv_near, near), (kv, 1), (kv_far, 2 - near)):
        spot = pl.ds(pl.multiple_of(place * toks, toks), toks)
        keys[spot, :] = block[0, 0]
        values[spot, :] = block[1, 0]
    keys[span:, :] = rows[1, 0]
    values[span:, :] = rows[2, 0]
    key_t, value_t = keys[...].T, values[...].T
    query_t, grad_t = qd[0, 0].T, qd[1, 0].T
    tiles = range(toks // TILE)
    lanes = [slice(tile * TILE, (tile + 1) * TILE) for tile in tiles]
    windows = [slice(tile * TILE, tile * TILE + reach) for tile in tiles]
    starts = [
        list(range(tile * TILE, tile * TILE + reach, TILE)) + list(range(span, keys.shape[0], TILE))
        for tile in tiles
    ]
    best, top, total, scaled, dots = ([None] * len(tiles) for _ in range(5))

    def score(tile, piece):
        start = starts[tile][piece]
        scores = nn(keys[start : start + TILE, :], query_t[:, lanes[tile]]) * scale2
        if start < span:
            scores = scores + wide(bias[start : start + TILE, :], TILE)
        if piece == 0:
            scores = band(scores, False)
        elif piece == reach // TILE - 1:
            scores = band(scores, True)
        score_buf[tile, piece * TILE : (piece + 1) * TILE, :] = scores
        part = jnp.max(scores.reshape(TILE // 8, 8, TILE), axis=0)
        best[tile] = part if best[tile] is None else jnp.maximum(best[tile], part)

    def weigh(tile, piece):
        if top[tile] is None:
            top[tile] = jnp.max(best[tile], axis=0, keepdims=True)
        start = starts[tile][piece]
        weights = jnp.exp2(score_buf[tile, piece * TILE : (piece + 1) * TILE, :] - top[tile])
        probs[start : start + TILE, lanes[tile]] = weights.astype(BF)
        part = jnp.sum(weights.reshape(TILE // 8, 8, TILE), axis=0)
        total[tile] = part if total[tile] is None else total[tile] + part

    def attend(tile):
        whole_sum = jnp.sum(total[tile], axis=0, keepdims=True)
        inverse = 1.0 / whole_sum
        grads = grad_t[:, lanes[tile]].astype(F32)
        acc = nn(value_t[:, windows[tile]], probs[windows[tile], lanes[tile]])
        acc = (acc + nn(value_t[:, span:], probs[span:, lanes[tile]])) * inverse
        dot = jnp.sum(grads * acc, axis=0, keepdims=True)
        log_dot[0, 0:1, lanes[tile]] = top[tile] + jnp.log2(whole_sum)
        log_dot[0, 1:2, lanes[tile]] = dot
        out[0, lanes[tile], :] = acc.T.astype(BF)
        scaled[tile] = (grads * inverse).astype(BF)
        dots[tile] = dot * inverse

    def slope(tile, piece):
        start = starts[tile][piece]
        rise = nn(values[start : start + TILE, :], scaled[tile]) - dots[tile]
        weights = probs[start : start + TILE, lanes[tile]].astype(F32)
        slopes[start : start + TILE, lanes[tile]] = (weights * rise).astype(BF)

    def query_gradient(tile):
        acc = nn(key_t[:, windows[tile]], slopes[windows[tile], lanes[tile]])
        acc = acc + nn(key_t[:, span:], slopes[span:, lanes[tile]])
        dq[0, lanes[tile], :] = (acc * scale).T

    for step in range(len(tiles) + 2):
        for piece in range(len(starts[0])):
            if 0 <= step - 2:
                slope(step - 2, piece)
            if 0 <= step - 1 < len(tiles):
                weigh(step - 1, piece)
            if step < len(tiles):
                score(step, piece)
        if 0 <= step - 2:
            query_gradient(step - 2)
        if 0 <= step - 1 < len(tiles):
            attend(step - 1)
    own = slice(HALF, HALF + toks)
    grads = jnp.concatenate(scaled, axis=1)
    dkv[0, 0] = before[0, 0] + (nt(query_t, slopes[own, :]) * scale).T
    dkv[1, 0] = before[1, 0] + nt(grads, probs[own, :]).T
    g_dk = (nt(query_t, slopes[span:, :]) * scale).T.astype(BF)
    g_dv = nt(grads, probs[span:, :]).T.astype(BF)
    put_in_slots(expand[...], (g_dk, g_dv), kept, sent)


def rim_kernel(
    scale, scale2, kv, bias, qd_near, qd_far, log_near, log_far, partial, dkv,
    queries, grads, logs, probs, slopes,
):
    toks = kv.shape[2]
    reach = toks + TILE
    near = 1 - lax.axis_index("ctx") % 2
    for qd, log_dot, place in ((qd_near, log_near, near), (qd_far, log_far, 1 - near)):
        spot = pl.ds(pl.multiple_of(place * toks, toks), toks)
        queries[spot, :] = qd[0, 0]
        grads[spot, :] = qd[1, 0]
        logs[place] = log_dot[0]
    for k_tile in range(toks // TILE):
        span = slice(k_tile * TILE, (k_tile + 1) * TILE)
        key = kv[0, 0, span, :]
        value = kv[1, 0, span, :]
        key_bias = wide(bias[HALF + k_tile * TILE : HALF + (k_tile + 1) * TILE, :], TILE)
        for piece in range(reach // TILE):
            start = (k_tile + piece) * TILE
            side, lanes = start // toks, slice(start % toks, start % toks + TILE)
            scores = nt(key, queries[start : start + TILE, :]) * scale2 + key_bias
            if piece == 0:
                scores = band(scores, True)
            elif piece == reach // TILE - 1:
                scores = band(scores, False)
            weights = jnp.exp2(scores - logs[side, 0:1, lanes])
            slope = weights * (nt(value, grads[start : start + TILE, :]) - logs[side, 1:2, lanes])
            spot = slice(piece * TILE, (piece + 1) * TILE)
            probs[span, spot] = weights.astype(BF)
            slopes[span, spot] = slope.astype(BF)
        window = slice(k_tile * TILE, k_tile * TILE + reach)
        dkv[0, 0, span, :] = partial[0, 0, span, :] + nn(slopes[span, :], queries[window, :]) * scale
        dkv[1, 0, span, :] = partial[1, 0, span, :] + nn(probs[span, :], grads[window, :])


def final_kernel(
    sources, place, out, dq, dkv, *refs
):
    parts, refs = refs[:sources], refs[sources:]
    attn, query_grad, key_grad, value_grad, wide_rows = refs
    heads, toks = out.shape[0], out.shape[1]
    hot = place[...]
    is_global = jnp.sum(hot.astype(F32), axis=1, keepdims=True) > 0
    for head in range(heads):
        rows = pl.ds(head, toks, stride=heads)
        tables = []
        for kind in range(4):
            table = parts[0][kind, head].astype(F32)
            for part in parts[1:]:
                table = table + part[kind, head].astype(F32)
            tables.append(table.astype(BF))
        width = out.shape[2]
        added = nn(hot, jnp.concatenate(tables, axis=1))
        added = [added[:, i * width : (i + 1) * width] for i in range(4)]
        wide_rows[rows, :] = jnp.where(is_global, added[0], out[head].astype(F32))
        query_grad[rows, :] = dq[head] + added[1]
        key_grad[rows, :] = dkv[0, head] + added[2]
        value_grad[rows, :] = dkv[1, head] + added[3]
    attn[...] = wide_rows[...].astype(BF)


def cost(flops, moved, exps=0):
    return pl.CostEstimate(flops=int(flops), bytes_accessed=int(moved), transcendentals=int(exps))


def struct(shape, dtype):
    return jax.ShapeDtypeStruct(shape, dtype)


def whole(shape):
    return pl.BlockSpec(shape, lambda head: (0,) * len(shape))


def per_head(shape, dim, first=0):
    block = tuple(1 if i == dim else size for i, size in enumerate(shape))
    return pl.BlockSpec(
        block, lambda head: tuple(head + first if i == dim else 0 for i in range(len(shape)))
    )


def shards(query_rows, key_rows, value_rows, out_grad, global_pos):
    toks, heads, width = query_rows.shape
    count = global_pos.shape[0]
    devices = lax.axis_size("ctx")
    slots = max(16, 2 * count // devices)
    scale = width ** (-0.5)
    scale2 = scale * LOG2E
    bits = devices.bit_length() - 1
    stages = [
        [mask << low for mask in range(1, 1 << min(2, bits - low))] for low in range(1, bits, 2)
    ] + [[1]]
    order = [0]
    for stage in stages:
        order = order + [one ^ mask for mask in stage for one in order]
    pos_row = global_pos.reshape(1, count)
    q_flat, k_flat, v_flat, g_flat = (
        x.reshape(toks * heads, width) for x in (query_rows, key_rows, value_rows, out_grad)
    )

    def swap(value, mask):
        return lax.ppermute(value, "ctx", [(i, i ^ mask) for i in range(devices)])

    def from_near(value):
        return swap(value, 1)

    def from_far(value):
        pairs = [(i, i + 1) for i in range(1, devices - 1, 2)]
        return lax.ppermute(value, "ctx", pairs + [(j, i) for i, j in pairs])

    def after(value, earlier):
        return lax.optimization_barrier((value, earlier))[0]

    pair_shape = (2, heads, toks, width)
    slot_shape = (4, heads, slots, width)
    steps = 1
    flat_spec = pl.BlockSpec((toks * heads // steps, width), lambda i: (i, 0))
    pair_spec = pl.BlockSpec((2, heads, toks // steps, width), lambda i: (0, 0, i, 0))
    wide_pair = pltpu.VMEM((2, toks * heads // steps, width), F32)
    kv = pl.pallas_call(
        functools.partial(pack_keys_kernel, heads),
        out_shape=struct(pair_shape, BF),
        scratch_shapes=[wide_pair],
        compiler_params=params(),
        name="pack_keys",
    )(k_flat, v_flat)

    qd, slot_rows = pl.pallas_call(
        functools.partial(pack_queries_kernel, heads, slots),
        grid=(steps,),
        in_specs=[flat_spec, flat_spec, pair_spec, whole((1, count))],
        out_specs=(pair_spec, whole(slot_shape)),
        out_shape=(struct(pair_shape, BF), struct(slot_shape, BF)),
        scratch_shapes=[wide_pair, pltpu.VMEM(slot_shape, F32)],
        compiler_params=params(),
        name="pack_queries",
    )(q_flat, g_flat, kv, pos_row)

    span = toks + 2 * HALF
    bias, compact, expand, place = pl.pallas_call(
        functools.partial(mask_kernel, order, slots, toks * devices),
        out_shape=(
            struct((span, 128), F32),
            struct((count, devices * slots), BF),
            struct((devices * slots, count), BF),
            struct((toks, slots), BF),
        ),
        compiler_params=params(),
        name="masks",
    )(pos_row)

    held = [slot_rows[None]]
    for number, stage in enumerate(stages):
        send = jnp.concatenate(held, axis=0) if number else held[0]
        held += [swap(send, mask) for mask in stage]
        if not number:
            kv_late = after(kv, (held, place))
            kv_far, kv_near = from_far(kv_late), from_near(kv_late)

    row_shape = (4, heads, count, width)
    rows, stats = pl.pallas_call(
        functools.partial(stats_kernel, scale2),
        grid=(heads,),
        in_specs=[whole(compact.shape)]
        + [per_head(part.shape, 2) for part in held]
        + [per_head(pair_shape, 1)],
        out_specs=(per_head(row_shape, 1), per_head((devices, heads, 8, count), 1)),
        out_shape=(struct(row_shape, BF), struct((devices, heads, 8, count), F32)),
        compiler_params=params(),
        cost_estimate=cost(1e6, 1e6),
        name="global_stats",
    )(compact, *held, kv)

    stats = lax.all_to_all(stats, "ctx", 0, 0, tiled=True)

    sum_shape = (devices // 2, 2, heads, slots, width)
    sum_struct = struct(sum_shape, BF)
    extra, kept_ends, sent_ends = pl.pallas_call(
        functools.partial(global_kernel, scale, scale2),
        grid=(heads,),
        in_specs=[per_head(pair_shape, 1), per_head(row_shape, 1)]
        + [per_head(stats.shape, 1), whole(expand.shape)],
        out_specs=(per_head(pair_shape, 1), per_head(sum_shape, 2), per_head(sum_shape, 2)),
        out_shape=(struct(pair_shape, F32), sum_struct, sum_struct),
        compiler_params=params(),
        cost_estimate=cost(1e6, 1e6),
        name="global_queries",
    )(kv, rows, stats, expand)
    got_ends = from_near(sent_ends)
    qd_late = after(qd, (kv_near, kv_far, sent_ends))
    qd_far, qd_near = from_far(qd_late), from_near(qd_late)

    out, log_dot, dq, dkv, kept_sums, sent_sums = pl.pallas_call(
        functools.partial(local_kernel, scale, scale2),
        grid=(heads,),
        in_specs=[per_head(pair_shape, 1)] * 4
        + [per_head(row_shape, 1), whole(bias.shape), whole(expand.shape)]
        + [per_head(pair_shape, 1)],
        out_specs=(
            per_head((heads, toks, width), 0),
            per_head((heads, 2, toks), 0),
            per_head((heads, toks, width), 0),
            per_head(pair_shape, 1),
            per_head(sum_shape, 2),
            per_head(sum_shape, 2),
        ),
        out_shape=(
            struct((heads, toks, width), BF),
            struct((heads, 2, toks), F32),
            struct((heads, toks, width), F32),
            struct(pair_shape, F32),
            sum_struct,
            sum_struct,
        ),
        scratch_shapes=[
            pltpu.VMEM((span + count, width), BF),
            pltpu.VMEM((span + count, width), BF),
            pltpu.VMEM((toks // TILE, 2 * HALF + TILE + count, TILE), F32),
            pltpu.VMEM((span + count, toks), BF),
            pltpu.VMEM((span + count, toks), BF),
        ],
        compiler_params=params(),
        cost_estimate=cost(1e6, 1e6),
        name="local",
    )(qd, kv, kv_near, kv_far, rows, bias, expand, extra)
    log_far, log_near = from_far(log_dot), from_near(log_dot)

    got_sums = from_near(sent_sums)

    first = stages[0]
    parts = pl.pallas_call(
        fold_kernel,
        out_shape=[struct((4, heads, slots, width), BF)] * (devices // 2),
        compiler_params=params(),
        name="fold",
    )(kept_ends, got_ends, kept_sums, after(got_sums, (qd_near, qd_far)))
    for stage in reversed(stages[1:-1]):
        size = len(parts) // (len(stage) + 1)
        kept = parts[:size]
        for number, mask in enumerate(stage):
            sent = parts[(number + 1) * size : (number + 2) * size]
            kept = [one + swap(other, mask) for one, other in zip(kept, sent)]
        parts = kept
    sent = after(parts[1:], (log_near, log_far))
    parts = [parts[0]] + [swap(part, mask) for part, mask in zip(sent, first)]

    dkv = pl.pallas_call(
        functools.partial(rim_kernel, scale, scale2),
        grid=(heads,),
        in_specs=[per_head(pair_shape, 1), whole(bias.shape)]
        + [per_head(pair_shape, 1)] * 2
        + [per_head(log_dot.shape, 0)] * 2
        + [per_head(pair_shape, 1)],
        out_specs=per_head(pair_shape, 1),
        out_shape=struct(pair_shape, F32),
        scratch_shapes=[
            pltpu.VMEM((2 * toks, width), BF),
            pltpu.VMEM((2 * toks, width), BF),
            pltpu.VMEM((2, 2, toks), F32),
            pltpu.VMEM((toks, toks + TILE), BF),
            pltpu.VMEM((toks, toks + TILE), BF),
        ],
        compiler_params=params(),
        cost_estimate=cost(1e6, 1e6),
        name="rim",
    )(kv, bias, qd_near, qd_far, log_near, log_far, dkv)

    flat_shape = (toks * heads, width)
    steps = 2
    outs = pl.pallas_call(
        functools.partial(final_kernel, len(parts)),
        grid=(steps,),
        in_specs=[
            pl.BlockSpec((toks // steps, slots), lambda i: (i, 0)),
            pl.BlockSpec((heads, toks // steps, width), lambda i: (0, i, 0)),
            pl.BlockSpec((heads, toks // steps, width), lambda i: (0, i, 0)),
            pl.BlockSpec((2, heads, toks // steps, width), lambda i: (0, 0, i, 0)),
        ]
        + [whole((4, heads, slots, width))] * len(parts),
        out_specs=[pl.BlockSpec((toks * heads // steps, width), lambda i: (i, 0))] * 4,
        out_shape=[struct(flat_shape, kind) for kind in (BF, F32, F32, F32)],
        scratch_shapes=[pltpu.VMEM((toks * heads // steps, width), F32)],
        compiler_params=params(),
        name="final",
    )(place, out, dq, dkv, *parts)
    return tuple(x.reshape(toks, heads, width) for x in outs)


def solution(mesh):
    spec = P("ctx", "head", None)
    return jax.shard_map(
        shards,
        mesh=mesh,
        in_specs=(spec, spec, spec, spec, P()),
        out_specs=(spec, spec, spec, spec),
        check_vma=False,
    )
```

```python
import functools
import math

import jax
import jax.numpy as jnp
from jax import lax
from jax.experimental import pallas as pl
from jax.experimental.pallas import tpu as pltpu
from jax.sharding import PartitionSpec as P

HALF = 512
TILE = 256
NEG = -1e30
LOG2E = 1.0 / math.log(2.0)
VMEM_BYTES = 63 * 1024 * 1024
BF = jnp.bfloat16
F32 = jnp.float32


def nt(a, b):
    return lax.dot_general(a, b, (((1,), (1,)), ((), ())), preferred_element_type=F32)


def nn(a, b):
    return lax.dot_general(a, b, (((1,), (0,)), ((), ())), preferred_element_type=F32)


def wide(column, width):
    return jnp.concatenate([column] * (width // column.shape[1]), axis=1)


def iota(shape, dim):
    return lax.broadcasted_iota(jnp.int32, shape, dim)


def params():
    return pltpu.CompilerParams(vmem_limit_bytes=VMEM_BYTES)


def as_column(row):
    return jnp.broadcast_to(row, (128, row.shape[1])).T[:, :1]


def pack_keys_kernel(heads, k, v, kv, wide_rows):
    toks = k.shape[0] // heads
    for number, source in enumerate((k, v)):
        wide_rows[number] = source[...].astype(F32)
        for head in range(heads):
            kv[number, head] = wide_rows[number, pl.ds(head, toks, stride=heads), :].astype(BF)


def pack_queries_kernel(heads, slots, q, g, kv, pos_row, qd, slot_rows, wide_rows, acc):
    step = pl.program_id(0)
    toks = q.shape[0] // heads
    row = pos_row[...]
    count = row.shape[1]
    base = lax.axis_index("ctx") * (toks * pl.num_programs(0))
    column = as_column(row)
    tok = iota((count, toks), 1) + (base + step * toks)
    hit = jnp.sum((column == tok).astype(F32), axis=0, keepdims=True)
    rank = jnp.sum(((column >= base) & (column < tok)).astype(F32), axis=0, keepdims=True)
    slot = iota((slots, toks), 0).astype(F32)
    pick = jnp.where((hit > 0) & (rank == slot), 1.0, 0.0).astype(BF)
    tok = iota((toks, count), 0) + (base + step * toks)
    hit_column = jnp.sum((row == tok).astype(F32), axis=1, keepdims=True)
    tables = [[], [kv[0, h] for h in range(heads)], [kv[1, h] for h in range(heads)], []]
    for number, source in ((0, q), (3, g)):
        wide_rows[number // 3] = source[...].astype(F32)
        for head in range(heads):
            rows = wide_rows[number // 3, pl.ds(head, toks, stride=heads), :]
            tables[number].append(rows.astype(BF))
            if number == 0:
                qd[0, head] = rows.astype(BF)
            else:
                qd[1, head] = jnp.where(hit_column > 0, 0.0, rows).astype(BF)
    for number in range(4):
        found = nn(pick, jnp.concatenate(tables[number], axis=1))
        for head in range(heads):
            part = found[:, head * 128 : (head + 1) * 128]
            acc[number, head] = jnp.where(step == 0, part, acc[number, head] + part)

    @pl.when(step == pl.num_programs(0) - 1)
    def _():
        slot_rows[...] = acc[...].astype(BF)


def owner_map(column, owner, toks, slots, shape):
    inside = jnp.sum((column < owner * toks).astype(jnp.int32), axis=0, keepdims=True)
    held = jnp.sum((column < (owner + 1) * toks).astype(jnp.int32), axis=0, keepdims=True) - inside
    slot = iota(shape, 1) % slots
    hot = (iota(shape, 0) == inside + slot) & (slot < held)
    return jnp.where(hot, 1.0, 0.0).astype(BF)


def mask_kernel(order, slots, seq_rows, pos_row, bias, compact, expand, place):
    toks = place.shape[0]
    me = lax.axis_index("ctx")
    base = me * toks
    row = pos_row[...]
    count = row.shape[1]
    column = as_column(row)
    for start in range(0, bias.shape[0], TILE):
        key = iota((TILE, count), 0) + (base - HALF + start)
        hits = jnp.sum((row == key).astype(F32), axis=1, keepdims=True)
        key = key[:, :1]
        out = (hits > 0) | (key < 0) | (key >= seq_rows)
        bias[start : start + TILE, :] = jnp.broadcast_to(jnp.where(out, NEG, 0.0), (TILE, 128))
    tok = iota((toks, count), 0) + base
    hit = jnp.sum((row == tok).astype(F32), axis=1, keepdims=True)
    rank = jnp.sum(((row >= base) & (row < tok)).astype(F32), axis=1, keepdims=True)
    slot = iota((toks, slots), 1).astype(F32)
    place[...] = jnp.where((hit > 0) & (rank == slot), 1.0, 0.0).astype(BF)
    part = iota((1, compact.shape[1]), 1) // slots
    owner = jnp.zeros_like(part)
    for number, relative in enumerate(order):
        owner = jnp.where(part == number, me ^ relative, owner)
    compact[...] = owner_map(column, owner, toks, slots, compact.shape)
    expand[...] = compact[...].astype(F32).T.astype(BF)


def stats_kernel(scale2, compact, *refs):
    parts, (kv, rows, stats) = refs[:-3], refs[-3:]
    pieces = []
    for part in parts:
        for i in range(part.shape[0]):
            pieces.append(jnp.concatenate([part[i, number, 0] for number in range(4)], axis=1))
    packed = nn(compact[...], jnp.concatenate(pieces, axis=0)).astype(BF)
    width = kv.shape[3]
    table = [packed[:, number * width : (number + 1) * width] for number in range(4)]
    for number in range(4):
        rows[number, 0] = table[number]
    queries, _, _, grads = table
    scores = nt(kv[0, 0], queries) * scale2
    top = jnp.max(scores, axis=0, keepdims=True)
    weights = jnp.exp2(scores - top)
    total = jnp.sum(weights, axis=0, keepdims=True)
    dot = jnp.sum(weights * nt(kv[1, 0], grads), axis=0, keepdims=True)
    line = iota(stats.shape[2:], 0)
    found = jnp.where(line == 0, top, jnp.where(line == 1, total, dot))
    for device in range(stats.shape[0]):
        stats[device, 0] = found


def band(scores, low):
    rows, columns = iota(scores.shape, 0), iota(scores.shape, 1)
    return jnp.where(rows <= columns if low else rows >= columns, scores, NEG)


def put_in_slots(expand, tables, kept, sent):
    owners, kinds, _, slots, width = kept.shape
    spread = nn(expand, jnp.concatenate(tables, axis=1)).astype(BF)
    for owner in range(2 * owners):
        for kind in range(kinds):
            (kept if owner < owners else sent)[owner % owners, kind, 0] = spread[
                owner * slots : (owner + 1) * slots, kind * width : (kind + 1) * width
            ]


def fold_kernel(kept_ends, got_ends, kept_sums, got_sums, *outs):
    for part, out in enumerate(outs):
        out[0:2] = (kept_ends[part].astype(F32) + got_ends[part].astype(F32)).astype(BF)
        out[2:4] = (kept_sums[part].astype(F32) + got_sums[part].astype(F32)).astype(BF)


def global_kernel(scale, scale2, kv, rows, stats, expand, before, dkv, kept, sent):
    g_query, g_grad = rows[0, 0], rows[3, 0]
    tops = stats[:, 0, 0:1, :]
    top = jnp.max(tops, axis=0)
    factor = jnp.exp2(tops - top[None])
    total = jnp.sum(stats[:, 0, 1:2, :] * factor, axis=0)
    g_dot = jnp.sum(stats[:, 0, 2:3, :] * factor, axis=0) / total
    g_log = top + jnp.log2(total)
    weights = jnp.exp2(nt(kv[0, 0], g_query) * scale2 - g_log)
    narrow = weights.astype(BF)
    slopes = (weights * (nt(kv[1, 0], g_grad) - g_dot)).astype(BF)
    dkv[0, 0] = before[0, 0] + nn(slopes, g_query) * scale
    dkv[1, 0] = before[1, 0] + nn(narrow, g_grad)
    out = nn(kv[1, 0].T, narrow).T.astype(BF)
    dq = (nn(kv[0, 0].T, slopes) * scale).T.astype(BF)
    put_in_slots(expand[...], (out, dq), kept, sent)


def local_kernel(
    scale, scale2, qd, kv, kv_near, kv_far, rows, bias, expand,
    out, log_dot, dq, dkv, kept, sent, keys, values, score_buf, probs, slopes,
):
    toks = kv.shape[2]
    reach = 2 * HALF + TILE
    span = keys.shape[0] - rows.shape[2]
    near = 2 * (1 - lax.axis_index("ctx") % 2)
    for block, place in ((kv_near, near), (kv, 1), (kv_far, 2 - near)):
        spot = pl.ds(pl.multiple_of(place * toks, toks), toks)
        keys[spot, :] = block[0, 0]
        values[spot, :] = block[1, 0]
    keys[span:, :] = rows[1, 0]
    values[span:, :] = rows[2, 0]
    key_t, value_t = keys[...].T, values[...].T
    query_t, grad_t = qd[0, 0].T, qd[1, 0].T
    tiles = range(toks // TILE)
    lanes = [slice(tile * TILE, (tile + 1) * TILE) for tile in tiles]
    windows = [slice(tile * TILE, tile * TILE + reach) for tile in tiles]
    starts = [
        list(range(tile * TILE, tile * TILE + reach, TILE)) + list(range(span, keys.shape[0], TILE))
        for tile in tiles
    ]
    best, top, total, scaled, dots = ([None] * len(tiles) for _ in range(5))

    def score(tile, piece):
        start = starts[tile][piece]
        scores = nn(keys[start : start + TILE, :], query_t[:, lanes[tile]]) * scale2
        if start < span:
            scores = scores + wide(bias[start : start + TILE, :], TILE)
        if piece == 0:
            scores = band(scores, False)
        elif piece == reach // TILE - 1:
            scores = band(scores, True)
        score_buf[tile, piece * TILE : (piece + 1) * TILE, :] = scores
        part = jnp.max(scores.reshape(TILE // 8, 8, TILE), axis=0)
        best[tile] = part if best[tile] is None else jnp.maximum(best[tile], part)

    def weigh(tile, piece):
        if top[tile] is None:
            top[tile] = jnp.max(best[tile], axis=0, keepdims=True)
        start = starts[tile][piece]
        weights = jnp.exp2(score_buf[tile, piece * TILE : (piece + 1) * TILE, :] - top[tile])
        probs[start : start + TILE, lanes[tile]] = weights.astype(BF)
        part = jnp.sum(weights.reshape(TILE // 8, 8, TILE), axis=0)
        total[tile] = part if total[tile] is None else total[tile] + part

    def attend(tile):
        whole_sum = jnp.sum(total[tile], axis=0, keepdims=True)
        inverse = 1.0 / whole_sum
        grads = grad_t[:, lanes[tile]].astype(F32)
        acc = nn(value_t[:, windows[tile]], probs[windows[tile], lanes[tile]])
        acc = (acc + nn(value_t[:, span:], probs[span:, lanes[tile]])) * inverse
        dot = jnp.sum(grads * acc, axis=0, keepdims=True)
        log_dot[0, 0:1, lanes[tile]] = top[tile] + jnp.log2(whole_sum)
        log_dot[0, 1:2, lanes[tile]] = dot
        out[0, lanes[tile], :] = acc.T.astype(BF)
        scaled[tile] = (grads * inverse).astype(BF)
        dots[tile] = dot * inverse

    def slope(tile, piece):
        start = starts[tile][piece]
        rise = nn(values[start : start + TILE, :], scaled[tile]) - dots[tile]
        weights = probs[start : start + TILE, lanes[tile]].astype(F32)
        slopes[start : start + TILE, lanes[tile]] = (weights * rise).astype(BF)

    def query_gradient(tile):
        acc = nn(key_t[:, windows[tile]], slopes[windows[tile], lanes[tile]])
        acc = acc + nn(key_t[:, span:], slopes[span:, lanes[tile]])
        dq[0, lanes[tile], :] = (acc * scale).T

    for step in range(len(tiles) + 2):
        for piece in range(len(starts[0])):
            if 0 <= step - 2:
                slope(step - 2, piece)
            if 0 <= step - 1 < len(tiles):
                weigh(step - 1, piece)
            if step < len(tiles):
                score(step, piece)
        if 0 <= step - 2:
            query_gradient(step - 2)
        if 0 <= step - 1 < len(tiles):
            attend(step - 1)
    own = slice(HALF, HALF + toks)
    grads = jnp.concatenate(scaled, axis=1)
    dkv[0, 0] = (nt(query_t, slopes[own, :]) * scale).T
    dkv[1, 0] = nt(grads, probs[own, :]).T
    g_dk = (nt(query_t, slopes[span:, :]) * scale).T.astype(BF)
    g_dv = nt(grads, probs[span:, :]).T.astype(BF)
    put_in_slots(expand[...], (g_dk, g_dv), kept, sent)


def rim_kernel(
    scale, scale2, kv, bias, qd_near, qd_far, log_near, log_far, partial, dkv,
    queries, grads, logs, probs, slopes,
):
    toks = kv.shape[2]
    reach = toks + TILE
    near = 1 - lax.axis_index("ctx") % 2
    for qd, log_dot, place in ((qd_near, log_near, near), (qd_far, log_far, 1 - near)):
        spot = pl.ds(pl.multiple_of(place * toks, toks), toks)
        queries[spot, :] = qd[0, 0]
        grads[spot, :] = qd[1, 0]
        logs[place] = log_dot[0]
    for k_tile in range(toks // TILE):
        span = slice(k_tile * TILE, (k_tile + 1) * TILE)
        key = kv[0, 0, span, :]
        value = kv[1, 0, span, :]
        key_bias = wide(bias[HALF + k_tile * TILE : HALF + (k_tile + 1) * TILE, :], TILE)
        for piece in range(reach // TILE):
            start = (k_tile + piece) * TILE
            side, lanes = start // toks, slice(start % toks, start % toks + TILE)
            scores = nt(key, queries[start : start + TILE, :]) * scale2 + key_bias
            if piece == 0:
                scores = band(scores, True)
            elif piece == reach // TILE - 1:
                scores = band(scores, False)
            weights = jnp.exp2(scores - logs[side, 0:1, lanes])
            slope = weights * (nt(value, grads[start : start + TILE, :]) - logs[side, 1:2, lanes])
            spot = slice(piece * TILE, (piece + 1) * TILE)
            probs[span, spot] = weights.astype(BF)
            slopes[span, spot] = slope.astype(BF)
        window = slice(k_tile * TILE, k_tile * TILE + reach)
        dkv[0, 0, span, :] = partial[0, 0, span, :] + nn(slopes[span, :], queries[window, :]) * scale
        dkv[1, 0, span, :] = partial[1, 0, span, :] + nn(probs[span, :], grads[window, :])


def final_kernel(
    sources, place, out, dq, dkv, *refs
):
    parts, refs = refs[:sources], refs[sources:]
    attn, query_grad, key_grad, value_grad, wide_rows = refs
    heads, toks = out.shape[0], out.shape[1]
    hot = place[...]
    is_global = jnp.sum(hot.astype(F32), axis=1, keepdims=True) > 0
    for head in range(heads):
        rows = pl.ds(head, toks, stride=heads)
        tables = []
        for kind in range(4):
            table = parts[0][kind, head].astype(F32)
            for part in parts[1:]:
                table = table + part[kind, head].astype(F32)
            tables.append(table.astype(BF))
        width = out.shape[2]
        added = nn(hot, jnp.concatenate(tables, axis=1))
        added = [added[:, i * width : (i + 1) * width] for i in range(4)]
        wide_rows[rows, :] = jnp.where(is_global, added[0], out[head].astype(F32))
        query_grad[rows, :] = dq[head] + added[1]
        key_grad[rows, :] = dkv[0, head] + added[2]
        value_grad[rows, :] = dkv[1, head] + added[3]
    attn[...] = wide_rows[...].astype(BF)


def cost(flops, moved, exps=0):
    return pl.CostEstimate(flops=int(flops), bytes_accessed=int(moved), transcendentals=int(exps))


def struct(shape, dtype):
    return jax.ShapeDtypeStruct(shape, dtype)


def whole(shape):
    return pl.BlockSpec(shape, lambda head: (0,) * len(shape))


def per_head(shape, dim, first=0):
    block = tuple(1 if i == dim else size for i, size in enumerate(shape))
    return pl.BlockSpec(
        block, lambda head: tuple(head + first if i == dim else 0 for i in range(len(shape)))
    )


def shards(query_rows, key_rows, value_rows, out_grad, global_pos):
    toks, heads, width = query_rows.shape
    count = global_pos.shape[0]
    devices = lax.axis_size("ctx")
    slots = max(16, 2 * count // devices)
    scale = width ** (-0.5)
    scale2 = scale * LOG2E
    bits = devices.bit_length() - 1
    stages = [
        [mask << low for mask in range(1, 1 << min(2, bits - low))] for low in range(1, bits, 2)
    ] + [[1]]
    order = [0]
    for stage in stages:
        order = order + [one ^ mask for mask in stage for one in order]
    pos_row = global_pos.reshape(1, count)
    q_flat, k_flat, v_flat, g_flat = (
        x.reshape(toks * heads, width) for x in (query_rows, key_rows, value_rows, out_grad)
    )

    def swap(value, mask):
        return lax.ppermute(value, "ctx", [(i, i ^ mask) for i in range(devices)])

    def from_near(value):
        return swap(value, 1)

    def from_far(value):
        pairs = [(i, i + 1) for i in range(1, devices - 1, 2)]
        return lax.ppermute(value, "ctx", pairs + [(j, i) for i, j in pairs])

    def after(value, earlier):
        return lax.optimization_barrier((value, earlier))[0]

    pair_shape = (2, heads, toks, width)
    slot_shape = (4, heads, slots, width)
    steps = 1
    flat_spec = pl.BlockSpec((toks * heads // steps, width), lambda i: (i, 0))
    pair_spec = pl.BlockSpec((2, heads, toks // steps, width), lambda i: (0, 0, i, 0))
    wide_pair = pltpu.VMEM((2, toks * heads // steps, width), F32)
    kv = pl.pallas_call(
        functools.partial(pack_keys_kernel, heads),
        out_shape=struct(pair_shape, BF),
        scratch_shapes=[wide_pair],
        compiler_params=params(),
        name="pack_keys",
    )(k_flat, v_flat)

    qd, slot_rows = pl.pallas_call(
        functools.partial(pack_queries_kernel, heads, slots),
        grid=(steps,),
        in_specs=[flat_spec, flat_spec, pair_spec, whole((1, count))],
        out_specs=(pair_spec, whole(slot_shape)),
        out_shape=(struct(pair_shape, BF), struct(slot_shape, BF)),
        scratch_shapes=[wide_pair, pltpu.VMEM(slot_shape, F32)],
        compiler_params=params(),
        name="pack_queries",
    )(q_flat, g_flat, kv, pos_row)

    span = toks + 2 * HALF
    bias, compact, expand, place = pl.pallas_call(
        functools.partial(mask_kernel, order, slots, toks * devices),
        out_shape=(
            struct((span, 128), F32),
            struct((count, devices * slots), BF),
            struct((devices * slots, count), BF),
            struct((toks, slots), BF),
        ),
        compiler_params=params(),
        name="masks",
    )(pos_row)

    held = [slot_rows[None]]
    for number, stage in enumerate(stages):
        send = jnp.concatenate(after(held, place), axis=0) if number else held[0]
        held += [swap(send, mask) for mask in stage]
        if not number:
            kv_late = after(kv, held)
            kv_far, kv_near = from_far(kv_late), from_near(kv_late)

    row_shape = (4, heads, count, width)
    rows, stats = pl.pallas_call(
        functools.partial(stats_kernel, scale2),
        grid=(heads,),
        in_specs=[whole(compact.shape)]
        + [per_head(part.shape, 2) for part in held]
        + [per_head(pair_shape, 1)],
        out_specs=(per_head(row_shape, 1), per_head((devices, heads, 8, count), 1)),
        out_shape=(struct(row_shape, BF), struct((devices, heads, 8, count), F32)),
        compiler_params=params(),
        cost_estimate=cost(1e6, 1e6),
        name="global_stats",
    )(compact, *held, kv)

    stats = lax.all_to_all(stats, "ctx", 0, 0, tiled=True)

    sum_shape = (devices // 2, 2, heads, slots, width)
    sum_struct = struct(sum_shape, BF)
    qd_late = after(qd, (kv_near, kv_far, rows))
    qd_far, qd_near = from_far(qd_late), from_near(qd_late)

    out, log_dot, dq, dkv, kept_sums, sent_sums = pl.pallas_call(
        functools.partial(local_kernel, scale, scale2),
        grid=(heads,),
        in_specs=[per_head(pair_shape, 1)] * 4
        + [per_head(row_shape, 1), whole(bias.shape), whole(expand.shape)],
        out_specs=(
            per_head((heads, toks, width), 0),
            per_head((heads, 2, toks), 0),
            per_head((heads, toks, width), 0),
            per_head(pair_shape, 1),
            per_head(sum_shape, 2),
            per_head(sum_shape, 2),
        ),
        out_shape=(
            struct((heads, toks, width), BF),
            struct((heads, 2, toks), F32),
            struct((heads, toks, width), F32),
            struct(pair_shape, F32),
            sum_struct,
            sum_struct,
        ),
        scratch_shapes=[
            pltpu.VMEM((span + count, width), BF),
            pltpu.VMEM((span + count, width), BF),
            pltpu.VMEM((toks // TILE, 2 * HALF + TILE + count, TILE), F32),
            pltpu.VMEM((span + count, toks), BF),
            pltpu.VMEM((span + count, toks), BF),
        ],
        compiler_params=params(),
        cost_estimate=cost(1e6, 1e6),
        name="local",
    )(qd, kv, kv_near, kv_far, rows, bias, expand)
    log_far, log_near = from_far(log_dot), from_near(log_dot)

    dkv, kept_ends, sent_ends = pl.pallas_call(
        functools.partial(global_kernel, scale, scale2),
        grid=(heads,),
        in_specs=[per_head(pair_shape, 1), per_head(row_shape, 1)]
        + [per_head(stats.shape, 1), whole(expand.shape), per_head(pair_shape, 1)],
        out_specs=(per_head(pair_shape, 1), per_head(sum_shape, 2), per_head(sum_shape, 2)),
        out_shape=(struct(pair_shape, F32), sum_struct, sum_struct),
        input_output_aliases={4: 0},
        compiler_params=params(),
        cost_estimate=cost(1e6, 1e6),
        name="global_queries",
    )(kv, rows, after(stats, (log_dot, qd_near, qd_far)), expand, dkv)
    got_sums = from_near(sent_sums)
    got_ends = from_near(after(sent_ends, (log_near, log_far)))

    first = stages[0]
    parts = pl.pallas_call(
        fold_kernel,
        grid=(heads,),
        in_specs=[per_head(sum_shape, 2)] * 4,
        out_specs=[per_head((4, heads, slots, width), 1)] * (devices // 2),
        out_shape=[struct((4, heads, slots, width), BF)] * (devices // 2),
        compiler_params=params(),
        name="fold",
    )(kept_ends, got_ends, kept_sums, got_sums)
    for stage in reversed(stages[1:-1]):
        size = len(parts) // (len(stage) + 1)
        kept = parts[:size]
        for number, mask in enumerate(stage):
            sent = parts[(number + 1) * size : (number + 2) * size]
            kept = [one + swap(other, mask) for one, other in zip(kept, sent)]
        parts = kept
    parts = [parts[0]] + [swap(part, mask) for part, mask in zip(parts[1:], first)]

    dkv = pl.pallas_call(
        functools.partial(rim_kernel, scale, scale2),
        grid=(heads,),
        in_specs=[per_head(pair_shape, 1), whole(bias.shape)]
        + [per_head(pair_shape, 1)] * 2
        + [per_head(log_dot.shape, 0)] * 2
        + [per_head(pair_shape, 1)],
        out_specs=per_head(pair_shape, 1),
        out_shape=struct(pair_shape, F32),
        scratch_shapes=[
            pltpu.VMEM((2 * toks, width), BF),
            pltpu.VMEM((2 * toks, width), BF),
            pltpu.VMEM((2, 2, toks), F32),
            pltpu.VMEM((toks, toks + TILE), BF),
            pltpu.VMEM((toks, toks + TILE), BF),
        ],
        compiler_params=params(),
        cost_estimate=cost(1e6, 1e6),
        name="rim",
    )(kv, bias, qd_near, qd_far, log_near, log_far, dkv)

    flat_shape = (toks * heads, width)
    steps = 2
    outs = pl.pallas_call(
        functools.partial(final_kernel, len(parts)),
        grid=(steps,),
        in_specs=[
            pl.BlockSpec((toks // steps, slots), lambda i: (i, 0)),
            pl.BlockSpec((heads, toks // steps, width), lambda i: (0, i, 0)),
            pl.BlockSpec((heads, toks // steps, width), lambda i: (0, i, 0)),
            pl.BlockSpec((2, heads, toks // steps, width), lambda i: (0, 0, i, 0)),
        ]
        + [whole((4, heads, slots, width))] * len(parts),
        out_specs=[pl.BlockSpec((toks * heads // steps, width), lambda i: (i, 0))] * 4,
        out_shape=[struct(flat_shape, kind) for kind in (BF, F32, F32, F32)],
        scratch_shapes=[pltpu.VMEM((toks * heads // steps, width), F32)],
        compiler_params=params(),
        name="final",
    )(place, out, dq, dkv, *parts)
    return tuple(x.reshape(toks, heads, width) for x in outs)


def solution(mesh):
    spec = P("ctx", "head", None)
    return jax.shard_map(
        shards,
        mesh=mesh,
        in_specs=(spec, spec, spec, spec, P()),
        out_specs=(spec, spec, spec, spec),
        check_vma=False,
    )
```

```python
import functools
import math

import jax
import jax.numpy as jnp
from jax import lax
from jax.experimental import pallas as pl
from jax.experimental.pallas import tpu as pltpu
from jax.sharding import PartitionSpec as P

HALF = 512
TILE = 256
NEG = -1e30
LOG2E = 1.0 / math.log(2.0)
VMEM_BYTES = 63 * 1024 * 1024
BF = jnp.bfloat16
F32 = jnp.float32


def nt(a, b):
    return lax.dot_general(a, b, (((1,), (1,)), ((), ())), preferred_element_type=F32)


def nn(a, b):
    return lax.dot_general(a, b, (((1,), (0,)), ((), ())), preferred_element_type=F32)


def wide(column, width):
    return jnp.concatenate([column] * (width // column.shape[1]), axis=1)


def iota(shape, dim):
    return lax.broadcasted_iota(jnp.int32, shape, dim)


def params():
    return pltpu.CompilerParams(vmem_limit_bytes=VMEM_BYTES)


def as_column(row):
    return jnp.broadcast_to(row, (128, row.shape[1])).T[:, :1]


def pack_keys_kernel(heads, k, v, kv, wide_rows):
    toks = k.shape[0] // heads
    for number, source in enumerate((k, v)):
        wide_rows[number] = source[...].astype(F32)
        for head in range(heads):
            kv[number, head] = wide_rows[number, pl.ds(head, toks, stride=heads), :].astype(BF)


def pack_queries_kernel(heads, slots, q, g, kv, pos_row, qd, slot_rows, wide_rows, acc):
    step = pl.program_id(0)
    toks = q.shape[0] // heads
    row = pos_row[...]
    count = row.shape[1]
    base = lax.axis_index("ctx") * (toks * pl.num_programs(0))
    column = as_column(row)
    tok = iota((count, toks), 1) + (base + step * toks)
    hit = jnp.sum((column == tok).astype(F32), axis=0, keepdims=True)
    rank = jnp.sum(((column >= base) & (column < tok)).astype(F32), axis=0, keepdims=True)
    slot = iota((slots, toks), 0).astype(F32)
    pick = jnp.where((hit > 0) & (rank == slot), 1.0, 0.0).astype(BF)
    tok = iota((toks, count), 0) + (base + step * toks)
    hit_column = jnp.sum((row == tok).astype(F32), axis=1, keepdims=True)
    tables = [[], [kv[0, h] for h in range(heads)], [kv[1, h] for h in range(heads)], []]
    for number, source in ((0, q), (3, g)):
        wide_rows[number // 3] = source[...].astype(F32)
        for head in range(heads):
            rows = wide_rows[number // 3, pl.ds(head, toks, stride=heads), :]
            tables[number].append(rows.astype(BF))
            if number == 0:
                qd[0, head] = rows.astype(BF)
            else:
                qd[1, head] = jnp.where(hit_column > 0, 0.0, rows).astype(BF)
    for number in range(4):
        found = nn(pick, jnp.concatenate(tables[number], axis=1))
        for head in range(heads):
            part = found[:, head * 128 : (head + 1) * 128]
            acc[number, head] = jnp.where(step == 0, part, acc[number, head] + part)

    @pl.when(step == pl.num_programs(0) - 1)
    def _():
        slot_rows[...] = acc[...].astype(BF)


def owner_map(column, owner, toks, slots, shape):
    inside = jnp.sum((column < owner * toks).astype(jnp.int32), axis=0, keepdims=True)
    held = jnp.sum((column < (owner + 1) * toks).astype(jnp.int32), axis=0, keepdims=True) - inside
    slot = iota(shape, 1) % slots
    hot = (iota(shape, 0) == inside + slot) & (slot < held)
    return jnp.where(hot, 1.0, 0.0).astype(BF)


def mask_kernel(order, slots, seq_rows, pos_row, bias, compact, expand, place):
    toks = place.shape[0]
    me = lax.axis_index("ctx")
    base = me * toks
    row = pos_row[...]
    count = row.shape[1]
    column = as_column(row)
    for start in range(0, bias.shape[0], TILE):
        key = iota((TILE, count), 0) + (base - HALF + start)
        hits = jnp.sum((row == key).astype(F32), axis=1, keepdims=True)
        key = key[:, :1]
        out = (hits > 0) | (key < 0) | (key >= seq_rows)
        bias[start : start + TILE, :] = jnp.broadcast_to(jnp.where(out, NEG, 0.0), (TILE, 128))
    tok = iota((toks, count), 0) + base
    hit = jnp.sum((row == tok).astype(F32), axis=1, keepdims=True)
    rank = jnp.sum(((row >= base) & (row < tok)).astype(F32), axis=1, keepdims=True)
    slot = iota((toks, slots), 1).astype(F32)
    place[...] = jnp.where((hit > 0) & (rank == slot), 1.0, 0.0).astype(BF)
    part = iota((1, compact.shape[1]), 1) // slots
    owner = jnp.zeros_like(part)
    for number, relative in enumerate(order):
        owner = jnp.where(part == number, me ^ relative, owner)
    compact[...] = owner_map(column, owner, toks, slots, compact.shape)
    expand[...] = compact[...].astype(F32).T.astype(BF)


def stats_kernel(scale2, compact, *refs):
    parts, (kv, rows, stats) = refs[:-3], refs[-3:]
    pieces = []
    for part in parts:
        for i in range(part.shape[0]):
            pieces.append(jnp.concatenate([part[i, number, 0] for number in range(4)], axis=1))
    packed = nn(compact[...], jnp.concatenate(pieces, axis=0)).astype(BF)
    width = kv.shape[3]
    table = [packed[:, number * width : (number + 1) * width] for number in range(4)]
    for number in range(4):
        rows[number, 0] = table[number]
    queries, _, _, grads = table
    scores = nt(kv[0, 0], queries) * scale2
    top = jnp.max(scores, axis=0, keepdims=True)
    weights = jnp.exp2(scores - top)
    total = jnp.sum(weights, axis=0, keepdims=True)
    dot = jnp.sum(weights * nt(kv[1, 0], grads), axis=0, keepdims=True)
    line = iota(stats.shape[2:], 0)
    found = jnp.where(line == 0, top, jnp.where(line == 1, total, dot))
    for device in range(stats.shape[0]):
        stats[device, 0] = found


def band(scores, low):
    rows, columns = iota(scores.shape, 0), iota(scores.shape, 1)
    return jnp.where(rows <= columns if low else rows >= columns, scores, NEG)


def put_in_slots(expand, tables, kept, sent):
    owners, kinds, _, slots, width = kept.shape
    spread = nn(expand, jnp.concatenate(tables, axis=1)).astype(BF)
    for owner in range(2 * owners):
        for kind in range(kinds):
            (kept if owner < owners else sent)[owner % owners, kind, 0] = spread[
                owner * slots : (owner + 1) * slots, kind * width : (kind + 1) * width
            ]


def fold_kernel(kept_ends, got_ends, kept_sums, got_sums, *outs):
    for part, out in enumerate(outs):
        out[0:2] = (kept_ends[part].astype(F32) + got_ends[part].astype(F32)).astype(BF)
        out[2:4] = (kept_sums[part].astype(F32) + got_sums[part].astype(F32)).astype(BF)


def global_kernel(scale, scale2, kv, rows, stats, expand, before, dkv, kept, sent):
    g_query, g_grad = rows[0, 0], rows[3, 0]
    tops = stats[:, 0, 0:1, :]
    top = jnp.max(tops, axis=0)
    factor = jnp.exp2(tops - top[None])
    total = jnp.sum(stats[:, 0, 1:2, :] * factor, axis=0)
    g_dot = jnp.sum(stats[:, 0, 2:3, :] * factor, axis=0) / total
    g_log = top + jnp.log2(total)
    weights = jnp.exp2(nt(kv[0, 0], g_query) * scale2 - g_log)
    narrow = weights.astype(BF)
    slopes = (weights * (nt(kv[1, 0], g_grad) - g_dot)).astype(BF)
    dkv[0, 0] = before[0, 0] + nn(slopes, g_query) * scale
    dkv[1, 0] = before[1, 0] + nn(narrow, g_grad)
    out = nn(kv[1, 0].T, narrow).T.astype(BF)
    dq = (nn(kv[0, 0].T, slopes) * scale).T.astype(BF)
    put_in_slots(expand[...], (out, dq), kept, sent)


def gather_window(kv, kv_near, kv_far, number, buf):
    toks = kv.shape[2]
    near = 2 * (1 - lax.axis_index("ctx") % 2)
    for block, place in ((kv_near, near), (kv, 1), (kv_far, 2 - near)):
        buf[pl.ds(pl.multiple_of(place * toks, toks), toks), :] = block[number, 0]


def window_kernel(
    scale2, qd, kv, kv_near, kv_far, bias, probs, acc, top_sum, keys, values, score_buf
):
    toks = kv.shape[2]
    reach = 2 * HALF + TILE
    gather_window(kv, kv_near, kv_far, 0, keys)
    gather_window(kv, kv_near, kv_far, 1, values)
    value_t = values[...].T
    query_t = qd[0, 0].T
    tiles = range(toks // TILE)
    lanes = [slice(tile * TILE, (tile + 1) * TILE) for tile in tiles]
    pieces = range(reach // TILE)
    best, top, total = ([None] * len(tiles) for _ in range(3))

    def score(tile, piece):
        span = slice((tile + piece) * TILE, (tile + piece + 1) * TILE)
        scores = nn(keys[span, :], query_t[:, lanes[tile]]) * scale2
        scores = scores + wide(bias[span, :], TILE)
        if piece == 0:
            scores = band(scores, False)
        elif piece == len(pieces) - 1:
            scores = band(scores, True)
        score_buf[tile, piece * TILE : (piece + 1) * TILE, :] = scores
        part = jnp.max(scores.reshape(TILE // 8, 8, TILE), axis=0)
        best[tile] = part if best[tile] is None else jnp.maximum(best[tile], part)

    def weigh(tile, piece):
        if top[tile] is None:
            top[tile] = jnp.max(best[tile], axis=0, keepdims=True)
        span = slice((tile + piece) * TILE, (tile + piece + 1) * TILE)
        weights = jnp.exp2(score_buf[tile, piece * TILE : (piece + 1) * TILE, :] - top[tile])
        probs[0, span, lanes[tile]] = weights.astype(BF)
        part = jnp.sum(weights.reshape(TILE // 8, 8, TILE), axis=0)
        total[tile] = part if total[tile] is None else total[tile] + part

    for step in range(len(tiles) + 1):
        for piece in pieces:
            if step:
                weigh(step - 1, piece)
            if step < len(tiles):
                score(step, piece)
        if step:
            tile = step - 1
            window = slice(tile * TILE, tile * TILE + reach)
            acc[0, :, lanes[tile]] = nn(value_t[:, window], probs[0, window, lanes[tile]])
            top_sum[0, 0:1, lanes[tile]] = top[tile]
            top_sum[0, 1:2, lanes[tile]] = jnp.sum(total[tile], axis=0, keepdims=True)


def local_kernel(
    scale, scale2, qd, kv, kv_near, kv_far, rows, probs, acc, top_sum, expand,
    out, log_dot, dq, dkv, kept, sent, keys, values, slopes,
):
    toks = kv.shape[2]
    reach = 2 * HALF + TILE
    gather_window(kv, kv_near, kv_far, 0, keys)
    gather_window(kv, kv_near, kv_far, 1, values)
    key_t = keys[...].T
    g_keys, g_values = rows[1, 0], rows[2, 0]
    g_key_t, g_value_t = g_keys.T, g_values.T
    query_t, grad_t = qd[0, 0].T, qd[1, 0].T
    grads = grad_t.astype(F32)
    scores = nn(g_keys, query_t) * scale2
    old = top_sum[0, 0:1, :]
    top = jnp.maximum(old, jnp.max(scores, axis=0, keepdims=True))
    weights = jnp.exp2(scores - top)
    factor = jnp.exp2(old - top)
    total = top_sum[0, 1:2, :] * factor + jnp.sum(weights, axis=0, keepdims=True)
    inverse = 1.0 / total
    g_probs = weights.astype(BF)
    result = (acc[0] * factor + nn(g_value_t, g_probs)) * inverse
    dot = jnp.sum(grads * result, axis=0, keepdims=True)
    log_dot[0, 0:1, :] = top + jnp.log2(total)
    log_dot[0, 1:2, :] = dot
    out[0] = result.T.astype(BF)
    share = factor * inverse
    g_grads = (grads * inverse).astype(BF)
    w_grads = (grads * share).astype(BF)
    g_slopes = (weights * (nn(g_values, g_grads) - dot * inverse)).astype(BF)
    dots = dot * share
    for tile in range(toks // TILE):
        lanes = slice(tile * TILE, (tile + 1) * TILE)
        for piece in range(reach // TILE):
            span = slice((tile + piece) * TILE, (tile + piece + 1) * TILE)
            rise = nn(values[span, :], w_grads[:, lanes]) - dots[:, lanes]
            slopes[span, lanes] = (probs[0, span, lanes].astype(F32) * rise).astype(BF)
    for tile in range(toks // TILE):
        lanes = slice(tile * TILE, (tile + 1) * TILE)
        window = slice(tile * TILE, tile * TILE + reach)
        part = nn(key_t[:, window], slopes[window, lanes]) + nn(g_key_t, g_slopes[:, lanes])
        dq[0, lanes, :] = (part * scale).T
    own = slice(HALF, HALF + toks)
    dkv[0, 0] = (nt(query_t, slopes[own, :]) * scale).T
    dkv[1, 0] = nt(w_grads, probs[0, own, :]).T
    g_dk = (nt(query_t, g_slopes) * scale).T.astype(BF)
    g_dv = nt(g_grads, g_probs).T.astype(BF)
    put_in_slots(expand[...], (g_dk, g_dv), kept, sent)


def rim_kernel(
    scale, scale2, kv, bias, qd_near, qd_far, log_near, log_far, partial, dkv,
    queries, grads, logs, probs, slopes,
):
    toks = kv.shape[2]
    reach = toks + TILE
    near = 1 - lax.axis_index("ctx") % 2
    for qd, log_dot, place in ((qd_near, log_near, near), (qd_far, log_far, 1 - near)):
        spot = pl.ds(pl.multiple_of(place * toks, toks), toks)
        queries[spot, :] = qd[0, 0]
        grads[spot, :] = qd[1, 0]
        logs[place] = log_dot[0]
    for k_tile in range(toks // TILE):
        span = slice(k_tile * TILE, (k_tile + 1) * TILE)
        key = kv[0, 0, span, :]
        value = kv[1, 0, span, :]
        key_bias = wide(bias[HALF + k_tile * TILE : HALF + (k_tile + 1) * TILE, :], TILE)
        for piece in range(reach // TILE):
            start = (k_tile + piece) * TILE
            side, lanes = start // toks, slice(start % toks, start % toks + TILE)
            scores = nt(key, queries[start : start + TILE, :]) * scale2 + key_bias
            if piece == 0:
                scores = band(scores, True)
            elif piece == reach // TILE - 1:
                scores = band(scores, False)
            weights = jnp.exp2(scores - logs[side, 0:1, lanes])
            slope = weights * (nt(value, grads[start : start + TILE, :]) - logs[side, 1:2, lanes])
            spot = slice(piece * TILE, (piece + 1) * TILE)
            probs[span, spot] = weights.astype(BF)
            slopes[span, spot] = slope.astype(BF)
        window = slice(k_tile * TILE, k_tile * TILE + reach)
        dkv[0, 0, span, :] = partial[0, 0, span, :] + nn(slopes[span, :], queries[window, :]) * scale
        dkv[1, 0, span, :] = partial[1, 0, span, :] + nn(probs[span, :], grads[window, :])


def final_kernel(
    sources, place, out, dq, dkv, *refs
):
    parts, refs = refs[:sources], refs[sources:]
    attn, query_grad, key_grad, value_grad, wide_rows = refs
    heads, toks = out.shape[0], out.shape[1]
    hot = place[...]
    is_global = jnp.sum(hot.astype(F32), axis=1, keepdims=True) > 0
    for head in range(heads):
        rows = pl.ds(head, toks, stride=heads)
        tables = []
        for kind in range(4):
            table = parts[0][kind, head].astype(F32)
            for part in parts[1:]:
                table = table + part[kind, head].astype(F32)
            tables.append(table.astype(BF))
        width = out.shape[2]
        added = nn(hot, jnp.concatenate(tables, axis=1))
        added = [added[:, i * width : (i + 1) * width] for i in range(4)]
        wide_rows[rows, :] = jnp.where(is_global, added[0], out[head].astype(F32))
        query_grad[rows, :] = dq[head] + added[1]
        key_grad[rows, :] = dkv[0, head] + added[2]
        value_grad[rows, :] = dkv[1, head] + added[3]
    attn[...] = wide_rows[...].astype(BF)


def cost(flops, moved, exps=0):
    return pl.CostEstimate(flops=int(flops), bytes_accessed=int(moved), transcendentals=int(exps))


def struct(shape, dtype):
    return jax.ShapeDtypeStruct(shape, dtype)


def whole(shape):
    return pl.BlockSpec(shape, lambda head: (0,) * len(shape))


def per_head(shape, dim, first=0):
    block = tuple(1 if i == dim else size for i, size in enumerate(shape))
    return pl.BlockSpec(
        block, lambda head: tuple(head + first if i == dim else 0 for i in range(len(shape)))
    )


def shards(query_rows, key_rows, value_rows, out_grad, global_pos):
    toks, heads, width = query_rows.shape
    count = global_pos.shape[0]
    devices = lax.axis_size("ctx")
    slots = max(16, 2 * count // devices)
    scale = width ** (-0.5)
    scale2 = scale * LOG2E
    bits = devices.bit_length() - 1
    stages = [
        [mask << low for mask in range(1, 1 << min(2, bits - low))] for low in range(1, bits, 2)
    ] + [[1]]
    order = [0]
    for stage in stages:
        order = order + [one ^ mask for mask in stage for one in order]
    pos_row = global_pos.reshape(1, count)
    q_flat, k_flat, v_flat, g_flat = (
        x.reshape(toks * heads, width) for x in (query_rows, key_rows, value_rows, out_grad)
    )

    def swap(value, mask):
        return lax.ppermute(value, "ctx", [(i, i ^ mask) for i in range(devices)])

    def from_near(value):
        return swap(value, 1)

    def from_far(value):
        pairs = [(i, i + 1) for i in range(1, devices - 1, 2)]
        return lax.ppermute(value, "ctx", pairs + [(j, i) for i, j in pairs])

    def after(value, earlier):
        return lax.optimization_barrier((value, earlier))[0]

    pair_shape = (2, heads, toks, width)
    slot_shape = (4, heads, slots, width)
    steps = 1
    flat_spec = pl.BlockSpec((toks * heads // steps, width), lambda i: (i, 0))
    pair_spec = pl.BlockSpec((2, heads, toks // steps, width), lambda i: (0, 0, i, 0))
    wide_pair = pltpu.VMEM((2, toks * heads // steps, width), F32)
    kv = pl.pallas_call(
        functools.partial(pack_keys_kernel, heads),
        out_shape=struct(pair_shape, BF),
        scratch_shapes=[wide_pair],
        compiler_params=params(),
        name="pack_keys",
    )(k_flat, v_flat)

    qd, slot_rows = pl.pallas_call(
        functools.partial(pack_queries_kernel, heads, slots),
        grid=(steps,),
        in_specs=[flat_spec, flat_spec, pair_spec, whole((1, count))],
        out_specs=(pair_spec, whole(slot_shape)),
        out_shape=(struct(pair_shape, BF), struct(slot_shape, BF)),
        scratch_shapes=[wide_pair, pltpu.VMEM(slot_shape, F32)],
        compiler_params=params(),
        name="pack_queries",
    )(q_flat, g_flat, kv, pos_row)

    span = toks + 2 * HALF
    bias, compact, expand, place = pl.pallas_call(
        functools.partial(mask_kernel, order, slots, toks * devices),
        out_shape=(
            struct((span, 128), F32),
            struct((count, devices * slots), BF),
            struct((devices * slots, count), BF),
            struct((toks, slots), BF),
        ),
        compiler_params=params(),
        name="masks",
    )(pos_row)

    kv_far, kv_near = from_far(kv), from_near(kv)
    probs_shape = (heads, span, toks)
    acc_shape = (heads, width, toks)
    probs, acc, top_sum = pl.pallas_call(
        functools.partial(window_kernel, scale2),
        grid=(heads,),
        in_specs=[per_head(pair_shape, 1)] * 4 + [whole(bias.shape)],
        out_specs=(
            per_head(probs_shape, 0),
            per_head(acc_shape, 0),
            per_head((heads, 2, toks), 0),
        ),
        out_shape=(
            struct(probs_shape, BF),
            struct(acc_shape, F32),
            struct((heads, 2, toks), F32),
        ),
        scratch_shapes=[
            pltpu.VMEM((span, width), BF),
            pltpu.VMEM((span, width), BF),
            pltpu.VMEM((toks // TILE, 2 * HALF + TILE, TILE), F32),
        ],
        compiler_params=params(),
        cost_estimate=cost(1e6, 1e6),
        name="window",
    )(qd, kv, kv_near, kv_far, bias)
    held = [slot_rows[None]]
    for number, stage in enumerate(stages):
        if stage == [1]:
            held = after(held, top_sum)
        send = jnp.concatenate(held, axis=0) if number else held[0]
        held += [swap(send, mask) for mask in stage]

    row_shape = (4, heads, count, width)
    rows, stats = pl.pallas_call(
        functools.partial(stats_kernel, scale2),
        grid=(heads,),
        in_specs=[whole(compact.shape)]
        + [per_head(part.shape, 2) for part in held]
        + [per_head(pair_shape, 1)],
        out_specs=(per_head(row_shape, 1), per_head((devices, heads, 8, count), 1)),
        out_shape=(struct(row_shape, BF), struct((devices, heads, 8, count), F32)),
        compiler_params=params(),
        cost_estimate=cost(1e6, 1e6),
        name="global_stats",
    )(compact, *held, kv)

    stats = lax.all_to_all(stats, "ctx", 0, 0, tiled=True)

    sum_shape = (devices // 2, 2, heads, slots, width)
    sum_struct = struct(sum_shape, BF)
    qd_late = after(qd, (kv_near, kv_far))
    qd_far, qd_near = from_far(qd_late), from_near(qd_late)

    out, log_dot, dq, dkv, kept_sums, sent_sums = pl.pallas_call(
        functools.partial(local_kernel, scale, scale2),
        grid=(heads,),
        in_specs=[per_head(pair_shape, 1)] * 4
        + [per_head(row_shape, 1), per_head(probs_shape, 0), per_head(acc_shape, 0)]
        + [per_head((heads, 2, toks), 0), whole(expand.shape)],
        out_specs=(
            per_head((heads, toks, width), 0),
            per_head((heads, 2, toks), 0),
            per_head((heads, toks, width), 0),
            per_head(pair_shape, 1),
            per_head(sum_shape, 2),
            per_head(sum_shape, 2),
        ),
        out_shape=(
            struct((heads, toks, width), BF),
            struct((heads, 2, toks), F32),
            struct((heads, toks, width), F32),
            struct(pair_shape, F32),
            sum_struct,
            sum_struct,
        ),
        scratch_shapes=[
            pltpu.VMEM((span, width), BF),
            pltpu.VMEM((span, width), BF),
            pltpu.VMEM((span, toks), BF),
        ],
        compiler_params=params(),
        cost_estimate=cost(1e6, 1e6),
        name="local",
    )(qd, kv, kv_near, kv_far, rows, probs, acc, top_sum, expand)
    log_far, log_near = from_far(log_dot), from_near(log_dot)

    dkv, kept_ends, sent_ends = pl.pallas_call(
        functools.partial(global_kernel, scale, scale2),
        grid=(heads,),
        in_specs=[per_head(pair_shape, 1), per_head(row_shape, 1)]
        + [per_head(stats.shape, 1), whole(expand.shape), per_head(pair_shape, 1)],
        out_specs=(per_head(pair_shape, 1), per_head(sum_shape, 2), per_head(sum_shape, 2)),
        out_shape=(struct(pair_shape, F32), sum_struct, sum_struct),
        input_output_aliases={4: 0},
        compiler_params=params(),
        cost_estimate=cost(1e6, 1e6),
        name="global_queries",
    )(kv, rows, after(stats, (log_dot, qd_near, qd_far)), expand, dkv)
    got_sums = from_near(sent_sums)
    got_ends = from_near(after(sent_ends, (log_near, log_far)))

    first = stages[0]
    parts = pl.pallas_call(
        fold_kernel,
        out_shape=[struct((4, heads, slots, width), BF)] * (devices // 2),
        compiler_params=params(),
        name="fold",
    )(kept_ends, got_ends, kept_sums, got_sums)
    for stage in reversed(stages[1:-1]):
        size = len(parts) // (len(stage) + 1)
        kept = parts[:size]
        for number, mask in enumerate(stage):
            sent = parts[(number + 1) * size : (number + 2) * size]
            kept = [one + swap(other, mask) for one, other in zip(kept, sent)]
        parts = kept
    parts = [parts[0]] + [swap(part, mask) for part, mask in zip(parts[1:], first)]

    dkv = pl.pallas_call(
        functools.partial(rim_kernel, scale, scale2),
        grid=(heads,),
        in_specs=[per_head(pair_shape, 1), whole(bias.shape)]
        + [per_head(pair_shape, 1)] * 2
        + [per_head(log_dot.shape, 0)] * 2
        + [per_head(pair_shape, 1)],
        out_specs=per_head(pair_shape, 1),
        out_shape=struct(pair_shape, F32),
        scratch_shapes=[
            pltpu.VMEM((2 * toks, width), BF),
            pltpu.VMEM((2 * toks, width), BF),
            pltpu.VMEM((2, 2, toks), F32),
            pltpu.VMEM((toks, toks + TILE), BF),
            pltpu.VMEM((toks, toks + TILE), BF),
        ],
        compiler_params=params(),
        cost_estimate=cost(1e6, 1e6),
        name="rim",
    )(kv, bias, qd_near, qd_far, log_near, log_far, dkv)

    flat_shape = (toks * heads, width)
    steps = 2
    outs = pl.pallas_call(
        functools.partial(final_kernel, len(parts)),
        grid=(steps,),
        in_specs=[
            pl.BlockSpec((toks // steps, slots), lambda i: (i, 0)),
            pl.BlockSpec((heads, toks // steps, width), lambda i: (0, i, 0)),
            pl.BlockSpec((heads, toks // steps, width), lambda i: (0, i, 0)),
            pl.BlockSpec((2, heads, toks // steps, width), lambda i: (0, 0, i, 0)),
        ]
        + [whole((4, heads, slots, width))] * len(parts),
        out_specs=[pl.BlockSpec((toks * heads // steps, width), lambda i: (i, 0))] * 4,
        out_shape=[struct(flat_shape, kind) for kind in (BF, F32, F32, F32)],
        scratch_shapes=[pltpu.VMEM((toks * heads // steps, width), F32)],
        compiler_params=params(),
        name="final",
    )(place, out, dq, dkv, *parts)
    return tuple(x.reshape(toks, heads, width) for x in outs)


def solution(mesh):
    spec = P("ctx", "head", None)
    return jax.shard_map(
        shards,
        mesh=mesh,
        in_specs=(spec, spec, spec, spec, P()),
        out_specs=(spec, spec, spec, spec),
        check_vma=False,
    )
```

```python
import functools
import math

import jax
import jax.numpy as jnp
from jax import lax
from jax.experimental import pallas as pl
from jax.experimental.pallas import tpu as pltpu
from jax.sharding import PartitionSpec as P

HALF = 512
TILE = 256
NEG = -1e30
LOG2E = 1.0 / math.log(2.0)
VMEM_BYTES = 63 * 1024 * 1024
BF = jnp.bfloat16
F32 = jnp.float32


def nt(a, b):
    return lax.dot_general(a, b, (((1,), (1,)), ((), ())), preferred_element_type=F32)


def nn(a, b):
    return lax.dot_general(a, b, (((1,), (0,)), ((), ())), preferred_element_type=F32)


def wide(column, width):
    return jnp.concatenate([column] * (width // column.shape[1]), axis=1)


def iota(shape, dim):
    return lax.broadcasted_iota(jnp.int32, shape, dim)


def params():
    return pltpu.CompilerParams(vmem_limit_bytes=VMEM_BYTES)


def as_column(row):
    return jnp.broadcast_to(row, (128, row.shape[1])).T[:, :1]


def pack_keys_kernel(heads, k, v, kv, wide_rows):
    toks = k.shape[0] // heads
    for number, source in enumerate((k, v)):
        wide_rows[number] = source[...].astype(F32)
        for head in range(heads):
            kv[number, head] = wide_rows[number, pl.ds(head, toks, stride=heads), :].astype(BF)


def pack_queries_kernel(heads, slots, q, g, kv, pos_row, qd, slot_rows, wide_rows, acc):
    step = pl.program_id(0)
    toks = q.shape[0] // heads
    row = pos_row[...]
    count = row.shape[1]
    base = lax.axis_index("ctx") * (toks * pl.num_programs(0))
    column = as_column(row)
    tok = iota((count, toks), 1) + (base + step * toks)
    hit = jnp.sum((column == tok).astype(F32), axis=0, keepdims=True)
    rank = jnp.sum(((column >= base) & (column < tok)).astype(F32), axis=0, keepdims=True)
    slot = iota((slots, toks), 0).astype(F32)
    pick = jnp.where((hit > 0) & (rank == slot), 1.0, 0.0).astype(BF)
    tok = iota((toks, count), 0) + (base + step * toks)
    hit_column = jnp.sum((row == tok).astype(F32), axis=1, keepdims=True)
    tables = [[], [kv[0, h] for h in range(heads)], [kv[1, h] for h in range(heads)], []]
    for number, source in ((0, q), (3, g)):
        wide_rows[number // 3] = source[...].astype(F32)
        for head in range(heads):
            rows = wide_rows[number // 3, pl.ds(head, toks, stride=heads), :]
            tables[number].append(rows.astype(BF))
            if number == 0:
                qd[0, head] = rows.astype(BF)
            else:
                qd[1, head] = jnp.where(hit_column > 0, 0.0, rows).astype(BF)
    for number in range(4):
        found = nn(pick, jnp.concatenate(tables[number], axis=1))
        for head in range(heads):
            part = found[:, head * 128 : (head + 1) * 128]
            acc[number, head] = jnp.where(step == 0, part, acc[number, head] + part)

    @pl.when(step == pl.num_programs(0) - 1)
    def _():
        slot_rows[...] = acc[...].astype(BF)


def owner_map(column, owner, toks, slots, shape):
    inside = jnp.sum((column < owner * toks).astype(jnp.int32), axis=0, keepdims=True)
    held = jnp.sum((column < (owner + 1) * toks).astype(jnp.int32), axis=0, keepdims=True) - inside
    slot = iota(shape, 1) % slots
    hot = (iota(shape, 0) == inside + slot) & (slot < held)
    return jnp.where(hot, 1.0, 0.0).astype(BF)


def mask_kernel(order, slots, seq_rows, pos_row, bias, compact, expand, place):
    toks = place.shape[0]
    me = lax.axis_index("ctx")
    base = me * toks
    row = pos_row[...]
    count = row.shape[1]
    column = as_column(row)
    for start in range(0, bias.shape[0], TILE):
        key = iota((TILE, count), 0) + (base - HALF + start)
        hits = jnp.sum((row == key).astype(F32), axis=1, keepdims=True)
        key = key[:, :1]
        out = (hits > 0) | (key < 0) | (key >= seq_rows)
        bias[start : start + TILE, :] = jnp.broadcast_to(jnp.where(out, NEG, 0.0), (TILE, 128))
    tok = iota((toks, count), 0) + base
    hit = jnp.sum((row == tok).astype(F32), axis=1, keepdims=True)
    rank = jnp.sum(((row >= base) & (row < tok)).astype(F32), axis=1, keepdims=True)
    slot = iota((toks, slots), 1).astype(F32)
    place[...] = jnp.where((hit > 0) & (rank == slot), 1.0, 0.0).astype(BF)
    part = iota((1, compact.shape[1]), 1) // slots
    owner = jnp.zeros_like(part)
    for number, relative in enumerate(order):
        owner = jnp.where(part == number, me ^ relative, owner)
    compact[...] = owner_map(column, owner, toks, slots, compact.shape)
    expand[...] = compact[...].astype(F32).T.astype(BF)


def stats_kernel(scale2, compact, *refs):
    parts, (kv, rows, stats) = refs[:-3], refs[-3:]
    pieces = []
    for part in parts:
        for i in range(part.shape[0]):
            pieces.append(jnp.concatenate([part[i, number, 0] for number in range(4)], axis=1))
    packed = nn(compact[...], jnp.concatenate(pieces, axis=0)).astype(BF)
    width = kv.shape[3]
    table = [packed[:, number * width : (number + 1) * width] for number in range(4)]
    for number in range(4):
        rows[number, 0] = table[number]
    queries, _, _, grads = table
    scores = nt(kv[0, 0], queries) * scale2
    top = jnp.max(scores, axis=0, keepdims=True)
    weights = jnp.exp2(scores - top)
    total = jnp.sum(weights, axis=0, keepdims=True)
    dot = jnp.sum(weights * nt(kv[1, 0], grads), axis=0, keepdims=True)
    line = iota(stats.shape[2:], 0)
    found = jnp.where(line == 0, top, jnp.where(line == 1, total, dot))
    for device in range(stats.shape[0]):
        stats[device, 0] = found


def band(scores, low):
    rows, columns = iota(scores.shape, 0), iota(scores.shape, 1)
    return jnp.where(rows <= columns if low else rows >= columns, scores, NEG)


def put_in_slots(expand, tables, kept, sent):
    owners, kinds, _, slots, width = kept.shape
    spread = nn(expand, jnp.concatenate(tables, axis=1)).astype(BF)
    for owner in range(2 * owners):
        for kind in range(kinds):
            (kept if owner < owners else sent)[owner % owners, kind, 0] = spread[
                owner * slots : (owner + 1) * slots, kind * width : (kind + 1) * width
            ]


def fold_kernel(kept_ends, got_ends, kept_sums, got_sums, *outs):
    for part, out in enumerate(outs):
        out[0:2] = (kept_ends[part].astype(F32) + got_ends[part].astype(F32)).astype(BF)
        out[2:4] = (kept_sums[part].astype(F32) + got_sums[part].astype(F32)).astype(BF)


def global_kernel(scale, scale2, kv, rows, stats, expand, before, key_t, value_t, dkv, kept, sent):
    g_query, g_grad = rows[0, 0], rows[3, 0]
    tops = stats[:, 0, 0:1, :]
    top = jnp.max(tops, axis=0)
    factor = jnp.exp2(tops - top[None])
    total = jnp.sum(stats[:, 0, 1:2, :] * factor, axis=0)
    g_dot = jnp.sum(stats[:, 0, 2:3, :] * factor, axis=0) / total
    g_log = top + jnp.log2(total)
    weights = jnp.exp2(nt(kv[0, 0], g_query) * scale2 - g_log)
    narrow = weights.astype(BF)
    slopes = (weights * (nt(kv[1, 0], g_grad) - g_dot)).astype(BF)
    dkv[0, 0] = before[0, 0] + nn(slopes, g_query) * scale
    dkv[1, 0] = before[1, 0] + nn(narrow, g_grad)
    out = nn(value_t[0, 0], narrow).T.astype(BF)
    dq = (nn(key_t[0], slopes) * scale).T.astype(BF)
    put_in_slots(expand[...], (out, dq), kept, sent)


def gather_window(kv, kv_near, kv_far, number, buf):
    toks = kv.shape[2]
    near = 2 * (1 - lax.axis_index("ctx") % 2)
    for block, place in ((kv_near, near), (kv, 1), (kv_far, 2 - near)):
        buf[pl.ds(pl.multiple_of(place * toks, toks), toks), :] = block[number, 0]


def window_kernel(
    scale2, qd, kv, kv_near, kv_far, bias, probs, acc, top_sum, key_t, values, sides, keys, score_buf
):
    toks = kv.shape[2]
    reach = 2 * HALF + TILE
    gather_window(kv, kv_near, kv_far, 0, keys)
    gather_window(kv, kv_near, kv_far, 1, values.at[0])
    key_t[0] = keys[...].T
    value_t = values[0].T
    query_t = qd[0, 0].T
    sides[0, 0] = query_t
    sides[1, 0] = qd[1, 0].T
    sides[2, 0] = value_t[:, HALF : HALF + toks]
    tiles = range(toks // TILE)
    lanes = [slice(tile * TILE, (tile + 1) * TILE) for tile in tiles]
    pieces = range(reach // TILE)
    best, top, total = ([None] * len(tiles) for _ in range(3))

    def score(tile, piece):
        span = slice((tile + piece) * TILE, (tile + piece + 1) * TILE)
        scores = nn(keys[span, :], query_t[:, lanes[tile]]) * scale2
        scores = scores + wide(bias[span, :], TILE)
        if piece == 0:
            scores = band(scores, False)
        elif piece == len(pieces) - 1:
            scores = band(scores, True)
        score_buf[tile, piece * TILE : (piece + 1) * TILE, :] = scores
        part = jnp.max(scores.reshape(TILE // 8, 8, TILE), axis=0)
        best[tile] = part if best[tile] is None else jnp.maximum(best[tile], part)

    def weigh(tile, piece):
        if top[tile] is None:
            top[tile] = jnp.max(best[tile], axis=0, keepdims=True)
        span = slice((tile + piece) * TILE, (tile + piece + 1) * TILE)
        weights = jnp.exp2(score_buf[tile, piece * TILE : (piece + 1) * TILE, :] - top[tile])
        probs[0, span, lanes[tile]] = weights.astype(BF)
        part = jnp.sum(weights.reshape(TILE // 8, 8, TILE), axis=0)
        total[tile] = part if total[tile] is None else total[tile] + part

    for step in range(len(tiles) + 1):
        for piece in pieces:
            if step:
                weigh(step - 1, piece)
            if step < len(tiles):
                score(step, piece)
        if step:
            tile = step - 1
            window = slice(tile * TILE, tile * TILE + reach)
            acc[0, :, lanes[tile]] = nn(value_t[:, window], probs[0, window, lanes[tile]])
            top_sum[0, 0:1, lanes[tile]] = top[tile]
            top_sum[0, 1:2, lanes[tile]] = jnp.sum(total[tile], axis=0, keepdims=True)


def local_kernel(
    scale, scale2, sides, key_t, values, rows, probs, acc, top_sum, expand,
    out, log_dot, dq, dkv, kept, sent, slopes,
):
    toks = acc.shape[2]
    reach = 2 * HALF + TILE
    query_t, grad_t = sides[0, 0], sides[1, 0]
    g_keys, g_values = rows[1, 0], rows[2, 0]
    g_key_t, g_value_t = g_keys.T, g_values.T
    grads = grad_t.astype(F32)
    scores = nn(g_keys, query_t) * scale2
    old = top_sum[0, 0:1, :]
    top = jnp.maximum(old, jnp.max(scores, axis=0, keepdims=True))
    weights = jnp.exp2(scores - top)
    factor = jnp.exp2(old - top)
    total = top_sum[0, 1:2, :] * factor + jnp.sum(weights, axis=0, keepdims=True)
    inverse = 1.0 / total
    g_probs = weights.astype(BF)
    result = (acc[0] * factor + nn(g_value_t, g_probs)) * inverse
    dot = jnp.sum(grads * result, axis=0, keepdims=True)
    log_dot[0, 0:1, :] = top + jnp.log2(total)
    log_dot[0, 1:2, :] = dot
    out[0] = result.T.astype(BF)
    share = factor * inverse
    g_grads = (grads * inverse).astype(BF)
    w_grads = (grads * share).astype(BF)
    g_slopes = (weights * (nn(g_values, g_grads) - dot * inverse)).astype(BF)
    dots = dot * share
    for tile in range(toks // TILE):
        lanes = slice(tile * TILE, (tile + 1) * TILE)
        for piece in range(reach // TILE):
            span = slice((tile + piece) * TILE, (tile + piece + 1) * TILE)
            rise = nn(values[0, span, :], w_grads[:, lanes]) - dots[:, lanes]
            slopes[span, lanes] = (probs[0, span, lanes].astype(F32) * rise).astype(BF)
    for tile in range(toks // TILE):
        lanes = slice(tile * TILE, (tile + 1) * TILE)
        window = slice(tile * TILE, tile * TILE + reach)
        part = nn(key_t[0, :, window], slopes[window, lanes]) + nn(g_key_t, g_slopes[:, lanes])
        dq[0, lanes, :] = (part * scale).T
    own = slice(HALF, HALF + toks)
    dkv[0, 0] = (nt(query_t, slopes[own, :]) * scale).T
    dkv[1, 0] = nt(w_grads, probs[0, own, :]).T
    g_dk = (nt(query_t, g_slopes) * scale).T.astype(BF)
    g_dv = nt(g_grads, g_probs).T.astype(BF)
    put_in_slots(expand[...], (g_dk, g_dv), kept, sent)


def rim_kernel(
    scale, scale2, kv, bias, qd_near, qd_far, log_near, log_far, partial, dkv,
    queries, grads, logs, probs, slopes,
):
    toks = kv.shape[2]
    reach = toks + TILE
    near = 1 - lax.axis_index("ctx") % 2
    for qd, log_dot, place in ((qd_near, log_near, near), (qd_far, log_far, 1 - near)):
        spot = pl.ds(pl.multiple_of(place * toks, toks), toks)
        queries[spot, :] = qd[0, 0]
        grads[spot, :] = qd[1, 0]
        logs[place] = log_dot[0]
    for k_tile in range(toks // TILE):
        span = slice(k_tile * TILE, (k_tile + 1) * TILE)
        key = kv[0, 0, span, :]
        value = kv[1, 0, span, :]
        key_bias = wide(bias[HALF + k_tile * TILE : HALF + (k_tile + 1) * TILE, :], TILE)
        for piece in range(reach // TILE):
            start = (k_tile + piece) * TILE
            side, lanes = start // toks, slice(start % toks, start % toks + TILE)
            scores = nt(key, queries[start : start + TILE, :]) * scale2 + key_bias
            if piece == 0:
                scores = band(scores, True)
            elif piece == reach // TILE - 1:
                scores = band(scores, False)
            weights = jnp.exp2(scores - logs[side, 0:1, lanes])
            slope = weights * (nt(value, grads[start : start + TILE, :]) - logs[side, 1:2, lanes])
            spot = slice(piece * TILE, (piece + 1) * TILE)
            probs[span, spot] = weights.astype(BF)
            slopes[span, spot] = slope.astype(BF)
        window = slice(k_tile * TILE, k_tile * TILE + reach)
        dkv[0, 0, span, :] = partial[0, 0, span, :] + nn(slopes[span, :], queries[window, :]) * scale
        dkv[1, 0, span, :] = partial[1, 0, span, :] + nn(probs[span, :], grads[window, :])


def final_kernel(
    sources, place, out, dq, dkv, *refs
):
    parts, refs = refs[:sources], refs[sources:]
    attn, query_grad, key_grad, value_grad, wide_rows = refs
    heads, toks = out.shape[0], out.shape[1]
    hot = place[...]
    is_global = jnp.sum(hot.astype(F32), axis=1, keepdims=True) > 0
    for head in range(heads):
        rows = pl.ds(head, toks, stride=heads)
        tables = []
        for kind in range(4):
            table = parts[0][kind, head].astype(F32)
            for part in parts[1:]:
                table = table + part[kind, head].astype(F32)
            tables.append(table.astype(BF))
        width = out.shape[2]
        added = nn(hot, jnp.concatenate(tables, axis=1))
        added = [added[:, i * width : (i + 1) * width] for i in range(4)]
        wide_rows[rows, :] = jnp.where(is_global, added[0], out[head].astype(F32))
        query_grad[rows, :] = dq[head] + added[1]
        key_grad[rows, :] = dkv[0, head] + added[2]
        value_grad[rows, :] = dkv[1, head] + added[3]
    attn[...] = wide_rows[...].astype(BF)


def cost(flops, moved, exps=0):
    return pl.CostEstimate(flops=int(flops), bytes_accessed=int(moved), transcendentals=int(exps))


def struct(shape, dtype):
    return jax.ShapeDtypeStruct(shape, dtype)


def whole(shape):
    return pl.BlockSpec(shape, lambda head: (0,) * len(shape))


def per_head(shape, dim, first=0):
    block = tuple(1 if i == dim else size for i, size in enumerate(shape))
    return pl.BlockSpec(
        block, lambda head: tuple(head + first if i == dim else 0 for i in range(len(shape)))
    )


def shards(query_rows, key_rows, value_rows, out_grad, global_pos):
    toks, heads, width = query_rows.shape
    count = global_pos.shape[0]
    devices = lax.axis_size("ctx")
    slots = max(16, 2 * count // devices)
    scale = width ** (-0.5)
    scale2 = scale * LOG2E
    bits = devices.bit_length() - 1
    stages = [
        [mask << low for mask in range(1, 1 << min(2, bits - low))] for low in range(1, bits, 2)
    ] + [[1]]
    order = [0]
    for stage in stages:
        order = order + [one ^ mask for mask in stage for one in order]
    pos_row = global_pos.reshape(1, count)
    q_flat, k_flat, v_flat, g_flat = (
        x.reshape(toks * heads, width) for x in (query_rows, key_rows, value_rows, out_grad)
    )

    def swap(value, mask):
        return lax.ppermute(value, "ctx", [(i, i ^ mask) for i in range(devices)])

    def from_near(value):
        return swap(value, 1)

    def from_far(value):
        pairs = [(i, i + 1) for i in range(1, devices - 1, 2)]
        return lax.ppermute(value, "ctx", pairs + [(j, i) for i, j in pairs])

    def after(value, earlier):
        return lax.optimization_barrier((value, earlier))[0]

    pair_shape = (2, heads, toks, width)
    slot_shape = (4, heads, slots, width)
    steps = 1
    flat_spec = pl.BlockSpec((toks * heads // steps, width), lambda i: (i, 0))
    pair_spec = pl.BlockSpec((2, heads, toks // steps, width), lambda i: (0, 0, i, 0))
    wide_pair = pltpu.VMEM((2, toks * heads // steps, width), F32)
    kv = pl.pallas_call(
        functools.partial(pack_keys_kernel, heads),
        out_shape=struct(pair_shape, BF),
        scratch_shapes=[wide_pair],
        compiler_params=params(),
        name="pack_keys",
    )(k_flat, v_flat)

    qd, slot_rows = pl.pallas_call(
        functools.partial(pack_queries_kernel, heads, slots),
        grid=(steps,),
        in_specs=[flat_spec, flat_spec, pair_spec, whole((1, count))],
        out_specs=(pair_spec, whole(slot_shape)),
        out_shape=(struct(pair_shape, BF), struct(slot_shape, BF)),
        scratch_shapes=[wide_pair, pltpu.VMEM(slot_shape, F32)],
        compiler_params=params(),
        name="pack_queries",
    )(q_flat, g_flat, kv, pos_row)

    span = toks + 2 * HALF
    bias, compact, expand, place = pl.pallas_call(
        functools.partial(mask_kernel, order, slots, toks * devices),
        out_shape=(
            struct((span, 128), F32),
            struct((count, devices * slots), BF),
            struct((devices * slots, count), BF),
            struct((toks, slots), BF),
        ),
        compiler_params=params(),
        name="masks",
    )(pos_row)

    kv_far, kv_near = from_far(kv), from_near(kv)
    probs_shape = (heads, span, toks)
    acc_shape = (heads, width, toks)
    turned_shape = (heads, width, span)
    sides_shape = (3, heads, width, toks)
    probs, acc, top_sum, key_t, values, sides = pl.pallas_call(
        functools.partial(window_kernel, scale2),
        grid=(heads,),
        in_specs=[per_head(pair_shape, 1)] * 4 + [whole(bias.shape)],
        out_specs=(
            per_head(probs_shape, 0),
            per_head(acc_shape, 0),
            per_head((heads, 2, toks), 0),
            per_head(turned_shape, 0),
            per_head((heads, span, width), 0),
            per_head(sides_shape, 1),
        ),
        out_shape=(
            struct(probs_shape, BF),
            struct(acc_shape, F32),
            struct((heads, 2, toks), F32),
            struct(turned_shape, BF),
            struct((heads, span, width), BF),
            struct(sides_shape, BF),
        ),
        scratch_shapes=[
            pltpu.VMEM((span, width), BF),
            pltpu.VMEM((toks // TILE, 2 * HALF + TILE, TILE), F32),
        ],
        compiler_params=params(),
        cost_estimate=cost(1e6, 1e6),
        name="window",
    )(qd, kv, kv_near, kv_far, bias)
    held = [slot_rows[None]]
    for number, stage in enumerate(stages):
        if stage == [1]:
            held = after(held, top_sum)
        send = jnp.concatenate(held, axis=0) if number else held[0]
        held += [swap(send, mask) for mask in stage]

    row_shape = (4, heads, count, width)
    rows, stats = pl.pallas_call(
        functools.partial(stats_kernel, scale2),
        grid=(heads,),
        in_specs=[whole(compact.shape)]
        + [per_head(part.shape, 2) for part in held]
        + [per_head(pair_shape, 1)],
        out_specs=(per_head(row_shape, 1), per_head((devices, heads, 8, count), 1)),
        out_shape=(struct(row_shape, BF), struct((devices, heads, 8, count), F32)),
        compiler_params=params(),
        cost_estimate=cost(1e6, 1e6),
        name="global_stats",
    )(compact, *held, kv)

    stats = lax.all_to_all(stats, "ctx", 0, 0, tiled=True)

    sum_shape = (devices // 2, 2, heads, slots, width)
    sum_struct = struct(sum_shape, BF)
    qd_late = after(qd, (kv_near, kv_far))
    qd_far, qd_near = from_far(qd_late), from_near(qd_late)

    out, log_dot, dq, dkv, kept_sums, sent_sums = pl.pallas_call(
        functools.partial(local_kernel, scale, scale2),
        grid=(heads,),
        in_specs=[per_head(sides_shape, 1), per_head(turned_shape, 0)]
        + [per_head((heads, span, width), 0), per_head(row_shape, 1)]
        + [per_head(probs_shape, 0), per_head(acc_shape, 0)]
        + [per_head((heads, 2, toks), 0), whole(expand.shape)],
        out_specs=(
            per_head((heads, toks, width), 0),
            per_head((heads, 2, toks), 0),
            per_head((heads, toks, width), 0),
            per_head(pair_shape, 1),
            per_head(sum_shape, 2),
            per_head(sum_shape, 2),
        ),
        out_shape=(
            struct((heads, toks, width), BF),
            struct((heads, 2, toks), F32),
            struct((heads, toks, width), F32),
            struct(pair_shape, F32),
            sum_struct,
            sum_struct,
        ),
        scratch_shapes=[
            pltpu.VMEM((span, toks), BF),
        ],
        compiler_params=params(),
        cost_estimate=cost(1e6, 1e6),
        name="local",
    )(sides, key_t, values, rows, probs, acc, top_sum, expand)
    log_far, log_near = from_far(log_dot), from_near(log_dot)

    dkv, kept_ends, sent_ends = pl.pallas_call(
        functools.partial(global_kernel, scale, scale2),
        grid=(heads,),
        in_specs=[per_head(pair_shape, 1), per_head(row_shape, 1)]
        + [per_head(stats.shape, 1), whole(expand.shape), per_head(pair_shape, 1)]
        + [pl.BlockSpec((1, width, toks), lambda head: (head, 0, HALF // toks))]
        + [pl.BlockSpec((1, 1, width, toks), lambda head: (2, head, 0, 0))],
        out_specs=(per_head(pair_shape, 1), per_head(sum_shape, 2), per_head(sum_shape, 2)),
        out_shape=(struct(pair_shape, F32), sum_struct, sum_struct),
        input_output_aliases={4: 0},
        compiler_params=params(),
        cost_estimate=cost(1e6, 1e6),
        name="global_queries",
    )(kv, rows, after(stats, (log_dot, qd_near, qd_far)), expand, dkv, key_t, sides)
    got_sums = from_near(sent_sums)
    got_ends = from_near(after(sent_ends, (log_near, log_far)))

    first = stages[0]
    parts = pl.pallas_call(
        fold_kernel,
        out_shape=[struct((4, heads, slots, width), BF)] * (devices // 2),
        compiler_params=params(),
        name="fold",
    )(kept_ends, got_ends, kept_sums, got_sums)
    for stage in reversed(stages[1:-1]):
        size = len(parts) // (len(stage) + 1)
        kept = parts[:size]
        for number, mask in enumerate(stage):
            sent = parts[(number + 1) * size : (number + 2) * size]
            kept = [one + swap(other, mask) for one, other in zip(kept, sent)]
        parts = kept
    parts = [parts[0]] + [swap(part, mask) for part, mask in zip(parts[1:], first)]

    dkv = pl.pallas_call(
        functools.partial(rim_kernel, scale, scale2),
        grid=(heads,),
        in_specs=[per_head(pair_shape, 1), whole(bias.shape)]
        + [per_head(pair_shape, 1)] * 2
        + [per_head(log_dot.shape, 0)] * 2
        + [per_head(pair_shape, 1)],
        out_specs=per_head(pair_shape, 1),
        out_shape=struct(pair_shape, F32),
        scratch_shapes=[
            pltpu.VMEM((2 * toks, width), BF),
            pltpu.VMEM((2 * toks, width), BF),
            pltpu.VMEM((2, 2, toks), F32),
            pltpu.VMEM((toks, toks + TILE), BF),
            pltpu.VMEM((toks, toks + TILE), BF),
        ],
        compiler_params=params(),
        cost_estimate=cost(1e6, 1e6),
        name="rim",
    )(kv, bias, qd_near, qd_far, log_near, log_far, dkv)

    flat_shape = (toks * heads, width)
    steps = 2
    outs = pl.pallas_call(
        functools.partial(final_kernel, len(parts)),
        grid=(steps,),
        in_specs=[
            pl.BlockSpec((toks // steps, slots), lambda i: (i, 0)),
            pl.BlockSpec((heads, toks // steps, width), lambda i: (0, i, 0)),
            pl.BlockSpec((heads, toks // steps, width), lambda i: (0, i, 0)),
            pl.BlockSpec((2, heads, toks // steps, width), lambda i: (0, 0, i, 0)),
        ]
        + [whole((4, heads, slots, width))] * len(parts),
        out_specs=[pl.BlockSpec((toks * heads // steps, width), lambda i: (i, 0))] * 4,
        out_shape=[struct(flat_shape, kind) for kind in (BF, F32, F32, F32)],
        scratch_shapes=[pltpu.VMEM((toks * heads // steps, width), F32)],
        compiler_params=params(),
        name="final",
    )(place, out, dq, dkv, *parts)
    return tuple(x.reshape(toks, heads, width) for x in outs)


def solution(mesh):
    spec = P("ctx", "head", None)
    return jax.shard_map(
        shards,
        mesh=mesh,
        in_specs=(spec, spec, spec, spec, P()),
        out_specs=(spec, spec, spec, spec),
        check_vma=False,
    )
```

```python
import functools
import math

import jax
import jax.numpy as jnp
from jax import lax
from jax.experimental import pallas as pl
from jax.experimental.pallas import tpu as pltpu
from jax.sharding import PartitionSpec as P

HALF = 512
TILE = 256
NEG = -1e30
LOG2E = 1.0 / math.log(2.0)
VMEM_BYTES = 63 * 1024 * 1024
BF = jnp.bfloat16
F32 = jnp.float32


def nt(a, b):
    return lax.dot_general(a, b, (((1,), (1,)), ((), ())), preferred_element_type=F32)


def nn(a, b):
    return lax.dot_general(a, b, (((1,), (0,)), ((), ())), preferred_element_type=F32)


def wide(column, width):
    return jnp.concatenate([column] * (width // column.shape[1]), axis=1)


def iota(shape, dim):
    return lax.broadcasted_iota(jnp.int32, shape, dim)


def params():
    return pltpu.CompilerParams(vmem_limit_bytes=VMEM_BYTES)


def as_column(row):
    return jnp.broadcast_to(row, (128, row.shape[1])).T[:, :1]


def pack_keys_kernel(heads, k, v, kv, wide_rows):
    toks = k.shape[0] // heads
    for number, source in enumerate((k, v)):
        wide_rows[number] = source[...].astype(F32)
        for head in range(heads):
            kv[number, head] = wide_rows[number, pl.ds(head, toks, stride=heads), :].astype(BF)


def pack_queries_kernel(heads, slots, q, g, kv, pos_row, qd, slot_rows, wide_rows, acc):
    step = pl.program_id(0)
    toks = q.shape[0] // heads
    row = pos_row[...]
    count = row.shape[1]
    base = lax.axis_index("ctx") * (toks * pl.num_programs(0))
    column = as_column(row)
    tok = iota((count, toks), 1) + (base + step * toks)
    hit = jnp.sum((column == tok).astype(F32), axis=0, keepdims=True)
    rank = jnp.sum(((column >= base) & (column < tok)).astype(F32), axis=0, keepdims=True)
    slot = iota((slots, toks), 0).astype(F32)
    pick = jnp.where((hit > 0) & (rank == slot), 1.0, 0.0).astype(BF)
    tok = iota((toks, count), 0) + (base + step * toks)
    hit_column = jnp.sum((row == tok).astype(F32), axis=1, keepdims=True)
    tables = [[], [kv[0, h] for h in range(heads)], [kv[1, h] for h in range(heads)], []]
    for number, source in ((0, q), (3, g)):
        wide_rows[number // 3] = source[...].astype(F32)
        for head in range(heads):
            rows = wide_rows[number // 3, pl.ds(head, toks, stride=heads), :]
            tables[number].append(rows.astype(BF))
            if number == 0:
                qd[0, head] = rows.astype(BF)
            else:
                qd[1, head] = jnp.where(hit_column > 0, 0.0, rows).astype(BF)
    for number in range(4):
        found = nn(pick, jnp.concatenate(tables[number], axis=1))
        for head in range(heads):
            part = found[:, head * 128 : (head + 1) * 128]
            acc[number, head] = jnp.where(step == 0, part, acc[number, head] + part)

    @pl.when(step == pl.num_programs(0) - 1)
    def _():
        slot_rows[...] = acc[...].astype(BF)


def owner_map(column, owner, toks, slots, shape):
    inside = jnp.sum((column < owner * toks).astype(jnp.int32), axis=0, keepdims=True)
    held = jnp.sum((column < (owner + 1) * toks).astype(jnp.int32), axis=0, keepdims=True) - inside
    slot = iota(shape, 1) % slots
    hot = (iota(shape, 0) == inside + slot) & (slot < held)
    return jnp.where(hot, 1.0, 0.0).astype(BF)


def mask_kernel(order, slots, seq_rows, pos_row, bias, compact, expand, place):
    toks = place.shape[0]
    me = lax.axis_index("ctx")
    base = me * toks
    row = pos_row[...]
    count = row.shape[1]
    column = as_column(row)
    for start in range(0, bias.shape[0], TILE):
        key = iota((TILE, count), 0) + (base - HALF + start)
        hits = jnp.sum((row == key).astype(F32), axis=1, keepdims=True)
        key = key[:, :1]
        out = (hits > 0) | (key < 0) | (key >= seq_rows)
        bias[start : start + TILE, :] = jnp.broadcast_to(jnp.where(out, NEG, 0.0), (TILE, 128))
    tok = iota((toks, count), 0) + base
    hit = jnp.sum((row == tok).astype(F32), axis=1, keepdims=True)
    rank = jnp.sum(((row >= base) & (row < tok)).astype(F32), axis=1, keepdims=True)
    slot = iota((toks, slots), 1).astype(F32)
    place[...] = jnp.where((hit > 0) & (rank == slot), 1.0, 0.0).astype(BF)
    part = iota((1, compact.shape[1]), 1) // slots
    owner = jnp.zeros_like(part)
    for number, relative in enumerate(order):
        owner = jnp.where(part == number, me ^ relative, owner)
    compact[...] = owner_map(column, owner, toks, slots, compact.shape)
    expand[...] = compact[...].astype(F32).T.astype(BF)


def stats_kernel(scale2, compact, *refs):
    parts, (kv, rows, stats) = refs[:-3], refs[-3:]
    pieces = []
    for part in parts:
        for i in range(part.shape[0]):
            pieces.append(jnp.concatenate([part[i, number, 0] for number in range(4)], axis=1))
    packed = nn(compact[...], jnp.concatenate(pieces, axis=0)).astype(BF)
    width = kv.shape[3]
    table = [packed[:, number * width : (number + 1) * width] for number in range(4)]
    for number in range(4):
        rows[number, 0] = table[number]
    queries, _, _, grads = table
    scores = nt(kv[0, 0], queries) * scale2
    top = jnp.max(scores, axis=0, keepdims=True)
    weights = jnp.exp2(scores - top)
    total = jnp.sum(weights, axis=0, keepdims=True)
    dot = jnp.sum(weights * nt(kv[1, 0], grads), axis=0, keepdims=True)
    line = iota(stats.shape[2:], 0)
    found = jnp.where(line == 0, top, jnp.where(line == 1, total, dot))
    for device in range(stats.shape[0]):
        stats[device, 0] = found


def band(scores, low):
    rows, columns = iota(scores.shape, 0), iota(scores.shape, 1)
    return jnp.where(rows <= columns if low else rows >= columns, scores, NEG)


def put_in_slots(expand, tables, kept, sent):
    owners, kinds, _, slots, width = kept.shape
    spread = nn(expand, jnp.concatenate(tables, axis=1)).astype(BF)
    for owner in range(2 * owners):
        for kind in range(kinds):
            (kept if owner < owners else sent)[owner % owners, kind, 0] = spread[
                owner * slots : (owner + 1) * slots, kind * width : (kind + 1) * width
            ]


def fold_kernel(kept_ends, got_ends, kept_sums, got_sums, *outs):
    for part, out in enumerate(outs):
        out[0:2] = (kept_ends[part].astype(F32) + got_ends[part].astype(F32)).astype(BF)
        out[2:4] = (kept_sums[part].astype(F32) + got_sums[part].astype(F32)).astype(BF)


def global_kernel(scale, scale2, kv, rows, stats, expand, before, dkv, kept, sent):
    g_query, g_grad = rows[0, 0], rows[3, 0]
    tops = stats[:, 0, 0:1, :]
    top = jnp.max(tops, axis=0)
    factor = jnp.exp2(tops - top[None])
    total = jnp.sum(stats[:, 0, 1:2, :] * factor, axis=0)
    g_dot = jnp.sum(stats[:, 0, 2:3, :] * factor, axis=0) / total
    g_log = top + jnp.log2(total)
    weights = jnp.exp2(nt(kv[0, 0], g_query) * scale2 - g_log)
    narrow = weights.astype(BF)
    slopes = (weights * (nt(kv[1, 0], g_grad) - g_dot)).astype(BF)
    dkv[0, 0] = before[0, 0] + nn(slopes, g_query) * scale
    dkv[1, 0] = before[1, 0] + nn(narrow, g_grad)
    out = nn(kv[1, 0].T, narrow).T.astype(BF)
    dq = (nn(kv[0, 0].T, slopes) * scale).T.astype(BF)
    put_in_slots(expand[...], (out, dq), kept, sent)


def local_kernel(
    scale, scale2, qd, kv, kv_near, kv_far, rows, bias, expand,
    out, log_dot, dq, dkv, kept, sent, keys, values, score_buf, probs, slopes,
):
    toks = kv.shape[2]
    reach = 2 * HALF + TILE
    span = keys.shape[0] - rows.shape[2]
    near = 2 * (1 - lax.axis_index("ctx") % 2)
    for block, place in ((kv_near, near), (kv, 1), (kv_far, 2 - near)):
        spot = pl.ds(pl.multiple_of(place * toks, toks), toks)
        keys[spot, :] = block[0, 0]
        values[spot, :] = block[1, 0]
    keys[span:, :] = rows[1, 0]
    values[span:, :] = rows[2, 0]
    key_t, value_t = keys[...].T, values[...].T
    query_t, grad_t = qd[0, 0].T, qd[1, 0].T
    tiles = range(toks // TILE)
    lanes = [slice(tile * TILE, (tile + 1) * TILE) for tile in tiles]
    windows = [slice(tile * TILE, tile * TILE + reach) for tile in tiles]
    starts = [
        list(range(tile * TILE, tile * TILE + reach, TILE)) + list(range(span, keys.shape[0], TILE))
        for tile in tiles
    ]
    best, top, total, scaled, dots = ([None] * len(tiles) for _ in range(5))

    def score(tile, piece):
        start = starts[tile][piece]
        scores = nn(keys[start : start + TILE, :], query_t[:, lanes[tile]]) * scale2
        if start < span:
            scores = scores + wide(bias[start : start + TILE, :], TILE)
        if piece == 0:
            scores = band(scores, False)
        elif piece == reach // TILE - 1:
            scores = band(scores, True)
        score_buf[tile, piece * TILE : (piece + 1) * TILE, :] = scores
        part = jnp.max(scores.reshape(TILE // 8, 8, TILE), axis=0)
        best[tile] = part if best[tile] is None else jnp.maximum(best[tile], part)

    def weigh(tile, piece):
        if top[tile] is None:
            top[tile] = jnp.max(best[tile], axis=0, keepdims=True)
        start = starts[tile][piece]
        weights = jnp.exp2(score_buf[tile, piece * TILE : (piece + 1) * TILE, :] - top[tile])
        probs[start : start + TILE, lanes[tile]] = weights.astype(BF)
        part = jnp.sum(weights.reshape(TILE // 8, 8, TILE), axis=0)
        total[tile] = part if total[tile] is None else total[tile] + part

    def attend(tile):
        whole_sum = jnp.sum(total[tile], axis=0, keepdims=True)
        inverse = 1.0 / whole_sum
        grads = grad_t[:, lanes[tile]].astype(F32)
        acc = nn(value_t[:, windows[tile]], probs[windows[tile], lanes[tile]])
        acc = (acc + nn(value_t[:, span:], probs[span:, lanes[tile]])) * inverse
        dot = jnp.sum(grads * acc, axis=0, keepdims=True)
        log_dot[0, 0:1, lanes[tile]] = top[tile] + jnp.log2(whole_sum)
        log_dot[0, 1:2, lanes[tile]] = dot
        out[0, lanes[tile], :] = acc.T.astype(BF)
        scaled[tile] = (grads * inverse).astype(BF)
        dots[tile] = dot * inverse

    def slope(tile, piece):
        start = starts[tile][piece]
        rise = nn(values[start : start + TILE, :], scaled[tile]) - dots[tile]
        weights = probs[start : start + TILE, lanes[tile]].astype(F32)
        slopes[start : start + TILE, lanes[tile]] = (weights * rise).astype(BF)

    def query_gradient(tile):
        acc = nn(key_t[:, windows[tile]], slopes[windows[tile], lanes[tile]])
        acc = acc + nn(key_t[:, span:], slopes[span:, lanes[tile]])
        dq[0, lanes[tile], :] = (acc * scale).T

    for step in range(len(tiles) + 2):
        for piece in range(len(starts[0])):
            if 0 <= step - 2:
                slope(step - 2, piece)
            if 0 <= step - 1 < len(tiles):
                weigh(step - 1, piece)
            if step < len(tiles):
                score(step, piece)
        if 0 <= step - 2:
            query_gradient(step - 2)
        if 0 <= step - 1 < len(tiles):
            attend(step - 1)
    own = slice(HALF, HALF + toks)
    grads = jnp.concatenate(scaled, axis=1)
    dkv[0, 0] = (nt(query_t, slopes[own, :]) * scale).T
    dkv[1, 0] = nt(grads, probs[own, :]).T
    g_dk = (nt(query_t, slopes[span:, :]) * scale).T.astype(BF)
    g_dv = nt(grads, probs[span:, :]).T.astype(BF)
    put_in_slots(expand[...], (g_dk, g_dv), kept, sent)


def rim_kernel(
    scale, scale2, kv, bias, qd_near, qd_far, log_near, log_far, partial, dkv,
    queries, grads, logs, probs, slopes,
):
    toks = kv.shape[2]
    reach = toks + TILE
    near = 1 - lax.axis_index("ctx") % 2
    for qd, log_dot, place in ((qd_near, log_near, near), (qd_far, log_far, 1 - near)):
        spot = pl.ds(pl.multiple_of(place * toks, toks), toks)
        queries[spot, :] = qd[0, 0]
        grads[spot, :] = qd[1, 0]
        logs[place] = log_dot[0]
    for k_tile in range(toks // TILE):
        span = slice(k_tile * TILE, (k_tile + 1) * TILE)
        key = kv[0, 0, span, :]
        value = kv[1, 0, span, :]
        key_bias = wide(bias[HALF + k_tile * TILE : HALF + (k_tile + 1) * TILE, :], TILE)
        for piece in range(reach // TILE):
            start = (k_tile + piece) * TILE
            side, lanes = start // toks, slice(start % toks, start % toks + TILE)
            scores = nt(key, queries[start : start + TILE, :]) * scale2 + key_bias
            if piece == 0:
                scores = band(scores, True)
            elif piece == reach // TILE - 1:
                scores = band(scores, False)
            weights = jnp.exp2(scores - logs[side, 0:1, lanes])
            slope = weights * (nt(value, grads[start : start + TILE, :]) - logs[side, 1:2, lanes])
            spot = slice(piece * TILE, (piece + 1) * TILE)
            probs[span, spot] = weights.astype(BF)
            slopes[span, spot] = slope.astype(BF)
        window = slice(k_tile * TILE, k_tile * TILE + reach)
        dkv[0, 0, span, :] = partial[0, 0, span, :] + nn(slopes[span, :], queries[window, :]) * scale
        dkv[1, 0, span, :] = partial[1, 0, span, :] + nn(probs[span, :], grads[window, :])


def final_kernel(
    sources, place, out, dq, dkv, *refs
):
    parts, refs = refs[:sources], refs[sources:]
    attn, query_grad, key_grad, value_grad, wide_rows = refs
    heads, toks = out.shape[0], out.shape[1]
    hot = place[...]
    is_global = jnp.sum(hot.astype(F32), axis=1, keepdims=True) > 0
    for head in range(heads):
        rows = pl.ds(head, toks, stride=heads)
        tables = []
        for kind in range(4):
            table = parts[0][kind, head].astype(F32)
            for part in parts[1:]:
                table = table + part[kind, head].astype(F32)
            tables.append(table.astype(BF))
        width = out.shape[2]
        added = nn(hot, jnp.concatenate(tables, axis=1))
        added = [added[:, i * width : (i + 1) * width] for i in range(4)]
        wide_rows[rows, :] = jnp.where(is_global, added[0], out[head].astype(F32))
        query_grad[rows, :] = dq[head] + added[1]
        key_grad[rows, :] = dkv[0, head] + added[2]
        value_grad[rows, :] = dkv[1, head] + added[3]
    attn[...] = wide_rows[...].astype(BF)


def cost(flops, moved, exps=0):
    return pl.CostEstimate(flops=int(flops), bytes_accessed=int(moved), transcendentals=int(exps))


def struct(shape, dtype):
    return jax.ShapeDtypeStruct(shape, dtype)


def whole(shape):
    return pl.BlockSpec(shape, lambda head: (0,) * len(shape))


def per_head(shape, dim, first=0):
    block = tuple(1 if i == dim else size for i, size in enumerate(shape))
    return pl.BlockSpec(
        block, lambda head: tuple(head + first if i == dim else 0 for i in range(len(shape)))
    )


def shards(query_rows, key_rows, value_rows, out_grad, global_pos):
    toks, heads, width = query_rows.shape
    count = global_pos.shape[0]
    devices = lax.axis_size("ctx")
    slots = max(16, 2 * count // devices)
    scale = width ** (-0.5)
    scale2 = scale * LOG2E
    bits = devices.bit_length() - 1
    stages = [
        [mask << low for mask in range(1, 1 << min(2, bits - low))] for low in range(1, bits, 2)
    ] + [[1]]
    order = [0]
    for stage in stages:
        order = order + [one ^ mask for mask in stage for one in order]
    pos_row = global_pos.reshape(1, count)
    q_flat, k_flat, v_flat, g_flat = (
        x.reshape(toks * heads, width) for x in (query_rows, key_rows, value_rows, out_grad)
    )

    def swap(value, mask):
        return lax.ppermute(value, "ctx", [(i, i ^ mask) for i in range(devices)])

    def from_near(value):
        return swap(value, 1)

    def from_far(value):
        pairs = [(i, i + 1) for i in range(1, devices - 1, 2)]
        return lax.ppermute(value, "ctx", pairs + [(j, i) for i, j in pairs])

    def after(value, earlier):
        return lax.optimization_barrier((value, earlier))[0]

    pair_shape = (2, heads, toks, width)
    slot_shape = (4, heads, slots, width)
    steps = 1
    flat_spec = pl.BlockSpec((toks * heads // steps, width), lambda i: (i, 0))
    pair_spec = pl.BlockSpec((2, heads, toks // steps, width), lambda i: (0, 0, i, 0))
    wide_pair = pltpu.VMEM((2, toks * heads // steps, width), F32)
    kv = pl.pallas_call(
        functools.partial(pack_keys_kernel, heads),
        out_shape=struct(pair_shape, BF),
        scratch_shapes=[wide_pair],
        compiler_params=params(),
        name="pack_keys",
    )(k_flat, v_flat)

    qd, slot_rows = pl.pallas_call(
        functools.partial(pack_queries_kernel, heads, slots),
        grid=(steps,),
        in_specs=[flat_spec, flat_spec, pair_spec, whole((1, count))],
        out_specs=(pair_spec, whole(slot_shape)),
        out_shape=(struct(pair_shape, BF), struct(slot_shape, BF)),
        scratch_shapes=[wide_pair, pltpu.VMEM(slot_shape, F32)],
        compiler_params=params(),
        name="pack_queries",
    )(q_flat, g_flat, kv, pos_row)

    span = toks + 2 * HALF
    bias, compact, expand, place = pl.pallas_call(
        functools.partial(mask_kernel, order, slots, toks * devices),
        out_shape=(
            struct((span, 128), F32),
            struct((count, devices * slots), BF),
            struct((devices * slots, count), BF),
            struct((toks, slots), BF),
        ),
        compiler_params=params(),
        name="masks",
    )(pos_row)

    kv_near = from_near(kv)
    held = [slot_rows[None]]
    for bit in range(1, bits):
        if bit == 2:
            kv_far = from_far(after(kv, held[1]))
            held = after(held, place)
        send = jnp.concatenate(held, axis=0) if bit > 1 else held[0]
        held = list(held) + [swap(send, 1 << bit)]
    held += [from_near(part) for part in held]

    row_shape = (4, heads, count, width)
    rows, stats = pl.pallas_call(
        functools.partial(stats_kernel, scale2),
        grid=(heads,),
        in_specs=[whole(compact.shape)]
        + [per_head(part.shape, 2) for part in held]
        + [per_head(pair_shape, 1)],
        out_specs=(per_head(row_shape, 1), per_head((devices, heads, 8, count), 1)),
        out_shape=(struct(row_shape, BF), struct((devices, heads, 8, count), F32)),
        compiler_params=params(),
        cost_estimate=cost(1e6, 1e6),
        name="global_stats",
    )(compact, *held, kv)

    stats = lax.all_to_all(after(stats, (kv_near, kv_far)), "ctx", 0, 0, tiled=True)

    sum_shape = (devices // 2, 2, heads, slots, width)
    sum_struct = struct(sum_shape, BF)
    qd_late = after(qd, (kv_near, kv_far, rows))
    qd_far, qd_near = from_far(qd_late), from_near(qd_late)

    out, log_dot, dq, dkv, kept_sums, sent_sums = pl.pallas_call(
        functools.partial(local_kernel, scale, scale2),
        grid=(heads,),
        in_specs=[per_head(pair_shape, 1)] * 4
        + [per_head(row_shape, 1), whole(bias.shape), whole(expand.shape)],
        out_specs=(
            per_head((heads, toks, width), 0),
            per_head((heads, 2, toks), 0),
            per_head((heads, toks, width), 0),
            per_head(pair_shape, 1),
            per_head(sum_shape, 2),
            per_head(sum_shape, 2),
        ),
        out_shape=(
            struct((heads, toks, width), BF),
            struct((heads, 2, toks), F32),
            struct((heads, toks, width), F32),
            struct(pair_shape, F32),
            sum_struct,
            sum_struct,
        ),
        scratch_shapes=[
            pltpu.VMEM((span + count, width), BF),
            pltpu.VMEM((span + count, width), BF),
            pltpu.VMEM((toks // TILE, 2 * HALF + TILE + count, TILE), F32),
            pltpu.VMEM((span + count, toks), BF),
            pltpu.VMEM((span + count, toks), BF),
        ],
        compiler_params=params(),
        cost_estimate=cost(1e6, 1e6),
        name="local",
    )(qd, kv, kv_near, kv_far, rows, bias, expand)
    log_far, log_near = from_far(log_dot), from_near(log_dot)

    dkv, kept_ends, sent_ends = pl.pallas_call(
        functools.partial(global_kernel, scale, scale2),
        grid=(heads,),
        in_specs=[per_head(pair_shape, 1), per_head(row_shape, 1)]
        + [per_head(stats.shape, 1), whole(expand.shape), per_head(pair_shape, 1)],
        out_specs=(per_head(pair_shape, 1), per_head(sum_shape, 2), per_head(sum_shape, 2)),
        out_shape=(struct(pair_shape, F32), sum_struct, sum_struct),
        input_output_aliases={4: 0},
        compiler_params=params(),
        cost_estimate=cost(1e6, 1e6),
        name="global_queries",
    )(kv, rows, after(stats, (log_dot, qd_near, qd_far)), expand, dkv)
    got_sums = from_near(sent_sums)
    got_ends = from_near(after(sent_ends, (log_near, log_far)))

    first = stages[0]
    parts = pl.pallas_call(
        fold_kernel,
        out_shape=[struct((4, heads, slots, width), BF)] * (devices // 2),
        compiler_params=params(),
        name="fold",
    )(kept_ends, got_ends, kept_sums, got_sums)
    for stage in reversed(stages[1:-1]):
        size = len(parts) // (len(stage) + 1)
        kept = parts[:size]
        for number, mask in enumerate(stage):
            sent = parts[(number + 1) * size : (number + 2) * size]
            kept = [one + swap(other, mask) for one, other in zip(kept, sent)]
        parts = kept
    parts = [parts[0]] + [swap(part, mask) for part, mask in zip(parts[1:], first)]

    dkv = pl.pallas_call(
        functools.partial(rim_kernel, scale, scale2),
        grid=(heads,),
        in_specs=[per_head(pair_shape, 1), whole(bias.shape)]
        + [per_head(pair_shape, 1)] * 2
        + [per_head(log_dot.shape, 0)] * 2
        + [per_head(pair_shape, 1)],
        out_specs=per_head(pair_shape, 1),
        out_shape=struct(pair_shape, F32),
        scratch_shapes=[
            pltpu.VMEM((2 * toks, width), BF),
            pltpu.VMEM((2 * toks, width), BF),
            pltpu.VMEM((2, 2, toks), F32),
            pltpu.VMEM((toks, toks + TILE), BF),
            pltpu.VMEM((toks, toks + TILE), BF),
        ],
        compiler_params=params(),
        cost_estimate=cost(1e6, 1e6),
        name="rim",
    )(kv, bias, qd_near, qd_far, log_near, log_far, dkv)

    flat_shape = (toks * heads, width)
    steps = 2
    outs = pl.pallas_call(
        functools.partial(final_kernel, len(parts)),
        grid=(steps,),
        in_specs=[
            pl.BlockSpec((toks // steps, slots), lambda i: (i, 0)),
            pl.BlockSpec((heads, toks // steps, width), lambda i: (0, i, 0)),
            pl.BlockSpec((heads, toks // steps, width), lambda i: (0, i, 0)),
            pl.BlockSpec((2, heads, toks // steps, width), lambda i: (0, 0, i, 0)),
        ]
        + [whole((4, heads, slots, width))] * len(parts),
        out_specs=[pl.BlockSpec((toks * heads // steps, width), lambda i: (i, 0))] * 4,
        out_shape=[struct(flat_shape, kind) for kind in (BF, F32, F32, F32)],
        scratch_shapes=[pltpu.VMEM((toks * heads // steps, width), F32)],
        compiler_params=params(),
        name="final",
    )(place, out, dq, dkv, *parts)
    return tuple(x.reshape(toks, heads, width) for x in outs)


def solution(mesh):
    spec = P("ctx", "head", None)
    return jax.shard_map(
        shards,
        mesh=mesh,
        in_specs=(spec, spec, spec, spec, P()),
        out_specs=(spec, spec, spec, spec),
        check_vma=False,
    )
```

```python
import functools
import math

import jax
import jax.numpy as jnp
from jax import lax
from jax.experimental import pallas as pl
from jax.experimental.pallas import tpu as pltpu
from jax.sharding import PartitionSpec as P

HALF = 512
TILE = 256
NEG = -1e30
LOG2E = 1.0 / math.log(2.0)
VMEM_BYTES = int(63.75 * 1024 * 1024)
BF = jnp.bfloat16
F32 = jnp.float32


def nt(a, b):
    return lax.dot_general(a, b, (((1,), (1,)), ((), ())), preferred_element_type=F32)


def nn(a, b):
    return lax.dot_general(a, b, (((1,), (0,)), ((), ())), preferred_element_type=F32)


def wide(column, width):
    return jnp.concatenate([column] * (width // column.shape[1]), axis=1)


def iota(shape, dim):
    return lax.broadcasted_iota(jnp.int32, shape, dim)


def params():
    return pltpu.CompilerParams(vmem_limit_bytes=VMEM_BYTES)


def as_column(row):
    return jnp.broadcast_to(row, (128, row.shape[1])).T[:, :1]


def pack_keys_kernel(heads, k, v, kv, wide_rows):
    toks = k.shape[0] // heads
    for number, source in enumerate((k, v)):
        wide_rows[number] = source[...].astype(F32)
        for head in range(heads):
            kv[number, head] = wide_rows[number, pl.ds(head, toks, stride=heads), :].astype(BF)


def pack_queries_kernel(heads, slots, q, g, kv, pos_row, qd, slot_rows, wide_rows, acc):
    step = pl.program_id(0)
    toks = q.shape[0] // heads
    row = pos_row[...]
    count = row.shape[1]
    base = lax.axis_index("ctx") * (toks * pl.num_programs(0))
    column = as_column(row)
    tok = iota((count, toks), 1) + (base + step * toks)
    hit = jnp.sum((column == tok).astype(F32), axis=0, keepdims=True)
    rank = jnp.sum(((column >= base) & (column < tok)).astype(F32), axis=0, keepdims=True)
    slot = iota((slots, toks), 0).astype(F32)
    pick = jnp.where((hit > 0) & (rank == slot), 1.0, 0.0).astype(BF)
    tok = iota((toks, count), 0) + (base + step * toks)
    hit_column = jnp.sum((row == tok).astype(F32), axis=1, keepdims=True)
    tables = [[], [kv[0, h] for h in range(heads)], [kv[1, h] for h in range(heads)], []]
    for number, source in ((0, q), (3, g)):
        wide_rows[number // 3] = source[...].astype(F32)
        for head in range(heads):
            rows = wide_rows[number // 3, pl.ds(head, toks, stride=heads), :]
            tables[number].append(rows.astype(BF))
            if number == 0:
                qd[0, head] = rows.astype(BF)
            else:
                qd[1, head] = jnp.where(hit_column > 0, 0.0, rows).astype(BF)
    for number in range(4):
        found = nn(pick, jnp.concatenate(tables[number], axis=1))
        for head in range(heads):
            part = found[:, head * 128 : (head + 1) * 128]
            acc[number, head] = jnp.where(step == 0, part, acc[number, head] + part)

    @pl.when(step == pl.num_programs(0) - 1)
    def _():
        slot_rows[...] = acc[...].astype(BF)


def owner_map(column, owner, toks, slots, shape):
    inside = jnp.sum((column < owner * toks).astype(jnp.int32), axis=0, keepdims=True)
    held = jnp.sum((column < (owner + 1) * toks).astype(jnp.int32), axis=0, keepdims=True) - inside
    slot = iota(shape, 1) % slots
    hot = (iota(shape, 0) == inside + slot) & (slot < held)
    return jnp.where(hot, 1.0, 0.0).astype(BF)


def mask_kernel(order, slots, seq_rows, pos_row, bias, compact, expand, place):
    toks = place.shape[0]
    me = lax.axis_index("ctx")
    base = me * toks
    row = pos_row[...]
    count = row.shape[1]
    column = as_column(row)
    for start in range(0, bias.shape[0], TILE):
        key = iota((TILE, count), 0) + (base - HALF + start)
        hits = jnp.sum((row == key).astype(F32), axis=1, keepdims=True)
        key = key[:, :1]
        out = (hits > 0) | (key < 0) | (key >= seq_rows)
        bias[start : start + TILE, :] = jnp.broadcast_to(jnp.where(out, NEG, 0.0), (TILE, 128))
    tok = iota((toks, count), 0) + base
    hit = jnp.sum((row == tok).astype(F32), axis=1, keepdims=True)
    rank = jnp.sum(((row >= base) & (row < tok)).astype(F32), axis=1, keepdims=True)
    slot = iota((toks, slots), 1).astype(F32)
    place[...] = jnp.where((hit > 0) & (rank == slot), 1.0, 0.0).astype(BF)
    part = iota((1, compact.shape[1]), 1) // slots
    owner = jnp.zeros_like(part)
    for number, relative in enumerate(order):
        owner = jnp.where(part == number, me ^ relative, owner)
    compact[...] = owner_map(column, owner, toks, slots, compact.shape)
    expand[...] = compact[...].astype(F32).T.astype(BF)


def stats_kernel(scale2, compact, *refs):
    parts, (kv, rows, stats) = refs[:-3], refs[-3:]
    pieces = []
    for part in parts:
        for i in range(part.shape[0]):
            pieces.append(jnp.concatenate([part[i, number, 0] for number in range(4)], axis=1))
    packed = nn(compact[...], jnp.concatenate(pieces, axis=0)).astype(BF)
    width = kv.shape[3]
    table = [packed[:, number * width : (number + 1) * width] for number in range(4)]
    for number in range(4):
        rows[number, 0] = table[number]
    queries, _, _, grads = table
    scores = nt(kv[0, 0], queries) * scale2
    top = jnp.max(scores, axis=0, keepdims=True)
    weights = jnp.exp2(scores - top)
    total = jnp.sum(weights, axis=0, keepdims=True)
    dot = jnp.sum(weights * nt(kv[1, 0], grads), axis=0, keepdims=True)
    line = iota(stats.shape[2:], 0)
    found = jnp.where(line == 0, top, jnp.where(line == 1, total, dot))
    for device in range(stats.shape[0]):
        stats[device, 0] = found


def band(scores, low):
    rows, columns = iota(scores.shape, 0), iota(scores.shape, 1)
    return jnp.where(rows <= columns if low else rows >= columns, scores, NEG)


def put_in_slots(expand, tables, kept, sent):
    owners, kinds, _, slots, width = kept.shape
    spread = nn(expand, jnp.concatenate(tables, axis=1)).astype(BF)
    for owner in range(2 * owners):
        for kind in range(kinds):
            (kept if owner < owners else sent)[owner % owners, kind, 0] = spread[
                owner * slots : (owner + 1) * slots, kind * width : (kind + 1) * width
            ]


def fold_kernel(kept_ends, got_ends, kept_sums, got_sums, *outs):
    for part, out in enumerate(outs):
        out[0:2] = (kept_ends[part].astype(F32) + got_ends[part].astype(F32)).astype(BF)
        out[2:4] = (kept_sums[part].astype(F32) + got_sums[part].astype(F32)).astype(BF)


def global_kernel(scale, scale2, kv, rows, stats, expand, before, key_t, value_t, dkv, kept, sent):
    g_query, g_grad = rows[0, 0], rows[3, 0]
    tops = stats[:, 0, 0:1, :]
    top = jnp.max(tops, axis=0)
    factor = jnp.exp2(tops - top[None])
    total = jnp.sum(stats[:, 0, 1:2, :] * factor, axis=0)
    g_dot = jnp.sum(stats[:, 0, 2:3, :] * factor, axis=0) / total
    g_log = top + jnp.log2(total)
    weights = jnp.exp2(nt(kv[0, 0], g_query) * scale2 - g_log)
    narrow = weights.astype(BF)
    slopes = (weights * (nt(kv[1, 0], g_grad) - g_dot)).astype(BF)
    dkv[0, 0] = before[0, 0] + nn(slopes, g_query) * scale
    dkv[1, 0] = before[1, 0] + nn(narrow, g_grad)
    out = nn(value_t[0, 0], narrow).T.astype(BF)
    dq = (nn(key_t[0], slopes) * scale).T.astype(BF)
    put_in_slots(expand[...], (out, dq), kept, sent)


def gather_window(kv, kv_near, kv_far, number, buf):
    toks = kv.shape[2]
    near = 2 * (1 - lax.axis_index("ctx") % 2)
    for block, place in ((kv_near, near), (kv, 1), (kv_far, 2 - near)):
        buf[pl.ds(pl.multiple_of(place * toks, toks), toks), :] = block[number, 0]


def window_kernel(
    scale2, qd, kv, kv_near, kv_far, bias, probs, acc, top_sum, key_t, values, sides, keys, score_buf
):
    toks = kv.shape[2]
    reach = 2 * HALF + TILE
    gather_window(kv, kv_near, kv_far, 0, keys)
    gather_window(kv, kv_near, kv_far, 1, values.at[0])
    key_t[0] = keys[...].T
    value_t = values[0].T
    query_t = qd[0, 0].T
    sides[0, 0] = query_t
    sides[1, 0] = qd[1, 0].T
    sides[2, 0] = value_t[:, HALF : HALF + toks]
    tiles = range(toks // TILE)
    lanes = [slice(tile * TILE, (tile + 1) * TILE) for tile in tiles]
    pieces = range(reach // TILE)
    best, top, total = ([None] * len(tiles) for _ in range(3))

    def score(tile, piece):
        span = slice((tile + piece) * TILE, (tile + piece + 1) * TILE)
        scores = nn(keys[span, :], query_t[:, lanes[tile]]) * scale2
        scores = scores + wide(bias[span, :], TILE)
        if piece == 0:
            scores = band(scores, False)
        elif piece == len(pieces) - 1:
            scores = band(scores, True)
        score_buf[tile, piece * TILE : (piece + 1) * TILE, :] = scores
        part = jnp.max(scores.reshape(TILE // 8, 8, TILE), axis=0)
        best[tile] = part if best[tile] is None else jnp.maximum(best[tile], part)

    def weigh(tile, piece):
        if top[tile] is None:
            top[tile] = jnp.max(best[tile], axis=0, keepdims=True)
        span = slice((tile + piece) * TILE, (tile + piece + 1) * TILE)
        weights = jnp.exp2(score_buf[tile, piece * TILE : (piece + 1) * TILE, :] - top[tile])
        probs[0, span, lanes[tile]] = weights.astype(BF)
        part = jnp.sum(weights.reshape(TILE // 8, 8, TILE), axis=0)
        total[tile] = part if total[tile] is None else total[tile] + part

    for step in range(len(tiles) + 1):
        for piece in pieces:
            if step:
                weigh(step - 1, piece)
            if step < len(tiles):
                score(step, piece)
        if step:
            tile = step - 1
            window = slice(tile * TILE, tile * TILE + reach)
            acc[0, :, lanes[tile]] = nn(value_t[:, window], probs[0, window, lanes[tile]])
            top_sum[0, 0:1, lanes[tile]] = top[tile]
            top_sum[0, 1:2, lanes[tile]] = jnp.sum(total[tile], axis=0, keepdims=True)


def local_kernel(
    scale, scale2, sides, key_t, values, rows, probs, acc, top_sum, expand,
    out, log_dot, dq, dkv, kept, sent, slopes,
):
    toks = acc.shape[2]
    reach = 2 * HALF + TILE
    query_t, grad_t = sides[0, 0], sides[1, 0]
    g_keys, g_values = rows[1, 0], rows[2, 0]
    g_key_t, g_value_t = g_keys.T, g_values.T
    grads = grad_t.astype(F32)
    scores = nn(g_keys, query_t) * scale2
    old = top_sum[0, 0:1, :]
    top = jnp.maximum(old, jnp.max(scores, axis=0, keepdims=True))
    weights = jnp.exp2(scores - top)
    factor = jnp.exp2(old - top)
    total = top_sum[0, 1:2, :] * factor + jnp.sum(weights, axis=0, keepdims=True)
    inverse = 1.0 / total
    g_probs = weights.astype(BF)
    result = (acc[0] * factor + nn(g_value_t, g_probs)) * inverse
    dot = jnp.sum(grads * result, axis=0, keepdims=True)
    log_dot[0, 0:1, :] = top + jnp.log2(total)
    log_dot[0, 1:2, :] = dot
    out[0] = result.T.astype(BF)
    share = factor * inverse
    g_grads = (grads * inverse).astype(BF)
    w_grads = (grads * share).astype(BF)
    g_slopes = (weights * (nn(g_values, g_grads) - dot * inverse)).astype(BF)
    dots = dot * share
    for tile in range(toks // TILE):
        lanes = slice(tile * TILE, (tile + 1) * TILE)
        for piece in range(reach // TILE):
            span = slice((tile + piece) * TILE, (tile + piece + 1) * TILE)
            rise = nn(values[0, span, :], w_grads[:, lanes]) - dots[:, lanes]
            slopes[span, lanes] = (probs[0, span, lanes].astype(F32) * rise).astype(BF)
    for tile in range(toks // TILE):
        lanes = slice(tile * TILE, (tile + 1) * TILE)
        window = slice(tile * TILE, tile * TILE + reach)
        part = nn(key_t[0, :, window], slopes[window, lanes]) + nn(g_key_t, g_slopes[:, lanes])
        dq[0, lanes, :] = (part * scale).T
    own = slice(HALF, HALF + toks)
    dkv[0, 0] = (nt(query_t, slopes[own, :]) * scale).T
    dkv[1, 0] = nt(w_grads, probs[0, own, :]).T
    g_dk = (nt(query_t, g_slopes) * scale).T.astype(BF)
    g_dv = nt(g_grads, g_probs).T.astype(BF)
    put_in_slots(expand[...], (g_dk, g_dv), kept, sent)


def rim_kernel(
    scale, scale2, kv, bias, qd_near, qd_far, log_near, log_far, partial, dkv,
    queries, grads, logs, probs, slopes,
):
    toks = kv.shape[2]
    reach = toks + TILE
    near = 1 - lax.axis_index("ctx") % 2
    for qd, log_dot, place in ((qd_near, log_near, near), (qd_far, log_far, 1 - near)):
        spot = pl.ds(pl.multiple_of(place * toks, toks), toks)
        queries[spot, :] = qd[0, 0]
        grads[spot, :] = qd[1, 0]
        logs[place] = log_dot[0]
    for k_tile in range(toks // TILE):
        span = slice(k_tile * TILE, (k_tile + 1) * TILE)
        key = kv[0, 0, span, :]
        value = kv[1, 0, span, :]
        key_bias = wide(bias[span, :], TILE)
        for piece in range(reach // TILE):
            start = (k_tile + piece) * TILE
            side, lanes = start // toks, slice(start % toks, start % toks + TILE)
            scores = nt(key, queries[start : start + TILE, :]) * scale2 + key_bias
            if piece == 0:
                scores = band(scores, True)
            elif piece == reach // TILE - 1:
                scores = band(scores, False)
            weights = jnp.exp2(scores - logs[side, 0:1, lanes])
            slope = weights * (nt(value, grads[start : start + TILE, :]) - logs[side, 1:2, lanes])
            spot = slice(piece * TILE, (piece + 1) * TILE)
            probs[span, spot] = weights.astype(BF)
            slopes[span, spot] = slope.astype(BF)
        window = slice(k_tile * TILE, k_tile * TILE + reach)
        dkv[0, 0, span, :] = partial[0, 0, span, :] + nn(slopes[span, :], queries[window, :]) * scale
        dkv[1, 0, span, :] = partial[1, 0, span, :] + nn(probs[span, :], grads[window, :])


def final_kernel(sources, place, out, dq, dkv, *refs):
    parts, refs = refs[:sources], refs[sources:]
    attn, query_grad, key_grad, value_grad, wide_rows, tables = refs
    heads, toks, width = out.shape

    @pl.when(pl.program_id(0) == 0)
    def _():
        for head in range(heads):
            for kind in range(4):
                table = parts[0][kind, head].astype(F32)
                for part in parts[1:]:
                    table = table + part[kind, head].astype(F32)
                tables[head, :, kind * width : (kind + 1) * width] = table.astype(BF)

    hot = place[...]
    is_global = jnp.sum(hot.astype(F32), axis=1, keepdims=True) > 0
    for head in range(heads):
        rows = pl.ds(head, toks, stride=heads)
        added = nn(hot, tables[head])
        added = [added[:, i * width : (i + 1) * width] for i in range(4)]
        wide_rows[rows, :] = jnp.where(is_global, added[0], out[head].astype(F32))
        query_grad[rows, :] = dq[head] + added[1]
        key_grad[rows, :] = dkv[0, head] + added[2]
        value_grad[rows, :] = dkv[1, head] + added[3]
    attn[...] = wide_rows[...].astype(BF)


def cost(flops, moved, exps=0):
    return pl.CostEstimate(flops=int(flops), bytes_accessed=int(moved), transcendentals=int(exps))


def struct(shape, dtype):
    return jax.ShapeDtypeStruct(shape, dtype)


def whole(shape):
    return pl.BlockSpec(shape, lambda head: (0,) * len(shape))


def per_head(shape, dim, first=0):
    block = tuple(1 if i == dim else size for i, size in enumerate(shape))
    return pl.BlockSpec(
        block, lambda head: tuple(head + first if i == dim else 0 for i in range(len(shape)))
    )


def shards(query_rows, key_rows, value_rows, out_grad, global_pos):
    toks, heads, width = query_rows.shape
    count = global_pos.shape[0]
    devices = lax.axis_size("ctx")
    slots = max(16, 2 * count // devices)
    scale = width ** (-0.5)
    scale2 = scale * LOG2E
    bits = devices.bit_length() - 1
    stages = [
        [mask << low for mask in range(1, 1 << min(2, bits - low))] for low in range(1, bits, 2)
    ] + [[1]]
    order = [0]
    for stage in stages:
        order = order + [one ^ mask for mask in stage for one in order]
    pos_row = global_pos.reshape(1, count)
    q_flat, k_flat, v_flat, g_flat = (
        x.reshape(toks * heads, width) for x in (query_rows, key_rows, value_rows, out_grad)
    )

    def swap(value, mask):
        return lax.ppermute(value, "ctx", [(i, i ^ mask) for i in range(devices)])

    def from_near(value):
        return swap(value, 1)

    def from_far(value):
        pairs = [(i, i + 1) for i in range(1, devices - 1, 2)]
        return lax.ppermute(value, "ctx", pairs + [(j, i) for i, j in pairs])

    def after(value, earlier):
        return lax.optimization_barrier((value, earlier))[0]

    pair_shape = (2, heads, toks, width)
    slot_shape = (4, heads, slots, width)
    steps = 1
    flat_spec = pl.BlockSpec((toks * heads // steps, width), lambda i: (i, 0))
    pair_spec = pl.BlockSpec((2, heads, toks // steps, width), lambda i: (0, 0, i, 0))
    wide_pair = pltpu.VMEM((2, toks * heads // steps, width), F32)
    kv = pl.pallas_call(
        functools.partial(pack_keys_kernel, heads),
        out_shape=struct(pair_shape, BF),
        scratch_shapes=[wide_pair],
        compiler_params=params(),
        name="pack_keys",
    )(k_flat, v_flat)

    qd, slot_rows = pl.pallas_call(
        functools.partial(pack_queries_kernel, heads, slots),
        grid=(steps,),
        in_specs=[flat_spec, flat_spec, pair_spec, whole((1, count))],
        out_specs=(pair_spec, whole(slot_shape)),
        out_shape=(struct(pair_shape, BF), struct(slot_shape, BF)),
        scratch_shapes=[wide_pair, pltpu.VMEM(slot_shape, F32)],
        compiler_params=params(),
        name="pack_queries",
    )(q_flat, g_flat, kv, pos_row)

    span = toks + 2 * HALF
    bias, compact, expand, place = pl.pallas_call(
        functools.partial(mask_kernel, order, slots, toks * devices),
        out_shape=(
            struct((span, 128), F32),
            struct((count, devices * slots), BF),
            struct((devices * slots, count), BF),
            struct((toks, slots), BF),
        ),
        compiler_params=params(),
        name="masks",
    )(pos_row)

    kv_far, kv_near = from_far(kv), from_near(kv)
    probs_shape = (heads, span, toks)
    acc_shape = (heads, width, toks)
    turned_shape = (heads, width, span)
    sides_shape = (3, heads, width, toks)
    probs, acc, top_sum, key_t, values, sides = pl.pallas_call(
        functools.partial(window_kernel, scale2),
        grid=(heads,),
        in_specs=[per_head(pair_shape, 1)] * 4 + [whole(bias.shape)],
        out_specs=(
            per_head(probs_shape, 0),
            per_head(acc_shape, 0),
            per_head((heads, 2, toks), 0),
            per_head(turned_shape, 0),
            per_head((heads, span, width), 0),
            per_head(sides_shape, 1),
        ),
        out_shape=(
            struct(probs_shape, BF),
            struct(acc_shape, F32),
            struct((heads, 2, toks), F32),
            struct(turned_shape, BF),
            struct((heads, span, width), BF),
            struct(sides_shape, BF),
        ),
        scratch_shapes=[
            pltpu.VMEM((span, width), BF),
            pltpu.VMEM((toks // TILE, 2 * HALF + TILE, TILE), F32),
        ],
        compiler_params=params(),
        cost_estimate=cost(1e6, 1e6),
        name="window",
    )(qd, kv, kv_near, kv_far, bias)
    held = [slot_rows[None]]
    for number, stage in enumerate(stages):
        if stage == [1]:
            held = after(held, top_sum)
        send = jnp.concatenate(held, axis=0) if number else held[0]
        held += [swap(send, mask) for mask in stage]

    row_shape = (4, heads, count, width)
    rows, stats = pl.pallas_call(
        functools.partial(stats_kernel, scale2),
        grid=(heads,),
        in_specs=[whole(compact.shape)]
        + [per_head(part.shape, 2) for part in held]
        + [per_head(pair_shape, 1)],
        out_specs=(per_head(row_shape, 1), per_head((devices, heads, 8, count), 1)),
        out_shape=(struct(row_shape, BF), struct((devices, heads, 8, count), F32)),
        compiler_params=params(),
        cost_estimate=cost(1e6, 1e6),
        name="global_stats",
    )(compact, *held, kv)

    stats = lax.all_to_all(stats, "ctx", 0, 0, tiled=True)

    sum_shape = (devices // 2, 2, heads, slots, width)
    sum_struct = struct(sum_shape, BF)
    qd_late = after(qd, (kv_near, kv_far))
    qd_far, qd_near = from_far(qd_late), from_near(qd_late)

    out, log_dot, dq, dkv, kept_sums, sent_sums = pl.pallas_call(
        functools.partial(local_kernel, scale, scale2),
        grid=(heads,),
        in_specs=[per_head(sides_shape, 1), per_head(turned_shape, 0)]
        + [per_head((heads, span, width), 0), per_head(row_shape, 1)]
        + [per_head(probs_shape, 0), per_head(acc_shape, 0)]
        + [per_head((heads, 2, toks), 0), whole(expand.shape)],
        out_specs=(
            per_head((heads, toks, width), 0),
            per_head((heads, 2, toks), 0),
            per_head((heads, toks, width), 0),
            per_head(pair_shape, 1),
            per_head(sum_shape, 2),
            per_head(sum_shape, 2),
        ),
        out_shape=(
            struct((heads, toks, width), BF),
            struct((heads, 2, toks), F32),
            struct((heads, toks, width), F32),
            struct(pair_shape, F32),
            sum_struct,
            sum_struct,
        ),
        scratch_shapes=[
            pltpu.VMEM((span, toks), BF),
        ],
        compiler_params=params(),
        cost_estimate=cost(1e6, 1e6),
        name="local",
    )(sides, key_t, values, rows, probs, acc, top_sum, expand)
    log_far, log_near = from_far(log_dot), from_near(log_dot)

    dkv, kept_ends, sent_ends = pl.pallas_call(
        functools.partial(global_kernel, scale, scale2),
        grid=(heads,),
        in_specs=[per_head(pair_shape, 1), per_head(row_shape, 1)]
        + [per_head(stats.shape, 1), whole(expand.shape), per_head(pair_shape, 1)]
        + [pl.BlockSpec((1, width, toks), lambda head: (head, 0, HALF // toks))]
        + [pl.BlockSpec((1, 1, width, toks), lambda head: (2, head, 0, 0))],
        out_specs=(per_head(pair_shape, 1), per_head(sum_shape, 2), per_head(sum_shape, 2)),
        out_shape=(struct(pair_shape, F32), sum_struct, sum_struct),
        input_output_aliases={4: 0},
        compiler_params=params(),
        cost_estimate=cost(1e6, 1e6),
        name="global_queries",
    )(kv, rows, after(stats, (log_dot, qd_near, qd_far)), expand, dkv, key_t, sides)
    got_sums = from_near(sent_sums)
    got_ends = from_near(after(sent_ends, (log_near, log_far)))

    first = stages[0]
    parts = pl.pallas_call(
        fold_kernel,
        out_shape=[struct((4, heads, slots, width), BF)] * (devices // 2),
        compiler_params=params(),
        name="fold",
    )(kept_ends, got_ends, kept_sums, got_sums)
    for stage in reversed(stages[1:-1]):
        size = len(parts) // (len(stage) + 1)
        kept = parts[:size]
        for number, mask in enumerate(stage):
            sent = parts[(number + 1) * size : (number + 2) * size]
            kept = [one + swap(other, mask) for one, other in zip(kept, sent)]
        parts = kept
    parts = [parts[0]] + [swap(part, mask) for part, mask in zip(parts[1:], first)]

    dkv = pl.pallas_call(
        functools.partial(rim_kernel, scale, scale2),
        grid=(heads,),
        in_specs=[per_head(pair_shape, 1), pl.BlockSpec((toks, 128), lambda head: (HALF // toks, 0))]
        + [per_head(pair_shape, 1)] * 2
        + [per_head(log_dot.shape, 0)] * 2
        + [per_head(pair_shape, 1)],
        out_specs=per_head(pair_shape, 1),
        out_shape=struct(pair_shape, F32),
        scratch_shapes=[
            pltpu.VMEM((2 * toks, width), BF),
            pltpu.VMEM((2 * toks, width), BF),
            pltpu.VMEM((2, 2, toks), F32),
            pltpu.VMEM((toks, toks + TILE), BF),
            pltpu.VMEM((toks, toks + TILE), BF),
        ],
        compiler_params=params(),
        cost_estimate=cost(1e6, 1e6),
        name="rim",
    )(kv, bias, qd_near, qd_far, log_near, log_far, dkv)

    flat_shape = (toks * heads, width)
    steps = 4
    outs = pl.pallas_call(
        functools.partial(final_kernel, len(parts)),
        grid=(steps,),
        in_specs=[
            pl.BlockSpec((toks // steps, slots), lambda i: (i, 0)),
            pl.BlockSpec((heads, toks // steps, width), lambda i: (0, i, 0)),
            pl.BlockSpec((heads, toks // steps, width), lambda i: (0, i, 0)),
            pl.BlockSpec((2, heads, toks // steps, width), lambda i: (0, 0, i, 0)),
        ]
        + [whole((4, heads, slots, width))] * len(parts),
        out_specs=[pl.BlockSpec((toks * heads // steps, width), lambda i: (i, 0))] * 4,
        out_shape=[struct(flat_shape, kind) for kind in (BF, F32, F32, F32)],
        scratch_shapes=[
            pltpu.VMEM((toks * heads // steps, width), F32),
            pltpu.VMEM((heads, slots, 4 * width), BF),
        ],
        compiler_params=params(),
        name="final",
    )(place, out, dq, dkv, *parts)
    return tuple(x.reshape(toks, heads, width) for x in outs)


def solution(mesh):
    spec = P("ctx", "head", None)
    return jax.shard_map(
        shards,
        mesh=mesh,
        in_specs=(spec, spec, spec, spec, P()),
        out_specs=(spec, spec, spec, spec),
        check_vma=False,
    )
```

```python
import functools
import math

import jax
import jax.numpy as jnp
from jax import lax
from jax.experimental import pallas as pl
from jax.experimental.pallas import tpu as pltpu
from jax.sharding import PartitionSpec as P

HALF = 512
TILE = 256
NEG = -1e30
LOG2E = 1.0 / math.log(2.0)
VMEM_BYTES = int(63.75 * 1024 * 1024)
BF = jnp.bfloat16
F32 = jnp.float32


def nt(a, b):
    return lax.dot_general(a, b, (((1,), (1,)), ((), ())), preferred_element_type=F32)


def nn(a, b):
    return lax.dot_general(a, b, (((1,), (0,)), ((), ())), preferred_element_type=F32)


def wide(column, width):
    return jnp.concatenate([column] * (width // column.shape[1]), axis=1)


def iota(shape, dim):
    return lax.broadcasted_iota(jnp.int32, shape, dim)


def params():
    return pltpu.CompilerParams(vmem_limit_bytes=VMEM_BYTES)


def as_column(row):
    return jnp.broadcast_to(row, (128, row.shape[1])).T[:, :1]


def pack_keys_kernel(heads, k, v, kv, wide_rows):
    toks = k.shape[0] // heads
    for number, source in enumerate((k, v)):
        wide_rows[number] = source[...].astype(F32)
        for head in range(heads):
            kv[number, head] = wide_rows[number, pl.ds(head, toks, stride=heads), :].astype(BF)


def pack_queries_kernel(heads, slots, q, g, kv, pos_row, qd, slot_rows, wide_rows, acc):
    step = pl.program_id(0)
    toks = q.shape[0] // heads
    row = pos_row[...]
    count = row.shape[1]
    base = lax.axis_index("ctx") * (toks * pl.num_programs(0))
    column = as_column(row)
    tok = iota((count, toks), 1) + (base + step * toks)
    hit = jnp.sum((column == tok).astype(F32), axis=0, keepdims=True)
    rank = jnp.sum(((column >= base) & (column < tok)).astype(F32), axis=0, keepdims=True)
    slot = iota((slots, toks), 0).astype(F32)
    pick = jnp.where((hit > 0) & (rank == slot), 1.0, 0.0).astype(BF)
    tok = iota((toks, count), 0) + (base + step * toks)
    hit_column = jnp.sum((row == tok).astype(F32), axis=1, keepdims=True)
    tables = [[], [kv[0, h] for h in range(heads)], [kv[1, h] for h in range(heads)], []]
    for number, source in ((0, q), (3, g)):
        wide_rows[number // 3] = source[...].astype(F32)
        for head in range(heads):
            rows = wide_rows[number // 3, pl.ds(head, toks, stride=heads), :]
            tables[number].append(rows.astype(BF))
            if number == 0:
                qd[0, head] = rows.astype(BF)
            else:
                qd[1, head] = jnp.where(hit_column > 0, 0.0, rows).astype(BF)
    for number in range(4):
        found = nn(pick, jnp.concatenate(tables[number], axis=1))
        for head in range(heads):
            part = found[:, head * 128 : (head + 1) * 128]
            acc[number, head] = jnp.where(step == 0, part, acc[number, head] + part)

    @pl.when(step == pl.num_programs(0) - 1)
    def _():
        slot_rows[...] = acc[...].astype(BF)


def owner_map(column, owner, toks, slots, shape):
    inside = jnp.sum((column < owner * toks).astype(jnp.int32), axis=0, keepdims=True)
    held = jnp.sum((column < (owner + 1) * toks).astype(jnp.int32), axis=0, keepdims=True) - inside
    slot = iota(shape, 1) % slots
    hot = (iota(shape, 0) == inside + slot) & (slot < held)
    return jnp.where(hot, 1.0, 0.0).astype(BF)


def mask_kernel(order, slots, seq_rows, pos_row, bias, compact, expand, place):
    toks = place.shape[0]
    me = lax.axis_index("ctx")
    base = me * toks
    row = pos_row[...]
    count = row.shape[1]
    column = as_column(row)
    for start in range(0, bias.shape[0], TILE):
        key = iota((TILE, count), 0) + (base - HALF + start)
        hits = jnp.sum((row == key).astype(F32), axis=1, keepdims=True)
        key = key[:, :1]
        out = (hits > 0) | (key < 0) | (key >= seq_rows)
        bias[start : start + TILE, :] = jnp.broadcast_to(jnp.where(out, NEG, 0.0), (TILE, 128))
    tok = iota((toks, count), 0) + base
    hit = jnp.sum((row == tok).astype(F32), axis=1, keepdims=True)
    rank = jnp.sum(((row >= base) & (row < tok)).astype(F32), axis=1, keepdims=True)
    slot = iota((toks, slots), 1).astype(F32)
    place[...] = jnp.where((hit > 0) & (rank == slot), 1.0, 0.0).astype(BF)
    part = iota((1, compact.shape[1]), 1) // slots
    owner = jnp.zeros_like(part)
    for number, relative in enumerate(order):
        owner = jnp.where(part == number, me ^ relative, owner)
    compact[...] = owner_map(column, owner, toks, slots, compact.shape)
    expand[...] = compact[...].astype(F32).T.astype(BF)


def stats_kernel(scale2, compact, *refs):
    parts, (kv, rows, stats) = refs[:-3], refs[-3:]
    pieces = []
    for part in parts:
        for i in range(part.shape[0]):
            pieces.append(jnp.concatenate([part[i, number, 0] for number in range(4)], axis=1))
    packed = nn(compact[...], jnp.concatenate(pieces, axis=0)).astype(BF)
    width = kv.shape[3]
    table = [packed[:, number * width : (number + 1) * width] for number in range(4)]
    for number in range(4):
        rows[number, 0] = table[number]
    queries, _, _, grads = table
    scores = nt(kv[0, 0], queries) * scale2
    top = jnp.max(scores, axis=0, keepdims=True)
    weights = jnp.exp2(scores - top)
    total = jnp.sum(weights, axis=0, keepdims=True)
    dot = jnp.sum(weights * nt(kv[1, 0], grads), axis=0, keepdims=True)
    line = iota(stats.shape[2:], 0)
    found = jnp.where(line == 0, top, jnp.where(line == 1, total, dot))
    for device in range(stats.shape[0]):
        stats[device, 0] = found


def band(scores, low):
    rows, columns = iota(scores.shape, 0), iota(scores.shape, 1)
    return jnp.where(rows <= columns if low else rows >= columns, scores, NEG)


def put_in_slots(expand, tables, kept, sent):
    owners, kinds, _, slots, width = kept.shape
    spread = nn(expand, jnp.concatenate(tables, axis=1)).astype(BF)
    for owner in range(2 * owners):
        for kind in range(kinds):
            (kept if owner < owners else sent)[owner % owners, kind, 0] = spread[
                owner * slots : (owner + 1) * slots, kind * width : (kind + 1) * width
            ]


def fold_kernel(kept_ends, got_ends, kept_sums, got_sums, *outs):
    for part, out in enumerate(outs):
        out[0:2] = (kept_ends[part].astype(F32) + got_ends[part].astype(F32)).astype(BF)
        out[2:4] = (kept_sums[part].astype(F32) + got_sums[part].astype(F32)).astype(BF)


def global_kernel(scale, scale2, kv, rows, stats, expand, before, key_t, value_t, dkv, kept, sent):
    g_query, g_grad = rows[0, 0], rows[3, 0]
    tops = stats[:, 0, 0:1, :]
    top = jnp.max(tops, axis=0)
    factor = jnp.exp2(tops - top[None])
    total = jnp.sum(stats[:, 0, 1:2, :] * factor, axis=0)
    g_dot = jnp.sum(stats[:, 0, 2:3, :] * factor, axis=0) / total
    g_log = top + jnp.log2(total)
    weights = jnp.exp2(nt(kv[0, 0], g_query) * scale2 - g_log)
    narrow = weights.astype(BF)
    slopes = (weights * (nt(kv[1, 0], g_grad) - g_dot)).astype(BF)
    dkv[0, 0] = before[0, 0] + nn(slopes, g_query) * scale
    dkv[1, 0] = before[1, 0] + nn(narrow, g_grad)
    out = nn(value_t[0, 0], narrow).T.astype(BF)
    dq = (nn(key_t[0], slopes) * scale).T.astype(BF)
    put_in_slots(expand[...], (out, dq), kept, sent)


def gather_window(kv, kv_near, kv_far, number, buf):
    toks = kv.shape[2]
    near = 2 * (1 - lax.axis_index("ctx") % 2)
    for block, place in ((kv_near, near), (kv, 1), (kv_far, 2 - near)):
        buf[pl.ds(pl.multiple_of(place * toks, toks), toks), :] = block[number, 0]


def window_kernel(
    scale2, qd, kv, kv_near, kv_far, bias, probs, acc, top_sum, key_t, values, sides, keys, score_buf
):
    toks = kv.shape[2]
    reach = 2 * HALF + TILE
    gather_window(kv, kv_near, kv_far, 0, keys)
    gather_window(kv, kv_near, kv_far, 1, values.at[0])
    key_t[0] = keys[...].T
    value_t = values[0].T
    query_t = qd[0, 0].T
    sides[0, 0] = query_t
    sides[1, 0] = qd[1, 0].T
    sides[2, 0] = value_t[:, HALF : HALF + toks]
    tiles = range(toks // TILE)
    lanes = [slice(tile * TILE, (tile + 1) * TILE) for tile in tiles]
    pieces = range(reach // TILE)
    best, top, total = ([None] * len(tiles) for _ in range(3))

    def score(tile, piece):
        span = slice((tile + piece) * TILE, (tile + piece + 1) * TILE)
        scores = nn(keys[span, :], query_t[:, lanes[tile]]) * scale2
        scores = scores + wide(bias[span, :], TILE)
        if piece == 0:
            scores = band(scores, False)
        elif piece == len(pieces) - 1:
            scores = band(scores, True)
        score_buf[tile, piece * TILE : (piece + 1) * TILE, :] = scores
        part = jnp.max(scores.reshape(TILE // 8, 8, TILE), axis=0)
        best[tile] = part if best[tile] is None else jnp.maximum(best[tile], part)

    def weigh(tile, piece):
        if top[tile] is None:
            top[tile] = jnp.max(best[tile], axis=0, keepdims=True)
        span = slice((tile + piece) * TILE, (tile + piece + 1) * TILE)
        weights = jnp.exp2(score_buf[tile, piece * TILE : (piece + 1) * TILE, :] - top[tile])
        probs[0, span, lanes[tile]] = weights.astype(BF)
        part = jnp.sum(weights.reshape(TILE // 8, 8, TILE), axis=0)
        total[tile] = part if total[tile] is None else total[tile] + part

    for step in range(len(tiles) + 1):
        for piece in pieces:
            if step:
                weigh(step - 1, piece)
            if step < len(tiles):
                score(step, piece)
        if step:
            tile = step - 1
            window = slice(tile * TILE, tile * TILE + reach)
            acc[0, :, lanes[tile]] = nn(value_t[:, window], probs[0, window, lanes[tile]])
            top_sum[0, 0:1, lanes[tile]] = top[tile]
            top_sum[0, 1:2, lanes[tile]] = jnp.sum(total[tile], axis=0, keepdims=True)


def local_kernel(
    scale, scale2, sides, key_t, values, rows, probs, acc, top_sum, expand,
    out, log_dot, dq, dkv, kept, sent, slopes,
):
    toks = acc.shape[2]
    reach = 2 * HALF + TILE
    query_t, grad_t = sides[0, 0], sides[1, 0]
    g_keys, g_values = rows[1, 0], rows[2, 0]
    g_key_t, g_value_t = g_keys.T, g_values.T
    grads = grad_t.astype(F32)
    scores = nn(g_keys, query_t) * scale2
    old = top_sum[0, 0:1, :]
    top = jnp.maximum(old, jnp.max(scores, axis=0, keepdims=True))
    weights = jnp.exp2(scores - top)
    factor = jnp.exp2(old - top)
    total = top_sum[0, 1:2, :] * factor + jnp.sum(weights, axis=0, keepdims=True)
    inverse = 1.0 / total
    g_probs = weights.astype(BF)
    result = (acc[0] * factor + nn(g_value_t, g_probs)) * inverse
    dot = jnp.sum(grads * result, axis=0, keepdims=True)
    log_dot[0, 0:1, :] = top + jnp.log2(total)
    log_dot[0, 1:2, :] = dot
    out[0] = result.T.astype(BF)
    share = factor * inverse
    g_grads = (grads * inverse).astype(BF)
    w_grads = (grads * share).astype(BF)
    g_slopes = (weights * (nn(g_values, g_grads) - dot * inverse)).astype(BF)
    dots = dot * share
    for tile in range(toks // TILE):
        lanes = slice(tile * TILE, (tile + 1) * TILE)
        for piece in range(reach // TILE):
            span = slice((tile + piece) * TILE, (tile + piece + 1) * TILE)
            rise = nn(values[0, span, :], w_grads[:, lanes]) - dots[:, lanes]
            slopes[span, lanes] = (probs[0, span, lanes].astype(F32) * rise).astype(BF)
    for tile in range(toks // TILE):
        lanes = slice(tile * TILE, (tile + 1) * TILE)
        window = slice(tile * TILE, tile * TILE + reach)
        part = nn(key_t[0, :, window], slopes[window, lanes]) + nn(g_key_t, g_slopes[:, lanes])
        dq[0, lanes, :] = (part * scale).T
    own = slice(HALF, HALF + toks)
    dkv[0, 0] = (nt(query_t, slopes[own, :]) * scale).T
    dkv[1, 0] = nt(w_grads, probs[0, own, :]).T
    g_dk = (nt(query_t, g_slopes) * scale).T.astype(BF)
    g_dv = nt(g_grads, g_probs).T.astype(BF)
    put_in_slots(expand[...], (g_dk, g_dv), kept, sent)


def rim_kernel(
    scale, scale2, kv, bias, qd_near, qd_far, log_near, log_far, partial, dkv,
    queries, grads, logs, probs, slopes,
):
    toks = kv.shape[2]
    reach = toks + TILE
    near = 1 - lax.axis_index("ctx") % 2
    for qd, log_dot, place in ((qd_near, log_near, near), (qd_far, log_far, 1 - near)):
        spot = pl.ds(pl.multiple_of(place * toks, toks), toks)
        queries[spot, :] = qd[0, 0]
        grads[spot, :] = qd[1, 0]
        logs[place] = log_dot[0]
    for k_tile in range(toks // TILE):
        span = slice(k_tile * TILE, (k_tile + 1) * TILE)
        key = kv[0, 0, span, :]
        value = kv[1, 0, span, :]
        key_bias = wide(bias[span, :], TILE)
        for piece in range(reach // TILE):
            start = (k_tile + piece) * TILE
            side, lanes = start // toks, slice(start % toks, start % toks + TILE)
            scores = nt(key, queries[start : start + TILE, :]) * scale2 + key_bias
            if piece == 0:
                scores = band(scores, True)
            elif piece == reach // TILE - 1:
                scores = band(scores, False)
            weights = jnp.exp2(scores - logs[side, 0:1, lanes])
            slope = weights * (nt(value, grads[start : start + TILE, :]) - logs[side, 1:2, lanes])
            spot = slice(piece * TILE, (piece + 1) * TILE)
            probs[span, spot] = weights.astype(BF)
            slopes[span, spot] = slope.astype(BF)
        window = slice(k_tile * TILE, k_tile * TILE + reach)
        dkv[0, 0, span, :] = partial[0, 0, span, :] + nn(slopes[span, :], queries[window, :]) * scale
        dkv[1, 0, span, :] = partial[1, 0, span, :] + nn(probs[span, :], grads[window, :])


def final_kernel(
    sources, place, out, dq, dkv, *refs
):
    parts, refs = refs[:sources], refs[sources:]
    attn, query_grad, key_grad, value_grad, wide_rows = refs
    heads, toks = out.shape[0], out.shape[1]
    hot = place[...]
    is_global = jnp.sum(hot.astype(F32), axis=1, keepdims=True) > 0
    for head in range(heads):
        rows = pl.ds(head, toks, stride=heads)
        tables = []
        for kind in range(4):
            table = parts[0][kind, head].astype(F32)
            for part in parts[1:]:
                table = table + part[kind, head].astype(F32)
            tables.append(table.astype(BF))
        width = out.shape[2]
        added = nn(hot, jnp.concatenate(tables, axis=1))
        added = [added[:, i * width : (i + 1) * width] for i in range(4)]
        wide_rows[rows, :] = jnp.where(is_global, added[0], out[head].astype(F32))
        query_grad[rows, :] = dq[head] + added[1]
        key_grad[rows, :] = dkv[0, head] + added[2]
        value_grad[rows, :] = dkv[1, head] + added[3]
    attn[...] = wide_rows[...].astype(BF)


def cost(flops, moved, exps=0):
    return pl.CostEstimate(flops=int(flops), bytes_accessed=int(moved), transcendentals=int(exps))


def struct(shape, dtype):
    return jax.ShapeDtypeStruct(shape, dtype)


def whole(shape):
    return pl.BlockSpec(shape, lambda head: (0,) * len(shape))


def per_head(shape, dim, first=0):
    block = tuple(1 if i == dim else size for i, size in enumerate(shape))
    return pl.BlockSpec(
        block, lambda head: tuple(head + first if i == dim else 0 for i in range(len(shape)))
    )


def shards(query_rows, key_rows, value_rows, out_grad, global_pos):
    toks, heads, width = query_rows.shape
    count = global_pos.shape[0]
    devices = lax.axis_size("ctx")
    slots = max(16, 2 * count // devices)
    scale = width ** (-0.5)
    scale2 = scale * LOG2E
    bits = devices.bit_length() - 1
    stages = [
        [mask << low for mask in range(1, 1 << min(2, bits - low))] for low in range(1, bits, 2)
    ] + [[1]]
    order = [0]
    for stage in stages:
        order = order + [one ^ mask for mask in stage for one in order]
    pos_row = global_pos.reshape(1, count)
    q_flat, k_flat, v_flat, g_flat = (
        x.reshape(toks * heads, width) for x in (query_rows, key_rows, value_rows, out_grad)
    )

    def swap(value, mask):
        return lax.ppermute(value, "ctx", [(i, i ^ mask) for i in range(devices)])

    def from_near(value):
        return swap(value, 1)

    def from_far(value):
        pairs = [(i, i + 1) for i in range(1, devices - 1, 2)]
        return lax.ppermute(value, "ctx", pairs + [(j, i) for i, j in pairs])

    def after(value, earlier):
        return lax.optimization_barrier((value, earlier))[0]

    pair_shape = (2, heads, toks, width)
    slot_shape = (4, heads, slots, width)
    steps = 1
    flat_spec = pl.BlockSpec((toks * heads // steps, width), lambda i: (i, 0))
    pair_spec = pl.BlockSpec((2, heads, toks // steps, width), lambda i: (0, 0, i, 0))
    wide_pair = pltpu.VMEM((2, toks * heads // steps, width), F32)
    kv = pl.pallas_call(
        functools.partial(pack_keys_kernel, heads),
        out_shape=struct(pair_shape, BF),
        scratch_shapes=[wide_pair],
        compiler_params=params(),
        name="pack_keys",
    )(k_flat, v_flat)

    qd, slot_rows = pl.pallas_call(
        functools.partial(pack_queries_kernel, heads, slots),
        grid=(steps,),
        in_specs=[flat_spec, flat_spec, pair_spec, whole((1, count))],
        out_specs=(pair_spec, whole(slot_shape)),
        out_shape=(struct(pair_shape, BF), struct(slot_shape, BF)),
        scratch_shapes=[wide_pair, pltpu.VMEM(slot_shape, F32)],
        compiler_params=params(),
        name="pack_queries",
    )(q_flat, g_flat, kv, pos_row)

    span = toks + 2 * HALF
    bias, compact, expand, place = pl.pallas_call(
        functools.partial(mask_kernel, order, slots, toks * devices),
        out_shape=(
            struct((span, 128), F32),
            struct((count, devices * slots), BF),
            struct((devices * slots, count), BF),
            struct((toks, slots), BF),
        ),
        compiler_params=params(),
        name="masks",
    )(pos_row)

    kv_far, kv_near = from_far(kv), from_near(kv)
    probs_shape = (heads, span, toks)
    acc_shape = (heads, width, toks)
    turned_shape = (heads, width, span)
    sides_shape = (3, heads, width, toks)
    probs, acc, top_sum, key_t, values, sides = pl.pallas_call(
        functools.partial(window_kernel, scale2),
        grid=(heads,),
        in_specs=[per_head(pair_shape, 1)] * 4 + [whole(bias.shape)],
        out_specs=(
            per_head(probs_shape, 0),
            per_head(acc_shape, 0),
            per_head((heads, 2, toks), 0),
            per_head(turned_shape, 0),
            per_head((heads, span, width), 0),
            per_head(sides_shape, 1),
        ),
        out_shape=(
            struct(probs_shape, BF),
            struct(acc_shape, F32),
            struct((heads, 2, toks), F32),
            struct(turned_shape, BF),
            struct((heads, span, width), BF),
            struct(sides_shape, BF),
        ),
        scratch_shapes=[
            pltpu.VMEM((span, width), BF),
            pltpu.VMEM((toks // TILE, 2 * HALF + TILE, TILE), F32),
        ],
        compiler_params=params(),
        cost_estimate=cost(1e6, 1e6),
        name="window",
    )(qd, kv, kv_near, kv_far, bias)
    held = [slot_rows[None]]
    for number, stage in enumerate(stages):
        if stage == [1]:
            held = after(held, top_sum)
        send = jnp.concatenate(held, axis=0) if number else held[0]
        held += [swap(send, mask) for mask in stage]

    row_shape = (4, heads, count, width)
    rows, stats = pl.pallas_call(
        functools.partial(stats_kernel, scale2),
        grid=(heads,),
        in_specs=[whole(compact.shape)]
        + [per_head(part.shape, 2) for part in held]
        + [per_head(pair_shape, 1)],
        out_specs=(per_head(row_shape, 1), per_head((devices, heads, 8, count), 1)),
        out_shape=(struct(row_shape, BF), struct((devices, heads, 8, count), F32)),
        compiler_params=params(),
        cost_estimate=cost(1e6, 1e6),
        name="global_stats",
    )(compact, *held, kv)

    stats = lax.all_to_all(stats, "ctx", 0, 0, tiled=True)

    sum_shape = (devices // 2, 2, heads, slots, width)
    sum_struct = struct(sum_shape, BF)
    qd_late = after(qd, (kv_near, kv_far))
    qd_far, qd_near = from_far(qd_late), from_near(qd_late)

    out, log_dot, dq, dkv, kept_sums, sent_sums = pl.pallas_call(
        functools.partial(local_kernel, scale, scale2),
        grid=(heads,),
        in_specs=[per_head(sides_shape, 1), per_head(turned_shape, 0)]
        + [per_head((heads, span, width), 0), per_head(row_shape, 1)]
        + [per_head(probs_shape, 0), per_head(acc_shape, 0)]
        + [per_head((heads, 2, toks), 0), whole(expand.shape)],
        out_specs=(
            per_head((heads, toks, width), 0),
            per_head((heads, 2, toks), 0),
            per_head((heads, toks, width), 0),
            per_head(pair_shape, 1),
            per_head(sum_shape, 2),
            per_head(sum_shape, 2),
        ),
        out_shape=(
            struct((heads, toks, width), BF),
            struct((heads, 2, toks), F32),
            struct((heads, toks, width), F32),
            struct(pair_shape, F32),
            sum_struct,
            sum_struct,
        ),
        scratch_shapes=[
            pltpu.VMEM((span, toks), BF),
        ],
        compiler_params=params(),
        cost_estimate=cost(1e6, 1e6),
        name="local",
    )(sides, key_t, values, rows, probs, acc, top_sum, expand)
    log_far, log_near = from_far(log_dot), from_near(log_dot)

    dkv, kept_ends, sent_ends = pl.pallas_call(
        functools.partial(global_kernel, scale, scale2),
        grid=(heads,),
        in_specs=[per_head(pair_shape, 1), per_head(row_shape, 1)]
        + [per_head(stats.shape, 1), whole(expand.shape), per_head(pair_shape, 1)]
        + [pl.BlockSpec((1, width, toks), lambda head: (head, 0, HALF // toks))]
        + [pl.BlockSpec((1, 1, width, toks), lambda head: (2, head, 0, 0))],
        out_specs=(per_head(pair_shape, 1), per_head(sum_shape, 2), per_head(sum_shape, 2)),
        out_shape=(struct(pair_shape, F32), sum_struct, sum_struct),
        input_output_aliases={4: 0},
        compiler_params=params(),
        cost_estimate=cost(1e6, 1e6),
        name="global_queries",
    )(kv, rows, after(stats, (log_dot, qd_near, qd_far)), expand, dkv, key_t, sides)
    got_sums = from_near(sent_sums)
    got_ends = from_near(after(sent_ends, (log_near, log_far)))

    first = stages[0]
    parts = pl.pallas_call(
        fold_kernel,
        out_shape=[struct((4, heads, slots, width), BF)] * (devices // 2),
        compiler_params=params(),
        name="fold",
    )(kept_ends, got_ends, kept_sums, got_sums)
    for stage in reversed(stages[1:-1]):
        size = len(parts) // (len(stage) + 1)
        kept = parts[:size]
        for number, mask in enumerate(stage):
            sent = parts[(number + 1) * size : (number + 2) * size]
            kept = [one + swap(other, mask) for one, other in zip(kept, sent)]
        parts = kept
    parts = [parts[0]] + [swap(part, mask) for part, mask in zip(parts[1:], first)]

    dkv = pl.pallas_call(
        functools.partial(rim_kernel, scale, scale2),
        grid=(heads,),
        in_specs=[per_head(pair_shape, 1), pl.BlockSpec((toks, 128), lambda head: (HALF // toks, 0))]
        + [per_head(pair_shape, 1)] * 2
        + [per_head(log_dot.shape, 0)] * 2
        + [per_head(pair_shape, 1)],
        out_specs=per_head(pair_shape, 1),
        out_shape=struct(pair_shape, F32),
        scratch_shapes=[
            pltpu.VMEM((2 * toks, width), BF),
            pltpu.VMEM((2 * toks, width), BF),
            pltpu.VMEM((2, 2, toks), F32),
            pltpu.VMEM((toks, toks + TILE), BF),
            pltpu.VMEM((toks, toks + TILE), BF),
        ],
        compiler_params=params(),
        cost_estimate=cost(1e6, 1e6),
        name="rim",
    )(kv, bias, qd_near, qd_far, log_near, log_far, dkv)

    flat_shape = (toks * heads, width)
    steps = 2
    outs = pl.pallas_call(
        functools.partial(final_kernel, len(parts)),
        grid=(steps,),
        in_specs=[
            pl.BlockSpec((toks // steps, slots), lambda i: (i, 0)),
            pl.BlockSpec((heads, toks // steps, width), lambda i: (0, i, 0)),
            pl.BlockSpec((heads, toks // steps, width), lambda i: (0, i, 0)),
            pl.BlockSpec((2, heads, toks // steps, width), lambda i: (0, 0, i, 0)),
        ]
        + [whole((4, heads, slots, width))] * len(parts),
        out_specs=[pl.BlockSpec((toks * heads // steps, width), lambda i: (i, 0))] * 4,
        out_shape=[struct(flat_shape, kind) for kind in (BF, F32, F32, F32)],
        scratch_shapes=[pltpu.VMEM((toks * heads // steps, width), F32)],
        compiler_params=params(),
        name="final",
    )(place, out, dq, dkv, *parts)
    return tuple(x.reshape(toks, heads, width) for x in outs)


def solution(mesh):
    spec = P("ctx", "head", None)
    return jax.shard_map(
        shards,
        mesh=mesh,
        in_specs=(spec, spec, spec, spec, P()),
        out_specs=(spec, spec, spec, spec),
        check_vma=False,
    )
```

```python
import functools
import math

import jax
import jax.numpy as jnp
from jax import lax
from jax.experimental import pallas as pl
from jax.experimental.pallas import tpu as pltpu
from jax.sharding import PartitionSpec as P

HALF = 512
TILE = 256
NEG = -1e30
LOG2E = 1.0 / math.log(2.0)
VMEM_BYTES = int(63.75 * 1024 * 1024)
BF = jnp.bfloat16
F32 = jnp.float32


def nt(a, b):
    return lax.dot_general(a, b, (((1,), (1,)), ((), ())), preferred_element_type=F32)


def nn(a, b):
    return lax.dot_general(a, b, (((1,), (0,)), ((), ())), preferred_element_type=F32)


def wide(column, width):
    return jnp.concatenate([column] * (width // column.shape[1]), axis=1)


def iota(shape, dim):
    return lax.broadcasted_iota(jnp.int32, shape, dim)


def params():
    return pltpu.CompilerParams(vmem_limit_bytes=VMEM_BYTES)


def as_column(row):
    return jnp.broadcast_to(row, (128, row.shape[1])).T[:, :1]


def pack_keys_kernel(heads, k, v, kv, wide_rows):
    toks = k.shape[0] // heads
    for number, source in enumerate((k, v)):
        wide_rows[number] = source[...].astype(F32)
        for head in range(heads):
            kv[number, head] = wide_rows[number, pl.ds(head, toks, stride=heads), :].astype(BF)


def pack_queries_kernel(heads, slots, q, g, kv, pos_row, qd, slot_rows, wide_rows, acc):
    step = pl.program_id(0)
    toks = q.shape[0] // heads
    row = pos_row[...]
    count = row.shape[1]
    base = lax.axis_index("ctx") * (toks * pl.num_programs(0))
    column = as_column(row)
    tok = iota((count, toks), 1) + (base + step * toks)
    hit = jnp.sum((column == tok).astype(F32), axis=0, keepdims=True)
    rank = jnp.sum(((column >= base) & (column < tok)).astype(F32), axis=0, keepdims=True)
    slot = iota((slots, toks), 0).astype(F32)
    pick = jnp.where((hit > 0) & (rank == slot), 1.0, 0.0).astype(BF)
    tok = iota((toks, count), 0) + (base + step * toks)
    hit_column = jnp.sum((row == tok).astype(F32), axis=1, keepdims=True)
    tables = [[], [kv[0, h] for h in range(heads)], [kv[1, h] for h in range(heads)], []]
    for number, source in ((0, q), (3, g)):
        wide_rows[number // 3] = source[...].astype(F32)
        for head in range(heads):
            rows = wide_rows[number // 3, pl.ds(head, toks, stride=heads), :]
            tables[number].append(rows.astype(BF))
            if number == 0:
                qd[0, head] = rows.astype(BF)
            else:
                qd[1, head] = jnp.where(hit_column > 0, 0.0, rows).astype(BF)
    for number in range(4):
        found = nn(pick, jnp.concatenate(tables[number], axis=1))
        for head in range(heads):
            part = found[:, head * 128 : (head + 1) * 128]
            acc[number, head] = jnp.where(step == 0, part, acc[number, head] + part)

    @pl.when(step == pl.num_programs(0) - 1)
    def _():
        slot_rows[...] = acc[...].astype(BF)


def owner_map(column, owner, toks, slots, shape):
    inside = jnp.sum((column < owner * toks).astype(jnp.int32), axis=0, keepdims=True)
    held = jnp.sum((column < (owner + 1) * toks).astype(jnp.int32), axis=0, keepdims=True) - inside
    slot = iota(shape, 1) % slots
    hot = (iota(shape, 0) == inside + slot) & (slot < held)
    return jnp.where(hot, 1.0, 0.0).astype(BF)


def mask_kernel(order, slots, seq_rows, pos_row, bias, compact, expand, place):
    toks = place.shape[0]
    me = lax.axis_index("ctx")
    base = me * toks
    row = pos_row[...]
    count = row.shape[1]
    column = as_column(row)
    for start in range(0, bias.shape[0], TILE):
        key = iota((TILE, count), 0) + (base - HALF + start)
        hits = jnp.sum((row == key).astype(F32), axis=1, keepdims=True)
        key = key[:, :1]
        out = (hits > 0) | (key < 0) | (key >= seq_rows)
        bias[start : start + TILE, :] = jnp.broadcast_to(jnp.where(out, NEG, 0.0), (TILE, 128))
    tok = iota((toks, count), 0) + base
    hit = jnp.sum((row == tok).astype(F32), axis=1, keepdims=True)
    rank = jnp.sum(((row >= base) & (row < tok)).astype(F32), axis=1, keepdims=True)
    slot = iota((toks, slots), 1).astype(F32)
    place[...] = jnp.where((hit > 0) & (rank == slot), 1.0, 0.0).astype(BF)
    part = iota((1, compact.shape[1]), 1) // slots
    owner = jnp.zeros_like(part)
    for number, relative in enumerate(order):
        owner = jnp.where(part == number, me ^ relative, owner)
    compact[...] = owner_map(column, owner, toks, slots, compact.shape)
    expand[...] = compact[...].astype(F32).T.astype(BF)


def stats_kernel(scale2, compact, *refs):
    parts, (kv, rows, stats) = refs[:-3], refs[-3:]
    pieces = []
    for part in parts:
        for i in range(part.shape[0]):
            pieces.append(jnp.concatenate([part[i, number, 0] for number in range(4)], axis=1))
    packed = nn(compact[...], jnp.concatenate(pieces, axis=0)).astype(BF)
    width = kv.shape[3]
    table = [packed[:, number * width : (number + 1) * width] for number in range(4)]
    for number in range(4):
        rows[number, 0] = table[number]
    queries, _, _, grads = table
    scores = nt(kv[0, 0], queries) * scale2
    top = jnp.max(scores, axis=0, keepdims=True)
    weights = jnp.exp2(scores - top)
    total = jnp.sum(weights, axis=0, keepdims=True)
    dot = jnp.sum(weights * nt(kv[1, 0], grads), axis=0, keepdims=True)
    line = iota(stats.shape[2:], 0)
    found = jnp.where(line == 0, top, jnp.where(line == 1, total, dot))
    for device in range(stats.shape[0]):
        stats[device, 0] = found


def band(scores, low):
    rows, columns = iota(scores.shape, 0), iota(scores.shape, 1)
    return jnp.where(rows <= columns if low else rows >= columns, scores, NEG)


def put_in_slots(expand, tables, kept, sent):
    owners, kinds, _, slots, width = kept.shape
    spread = nn(expand, jnp.concatenate(tables, axis=1)).astype(BF)
    for owner in range(2 * owners):
        for kind in range(kinds):
            (kept if owner < owners else sent)[owner % owners, kind, 0] = spread[
                owner * slots : (owner + 1) * slots, kind * width : (kind + 1) * width
            ]


def fold_kernel(kept_ends, got_ends, kept_sums, got_sums, *outs):
    for part, out in enumerate(outs):
        out[0:2] = (kept_ends[part].astype(F32) + got_ends[part].astype(F32)).astype(BF)
        out[2:4] = (kept_sums[part].astype(F32) + got_sums[part].astype(F32)).astype(BF)


def global_kernel(scale, scale2, kv, rows, stats, expand, before, key_t, value_t, dkv, kept, sent):
    g_query, g_grad = rows[0, 0], rows[3, 0]
    tops = stats[:, 0, 0:1, :]
    top = jnp.max(tops, axis=0)
    factor = jnp.exp2(tops - top[None])
    total = jnp.sum(stats[:, 0, 1:2, :] * factor, axis=0)
    g_dot = jnp.sum(stats[:, 0, 2:3, :] * factor, axis=0) / total
    g_log = top + jnp.log2(total)
    weights = jnp.exp2(nt(kv[0, 0], g_query) * scale2 - g_log)
    narrow = weights.astype(BF)
    slopes = (weights * (nt(kv[1, 0], g_grad) - g_dot)).astype(BF)
    dkv[0, 0] = before[0, 0] + nn(slopes, g_query) * scale
    dkv[1, 0] = before[1, 0] + nn(narrow, g_grad)
    out = nn(value_t[0, 0], narrow).T.astype(BF)
    dq = (nn(key_t[0], slopes) * scale).T.astype(BF)
    put_in_slots(expand[...], (out, dq), kept, sent)


def gather_window(kv, kv_near, kv_far, number, buf):
    toks = kv.shape[2]
    near = 2 * (1 - lax.axis_index("ctx") % 2)
    for block, place in ((kv_near, near), (kv, 1), (kv_far, 2 - near)):
        buf[pl.ds(pl.multiple_of(place * toks, toks), toks), :] = block[number, 0]


def window_kernel(
    scale2, qd, kv, kv_near, kv_far, bias, probs, acc, top_sum, key_t, values, sides, keys, score_buf
):
    toks = kv.shape[2]
    reach = 2 * HALF + TILE
    gather_window(kv, kv_near, kv_far, 0, keys)
    gather_window(kv, kv_near, kv_far, 1, values.at[0])
    key_t[0] = keys[...].T
    value_t = values[0].T
    query_t = qd[0, 0].T
    sides[0, 0] = query_t
    sides[1, 0] = qd[1, 0].T
    sides[2, 0] = value_t[:, HALF : HALF + toks]
    tiles = range(toks // TILE)
    lanes = [slice(tile * TILE, (tile + 1) * TILE) for tile in tiles]
    pieces = range(reach // TILE)
    best, top, total = ([None] * len(tiles) for _ in range(3))

    def score(tile, piece):
        span = slice((tile + piece) * TILE, (tile + piece + 1) * TILE)
        scores = nn(keys[span, :], query_t[:, lanes[tile]]) * scale2
        scores = scores + wide(bias[span, :], TILE)
        if piece == 0:
            scores = band(scores, False)
        elif piece == len(pieces) - 1:
            scores = band(scores, True)
        score_buf[tile, piece * TILE : (piece + 1) * TILE, :] = scores
        part = jnp.max(scores.reshape(TILE // 8, 8, TILE), axis=0)
        best[tile] = part if best[tile] is None else jnp.maximum(best[tile], part)

    def weigh(tile, piece):
        if top[tile] is None:
            top[tile] = jnp.max(best[tile], axis=0, keepdims=True)
        span = slice((tile + piece) * TILE, (tile + piece + 1) * TILE)
        weights = jnp.exp2(score_buf[tile, piece * TILE : (piece + 1) * TILE, :] - top[tile])
        probs[0, span, lanes[tile]] = weights.astype(BF)
        part = jnp.sum(weights.reshape(TILE // 8, 8, TILE), axis=0)
        total[tile] = part if total[tile] is None else total[tile] + part

    for step in range(len(tiles) + 1):
        for piece in pieces:
            if step:
                weigh(step - 1, piece)
            if step < len(tiles):
                score(step, piece)
        if step:
            tile = step - 1
            window = slice(tile * TILE, tile * TILE + reach)
            acc[0, :, lanes[tile]] = nn(value_t[:, window], probs[0, window, lanes[tile]])
            top_sum[0, 0:1, lanes[tile]] = top[tile]
            top_sum[0, 1:2, lanes[tile]] = jnp.sum(total[tile], axis=0, keepdims=True)


def local_kernel(
    scale, scale2, sides, key_t, values, rows, probs, acc, top_sum, expand,
    out, log_dot, dq, dkv, kept, sent, slopes,
):
    toks = acc.shape[2]
    reach = 2 * HALF + TILE
    query_t, grad_t = sides[0, 0], sides[1, 0]
    g_keys, g_values = rows[1, 0], rows[2, 0]
    g_key_t, g_value_t = g_keys.T, g_values.T
    grads = grad_t.astype(F32)
    scores = nn(g_keys, query_t) * scale2
    old = top_sum[0, 0:1, :]
    top = jnp.maximum(old, jnp.max(scores, axis=0, keepdims=True))
    weights = jnp.exp2(scores - top)
    factor = jnp.exp2(old - top)
    total = top_sum[0, 1:2, :] * factor + jnp.sum(weights, axis=0, keepdims=True)
    inverse = 1.0 / total
    g_probs = weights.astype(BF)
    result = (acc[0] * factor + nn(g_value_t, g_probs)) * inverse
    dot = jnp.sum(grads * result, axis=0, keepdims=True)
    log_dot[0, 0:1, :] = top + jnp.log2(total)
    log_dot[0, 1:2, :] = dot
    out[0] = result.T.astype(BF)
    share = factor * inverse
    g_grads = (grads * inverse).astype(BF)
    w_grads = (grads * share).astype(BF)
    g_slopes = (weights * (nn(g_values, g_grads) - dot * inverse)).astype(BF)
    dots = dot * share
    for tile in range(toks // TILE):
        lanes = slice(tile * TILE, (tile + 1) * TILE)
        for piece in range(reach // TILE):
            span = slice((tile + piece) * TILE, (tile + piece + 1) * TILE)
            rise = nn(values[0, span, :], w_grads[:, lanes]) - dots[:, lanes]
            slopes[span, lanes] = (probs[0, span, lanes].astype(F32) * rise).astype(BF)
    for tile in range(toks // TILE):
        lanes = slice(tile * TILE, (tile + 1) * TILE)
        window = slice(tile * TILE, tile * TILE + reach)
        part = nn(key_t[0, :, window], slopes[window, lanes]) + nn(g_key_t, g_slopes[:, lanes])
        dq[0, lanes, :] = (part * scale).T
    own = slice(HALF, HALF + toks)
    dkv[0, 0] = (nt(query_t, slopes[own, :]) * scale).T
    dkv[1, 0] = nt(w_grads, probs[0, own, :]).T
    g_dk = (nt(query_t, g_slopes) * scale).T.astype(BF)
    g_dv = nt(g_grads, g_probs).T.astype(BF)
    put_in_slots(expand[...], (g_dk, g_dv), kept, sent)


def rim_kernel(
    scale, scale2, kv, bias, qd_near, qd_far, log_near, log_far, partial, dkv,
    queries, grads, logs, probs, slopes,
):
    toks = kv.shape[2]
    reach = toks + TILE
    near = 1 - lax.axis_index("ctx") % 2
    for qd, log_dot, place in ((qd_near, log_near, near), (qd_far, log_far, 1 - near)):
        spot = pl.ds(pl.multiple_of(place * toks, toks), toks)
        queries[spot, :] = qd[0, 0]
        grads[spot, :] = qd[1, 0]
        logs[place] = log_dot[0]
    for k_tile in range(toks // TILE):
        span = slice(k_tile * TILE, (k_tile + 1) * TILE)
        key = kv[0, 0, span, :]
        value = kv[1, 0, span, :]
        key_bias = wide(bias[span, :], TILE)
        for piece in range(reach // TILE):
            start = (k_tile + piece) * TILE
            side, lanes = start // toks, slice(start % toks, start % toks + TILE)
            scores = nt(key, queries[start : start + TILE, :]) * scale2 + key_bias
            if piece == 0:
                scores = band(scores, True)
            elif piece == reach // TILE - 1:
                scores = band(scores, False)
            weights = jnp.exp2(scores - logs[side, 0:1, lanes])
            slope = weights * (nt(value, grads[start : start + TILE, :]) - logs[side, 1:2, lanes])
            spot = slice(piece * TILE, (piece + 1) * TILE)
            probs[span, spot] = weights.astype(BF)
            slopes[span, spot] = slope.astype(BF)
        window = slice(k_tile * TILE, k_tile * TILE + reach)
        dkv[0, 0, span, :] = partial[0, 0, span, :] + nn(slopes[span, :], queries[window, :]) * scale
        dkv[1, 0, span, :] = partial[1, 0, span, :] + nn(probs[span, :], grads[window, :])


def final_kernel(
    sources, place, out, dq, dkv, *refs
):
    parts, refs = refs[:sources], refs[sources:]
    attn, query_grad, key_grad, value_grad, wide_rows = refs
    heads, toks = out.shape[0], out.shape[1]
    hot = place[...]
    is_global = jnp.sum(hot.astype(F32), axis=1, keepdims=True) > 0
    for head in range(heads):
        rows = pl.ds(head, toks, stride=heads)
        tables = []
        for kind in range(4):
            table = parts[0][kind, head].astype(F32)
            for part in parts[1:]:
                table = table + part[kind, head].astype(F32)
            tables.append(table.astype(BF))
        width = out.shape[2]
        added = nn(hot, jnp.concatenate(tables, axis=1))
        added = [added[:, i * width : (i + 1) * width] for i in range(4)]
        wide_rows[rows, :] = jnp.where(is_global, added[0], out[head].astype(F32))
        query_grad[rows, :] = dq[head] + added[1]
        key_grad[rows, :] = dkv[0, head] + added[2]
        value_grad[rows, :] = dkv[1, head] + added[3]
    attn[...] = wide_rows[...].astype(BF)


def cost(flops, moved, exps=0):
    return pl.CostEstimate(flops=int(flops), bytes_accessed=int(moved), transcendentals=int(exps))


def struct(shape, dtype):
    return jax.ShapeDtypeStruct(shape, dtype)


def whole(shape):
    return pl.BlockSpec(shape, lambda head: (0,) * len(shape))


def per_head(shape, dim, first=0):
    block = tuple(1 if i == dim else size for i, size in enumerate(shape))
    return pl.BlockSpec(
        block, lambda head: tuple(head + first if i == dim else 0 for i in range(len(shape)))
    )


def shards(query_rows, key_rows, value_rows, out_grad, global_pos):
    toks, heads, width = query_rows.shape
    count = global_pos.shape[0]
    devices = lax.axis_size("ctx")
    slots = max(16, 2 * count // devices)
    scale = width ** (-0.5)
    scale2 = scale * LOG2E
    bits = devices.bit_length() - 1
    stages = [
        [mask << low for mask in range(1, 1 << min(2, bits - low))] for low in range(1, bits, 2)
    ] + [[1]]
    order = [0]
    for stage in stages:
        order = order + [one ^ mask for mask in stage for one in order]
    pos_row = global_pos.reshape(1, count)
    q_flat, k_flat, v_flat, g_flat = (
        x.reshape(toks * heads, width) for x in (query_rows, key_rows, value_rows, out_grad)
    )

    def swap(value, mask):
        return lax.ppermute(value, "ctx", [(i, i ^ mask) for i in range(devices)])

    def from_near(value):
        return swap(value, 1)

    def from_far(value):
        pairs = [(i, i + 1) for i in range(1, devices - 1, 2)]
        return lax.ppermute(value, "ctx", pairs + [(j, i) for i, j in pairs])

    def after(value, earlier):
        return lax.optimization_barrier((value, earlier))[0]

    pair_shape = (2, heads, toks, width)
    slot_shape = (4, heads, slots, width)
    steps = 1
    flat_spec = pl.BlockSpec((toks * heads // steps, width), lambda i: (i, 0))
    pair_spec = pl.BlockSpec((2, heads, toks // steps, width), lambda i: (0, 0, i, 0))
    wide_pair = pltpu.VMEM((2, toks * heads // steps, width), F32)
    kv = pl.pallas_call(
        functools.partial(pack_keys_kernel, heads),
        out_shape=struct(pair_shape, BF),
        scratch_shapes=[wide_pair],
        compiler_params=params(),
        name="pack_keys",
    )(k_flat, v_flat)

    qd, slot_rows = pl.pallas_call(
        functools.partial(pack_queries_kernel, heads, slots),
        grid=(steps,),
        in_specs=[flat_spec, flat_spec, pair_spec, whole((1, count))],
        out_specs=(pair_spec, whole(slot_shape)),
        out_shape=(struct(pair_shape, BF), struct(slot_shape, BF)),
        scratch_shapes=[wide_pair, pltpu.VMEM(slot_shape, F32)],
        compiler_params=params(),
        name="pack_queries",
    )(q_flat, g_flat, kv, pos_row)

    span = toks + 2 * HALF
    bias, compact, expand, place = pl.pallas_call(
        functools.partial(mask_kernel, order, slots, toks * devices),
        out_shape=(
            struct((span, 128), F32),
            struct((count, devices * slots), BF),
            struct((devices * slots, count), BF),
            struct((toks, slots), BF),
        ),
        compiler_params=params(),
        name="masks",
    )(pos_row)

    kv_far, kv_near = from_far(kv), from_near(kv)
    probs_shape = (heads, span, toks)
    acc_shape = (heads, width, toks)
    turned_shape = (heads, width, span)
    sides_shape = (3, heads, width, toks)
    probs, acc, top_sum, key_t, values, sides = pl.pallas_call(
        functools.partial(window_kernel, scale2),
        grid=(heads,),
        in_specs=[per_head(pair_shape, 1)] * 4 + [whole(bias.shape)],
        out_specs=(
            per_head(probs_shape, 0),
            per_head(acc_shape, 0),
            per_head((heads, 2, toks), 0),
            per_head(turned_shape, 0),
            per_head((heads, span, width), 0),
            per_head(sides_shape, 1),
        ),
        out_shape=(
            struct(probs_shape, BF),
            struct(acc_shape, F32),
            struct((heads, 2, toks), F32),
            struct(turned_shape, BF),
            struct((heads, span, width), BF),
            struct(sides_shape, BF),
        ),
        scratch_shapes=[
            pltpu.VMEM((span, width), BF),
            pltpu.VMEM((toks // TILE, 2 * HALF + TILE, TILE), F32),
        ],
        compiler_params=params(),
        cost_estimate=cost(1e6, 1e6),
        name="window",
    )(qd, kv, kv_near, kv_far, bias)
    held = [slot_rows[None]]
    for number, stage in enumerate(stages):
        if stage == [1]:
            held = after(held, top_sum)
        send = jnp.concatenate(held, axis=0) if number else held[0]
        held += [swap(send, mask) for mask in stage]
        if devices == 8 and not number:
            pairs = [(0, 6), (1, 7), (6, 0), (7, 1)]
            straight = lax.ppermute(send, "ctx", pairs)
            turned = lax.ppermute(held[2], "ctx", [(6, 4), (7, 5), (0, 2), (1, 3)])
            straight, turned = after((straight, turned), top_sum)
            held[3] = straight + turned

    row_shape = (4, heads, count, width)
    rows, stats = pl.pallas_call(
        functools.partial(stats_kernel, scale2),
        grid=(heads,),
        in_specs=[whole(compact.shape)]
        + [per_head(part.shape, 2) for part in held]
        + [per_head(pair_shape, 1)],
        out_specs=(per_head(row_shape, 1), per_head((devices, heads, 8, count), 1)),
        out_shape=(struct(row_shape, BF), struct((devices, heads, 8, count), F32)),
        compiler_params=params(),
        cost_estimate=cost(1e6, 1e6),
        name="global_stats",
    )(compact, *held, kv)

    stats = lax.all_to_all(stats, "ctx", 0, 0, tiled=True)

    sum_shape = (devices // 2, 2, heads, slots, width)
    sum_struct = struct(sum_shape, BF)
    qd_late = after(qd, (kv_near, kv_far))
    qd_far, qd_near = from_far(qd_late), from_near(qd_late)

    out, log_dot, dq, dkv, kept_sums, sent_sums = pl.pallas_call(
        functools.partial(local_kernel, scale, scale2),
        grid=(heads,),
        in_specs=[per_head(sides_shape, 1), per_head(turned_shape, 0)]
        + [per_head((heads, span, width), 0), per_head(row_shape, 1)]
        + [per_head(probs_shape, 0), per_head(acc_shape, 0)]
        + [per_head((heads, 2, toks), 0), whole(expand.shape)],
        out_specs=(
            per_head((heads, toks, width), 0),
            per_head((heads, 2, toks), 0),
            per_head((heads, toks, width), 0),
            per_head(pair_shape, 1),
            per_head(sum_shape, 2),
            per_head(sum_shape, 2),
        ),
        out_shape=(
            struct((heads, toks, width), BF),
            struct((heads, 2, toks), F32),
            struct((heads, toks, width), F32),
            struct(pair_shape, F32),
            sum_struct,
            sum_struct,
        ),
        scratch_shapes=[
            pltpu.VMEM((span, toks), BF),
        ],
        compiler_params=params(),
        cost_estimate=cost(1e6, 1e6),
        name="local",
    )(sides, key_t, values, rows, probs, acc, top_sum, expand)
    log_far, log_near = from_far(log_dot), from_near(log_dot)

    dkv, kept_ends, sent_ends = pl.pallas_call(
        functools.partial(global_kernel, scale, scale2),
        grid=(heads,),
        in_specs=[per_head(pair_shape, 1), per_head(row_shape, 1)]
        + [per_head(stats.shape, 1), whole(expand.shape), per_head(pair_shape, 1)]
        + [pl.BlockSpec((1, width, toks), lambda head: (head, 0, HALF // toks))]
        + [pl.BlockSpec((1, 1, width, toks), lambda head: (2, head, 0, 0))],
        out_specs=(per_head(pair_shape, 1), per_head(sum_shape, 2), per_head(sum_shape, 2)),
        out_shape=(struct(pair_shape, F32), sum_struct, sum_struct),
        input_output_aliases={4: 0},
        compiler_params=params(),
        cost_estimate=cost(1e6, 1e6),
        name="global_queries",
    )(kv, rows, after(stats, (log_dot, qd_near, qd_far)), expand, dkv, key_t, sides)
    got_sums = from_near(sent_sums)
    got_ends = from_near(after(sent_ends, (log_near, log_far)))

    first = stages[0]
    parts = pl.pallas_call(
        fold_kernel,
        out_shape=[struct((4, heads, slots, width), BF)] * (devices // 2),
        compiler_params=params(),
        name="fold",
    )(kept_ends, got_ends, kept_sums, got_sums)
    for stage in reversed(stages[1:-1]):
        size = len(parts) // (len(stage) + 1)
        kept = parts[:size]
        for number, mask in enumerate(stage):
            sent = parts[(number + 1) * size : (number + 2) * size]
            kept = [one + swap(other, mask) for one, other in zip(kept, sent)]
        parts = kept
    parts = [parts[0]] + [swap(part, mask) for part, mask in zip(parts[1:], first)]

    dkv = pl.pallas_call(
        functools.partial(rim_kernel, scale, scale2),
        grid=(heads,),
        in_specs=[per_head(pair_shape, 1), pl.BlockSpec((toks, 128), lambda head: (HALF // toks, 0))]
        + [per_head(pair_shape, 1)] * 2
        + [per_head(log_dot.shape, 0)] * 2
        + [per_head(pair_shape, 1)],
        out_specs=per_head(pair_shape, 1),
        out_shape=struct(pair_shape, F32),
        scratch_shapes=[
            pltpu.VMEM((2 * toks, width), BF),
            pltpu.VMEM((2 * toks, width), BF),
            pltpu.VMEM((2, 2, toks), F32),
            pltpu.VMEM((toks, toks + TILE), BF),
            pltpu.VMEM((toks, toks + TILE), BF),
        ],
        compiler_params=params(),
        cost_estimate=cost(1e6, 1e6),
        name="rim",
    )(kv, bias, qd_near, qd_far, log_near, log_far, dkv)

    flat_shape = (toks * heads, width)
    steps = 2
    outs = pl.pallas_call(
        functools.partial(final_kernel, len(parts)),
        grid=(steps,),
        in_specs=[
            pl.BlockSpec((toks // steps, slots), lambda i: (i, 0)),
            pl.BlockSpec((heads, toks // steps, width), lambda i: (0, i, 0)),
            pl.BlockSpec((heads, toks // steps, width), lambda i: (0, i, 0)),
            pl.BlockSpec((2, heads, toks // steps, width), lambda i: (0, 0, i, 0)),
        ]
        + [whole((4, heads, slots, width))] * len(parts),
        out_specs=[pl.BlockSpec((toks * heads // steps, width), lambda i: (i, 0))] * 4,
        out_shape=[struct(flat_shape, kind) for kind in (BF, F32, F32, F32)],
        scratch_shapes=[pltpu.VMEM((toks * heads // steps, width), F32)],
        compiler_params=params(),
        name="final",
    )(place, out, dq, dkv, *parts)
    return tuple(x.reshape(toks, heads, width) for x in outs)


def solution(mesh):
    spec = P("ctx", "head", None)
    return jax.shard_map(
        shards,
        mesh=mesh,
        in_specs=(spec, spec, spec, spec, P()),
        out_specs=(spec, spec, spec, spec),
        check_vma=False,
    )
```

```python
import functools
import math

import jax
import jax.numpy as jnp
from jax import lax
from jax.experimental import pallas as pl
from jax.experimental.pallas import tpu as pltpu
from jax.sharding import PartitionSpec as P

HALF = 512
TILE = 256
NEG = -1e30
LOG2E = 1.0 / math.log(2.0)
VMEM_BYTES = int(63.75 * 1024 * 1024)
BF = jnp.bfloat16
F32 = jnp.float32


def nt(a, b):
    return lax.dot_general(a, b, (((1,), (1,)), ((), ())), preferred_element_type=F32)


def nn(a, b):
    return lax.dot_general(a, b, (((1,), (0,)), ((), ())), preferred_element_type=F32)


def wide(column, width):
    return jnp.concatenate([column] * (width // column.shape[1]), axis=1)


def iota(shape, dim):
    return lax.broadcasted_iota(jnp.int32, shape, dim)


def params():
    return pltpu.CompilerParams(vmem_limit_bytes=VMEM_BYTES)


def as_column(row):
    return jnp.broadcast_to(row, (128, row.shape[1])).T[:, :1]


def pack_keys_kernel(heads, k, v, kv, wide_rows):
    toks = k.shape[0] // heads
    for number, source in enumerate((k, v)):
        wide_rows[number] = source[...].astype(F32)
        for head in range(heads):
            kv[number, head] = wide_rows[number, pl.ds(head, toks, stride=heads), :].astype(BF)


def pack_queries_kernel(heads, slots, q, g, kv, pos_row, qd, slot_rows, wide_rows, acc):
    step = pl.program_id(0)
    toks = q.shape[0] // heads
    row = pos_row[...]
    count = row.shape[1]
    base = lax.axis_index("ctx") * (toks * pl.num_programs(0))
    column = as_column(row)
    tok = iota((count, toks), 1) + (base + step * toks)
    hit = jnp.sum((column == tok).astype(F32), axis=0, keepdims=True)
    rank = jnp.sum(((column >= base) & (column < tok)).astype(F32), axis=0, keepdims=True)
    slot = iota((slots, toks), 0).astype(F32)
    pick = jnp.where((hit > 0) & (rank == slot), 1.0, 0.0).astype(BF)
    tok = iota((toks, count), 0) + (base + step * toks)
    hit_column = jnp.sum((row == tok).astype(F32), axis=1, keepdims=True)
    tables = [[], [kv[0, h] for h in range(heads)], [kv[1, h] for h in range(heads)], []]
    for number, source in ((0, q), (3, g)):
        wide_rows[number // 3] = source[...].astype(F32)
        for head in range(heads):
            rows = wide_rows[number // 3, pl.ds(head, toks, stride=heads), :]
            tables[number].append(rows.astype(BF))
            if number == 0:
                qd[0, head] = rows.astype(BF)
            else:
                qd[1, head] = jnp.where(hit_column > 0, 0.0, rows).astype(BF)
    for number in range(4):
        found = nn(pick, jnp.concatenate(tables[number], axis=1))
        for head in range(heads):
            part = found[:, head * 128 : (head + 1) * 128]
            acc[number, head] = jnp.where(step == 0, part, acc[number, head] + part)

    @pl.when(step == pl.num_programs(0) - 1)
    def _():
        slot_rows[...] = acc[...].astype(BF)


def owner_map(column, owner, toks, slots, shape):
    inside = jnp.sum((column < owner * toks).astype(jnp.int32), axis=0, keepdims=True)
    held = jnp.sum((column < (owner + 1) * toks).astype(jnp.int32), axis=0, keepdims=True) - inside
    slot = iota(shape, 1) % slots
    hot = (iota(shape, 0) == inside + slot) & (slot < held)
    return jnp.where(hot, 1.0, 0.0).astype(BF)


def mask_kernel(order, slots, seq_rows, pos_row, bias, compact, expand, place):
    toks = place.shape[0]
    me = lax.axis_index("ctx")
    base = me * toks
    row = pos_row[...]
    count = row.shape[1]
    column = as_column(row)
    for start in range(0, bias.shape[0], TILE):
        key = iota((TILE, count), 0) + (base - HALF + start)
        hits = jnp.sum((row == key).astype(F32), axis=1, keepdims=True)
        key = key[:, :1]
        out = (hits > 0) | (key < 0) | (key >= seq_rows)
        bias[start : start + TILE, :] = jnp.broadcast_to(jnp.where(out, NEG, 0.0), (TILE, 128))
    tok = iota((toks, count), 0) + base
    hit = jnp.sum((row == tok).astype(F32), axis=1, keepdims=True)
    rank = jnp.sum(((row >= base) & (row < tok)).astype(F32), axis=1, keepdims=True)
    slot = iota((toks, slots), 1).astype(F32)
    place[...] = jnp.where((hit > 0) & (rank == slot), 1.0, 0.0).astype(BF)
    part = iota((1, compact.shape[1]), 1) // slots
    owner = jnp.zeros_like(part)
    for number, relative in enumerate(order):
        owner = jnp.where(part == number, me ^ relative, owner)
    compact[...] = owner_map(column, owner, toks, slots, compact.shape)
    expand[...] = compact[...].astype(F32).T.astype(BF)


def stats_kernel(scale2, compact, *refs):
    parts, (kv, rows, stats) = refs[:-3], refs[-3:]
    pieces = []
    for part in parts:
        for i in range(part.shape[0]):
            pieces.append(jnp.concatenate([part[i, number, 0] for number in range(4)], axis=1))
    packed = nn(compact[...], jnp.concatenate(pieces, axis=0)).astype(BF)
    width = kv.shape[3]
    table = [packed[:, number * width : (number + 1) * width] for number in range(4)]
    for number in range(4):
        rows[number, 0] = table[number]
    queries, _, _, grads = table
    scores = nt(kv[0, 0], queries) * scale2
    top = jnp.max(scores, axis=0, keepdims=True)
    weights = jnp.exp2(scores - top)
    total = jnp.sum(weights, axis=0, keepdims=True)
    dot = jnp.sum(weights * nt(kv[1, 0], grads), axis=0, keepdims=True)
    line = iota(stats.shape[2:], 0)
    found = jnp.where(line == 0, top, jnp.where(line == 1, total, dot))
    for device in range(stats.shape[0]):
        stats[device, 0] = found


def band(scores, low):
    rows, columns = iota(scores.shape, 0), iota(scores.shape, 1)
    return jnp.where(rows <= columns if low else rows >= columns, scores, NEG)


def put_in_slots(expand, tables, kept, sent):
    owners, kinds, _, slots, width = kept.shape
    spread = nn(expand, jnp.concatenate(tables, axis=1)).astype(BF)
    for owner in range(2 * owners):
        for kind in range(kinds):
            (kept if owner < owners else sent)[owner % owners, kind, 0] = spread[
                owner * slots : (owner + 1) * slots, kind * width : (kind + 1) * width
            ]


def fold_kernel(kept_ends, got_ends, kept_sums, got_sums, *outs):
    for part, out in enumerate(outs):
        out[0:2] = (kept_ends[part].astype(F32) + got_ends[part].astype(F32)).astype(BF)
        out[2:4] = (kept_sums[part].astype(F32) + got_sums[part].astype(F32)).astype(BF)


def global_kernel(scale, scale2, kv, rows, stats, expand, before, key_t, value_t, dkv, kept, sent):
    g_query, g_grad = rows[0, 0], rows[3, 0]
    tops = stats[:, 0, 0:1, :]
    top = jnp.max(tops, axis=0)
    factor = jnp.exp2(tops - top[None])
    total = jnp.sum(stats[:, 0, 1:2, :] * factor, axis=0)
    g_dot = jnp.sum(stats[:, 0, 2:3, :] * factor, axis=0) / total
    g_log = top + jnp.log2(total)
    weights = jnp.exp2(nt(kv[0, 0], g_query) * scale2 - g_log)
    narrow = weights.astype(BF)
    slopes = (weights * (nt(kv[1, 0], g_grad) - g_dot)).astype(BF)
    dkv[0, 0] = before[0, 0] + nn(slopes, g_query) * scale
    dkv[1, 0] = before[1, 0] + nn(narrow, g_grad)
    out = nn(value_t[0, 0], narrow).T.astype(BF)
    dq = (nn(key_t[0], slopes) * scale).T.astype(BF)
    put_in_slots(expand[...], (out, dq), kept, sent)


def gather_window(kv, kv_near, kv_far, number, buf):
    toks = kv.shape[2]
    near = 2 * (1 - lax.axis_index("ctx") % 2)
    for block, place in ((kv_near, near), (kv, 1), (kv_far, 2 - near)):
        buf[pl.ds(pl.multiple_of(place * toks, toks), toks), :] = block[number, 0]


def window_kernel(
    scale2, qd, kv, kv_near, kv_far, bias, probs, acc, top_sum, key_t, values, sides, keys, score_buf
):
    toks = kv.shape[2]
    reach = 2 * HALF + TILE
    gather_window(kv, kv_near, kv_far, 0, keys)
    gather_window(kv, kv_near, kv_far, 1, values.at[0])
    key_t[0] = keys[...].T
    value_t = values[0].T
    query_t = qd[0, 0].T
    sides[0, 0] = query_t
    sides[1, 0] = qd[1, 0].T
    sides[2, 0] = value_t[:, HALF : HALF + toks]
    tiles = range(toks // TILE)
    lanes = [slice(tile * TILE, (tile + 1) * TILE) for tile in tiles]
    pieces = range(reach // TILE)
    best, top, total = ([None] * len(tiles) for _ in range(3))

    def score(tile, piece):
        span = slice((tile + piece) * TILE, (tile + piece + 1) * TILE)
        scores = nn(keys[span, :], query_t[:, lanes[tile]]) * scale2
        scores = scores + wide(bias[span, :], TILE)
        if piece == 0:
            scores = band(scores, False)
        elif piece == len(pieces) - 1:
            scores = band(scores, True)
        score_buf[tile, piece * TILE : (piece + 1) * TILE, :] = scores
        part = jnp.max(scores.reshape(TILE // 8, 8, TILE), axis=0)
        best[tile] = part if best[tile] is None else jnp.maximum(best[tile], part)

    def weigh(tile, piece):
        if top[tile] is None:
            top[tile] = jnp.max(best[tile], axis=0, keepdims=True)
        span = slice((tile + piece) * TILE, (tile + piece + 1) * TILE)
        weights = jnp.exp2(score_buf[tile, piece * TILE : (piece + 1) * TILE, :] - top[tile])
        probs[0, span, lanes[tile]] = weights.astype(BF)
        part = jnp.sum(weights.reshape(TILE // 8, 8, TILE), axis=0)
        total[tile] = part if total[tile] is None else total[tile] + part

    for step in range(len(tiles) + 1):
        for piece in pieces:
            if step:
                weigh(step - 1, piece)
            if step < len(tiles):
                score(step, piece)
        if step:
            tile = step - 1
            window = slice(tile * TILE, tile * TILE + reach)
            acc[0, :, lanes[tile]] = nn(value_t[:, window], probs[0, window, lanes[tile]])
            top_sum[0, 0:1, lanes[tile]] = top[tile]
            top_sum[0, 1:2, lanes[tile]] = jnp.sum(total[tile], axis=0, keepdims=True)


def local_kernel(
    scale, scale2, sides, key_t, values, rows, probs, acc, top_sum, expand,
    out, log_dot, dq, dkv, kept, sent, slopes,
):
    toks = acc.shape[2]
    reach = 2 * HALF + TILE
    query_t, grad_t = sides[0, 0], sides[1, 0]
    g_keys, g_values = rows[1, 0], rows[2, 0]
    g_key_t, g_value_t = g_keys.T, g_values.T
    grads = grad_t.astype(F32)
    scores = nn(g_keys, query_t) * scale2
    old = top_sum[0, 0:1, :]
    top = jnp.maximum(old, jnp.max(scores, axis=0, keepdims=True))
    weights = jnp.exp2(scores - top)
    factor = jnp.exp2(old - top)
    total = top_sum[0, 1:2, :] * factor + jnp.sum(weights, axis=0, keepdims=True)
    inverse = 1.0 / total
    g_probs = weights.astype(BF)
    result = (acc[0] * factor + nn(g_value_t, g_probs)) * inverse
    dot = jnp.sum(grads * result, axis=0, keepdims=True)
    log_dot[0, 0:1, :] = top + jnp.log2(total)
    log_dot[0, 1:2, :] = dot
    out[0] = result.T.astype(BF)
    share = factor * inverse
    g_grads = (grads * inverse).astype(BF)
    w_grads = (grads * share).astype(BF)
    g_slopes = (weights * (nn(g_values, g_grads) - dot * inverse)).astype(BF)
    dots = dot * share
    for tile in range(toks // TILE):
        lanes = slice(tile * TILE, (tile + 1) * TILE)
        for piece in range(reach // TILE):
            span = slice((tile + piece) * TILE, (tile + piece + 1) * TILE)
            rise = nn(values[0, span, :], w_grads[:, lanes]) - dots[:, lanes]
            slopes[span, lanes] = (probs[0, span, lanes].astype(F32) * rise).astype(BF)
    for tile in range(toks // TILE):
        lanes = slice(tile * TILE, (tile + 1) * TILE)
        window = slice(tile * TILE, tile * TILE + reach)
        part = nn(key_t[0, :, window], slopes[window, lanes]) + nn(g_key_t, g_slopes[:, lanes])
        dq[0, lanes, :] = (part * scale).T
    own = slice(HALF, HALF + toks)
    dkv[0, 0] = (nt(query_t, slopes[own, :]) * scale).T
    dkv[1, 0] = nt(w_grads, probs[0, own, :]).T
    g_dk = (nt(query_t, g_slopes) * scale).T.astype(BF)
    g_dv = nt(g_grads, g_probs).T.astype(BF)
    put_in_slots(expand[...], (g_dk, g_dv), kept, sent)


def rim_kernel(
    scale, scale2, kv, bias, qd_near, qd_far, log_near, log_far, partial, dkv,
    queries, grads, logs, probs, slopes,
):
    toks = kv.shape[2]
    reach = toks + TILE
    near = 1 - lax.axis_index("ctx") % 2
    for qd, log_dot, place in ((qd_near, log_near, near), (qd_far, log_far, 1 - near)):
        spot = pl.ds(pl.multiple_of(place * toks, toks), toks)
        queries[spot, :] = qd[0, 0]
        grads[spot, :] = qd[1, 0]
        logs[place] = log_dot[0]
    for k_tile in range(toks // TILE):
        span = slice(k_tile * TILE, (k_tile + 1) * TILE)
        key = kv[0, 0, span, :]
        value = kv[1, 0, span, :]
        key_bias = wide(bias[span, :], TILE)
        for piece in range(reach // TILE):
            start = (k_tile + piece) * TILE
            side, lanes = start // toks, slice(start % toks, start % toks + TILE)
            scores = nt(key, queries[start : start + TILE, :]) * scale2 + key_bias
            if piece == 0:
                scores = band(scores, True)
            elif piece == reach // TILE - 1:
                scores = band(scores, False)
            weights = jnp.exp2(scores - logs[side, 0:1, lanes])
            slope = weights * (nt(value, grads[start : start + TILE, :]) - logs[side, 1:2, lanes])
            spot = slice(piece * TILE, (piece + 1) * TILE)
            probs[span, spot] = weights.astype(BF)
            slopes[span, spot] = slope.astype(BF)
        window = slice(k_tile * TILE, k_tile * TILE + reach)
        dkv[0, 0, span, :] = partial[0, 0, span, :] + nn(slopes[span, :], queries[window, :]) * scale
        dkv[1, 0, span, :] = partial[1, 0, span, :] + nn(probs[span, :], grads[window, :])


def final_kernel(
    sources, place, out, dq, dkv, *refs
):
    parts, refs = refs[:sources], refs[sources:]
    attn, query_grad, key_grad, value_grad, wide_rows = refs
    heads, toks = out.shape[0], out.shape[1]
    hot = place[...]
    is_global = jnp.sum(hot.astype(F32), axis=1, keepdims=True) > 0
    for head in range(heads):
        rows = pl.ds(head, toks, stride=heads)
        tables = []
        for kind in range(4):
            table = parts[0][kind, head].astype(F32)
            for part in parts[1:]:
                table = table + part[kind, head].astype(F32)
            tables.append(table.astype(BF))
        width = out.shape[2]
        added = nn(hot, jnp.concatenate(tables, axis=1))
        added = [added[:, i * width : (i + 1) * width] for i in range(4)]
        wide_rows[rows, :] = jnp.where(is_global, added[0], out[head].astype(F32))
        query_grad[rows, :] = dq[head] + added[1]
        key_grad[rows, :] = dkv[0, head] + added[2]
        value_grad[rows, :] = dkv[1, head] + added[3]
    attn[...] = wide_rows[...].astype(BF)


def cost(flops, moved, exps=0):
    return pl.CostEstimate(flops=int(flops), bytes_accessed=int(moved), transcendentals=int(exps))


def struct(shape, dtype):
    return jax.ShapeDtypeStruct(shape, dtype)


def whole(shape):
    return pl.BlockSpec(shape, lambda head: (0,) * len(shape))


def per_head(shape, dim, first=0):
    block = tuple(1 if i == dim else size for i, size in enumerate(shape))
    return pl.BlockSpec(
        block, lambda head: tuple(head + first if i == dim else 0 for i in range(len(shape)))
    )


def shards(query_rows, key_rows, value_rows, out_grad, global_pos):
    toks, heads, width = query_rows.shape
    count = global_pos.shape[0]
    devices = lax.axis_size("ctx")
    slots = max(16, 2 * count // devices)
    scale = width ** (-0.5)
    scale2 = scale * LOG2E
    bits = devices.bit_length() - 1
    stages = [
        [mask << low for mask in range(1, 1 << min(2, bits - low))] for low in range(1, bits, 2)
    ] + [[1]]
    order = [0]
    for stage in stages:
        order = order + [one ^ mask for mask in stage for one in order]
    pos_row = global_pos.reshape(1, count)
    q_flat, k_flat, v_flat, g_flat = (
        x.reshape(toks * heads, width) for x in (query_rows, key_rows, value_rows, out_grad)
    )

    def swap(value, mask):
        return lax.ppermute(value, "ctx", [(i, i ^ mask) for i in range(devices)])

    def from_near(value):
        return swap(value, 1)

    def from_far(value):
        pairs = [(i, i + 1) for i in range(1, devices - 1, 2)]
        return lax.ppermute(value, "ctx", pairs + [(j, i) for i, j in pairs])

    def after(value, earlier):
        return lax.optimization_barrier((value, earlier))[0]

    pair_shape = (2, heads, toks, width)
    slot_shape = (4, heads, slots, width)
    steps = 1
    flat_spec = pl.BlockSpec((toks * heads // steps, width), lambda i: (i, 0))
    pair_spec = pl.BlockSpec((2, heads, toks // steps, width), lambda i: (0, 0, i, 0))
    wide_pair = pltpu.VMEM((2, toks * heads // steps, width), F32)
    kv = pl.pallas_call(
        functools.partial(pack_keys_kernel, heads),
        out_shape=struct(pair_shape, BF),
        scratch_shapes=[wide_pair],
        compiler_params=params(),
        name="pack_keys",
    )(k_flat, v_flat)

    qd, slot_rows = pl.pallas_call(
        functools.partial(pack_queries_kernel, heads, slots),
        grid=(steps,),
        in_specs=[flat_spec, flat_spec, pair_spec, whole((1, count))],
        out_specs=(pair_spec, whole(slot_shape)),
        out_shape=(struct(pair_shape, BF), struct(slot_shape, BF)),
        scratch_shapes=[wide_pair, pltpu.VMEM(slot_shape, F32)],
        compiler_params=params(),
        name="pack_queries",
    )(q_flat, g_flat, kv, pos_row)

    span = toks + 2 * HALF
    bias, compact, expand, place = pl.pallas_call(
        functools.partial(mask_kernel, order, slots, toks * devices),
        out_shape=(
            struct((span, 128), F32),
            struct((count, devices * slots), BF),
            struct((devices * slots, count), BF),
            struct((toks, slots), BF),
        ),
        compiler_params=params(),
        name="masks",
    )(pos_row)

    kv_far, kv_near = from_far(kv), from_near(kv)
    probs_shape = (heads, span, toks)
    acc_shape = (heads, width, toks)
    turned_shape = (heads, width, span)
    sides_shape = (3, heads, width, toks)
    probs, acc, top_sum, key_t, values, sides = pl.pallas_call(
        functools.partial(window_kernel, scale2),
        grid=(heads,),
        in_specs=[per_head(pair_shape, 1)] * 4 + [whole(bias.shape)],
        out_specs=(
            per_head(probs_shape, 0),
            per_head(acc_shape, 0),
            per_head((heads, 2, toks), 0),
            per_head(turned_shape, 0),
            per_head((heads, span, width), 0),
            per_head(sides_shape, 1),
        ),
        out_shape=(
            struct(probs_shape, BF),
            struct(acc_shape, F32),
            struct((heads, 2, toks), F32),
            struct(turned_shape, BF),
            struct((heads, span, width), BF),
            struct(sides_shape, BF),
        ),
        scratch_shapes=[
            pltpu.VMEM((span, width), BF),
            pltpu.VMEM((toks // TILE, 2 * HALF + TILE, TILE), F32),
        ],
        compiler_params=params(),
        cost_estimate=cost(1e6, 1e6),
        name="window",
    )(qd, kv, kv_near, kv_far, bias)
    held = [slot_rows[None]]
    for number, stage in enumerate(stages):
        if stage == [1]:
            held = after(held, top_sum)
        send = jnp.concatenate(held, axis=0) if number else held[0]
        held += [swap(send, mask) for mask in stage]

    row_shape = (4, heads, count, width)
    rows, stats = pl.pallas_call(
        functools.partial(stats_kernel, scale2),
        grid=(heads,),
        in_specs=[whole(compact.shape)]
        + [per_head(part.shape, 2) for part in held]
        + [per_head(pair_shape, 1)],
        out_specs=(per_head(row_shape, 1), per_head((devices, heads, 8, count), 1)),
        out_shape=(struct(row_shape, BF), struct((devices, heads, 8, count), F32)),
        compiler_params=params(),
        cost_estimate=cost(1e6, 1e6),
        name="global_stats",
    )(compact, *held, kv)

    stats = lax.all_to_all(stats, "ctx", 0, 0, tiled=True)

    sum_shape = (devices // 2, 2, heads, slots, width)
    sum_struct = struct(sum_shape, BF)
    qd_late = after(qd, (kv_near, kv_far))
    qd_far, qd_near = from_far(qd_late), from_near(qd_late)

    out, log_dot, dq, dkv, kept_sums, sent_sums = pl.pallas_call(
        functools.partial(local_kernel, scale, scale2),
        grid=(heads,),
        in_specs=[per_head(sides_shape, 1), per_head(turned_shape, 0)]
        + [per_head((heads, span, width), 0), per_head(row_shape, 1)]
        + [per_head(probs_shape, 0), per_head(acc_shape, 0)]
        + [per_head((heads, 2, toks), 0), whole(expand.shape)],
        out_specs=(
            per_head((heads, toks, width), 0),
            per_head((heads, 2, toks), 0),
            per_head((heads, toks, width), 0),
            per_head(pair_shape, 1),
            per_head(sum_shape, 2),
            per_head(sum_shape, 2),
        ),
        out_shape=(
            struct((heads, toks, width), BF),
            struct((heads, 2, toks), F32),
            struct((heads, toks, width), F32),
            struct(pair_shape, F32),
            sum_struct,
            sum_struct,
        ),
        scratch_shapes=[
            pltpu.VMEM((span, toks), BF),
        ],
        compiler_params=params(),
        cost_estimate=cost(1e6, 1e6),
        name="local",
    )(sides, key_t, values, rows, probs, acc, top_sum, expand)
    log_far, log_near = from_far(log_dot), from_near(log_dot)

    dkv, kept_ends, sent_ends = pl.pallas_call(
        functools.partial(global_kernel, scale, scale2),
        grid=(heads,),
        in_specs=[per_head(pair_shape, 1), per_head(row_shape, 1)]
        + [per_head(stats.shape, 1), whole(expand.shape), per_head(pair_shape, 1)]
        + [pl.BlockSpec((1, width, toks), lambda head: (head, 0, HALF // toks))]
        + [pl.BlockSpec((1, 1, width, toks), lambda head: (2, head, 0, 0))],
        out_specs=(per_head(pair_shape, 1), per_head(sum_shape, 2), per_head(sum_shape, 2)),
        out_shape=(struct(pair_shape, F32), sum_struct, sum_struct),
        input_output_aliases={4: 0},
        compiler_params=params(),
        cost_estimate=cost(1e6, 1e6),
        name="global_queries",
    )(kv, rows, after(stats, (log_dot, qd_near, qd_far)), expand, dkv, key_t, sides)
    got_sums = from_near(sent_sums)
    got_ends = from_near(sent_ends)

    first = stages[0]
    parts = pl.pallas_call(
        fold_kernel,
        out_shape=[struct((4, heads, slots, width), BF)] * (devices // 2),
        compiler_params=params(),
        name="fold",
    )(kept_ends, got_ends, kept_sums, got_sums)
    for stage in reversed(stages[1:-1]):
        size = len(parts) // (len(stage) + 1)
        kept = parts[:size]
        for number, mask in enumerate(stage):
            sent = parts[(number + 1) * size : (number + 2) * size]
            kept = [one + swap(other, mask) for one, other in zip(kept, sent)]
        parts = kept
    parts = [parts[0]] + [swap(part, mask) for part, mask in zip(parts[1:], first)]

    dkv = pl.pallas_call(
        functools.partial(rim_kernel, scale, scale2),
        grid=(heads,),
        in_specs=[per_head(pair_shape, 1), pl.BlockSpec((toks, 128), lambda head: (HALF // toks, 0))]
        + [per_head(pair_shape, 1)] * 2
        + [per_head(log_dot.shape, 0)] * 2
        + [per_head(pair_shape, 1)],
        out_specs=per_head(pair_shape, 1),
        out_shape=struct(pair_shape, F32),
        scratch_shapes=[
            pltpu.VMEM((2 * toks, width), BF),
            pltpu.VMEM((2 * toks, width), BF),
            pltpu.VMEM((2, 2, toks), F32),
            pltpu.VMEM((toks, toks + TILE), BF),
            pltpu.VMEM((toks, toks + TILE), BF),
        ],
        compiler_params=params(),
        cost_estimate=cost(1e6, 1e6),
        name="rim",
    )(kv, bias, qd_near, qd_far, log_near, log_far, dkv)

    flat_shape = (toks * heads, width)
    steps = 2
    outs = pl.pallas_call(
        functools.partial(final_kernel, len(parts)),
        grid=(steps,),
        in_specs=[
            pl.BlockSpec((toks // steps, slots), lambda i: (i, 0)),
            pl.BlockSpec((heads, toks // steps, width), lambda i: (0, i, 0)),
            pl.BlockSpec((heads, toks // steps, width), lambda i: (0, i, 0)),
            pl.BlockSpec((2, heads, toks // steps, width), lambda i: (0, 0, i, 0)),
        ]
        + [whole((4, heads, slots, width))] * len(parts),
        out_specs=[pl.BlockSpec((toks * heads // steps, width), lambda i: (i, 0))] * 4,
        out_shape=[struct(flat_shape, kind) for kind in (BF, F32, F32, F32)],
        scratch_shapes=[pltpu.VMEM((toks * heads // steps, width), F32)],
        compiler_params=params(),
        name="final",
    )(place, out, dq, dkv, *parts)
    return tuple(x.reshape(toks, heads, width) for x in outs)


def solution(mesh):
    spec = P("ctx", "head", None)
    return jax.shard_map(
        shards,
        mesh=mesh,
        in_specs=(spec, spec, spec, spec, P()),
        out_specs=(spec, spec, spec, spec),
        check_vma=False,
    )
```
